32 devices in a mesh: pb: 4 (over y, x), pa: 8 (over z, core).
Axes of the slice: x: 2, y: 2, z: 4, core: 2. Of those that a mesh axis runs over, the one named last changes fastest.
Arguments:
- decoder_states: bfloat16 [4, 16, 64, 1024], P('pb', 'pa'), may hold values from -6 to 6
- encoder_memory: bfloat16 [4, 16, 512, 1024], P('pb', 'pa'), may hold values from -6 to 6
- target_tokens: int32 [4, 16, 64], P('pb', 'pa'), may hold values from 0 to 50303
- log_prior: float32 [4, 16], P('pb', 'pa'), may hold values from -24 to 2
- slot_counts: int32 [4], P('pb'), may hold values from 2 to 16, as said below
- slot_mask: int32 [4, 16], P('pb', 'pa'), may hold values from 0 to 1, as said below
- self_packed: bfloat16 [1024, 3072], P('pa'), may hold values from -0.1875 to 0.1875
- self_output: bfloat16 [1024, 1024], P('pa'), may hold values from -0.75 to 0.75
- cross_query: bfloat16 [1024, 1024], P('pa'), may hold values from -0.1875 to 0.1875
- cross_memory: bfloat16 [1024, 2048], P('pa'), may hold values from -0.1875 to 0.1875
- cross_output: bfloat16 [1024, 1024], P('pa'), may hold values from -1.5 to 1.5
- feed_expand: bfloat16 [1024, 4096], P('pa'), may hold values from -0.1875 to 0.1875
- feed_reduce: bfloat16 [4096, 1024], P('pa'), may hold values from -0.09375 to 0.09375
- embedding: bfloat16 [50304, 1024], P('pa'), may hold values from -0.40625 to 0.40625
- norm_gains: bfloat16 [3, 1024], P(None, 'pa'), may hold values from 0.5 to 1.5
- norm_shifts: bfloat16 [3, 1024], P(None, 'pa'), may hold values from -1.75 to 1.75
Outputs:
- mean_loss: float32 [], replicated
- grad_states: float32 [4, 16, 64, 1024], P('pb', 'pa')
- grad_memory: float32 [4, 16, 512, 1024], P('pb', 'pa')
- grad_prior: float32 [4, 16], P('pb', 'pa')
- grad_self_packed: float32 [1024, 3072], P('pa')
- grad_self_output: float32 [1024, 1024], P('pa')
- grad_cross_query: float32 [1024, 1024], P('pa')
- grad_cross_memory: float32 [1024, 2048], P('pa')
- grad_cross_output: float32 [1024, 1024], P('pa')
- grad_feed_expand: float32 [1024, 4096], P('pa')
- grad_feed_reduce: float32 [4096, 1024], P('pa')
- grad_embedding: float32 [50304, 1024], P('pa')
- grad_norm_gains: float32 [3, 1024], P(None, 'pa')
- grad_norm_shifts: float32 [3, 1024], P(None, 'pa')
The draws below stay inside these ranges and needn't reach their ends.
Inputs may be any that keep to these rules, and one draw needn't show every extreme that they name: `slot_counts`: for one question, drawn from the seed, all 16 slots are counted. `slot_mask`: slots 0 and 1 of every question are 1.
All inputs are finite; a program needn't handle non-finite values.
Results may differ from the reference program's by a relative error of at most 0.019.
Values may be sent and summed in bfloat16 or wider, within the bound.
A program may use at most 256 MiB of HBM per device.

```python
import math
from functools import partial
import jax
import jax.numpy as jnp
from jax import lax

WIDTH = 1024
HEADS = 16
HEAD_DIM = 64
FFN_UNITS = 4096
VOCAB = 50304
TGT_LEN = 64
MEM_LEN = 512
QUESTIONS = 4
SLOTS = 16


def draw_log_prior(key, part):
    key = jax.random.fold_in(key, 13)
    rising = jnp.arange(QUESTIONS, dtype=jnp.float32) / max(QUESTIONS - 1, 1)
    offset = -(2.0 + 18.0 * rising)
    noise = jnp.clip(jax.random.normal(key, (QUESTIONS, SLOTS), jnp.float32), -4.0, 4.0)
    return (noise + offset[:, None]).astype(jnp.float32)


def draw_slot_counts(key, part):
    key = jax.random.fold_in(key, 11)
    first_key, second_key = jax.random.split(key)
    drawn = jax.random.randint(first_key, (QUESTIONS,), 2, SLOTS + 1)
    filled = jax.random.randint(second_key, (), 0, QUESTIONS)
    return jnp.where(jnp.arange(QUESTIONS) == filled, SLOTS, drawn).astype(jnp.int32)


def draw_slot_mask(key, part):
    key = jax.random.fold_in(key, 12)
    levels = jax.random.randint(key, (QUESTIONS, SLOTS), 0, 4)
    keeping = (levels > 0) | (jnp.arange(SLOTS)[None, :] < 2)
    return keeping.astype(jnp.int32)


def draw_embedding(key, part):
    key = jax.random.fold_in(key, 14)
    rising = jnp.arange(VOCAB, dtype=jnp.float32) / max(VOCAB - 1, 1)
    row_scale = (1.1 + 2.1 * rising) / WIDTH ** 0.5
    noise = jnp.clip(jax.random.normal(key, (VOCAB, WIDTH), jnp.float32), -4.0, 4.0)
    return (noise * row_scale[:, None]).astype(jnp.bfloat16)


def set_ends(values, rng, smallest, largest):
    longest = values.shape.index(max(values.shape))
    spots = []
    for shift in (0, 1):
        where = [jax.random.randint(jax.random.fold_in(rng, axis), (), 0, length) for axis, length in enumerate(values.shape)]
        where[longest] = (where[longest] + shift) % values.shape[longest]
        spots.append(tuple(where))
    return values.at[spots[0]].set(smallest).at[spots[1]].set(largest)


def steps_of(own_key, dims, shards, least, top_value):
    gain = 1.0
    for position, parts in shards:
        heights = jax.random.uniform(jax.random.fold_in(jax.random.fold_in(own_key, 6), position), (parts,), jnp.float32, least / len(shards), top_value / len(shards))
        gain = gain * jnp.repeat(jnp.exp(heights), dims[position] // parts).reshape((-1,) + (1,) * (len(dims) - 1 - position))
    return gain


def gaussian(stream_key, dims, width, reach, cuts=(), held_as=jnp.bfloat16):
    array = jax.random.normal(stream_key, dims, jnp.float32) * width
    if len(cuts) > 0:
        array = steps_of(stream_key, dims, cuts, -0.22, 0.18) * array
    return jnp.clip(array, min=-reach, max=reach).astype(held_as)


def setup_inputs(seed: int = 0) -> dict:
    arg_keys = jax.random.split(jax.random.key(seed), 17)
    return {
        "decoder_states": gaussian(arg_keys[0], (QUESTIONS, SLOTS, TGT_LEN, WIDTH), 1.0, 6.0, ((0, 4), (1, 8))),
        "encoder_memory": gaussian(arg_keys[1], (QUESTIONS, SLOTS, MEM_LEN, WIDTH), 1.0, 6.0, ((0, 4), (1, 8))),
        "target_tokens": set_ends(jax.random.randint(arg_keys[2], (QUESTIONS, SLOTS, TGT_LEN), 0, VOCAB), jax.random.fold_in(arg_keys[2], 1), 0, VOCAB - 1).astype(jnp.int32),
        "log_prior": draw_log_prior(jax.random.fold_in(arg_keys[16], 71), 0),
        "slot_counts": draw_slot_counts(jax.random.fold_in(arg_keys[16], 71), 0),
        "slot_mask": draw_slot_mask(jax.random.fold_in(arg_keys[16], 71), 0),
        "self_packed": gaussian(arg_keys[6], (WIDTH, 3 * WIDTH), WIDTH ** -0.5, 0.1875, ((0, 8),)),
        "self_output": gaussian(arg_keys[7], (WIDTH, WIDTH), (WIDTH // 16) ** -0.5, 0.75, ((0, 8),)),
        "cross_query": gaussian(arg_keys[8], (WIDTH, WIDTH), WIDTH ** -0.5, 0.1875, ((0, 8),)),
        "cross_memory": gaussian(arg_keys[9], (WIDTH, 2 * WIDTH), WIDTH ** -0.5, 0.1875, ((0, 8),)),
        "cross_output": gaussian(arg_keys[10], (WIDTH, WIDTH), (WIDTH // 64) ** -0.5, 1.5, ((0, 8),)),
        "feed_expand": gaussian(arg_keys[11], (WIDTH, FFN_UNITS), WIDTH ** -0.5, 0.1875, ((0, 8),)),
        "feed_reduce": gaussian(arg_keys[12], (FFN_UNITS, WIDTH), FFN_UNITS ** -0.5, 0.09375, ((0, 8),)),
        "embedding": draw_embedding(jax.random.fold_in(arg_keys[16], 71), 0),
        "norm_gains": jnp.clip(1.0 + 0.1 * jax.random.normal(arg_keys[14], (3, WIDTH), jnp.float32), 0.5, 1.5).astype(jnp.bfloat16),
        "norm_shifts": gaussian(arg_keys[15], (3, WIDTH), 0.3, 1.75, ((1, 8),)),
    }


@jax.custom_vjp
def low(v):
    return lax.optimization_barrier(v.astype(jnp.bfloat16)).astype(jnp.float32)

@jax.custom_vjp
def low_back(v):
    return v

def low_keep(v):
    return (low(v), None)

def low_pass(kept, grad):
    return (grad,)

def back_keep(v):
    return (v, None)

def back_low(kept, grad):
    return (low(grad),)
low.defvjp(low_keep, low_pass)
low_back.defvjp(back_keep, back_low)
EPSILON = 1e-05
NEGATIVE = -1e+30
HIGHEST = lax.Precision.HIGHEST

def matmul(matrix_left, matrix_right):
    return jnp.matmul(matrix_left, matrix_right, precision=HIGHEST)

def layer_norm(values, gain_row, shift_row):
    centre = values - lax.optimization_barrier(jnp.mean(values, -1, keepdims=True))
    inverse = lax.rsqrt(lax.optimization_barrier(jnp.mean(centre * centre, -1, keepdims=True)) + EPSILON)
    return centre * inverse * gain_row + shift_row

def split_heads(values):
    return values.reshape(values.shape[0], values.shape[1], HEADS, HEAD_DIM)

def attention(queries, key_rows, values, allowed):
    score_scale = 1.0 / math.sqrt(HEAD_DIM)
    scores = low_back(jnp.einsum('nqhd,nkhd->nhqk', queries, key_rows, precision=HIGHEST) * score_scale)
    if allowed is not None:
        scores = jnp.where(allowed, scores, NEGATIVE)
    probs_low = low(jax.nn.softmax(scores, axis=-1))
    context = low(low_back(jnp.einsum('nhqk,nkhd->nqhd', probs_low, values, precision=HIGHEST)))
    return context.reshape(context.shape[0], context.shape[1], WIDTH)

def decoder_layer(inputs, encoded, params):
    packed_weight, output_weight, query_weight, memory_weight, cross_weight, expand_weight, reduce_weight, gains, shifts = params
    packed = low(low_back(matmul(inputs, packed_weight)))
    allowed = jnp.arange(TGT_LEN)[:, None] >= jnp.arange(TGT_LEN)[None, :]
    context = attention(split_heads(packed[..., :WIDTH]), split_heads(packed[..., WIDTH:2 * WIDTH]), split_heads(packed[..., 2 * WIDTH:]), allowed)
    first_norm = layer_norm(inputs + low_back(matmul(context, output_weight)), gains[0], shifts[0])
    cross_queries = low(low_back(matmul(low(first_norm), query_weight)))
    memory_pairs = low(low_back(matmul(encoded, memory_weight)))
    cross_context = attention(split_heads(cross_queries), split_heads(memory_pairs[..., :WIDTH]), split_heads(memory_pairs[..., WIDTH:]), None)
    second = layer_norm(first_norm + low_back(matmul(cross_context, cross_weight)), gains[1], shifts[1])
    inner_pre = low_back(matmul(low(second), expand_weight))
    active = low(jax.nn.gelu(inner_pre, approximate=False))
    third_norm = layer_norm(second + low_back(matmul(active, reduce_weight)), gains[2], shifts[2])
    return low(third_norm)

def head_block(embed_float, pieces):
    hidden_rows, token_rows = pieces
    logits = low_back(jnp.dot(hidden_rows, embed_float.T, precision=HIGHEST))
    picked = jnp.take_along_axis(logits, token_rows[:, None], axis=1)[:, 0]
    return picked - jax.nn.logsumexp(logits, axis=-1)

def group_log_probs(params, embed_float, inputs, encoded, token_rows):
    hidden = decoder_layer(inputs, encoded, params).reshape(-1, WIDTH)
    row_count = hidden.shape[0]
    block_rows = math.gcd(row_count, 512)
    pieces = (hidden.reshape(row_count // block_rows, block_rows, WIDTH), token_rows.reshape(row_count // block_rows, block_rows))
    log_probs = lax.map(jax.checkpoint(partial(head_block, embed_float)), pieces)
    return log_probs.reshape(inputs.shape[0], TGT_LEN)

def reference(decoder_states, encoder_memory, target_tokens, log_prior, slot_counts, slot_mask, self_packed, self_output, cross_query, cross_memory, cross_output, feed_expand, feed_reduce, embedding, norm_gains, norm_shifts):
    params = tuple((weight.astype(jnp.float32) for weight in (self_packed, self_output, cross_query, cross_memory, cross_output, feed_expand, feed_reduce, norm_gains, norm_shifts)))
    total_slots = QUESTIONS * SLOTS
    group_size = math.gcd(total_slots, max(1, 4096 // TGT_LEN))
    group_count = total_slots // group_size
    token_groups = target_tokens.reshape(group_count, group_size, TGT_LEN)

    def objective(states_float, memory_float, prior_float, weights, embed_float):
        inputs = states_float.reshape(group_count, group_size, TGT_LEN, WIDTH)
        encoded = memory_float.reshape(group_count, group_size, MEM_LEN, WIDTH)
        group_step = jax.checkpoint(partial(group_log_probs, weights, embed_float))

        def scan_step(carried, pieces):
            return (carried, group_step(pieces[0], pieces[1], pieces[2]))
        _, log_probs = lax.scan(scan_step, jnp.zeros((), jnp.float32), (inputs, encoded, token_groups))
        log_probs = log_probs.reshape(QUESTIONS, SLOTS, TGT_LEN)
        scores = prior_float + lax.optimization_barrier(jnp.mean(log_probs, -1))
        usable = (slot_mask == 1) & (jnp.arange(SLOTS)[None, :] < slot_counts[:, None])
        marginal = jax.nn.logsumexp(jnp.where(usable, scores, NEGATIVE), axis=1)
        return (-(SLOTS * TGT_LEN) * jnp.sum(marginal), -jnp.mean(marginal))
    value, pullback, loss_value = jax.vjp(objective, decoder_states.astype(jnp.float32), encoder_memory.astype(jnp.float32), log_prior, params, embedding.astype(jnp.float32), has_aux=True)
    grad_states, grad_memory, grad_prior, grad_params, grad_embedding = pullback(jnp.ones_like(value))
    return (loss_value, grad_states, grad_memory, grad_prior, grad_params[0], grad_params[1], grad_params[2], grad_params[3], grad_params[4], grad_params[5], grad_params[6], grad_embedding, grad_params[7], grad_params[8])
```

```python
import math

import jax
import jax.numpy as jnp
from jax import lax
from jax.sharding import PartitionSpec as P

HEADS = 16
HEAD_DIM = 64


EPSILON = 1e-05
NEGATIVE = -1e30
BFLOAT = jnp.bfloat16


def merged(part, axis, combine):
    gathered = jax.tree.map(lambda a: lax.all_gather(a, axis), part)

    def take(source):
        return jax.tree.map(lambda a: lax.dynamic_index_in_dim(a, source, 0, False), gathered)

    return lax.fori_loop(
        1, lax.axis_size(axis), lambda source, state: combine(state, take(source)), take(0)
    )


def matmul(matrix_left, matrix_right):
    return lax.dot_general(
        matrix_left,
        matrix_right,
        (((matrix_left.ndim - 1,), (0,)), ((), ())),
        preferred_element_type=jnp.float32,
    )


def matmul_back(matrix_left, matrix_right):
    return lax.dot_general(
        matrix_left,
        matrix_right,
        (((matrix_left.ndim - 1,), (1,)), ((), ())),
        preferred_element_type=jnp.float32,
    )


def outer_sum(matrix_left, matrix_right):
    flat_left = matrix_left.reshape(-1, matrix_left.shape[-1])
    flat_right = matrix_right.reshape(-1, matrix_right.shape[-1])
    return lax.dot_general(
        flat_left, flat_right, (((0,), (0,)), ((), ())), preferred_element_type=jnp.float32
    )


def split_heads(values):
    return values.reshape(values.shape[0], values.shape[1], HEADS, HEAD_DIM)


def join_heads(values):
    return values.reshape(values.shape[0], values.shape[1], HEADS * HEAD_DIM)


def exact_gelu(values):
    return jax.nn.gelu(values, approximate=False)


def norm_forward(values, gain_row, shift_row):
    centre = values - jnp.mean(values, -1, keepdims=True)
    inverse = lax.rsqrt(jnp.mean(centre * centre, -1, keepdims=True) + EPSILON)
    normed = centre * inverse
    return (normed * gain_row.astype(jnp.float32) + shift_row.astype(jnp.float32), normed, inverse)


def norm_backward(upstream, normed, inverse, gain_row):
    scaled = upstream * gain_row.astype(jnp.float32)
    mean_scaled = jnp.mean(scaled, -1, keepdims=True)
    along_normed = jnp.mean(scaled * normed, -1, keepdims=True)
    grad_values = inverse * (scaled - mean_scaled - normed * along_normed)
    model_width = upstream.shape[-1]
    grad_gain = jnp.sum((upstream * normed).reshape(-1, model_width), 0)
    grad_shift = jnp.sum(upstream.reshape(-1, model_width), 0)
    return (grad_values, grad_gain, grad_shift)


def score_block(queries, key_rows, causal):
    scores = jnp.einsum(
        "nqhd,nkhd->nhqk", queries, key_rows, preferred_element_type=jnp.float32
    ) * (1.0 / math.sqrt(HEAD_DIM))
    if causal:
        length = queries.shape[1]
        allowed = lax.broadcasted_iota(jnp.int32, (length, length), 0) >= lax.broadcasted_iota(
            jnp.int32, (length, length), 1
        )
        scores = jnp.where(allowed, scores, NEGATIVE)
    return scores


def attend(queries, key_rows, values, causal):
    scores = score_block(queries, key_rows, causal)
    highest = jnp.max(scores, -1, keepdims=True)
    totals = jnp.sum(jnp.exp(scores - highest), -1, keepdims=True)
    logsum = highest + jnp.log(totals)
    probs_low = jnp.exp(scores - logsum).astype(BFLOAT)
    context = jnp.einsum(
        "nhqk,nkhd->nqhd", probs_low, values, preferred_element_type=jnp.float32
    ).astype(BFLOAT)
    return (join_heads(context), logsum)


def attend_back(grad_context, queries, key_rows, values, logsum, causal):
    score_scale = 1.0 / math.sqrt(HEAD_DIM)
    probs_full = jnp.exp(score_block(queries, key_rows, causal) - logsum)
    grad_heads = split_heads(grad_context)
    grad_probs = jnp.einsum(
        "nqhd,nkhd->nhqk", grad_heads, values, preferred_element_type=jnp.float32
    )
    grad_values = jnp.einsum(
        "nhqk,nqhd->nkhd", probs_full.astype(BFLOAT), grad_heads, preferred_element_type=jnp.float32
    ).astype(BFLOAT)
    grad_scores = (
        probs_full * (grad_probs - jnp.sum(probs_full * grad_probs, -1, keepdims=True))
    ).astype(BFLOAT)
    grad_queries = (
        jnp.einsum("nhqk,nkhd->nqhd", grad_scores, key_rows, preferred_element_type=jnp.float32)
        * score_scale
    ).astype(BFLOAT)
    grad_keys = (
        jnp.einsum("nhqk,nqhd->nkhd", grad_scores, queries, preferred_element_type=jnp.float32)
        * score_scale
    ).astype(BFLOAT)
    return (join_heads(grad_queries), join_heads(grad_keys), join_heads(grad_values))


def layer_forward(inputs, encoded, weights):
    (
        packed_weight,
        output_weight,
        query_weight,
        memory_weight,
        cross_weight,
        expand_weight,
        reduce_weight,
        gains,
        shifts,
    ) = weights
    model_width = inputs.shape[-1]
    packed = matmul(inputs, packed_weight).astype(BFLOAT)
    context, self_logsum = attend(
        split_heads(packed[..., :model_width]),
        split_heads(packed[..., model_width : 2 * model_width]),
        split_heads(packed[..., 2 * model_width :]),
        True,
    )
    first_norm, first_normed, first_inverse = norm_forward(
        inputs.astype(jnp.float32) + matmul(context, output_weight), gains[0], shifts[0]
    )
    first_low = first_norm.astype(BFLOAT)
    cross_queries = matmul(first_low, query_weight).astype(BFLOAT)
    memory_pairs = matmul(encoded, memory_weight).astype(BFLOAT)
    cross_context, cross_logsum = attend(
        split_heads(cross_queries),
        split_heads(memory_pairs[..., :model_width]),
        split_heads(memory_pairs[..., model_width:]),
        False,
    )
    second, second_normed, second_inverse = norm_forward(
        first_norm + matmul(cross_context, cross_weight), gains[1], shifts[1]
    )
    second_low = second.astype(BFLOAT)
    inner_pre = matmul(second_low, expand_weight)
    active = exact_gelu(inner_pre).astype(BFLOAT)
    third_norm, third_normed, third_inverse = norm_forward(
        second + matmul(active, reduce_weight), gains[2], shifts[2]
    )
    stored = (
        packed,
        context,
        self_logsum,
        first_normed,
        first_inverse,
        first_low,
        cross_queries,
        memory_pairs,
        cross_context,
        cross_logsum,
        second_normed,
        second_inverse,
        second_low,
        inner_pre,
        active,
        third_normed,
        third_inverse,
    )
    return (third_norm.astype(BFLOAT), stored)


def layer_backward(grad_third, inputs, encoded, weights, stored):
    (
        packed_weight,
        output_weight,
        query_weight,
        memory_weight,
        cross_weight,
        expand_weight,
        reduce_weight,
        gains,
        shifts,
    ) = weights
    (
        packed,
        context,
        self_logsum,
        first_normed,
        first_inverse,
        first_low,
        cross_queries,
        memory_pairs,
        cross_context,
        cross_logsum,
        second_normed,
        second_inverse,
        second_low,
        inner_pre,
        active,
        third_normed,
        third_inverse,
    ) = stored
    model_width = inputs.shape[-1]
    grad_res3, gain_three, shift_three = norm_backward(
        grad_third, third_normed, third_inverse, gains[2]
    )
    grad_output = grad_res3.astype(BFLOAT)
    grad_reduce = outer_sum(active, grad_output)
    grad_active = matmul_back(grad_output, reduce_weight)
    _, gelu_pull = jax.vjp(exact_gelu, inner_pre)
    grad_inner = gelu_pull(grad_active)[0].astype(BFLOAT)
    grad_expand = outer_sum(second_low, grad_inner)
    grad_second = grad_res3 + matmul_back(grad_inner, expand_weight)
    grad_res2, gain_two, shift_two = norm_backward(
        grad_second, second_normed, second_inverse, gains[1]
    )
    grad_mixed = grad_res2.astype(BFLOAT)
    grad_cross_weight = outer_sum(cross_context, grad_mixed)
    grad_cross_context = matmul_back(grad_mixed, cross_weight).astype(BFLOAT)
    grad_cross_queries, grad_memory_keys, grad_memory_values = attend_back(
        grad_cross_context,
        split_heads(cross_queries),
        split_heads(memory_pairs[..., :model_width]),
        split_heads(memory_pairs[..., model_width:]),
        cross_logsum,
        False,
    )
    grad_query_weight = outer_sum(first_low, grad_cross_queries)
    grad_first = grad_res2 + matmul_back(grad_cross_queries, query_weight)
    grad_pairs = jnp.concatenate([grad_memory_keys, grad_memory_values], -1)
    grad_memory_weight = outer_sum(encoded, grad_pairs)
    grad_encoded = matmul_back(grad_pairs, memory_weight)
    grad_res1, gain_one, shift_one = norm_backward(
        grad_first, first_normed, first_inverse, gains[0]
    )
    grad_merged = grad_res1.astype(BFLOAT)
    grad_output_weight = outer_sum(context, grad_merged)
    grad_context = matmul_back(grad_merged, output_weight).astype(BFLOAT)
    grad_queries, grad_keys, grad_values = attend_back(
        grad_context,
        split_heads(packed[..., :model_width]),
        split_heads(packed[..., model_width : 2 * model_width]),
        split_heads(packed[..., 2 * model_width :]),
        self_logsum,
        True,
    )
    grad_packed = jnp.concatenate([grad_queries, grad_keys, grad_values], -1)
    grad_packed_weight = outer_sum(inputs, grad_packed)
    grad_inputs = grad_res1 + matmul_back(grad_packed, packed_weight)
    grad_gains = jnp.stack([gain_one, gain_two, gain_three])
    grad_shifts = jnp.stack([shift_one, shift_two, shift_three])
    return (
        grad_inputs,
        grad_encoded,
        (
            grad_packed_weight,
            grad_output_weight,
            grad_query_weight,
            grad_memory_weight,
            grad_cross_weight,
            grad_expand,
            grad_reduce,
            grad_gains,
            grad_shifts,
        ),
    )


def combine_scores(former, latter):
    highest = jnp.maximum(former[0], latter[0])
    totals = former[1] * jnp.exp(former[0] - highest) + latter[1] * jnp.exp(latter[0] - highest)
    return (highest, totals, former[2] + latter[2])


def combine_pairs(former, latter):
    highest = jnp.maximum(former[0], latter[0])
    totals = former[1] * jnp.exp(former[0] - highest) + latter[1] * jnp.exp(latter[0] - highest)
    return (highest, totals)


def per_device(
    decoder_states,
    encoder_memory,
    target_tokens,
    log_prior,
    slot_counts,
    slot_mask,
    self_packed,
    self_output,
    cross_query,
    cross_memory,
    cross_output,
    feed_expand,
    feed_reduce,
    embedding,
    norm_gains,
    norm_shifts,
):
    weights = (
        lax.all_gather(self_packed, "pa", axis=0, tiled=True),
        lax.all_gather(self_output, "pa", axis=0, tiled=True),
        lax.all_gather(cross_query, "pa", axis=0, tiled=True),
        lax.all_gather(cross_memory, "pa", axis=0, tiled=True),
        lax.all_gather(cross_output, "pa", axis=0, tiled=True),
        lax.all_gather(feed_expand, "pa", axis=0, tiled=True),
        lax.all_gather(feed_reduce, "pa", axis=0, tiled=True),
        lax.all_gather(norm_gains, "pa", axis=1, tiled=True),
        lax.all_gather(norm_shifts, "pa", axis=1, tiled=True),
    )
    questions, slots_here, length, model_width = decoder_states.shape
    mem_length = encoder_memory.shape[2]
    batch_size = questions * slots_here
    inputs = decoder_states.reshape(batch_size, length, model_width)
    encoded = encoder_memory.reshape(batch_size, mem_length, model_width)
    third_low, stored = layer_forward(inputs, encoded, weights)
    tokens_here = batch_size * length
    rows_all, tokens_all = (
        lax.all_gather(third_low.reshape(tokens_here, model_width), "pa", axis=0, tiled=True),
        lax.all_gather(target_tokens.reshape(tokens_here), "pa", axis=0, tiled=True),
    )
    total_rows = rows_all.shape[0]
    block_rows = min(total_rows, 2048)
    block_count = total_rows // block_rows
    vocab_start = lax.axis_index("pa") * embedding.shape[0]
    row_blocks = rows_all.reshape(block_count, block_rows, model_width)
    token_blocks = tokens_all.reshape(block_count, block_rows)

    def vocab_logits(hidden_rows, token_rows):
        logits = matmul_back(hidden_rows, embedding)
        column = lax.broadcasted_iota(jnp.int32, logits.shape, 1) + vocab_start
        return (logits, column == token_rows[:, None])

    def vocab_partial(pieces):
        logits, chosen = vocab_logits(pieces[0], pieces[1])
        highest = jnp.max(logits, -1)
        totals = jnp.sum(jnp.exp(logits - highest[:, None]), -1)
        picked = jnp.sum(jnp.where(chosen, logits, 0.0), -1)
        return (highest, totals, picked)

    highest, totals, picked = lax.map(vocab_partial, (row_blocks, token_blocks))
    highest, totals, picked = merged(
        (highest.reshape(total_rows), totals.reshape(total_rows), picked.reshape(total_rows)),
        "pa",
        combine_scores,
    )
    row_logsum = highest + jnp.log(totals)
    own_start = lax.axis_index("pa") * tokens_here
    own_logsum = lax.dynamic_slice_in_dim(row_logsum, own_start, tokens_here)
    own_picked = lax.dynamic_slice_in_dim(picked, own_start, tokens_here)
    log_probs = (own_picked - own_logsum).reshape(questions, slots_here, length)
    scores = log_prior + jnp.mean(log_probs, -1)
    slot_index = lax.axis_index("pa") * slots_here + lax.broadcasted_iota(
        jnp.int32, (questions, slots_here), 1
    )
    usable = (slot_mask == 1) & (slot_index < slot_counts[:, None])
    masked = jnp.where(usable, scores, NEGATIVE)
    local_high = jnp.max(masked, -1)
    local_total = jnp.sum(jnp.where(usable, jnp.exp(masked - local_high[:, None]), 0.0), -1)
    slot_high, slot_total = merged((local_high, local_total), "pa", combine_pairs)
    marginal = slot_high + jnp.log(slot_total)
    posterior = jnp.where(usable, jnp.exp(scores - marginal[:, None]), 0.0)
    loss_value = -lax.psum(jnp.sum(marginal), "pb") / (questions * lax.axis_size("pb"))
    slot_number = slots_here * lax.axis_size("pa")
    grad_prior = -(slot_number * length) * posterior
    token_grad = jnp.broadcast_to(
        (-slot_number * posterior)[:, :, None], (questions, slots_here, length)
    ).reshape(tokens_here)
    weights_all = lax.all_gather(token_grad, "pa", axis=0, tiled=True)

    def vocab_grads(accumulated, pieces):
        hidden_rows, token_rows, logsum_rows, weight_rows = pieces
        logits, chosen = vocab_logits(hidden_rows, token_rows)
        softmax_rows = jnp.exp(logits - logsum_rows[:, None])
        grad_logits = (weight_rows[:, None] * (jnp.where(chosen, 1.0, 0.0) - softmax_rows)).astype(
            BFLOAT
        )
        return (accumulated + outer_sum(grad_logits, hidden_rows), matmul(grad_logits, embedding))

    grad_embed, grad_rows = lax.scan(
        vocab_grads,
        jnp.zeros(embedding.shape, jnp.float32),
        (
            row_blocks,
            token_blocks,
            row_logsum.reshape(block_count, block_rows),
            weights_all.reshape(block_count, block_rows),
        ),
    )
    grad_third = lax.psum_scatter(
        grad_rows.reshape(total_rows, model_width).astype(BFLOAT),
        "pa",
        scatter_dimension=0,
        tiled=True,
    ).astype(jnp.float32).reshape(batch_size, length, model_width)
    grad_inputs, grad_encoded, grads = layer_backward(grad_third, inputs, encoded, weights, stored)
    shares = (
        lax.psum_scatter(grads[0].astype(BFLOAT), "pa", scatter_dimension=0, tiled=True),
        lax.psum_scatter(grads[1].astype(BFLOAT), "pa", scatter_dimension=0, tiled=True),
        lax.psum_scatter(grads[2].astype(BFLOAT), "pa", scatter_dimension=0, tiled=True),
        lax.psum_scatter(grads[3].astype(BFLOAT), "pa", scatter_dimension=0, tiled=True),
        lax.psum_scatter(grads[4].astype(BFLOAT), "pa", scatter_dimension=0, tiled=True),
        lax.psum_scatter(grads[5].astype(BFLOAT), "pa", scatter_dimension=0, tiled=True),
        lax.psum_scatter(grads[6].astype(BFLOAT), "pa", scatter_dimension=0, tiled=True),
        lax.psum_scatter(grads[7], "pa", scatter_dimension=1, tiled=True),
        lax.psum_scatter(grads[8], "pa", scatter_dimension=1, tiled=True),
    )
    outputs = lax.psum(
        (
            shares[0],
            shares[1],
            shares[2],
            shares[3],
            shares[4],
            shares[5],
            shares[6],
            shares[7],
            shares[8],
            grad_embed.astype(BFLOAT),
        ),
        "pb",
    )
    outputs = tuple(part.astype(jnp.float32) for part in outputs)
    return (
        loss_value,
        grad_inputs.reshape(decoder_states.shape),
        grad_encoded.reshape(encoder_memory.shape),
        grad_prior,
        outputs[0],
        outputs[1],
        outputs[2],
        outputs[3],
        outputs[4],
        outputs[5],
        outputs[6],
        outputs[9],
        outputs[7],
        outputs[8],
    )


def solution(mesh):
    return jax.shard_map(
        per_device,
        mesh=mesh,
        in_specs=(
            P("pb", "pa", None, None),
            P("pb", "pa", None, None),
            P("pb", "pa", None),
            P("pb", "pa"),
            P("pb"),
            P("pb", "pa"),
            P("pa", None),
            P("pa", None),
            P("pa", None),
            P("pa", None),
            P("pa", None),
            P("pa", None),
            P("pa", None),
            P("pa", None),
            P(None, "pa"),
            P(None, "pa"),
        ),
        out_specs=(
            P(),
            P("pb", "pa", None, None),
            P("pb", "pa", None, None),
            P("pb", "pa"),
            P("pa", None),
            P("pa", None),
            P("pa", None),
            P("pa", None),
            P("pa", None),
            P("pa", None),
            P("pa", None),
            P("pa", None),
            P(None, "pa"),
            P(None, "pa"),
        ),
        check_vma=False,
    )
```

```python
import functools
import math

import jax
import jax.numpy as jnp
from jax import lax
from jax.experimental import pallas as pl
from jax.experimental.pallas import tpu as pltpu
from jax.sharding import PartitionSpec as P

HEADS = 16
HEAD_DIM = 64


EPSILON = 1e-05
NEGATIVE = -1e30
BFLOAT = jnp.bfloat16
MESH = pl.DeviceIdType.MESH
TILE = 1024
ROWS = 128
WEIGHT_UNITS = (3, 1, 1, 2, 1, 4, 4)
UNITS = tuple((w, k) for w, n in enumerate(WEIGHT_UNITS) for k in range(n))
REDUCE_WEIGHT = 6


def whereami():
    pb = lax.axis_index("pb")
    pa = lax.axis_index("pa")
    return lax.rem(pb, 2), pb // 2, pa // 2, lax.rem(pa, 2)


def greet(peers):
    barrier = pltpu.get_barrier_semaphore()
    for peer in peers:
        pl.semaphore_signal(barrier, inc=1, device_id=peer, device_id_type=MESH)
    pl.semaphore_wait(barrier, len(peers))


def at(x, y, z, c):
    return (y * 2 + x, z * 2 + c)


def neighbours(x, y, z, c):
    return [at(1 - x, y, z, c), at(x, 1 - y, z, c), at(x, y, z, 1 - c)] + [
        at(x, y, lax.rem(z + d, 4), c) for d in (1, 2, 3)
    ]


def shard_view(ref, unit, start, size):
    weight, block = unit
    if weight == REDUCE_WEIGHT:
        return ref.at[pl.ds(block * ROWS + start, size), :]
    return ref.at[pl.ds(start, size), pl.ds(block * TILE, TILE)]


def full_view(ref, unit, place, core, start, size):
    weight, block = unit
    if weight == REDUCE_WEIGHT:
        return ref.at[place, core, block, pl.ds(start, size), :]
    return ref.at[place, core, pl.ds(start, size), pl.ds(block * TILE, TILE)]


Z_FULL = (9, 14)


def gather_kernel(*refs):
    shards, norm, fulls, norm_full = refs[:7], refs[7], refs[8:15], refs[15]
    (
        local_sem, z_send, z_recv, one_send, one_recv, two_send, two_recv, d_send, d_recv,
        norm_sem, nz_send, nz_recv, nd_send, nd_recv,
    ) = refs[16:]
    x, y, z, c = whereami()
    greet(neighbours(x, y, z, c))
    every = slice(None)

    def copies(u):
        unit = UNITS[u]
        shard, full = shards[unit[0]], fulls[unit[0]]
        wide = u in Z_FULL
        a, b = (x, y) if u % 2 == 0 else (y, x)
        first_peer = at(x, 1 - y, z, c) if u % 2 == 0 else at(1 - x, y, z, c)
        second_peer = at(1 - x, y, z, c) if u % 2 == 0 else at(x, 1 - y, z, c)
        quarter = pl.multiple_of(64 * a + 32 * b, 32)
        half = pl.multiple_of(64 * a, 64)
        rows = (0, ROWS) if wide else (quarter, 32)
        local = pltpu.make_async_copy(
            shard_view(shard, unit, *rows), full_view(full, unit, z, c, *rows), local_sem.at[u]
        )
        along = [
            pltpu.make_async_remote_copy(
                src_ref=shard_view(shard, unit, *rows),
                dst_ref=full_view(full, unit, z, c, *rows),
                send_sem=z_send.at[u, d - 1],
                recv_sem=z_recv.at[u, d - 1],
                device_id=at(x, y, lax.rem(z + d, 4), c),
                device_id_type=MESH,
            )
            for d in (1, 2, 3)
        ]

        def cross(start, size, sends, recvs, peer):
            part = full_view(full, unit, every, c, start, size)
            return pltpu.make_async_remote_copy(
                src_ref=part,
                dst_ref=part,
                send_sem=sends.at[u],
                recv_sem=recvs.at[u],
                device_id=peer,
                device_id_type=MESH,
            )

        first = None if wide else cross(quarter, 32, one_send, one_recv, first_peer)
        second = None if wide else cross(half, 64, two_send, two_recv, second_peer)
        sibling = cross(0, ROWS, d_send, d_recv, at(x, y, z, 1 - c))
        return local, along, first, second, sibling

    def norm_copy(src, dst, send, recv, peer):
        return pltpu.make_async_remote_copy(
            src_ref=src, dst_ref=dst, send_sem=send, recv_sem=recv, device_id=peer, device_id_type=MESH
        )

    norm_local = pltpu.make_async_copy(norm, norm_full.at[z, c], norm_sem)
    norm_along = [
        norm_copy(
            norm, norm_full.at[z, c], nz_send.at[d - 1], nz_recv.at[d - 1], at(x, y, lax.rem(z + d, 4), c)
        )
        for d in (1, 2, 3)
    ]
    norm_sibling = norm_copy(
        norm_full.at[:, c], norm_full.at[:, c], nd_send, nd_recv, at(x, y, z, 1 - c)
    )
    norm_local.start()
    for copy in norm_along:
        copy.start()
    count = len(UNITS)
    every_copy = [copies(u) for u in range(count)]
    for local, along, _, _, _ in every_copy:
        local.start()
        for copy in along:
            copy.start()
    norm_local.wait()
    for copy in norm_along:
        copy.wait()
    norm_sibling.start()
    norm_sibling.wait()
    lag_two, lag_sibling = 2, 4
    for i in range(count + lag_sibling):
        if i < count:
            local, along, first, _, _ = every_copy[i]
            local.wait()
            for copy in along:
                copy.wait_recv()
            if first is not None:
                first.start()
        if 0 <= i - lag_two < count:
            _, _, first, second, _ = every_copy[i - lag_two]
            if first is not None:
                first.wait_recv()
                second.start()
        if 0 <= i - lag_sibling < count:
            _, _, _, second, sibling = every_copy[i - lag_sibling]
            if second is not None:
                second.wait_recv()
            sibling.start()
    for _, along, first, second, sibling in every_copy:
        for copy in along:
            copy.wait_send()
        if first is not None:
            first.wait_send()
            second.wait_send()
        sibling.wait()


def gather_weights(weights, norm):
    count = len(UNITS)
    shapes = []
    for w, weight in enumerate(weights):
        if w == REDUCE_WEIGHT:
            shapes.append((4, 2, weight.shape[0] // ROWS, ROWS, weight.shape[1]))
        else:
            shapes.append((4, 2) + weight.shape)
    *fulls, norm_full = pl.pallas_call(
        gather_kernel,
        out_shape=tuple(jax.ShapeDtypeStruct(shape, BFLOAT) for shape in shapes)
        + (jax.ShapeDtypeStruct((4, 2) + norm.shape, norm.dtype),),
        in_specs=[pl.BlockSpec(memory_space=pl.ANY)] * 8,
        out_specs=(pl.BlockSpec(memory_space=pl.ANY),) * 8,
        scratch_shapes=[
            pltpu.SemaphoreType.DMA((count,)),
            pltpu.SemaphoreType.DMA((count, 3)),
            pltpu.SemaphoreType.DMA((count, 3)),
        ]
        + [pltpu.SemaphoreType.DMA((count,))] * 6
        + [pltpu.SemaphoreType.DMA]
        + [pltpu.SemaphoreType.DMA((3,))] * 2
        + [pltpu.SemaphoreType.DMA] * 2,
        compiler_params=pltpu.CompilerParams(collective_id=0, has_side_effects=True),
        name="gather_weights",
    )(*weights, norm)
    norm_full = norm_full.reshape(8, norm.shape[0], norm.shape[1]).transpose(1, 0, 2)
    return (
        tuple(full.reshape(-1, full.shape[-1]) for full in fulls),
        norm_full.reshape(norm.shape[0], -1),
    )


LAGS = (0, 2, 4, 6, 8, 10)


def reduce_kernel(*refs):
    grads, norm, outs, norm_out = refs[:7], refs[7], refs[8:15], refs[15]
    (
        own, got, one, two, line, done, norm_here, norm_there, norm_line,
        own_sem, d_send, d_recv, one_send, one_recv, two_send, two_recv,
        z_send, z_recv, ag_send, ag_recv, ah_send, ah_recv, out_sem,
        n_send, n_recv, nz_send, nz_recv,
    ) = refs[16:]
    x, y, z, c = whereami()
    greet(neighbours(x, y, z, c))
    count = len(UNITS)
    every = slice(None)

    def sibling_copy(u):
        return pltpu.make_async_remote_copy(
            src_ref=full_view(grads[UNITS[u][0]], UNITS[u], every, 1 - c, 0, ROWS),
            dst_ref=got.at[u],
            send_sem=d_send.at[u],
            recv_sem=d_recv.at[u],
            device_id=at(x, y, z, 1 - c),
            device_id_type=MESH,
        )

    def own_copy(u):
        return pltpu.make_async_copy(
            full_view(grads[UNITS[u][0]], UNITS[u], every, c, 0, ROWS),
            own.at[u % 2],
            own_sem.at[u % 2],
        )

    for u in range(count):
        sibling_copy(u).start()
    own_copy(0).start()

    def place(u):
        even = lax.rem(u, 2) == 0
        a = jnp.where(even, x, y)
        b = jnp.where(even, y, x)
        x_peer = y * 2 + (1 - x)
        y_peer = (1 - y) * 2 + x
        a_peer = (jnp.where(even, x_peer, y_peer), z * 2 + c)
        b_peer = (jnp.where(even, y_peer, x_peer), z * 2 + c)
        return a, b, a_peer, b_peer

    def remote(src, dst, send, recv, peer):
        return pltpu.make_async_remote_copy(
            src_ref=src, dst_ref=dst, send_sem=send, recv_sem=recv, device_id=peer, device_id_type=MESH
        )

    def one_copy(u):
        a, _, a_peer, _ = place(u)
        return remote(
            got.at[u, :, pl.ds(pl.multiple_of(64 * (1 - a), 64), 64), :],
            one.at[u], one_send.at[u], one_recv.at[u], a_peer,
        )

    def two_copy(u):
        _, b, _, b_peer = place(u)
        return remote(
            one.at[u, :, pl.ds(pl.multiple_of(32 * (1 - b), 32), 32), :],
            two.at[u], two_send.at[u], two_recv.at[u], b_peer,
        )

    def line_copy(u, d):
        other = lax.rem(z + d, 4)
        return remote(
            two.at[u, other], line.at[u, d - 1], z_send.at[u, d - 1], z_recv.at[u, d - 1],
            at(x, y, other, c),
        )

    def ag_copy(u):
        a, b, _, b_peer = place(u)
        part = done.at[u, pl.ds(pl.multiple_of(64 * a + 32 * b, 32), 32), :]
        return remote(part, part, ag_send.at[u], ag_recv.at[u], b_peer)

    def ah_copy(u):
        a, _, a_peer, _ = place(u)
        part = done.at[u, pl.ds(pl.multiple_of(64 * a, 64), 64), :]
        return remote(part, part, ah_send.at[u], ah_recv.at[u], a_peer)

    norm_peers = (at(x, y, z, 1 - c), at(1 - x, y, z, c), at(x, 1 - y, z, c))

    def norm_copy(n):
        return remote(norm_here.at[n], norm_there.at[n], n_send.at[n], n_recv.at[n], norm_peers[n])

    def norm_line_copy(d):
        return remote(
            norm_here.at[3], norm_line.at[d - 1], nz_send.at[d - 1], nz_recv.at[d - 1],
            at(x, y, lax.rem(z + d, 4), c),
        )

    norm_here[0] = norm[...]
    norm_copy(0).start()

    def out_copy(u):
        return pltpu.make_async_copy(
            done.at[u], shard_view(outs[UNITS[u][0]], UNITS[u], 0, ROWS), out_sem.at[u]
        )

    def total(*parts):
        out = parts[0].astype(jnp.float32)
        for part in parts[1:]:
            out = out + part.astype(jnp.float32)
        return out.astype(BFLOAT)

    @pl.loop(0, count + LAGS[-1])
    def _(i):
        u0 = i
        for k in range(1, count):
            @pl.when(i + 1 == k)
            def _():
                own_copy(k).start()

        @pl.when(i < count)
        def _():
            for k in range(count):
                @pl.when(i == k)
                def _():
                    own_copy(k).wait()
                    sibling_copy(k).wait_recv()

            slot = lax.rem(u0, 2)

            @pl.loop(0, 32)
            def _(j):
                zz, r = j // 8, pl.multiple_of(lax.rem(j, 8) * 16, 16)
                got[u0, zz, pl.ds(r, 16), :] = total(
                    got[u0, zz, pl.ds(r, 16), :], own[slot, zz, pl.ds(r, 16), :]
                )

            one_copy(u0).start()

        for n in range(3):
            @pl.when(i == 2 + 2 * n)
            def _():
                norm_copy(n).wait_recv()
                norm_here[n + 1] = norm_here[n] + norm_there[n]
                if n < 2:
                    norm_copy(n + 1).start()
                else:
                    for d in (1, 2, 3):
                        norm_line_copy(d).start()

        @pl.when(i == 9)
        def _():
            for d in (1, 2, 3):
                norm_line_copy(d).wait_recv()
            norm_out[...] = ((norm_here[3] + norm_line[0]) + norm_line[1]) + norm_line[2]

        u1 = i - LAGS[1]

        @pl.when((u1 >= 0) & (u1 < count))
        def _():
            one_copy(u1).wait_recv()
            a, _, _, _ = place(u1)

            @pl.loop(0, 16)
            def _(j):
                zz, r = j // 4, pl.multiple_of(lax.rem(j, 4) * 16, 16)
                one[u1, zz, pl.ds(r, 16), :] = total(
                    one[u1, zz, pl.ds(r, 16), :],
                    got[u1, zz, pl.ds(pl.multiple_of(64 * a + r, 16), 16), :],
                )

            two_copy(u1).start()

        u2 = i - LAGS[2]

        @pl.when((u2 >= 0) & (u2 < count))
        def _():
            two_copy(u2).wait_recv()
            _, b, _, _ = place(u2)

            @pl.loop(0, 8)
            def _(j):
                zz, r = j // 2, pl.multiple_of(lax.rem(j, 2) * 16, 16)
                two[u2, zz, pl.ds(r, 16), :] = total(
                    two[u2, zz, pl.ds(r, 16), :],
                    one[u2, zz, pl.ds(pl.multiple_of(32 * b + r, 16), 16), :],
                )

            for d in (1, 2, 3):
                line_copy(u2, d).start()

        u3 = i - LAGS[3]

        @pl.when((u3 >= 0) & (u3 < count))
        def _():
            for d in (1, 2, 3):
                line_copy(u3, d).wait_recv()
            a, b, _, _ = place(u3)

            @pl.loop(0, 2)
            def _(j):
                r = pl.multiple_of(j * 16, 16)
                done[u3, pl.ds(pl.multiple_of(64 * a + 32 * b + r, 16), 16), :] = total(
                    two[u3, z, pl.ds(r, 16), :],
                    line[u3, 0, pl.ds(r, 16), :],
                    line[u3, 1, pl.ds(r, 16), :],
                    line[u3, 2, pl.ds(r, 16), :],
                )

            ag_copy(u3).start()

        u4 = i - LAGS[4]

        @pl.when((u4 >= 0) & (u4 < count))
        def _():
            ag_copy(u4).wait_recv()
            ah_copy(u4).start()

        u5 = i - LAGS[5]

        @pl.when((u5 >= 0) & (u5 < count))
        def _():
            ah_copy(u5).wait_recv()
            for k in range(count):
                @pl.when(u5 == k)
                def _():
                    out_copy(k).start()

    for u in range(count):
        sibling_copy(u).wait_send()

    @pl.loop(0, count)
    def _(u):
        one_copy(u).wait_send()
        two_copy(u).wait_send()
        for d in (1, 2, 3):
            line_copy(u, d).wait_send()
        ag_copy(u).wait_send()
        ah_copy(u).wait_send()

    for u in range(count):
        out_copy(u).wait()
    for n in range(3):
        norm_copy(n).wait_send()
        norm_line_copy(n + 1).wait_send()


def reduce_grads(grads, norm):
    count = len(UNITS)
    views = []
    shapes = []
    for w, grad in enumerate(grads):
        rows, columns = grad.shape[0] // 8, grad.shape[1]
        shapes.append((rows, columns))
        if w == REDUCE_WEIGHT:
            views.append(grad.reshape(4, 2, rows // ROWS, ROWS, columns))
        else:
            views.append(grad.reshape(4, 2, rows, columns))
    sems = pltpu.SemaphoreType.DMA((count,))
    every = pl.BlockSpec(memory_space=pl.ANY)
    vmem = pl.BlockSpec(memory_space=pltpu.VMEM)
    *shares, norm_sum = pl.pallas_call(
        reduce_kernel,
        out_shape=tuple(jax.ShapeDtypeStruct(shape, BFLOAT) for shape in shapes)
        + (jax.ShapeDtypeStruct(norm.shape, norm.dtype),),
        in_specs=[every] * 7 + [vmem],
        out_specs=(every,) * 7 + (vmem,),
        scratch_shapes=[
            pltpu.VMEM((2, 4, ROWS, TILE), BFLOAT),
            pltpu.VMEM((count, 4, ROWS, TILE), BFLOAT),
            pltpu.VMEM((count, 4, 64, TILE), BFLOAT),
            pltpu.VMEM((count, 4, 32, TILE), BFLOAT),
            pltpu.VMEM((count, 3, 32, TILE), BFLOAT),
            pltpu.VMEM((count, ROWS, TILE), BFLOAT),
            pltpu.VMEM((4,) + norm.shape, norm.dtype),
            pltpu.VMEM((3,) + norm.shape, norm.dtype),
            pltpu.VMEM((3,) + norm.shape, norm.dtype),
            pltpu.SemaphoreType.DMA((2,)),
            sems, sems, sems, sems, sems, sems,
            pltpu.SemaphoreType.DMA((count, 3)),
            pltpu.SemaphoreType.DMA((count, 3)),
            sems, sems, sems, sems, sems,
        ]
        + [pltpu.SemaphoreType.DMA((3,))] * 4,
        compiler_params=pltpu.CompilerParams(
            collective_id=1, has_side_effects=True, vmem_limit_bytes=48 * 2**20
        ),
        name="reduce_grads",
    )(*views, norm)
    return tuple(share.astype(jnp.float32) for share in shares), norm_sum

VOCAB_CUTS = 3


def head_kernel(slots, length, vocab_here, *refs):
    hid, aux, emb, emb_t = refs[:4]
    small_out, gemb_out, third_out = refs[4:7]
    (
        held, marks, logit, expo, part, sib_part, part_one, part_two, part_z,
        mine, theirs, lined, prior, usable, weight, scaled, picked_grad,
    ) = refs[7:24]
    (
        local_sem, z_send, z_recv, one_send, one_recv, two_send, two_recv, sib_send, sib_recv,
        ax_send, ax_recv, axz_send, axz_recv, st_send, st_recv, stz_send, stz_recv,
        dd_send, dd_recv, r1_send, r1_recv, r2_send, r2_recv, rz_send, rz_recv,
    ) = refs[24:]
    x, y, z, c = whereami()
    pb, pa = y * 2 + x, z * 2 + c
    size = hid.shape[0]
    pair = 2 * size
    width = hid.shape[1]
    rows = emb.shape[0]
    cut = rows // VOCAB_CUTS
    start = jnp.minimum(pb * rows, vocab_here - rows)
    skip = pb * rows - start
    base = pa * vocab_here + start
    own = pb * 4 + z

    def remote(src, dst, send, recv, peer):
        return pltpu.make_async_remote_copy(
            src_ref=src, dst_ref=dst, send_sem=send, recv_sem=recv, device_id=peer, device_id_type=MESH
        )

    sibling = at(x, y, z, 1 - c)
    x_peer, y_peer = at(1 - x, y, z, c), at(x, 1 - y, z, c)

    def spot(k, core):
        return held.at[pl.ds(pl.multiple_of((k * 2 + core) * size, size), size), :]

    greet(neighbours(x, y, z, c))
    own_copy = pltpu.make_async_copy(hid, spot(own, c), local_sem.at[0])
    own_copy.start()
    lanes = pl.ds(pl.multiple_of(c * size, size), size)
    aux_copy = pltpu.make_async_copy(aux, marks.at[y, x, z, :, lanes], local_sem.at[1])
    aux_copy.start()
    own_copy.wait()

    def along_copy(d):
        other = lax.rem(z + d, 4)
        return remote(hid, spot(own, c), z_send.at[d - 1], z_recv.at[d - 1], at(x, y, other, c))

    def sib_copy(k):
        return remote(spot(k, c), spot(k, c), sib_send.at[k], sib_recv.at[k], sibling)

    def order(zz):
        x_first = zz < 2
        f = jnp.where(x_first, x, y)
        g = jnp.where(x_first, y, x)
        first_peer = (jnp.where(x_first, y * 2 + 1 - x, (1 - y) * 2 + x), pa)
        second_peer = (jnp.where(x_first, (1 - y) * 2 + x, y * 2 + 1 - x), pa)

        def block(first, second):
            return jnp.where(x_first, second * 2 + first, first * 2 + second) * 4 + zz

        return f, g, first_peer, second_peer, block

    def one_copy(zz):
        f, g, first_peer, _, block = order(zz)
        return remote(
            spot(block(f, g), c), spot(block(f, g), c), one_send.at[zz], one_recv.at[zz], first_peer
        )

    def two_copy(zz, j):
        f, g, _, second_peer, block = order(zz)
        k = block(f if j == 0 else 1 - f, g)
        return remote(spot(k, c), spot(k, c), two_send.at[zz, j], two_recv.at[zz, j], second_peer)

    for d in (1, 2, 3):
        along_copy(d).start()
    sib_copy(own).start()
    one_copy(z).start()

    aux_copy.wait()
    steps = (
        (marks.at[y, x, z, :, lanes], sibling),
        (marks.at[y, x, z], x_peer),
        (marks.at[y, :, z], y_peer),
    )
    for n, (block_ref, peer) in enumerate(steps):
        copy = remote(block_ref, block_ref, ax_send.at[n], ax_recv.at[n], peer)
        copy.start()
        copy.wait()

    def mark_copy(d):
        block_ref = marks.at[:, :, z]
        other = lax.rem(z + d, 4)
        return remote(block_ref, block_ref, axz_send.at[d - 1], axz_recv.at[d - 1], at(x, y, other, c))

    for d in (1, 2, 3):
        mark_copy(d).start()
    for d in (1, 2, 3):
        mark_copy(d).wait()

    def target_rows(k):
        ypart, xpart, zpart = k // 8, lax.rem(k // 4, 2), lax.rem(k, 4)
        target = marks[ypart, xpart, zpart, 0:1, :].astype(jnp.int32) - base
        return jnp.where(target >= skip, target, -1)

    def row_numbers(j):
        return lax.broadcasted_iota(jnp.int32, (cut, pair), 0) + j * cut

    def cut_rows(j):
        return pl.ds(pl.multiple_of(j * cut, cut), cut)

    def token_lanes(k):
        return pl.ds(pl.multiple_of(k * pair, pair), pair)

    def forward_block(k):
        target = target_rows(k)
        block = held[token_lanes(k), :]

        def scan_logits(j, carried):
            highest, picked = carried
            value = lax.dot_general(
                emb[cut_rows(j), :], block, (((1,), (1,)), ((), ())), preferred_element_type=jnp.float32
            )
            number = row_numbers(j)
            value = jnp.where(number >= skip, value, NEGATIVE)
            logit[cut_rows(j), :] = value
            return (
                jnp.maximum(highest, jnp.max(value, 0, keepdims=True)),
                picked + jnp.sum(jnp.where(number == target, value, 0.0), 0, keepdims=True),
            )

        highest, picked = lax.fori_loop(
            0,
            VOCAB_CUTS,
            scan_logits,
            (jnp.full((1, pair), NEGATIVE, jnp.float32), jnp.zeros((1, pair), jnp.float32)),
        )

        def scan_exp(j, total):
            value = jnp.exp(logit[cut_rows(j), :] - highest)
            expo[cut_rows(j), token_lanes(k)] = value.astype(BFLOAT)
            return total + jnp.sum(value, 0, keepdims=True)

        total = lax.fori_loop(0, VOCAB_CUTS, scan_exp, jnp.zeros((1, pair), jnp.float32))
        mine[0, 0, pl.ds(k, 1), :] = highest
        mine[0, 1, pl.ds(k, 1), :] = total
        mine[0, 2, pl.ds(k, 1), :] = picked

    @pl.loop(0, 16)
    def _(s):
        phase, t = s // 4, lax.rem(s, 4)
        zz = lax.rem(z - t + 4, 4)
        f, g, _, _, block = order(zz)
        k = jnp.where(
            phase == 0,
            block(f, g),
            jnp.where(
                phase == 1, block(1 - f, g), jnp.where(phase == 2, block(f, 1 - g), block(1 - f, 1 - g))
            ),
        )

        for d in (1, 2, 3):
            @pl.when(s == d)
            def _():
                along_copy(d).wait_recv()

        @pl.when((s > 0) & (phase == 0))
        def _():
            sib_copy(k).start()
            one_copy(zz).start()

        @pl.when(phase == 1)
        def _():
            one_copy(zz).wait_recv()
            sib_copy(k).start()
            for j in range(2):
                two_copy(zz, j).start()

        for j in range(2):
            @pl.when(phase == 2 + j)
            def _():
                two_copy(zz, j).wait_recv()
                sib_copy(k).start()

        sib_copy(k).wait_recv()
        forward_block(k)

    def joined(parts):
        highest = functools.reduce(jnp.maximum, [p[0] for p in parts])
        total = functools.reduce(jnp.add, [p[1] * jnp.exp(p[0] - highest) for p in parts])
        picked = functools.reduce(jnp.add, [p[2] for p in parts])
        return highest, total, picked

    def rows_of(ref, n):
        return ref[n, 0], ref[n, 1], ref[n, 2]

    for n, (peer, side) in enumerate(((sibling, c), (x_peer, x), (y_peer, y))):
        copy = remote(mine.at[n], theirs.at[n], st_send.at[n], st_recv.at[n], peer)
        copy.start()
        copy.wait()
        here, there = rows_of(mine, n), rows_of(theirs, n)
        early = tuple(jnp.where(side == 0, a, b) for a, b in zip(here, there))
        late = tuple(jnp.where(side == 0, b, a) for a, b in zip(here, there))
        for r, value in enumerate(joined((early, late))):
            mine[n + 1, r] = value

    def stat_copy(d):
        other = lax.rem(z + d, 4)
        return remote(mine.at[3], lined.at[z], stz_send.at[d - 1], stz_recv.at[d - 1], at(x, y, other, c))

    for d in (1, 2, 3):
        stat_copy(d).start()
    for r in range(3):
        lined[z, r] = mine[3, r]
    for d in (1, 2, 3):
        stat_copy(d).wait()
    highest, total, picked = joined([rows_of(lined, n) for n in range(4)])
    logsum = highest + jnp.log(total)
    log_probs = picked - logsum
    for k in range(16):
        prior[k : k + 1, :] = marks[k // 8, (k // 4) % 2, k % 4, 1:2, :]
        usable[k : k + 1, :] = marks[k // 8, (k // 4) % 2, k % 4, 2:3, :]
    lane = lax.broadcasted_iota(jnp.int32, (16, pair), 1) // length
    mean = jnp.zeros((16, pair), jnp.float32)
    for n in range(pair // length):
        inside = lane == n
        slot_sum = jnp.sum(jnp.where(inside, log_probs, 0.0), 1, keepdims=True)
        mean = jnp.where(inside, slot_sum * (1.0 / length), mean)
    scores = prior[...] + mean
    counted = usable[...] > 0.5
    masked = jnp.where(counted, scores, NEGATIVE)
    question = lax.broadcasted_iota(jnp.int32, (16, pair), 0) // 4
    marginal = jnp.zeros((16, pair), jnp.float32)
    loss = jnp.zeros((1, 1), jnp.float32)
    for n in range(4):
        inside = question == n
        high = jnp.max(
            jnp.max(jnp.where(inside, masked, NEGATIVE), 1, keepdims=True), 0, keepdims=True
        )
        terms = jnp.where(inside & counted, jnp.exp(masked - high), 0.0)
        mass = jnp.sum(jnp.sum(terms, 1, keepdims=True), 0, keepdims=True) * (1.0 / length)
        value = high + jnp.log(mass)
        marginal = jnp.where(inside, value, marginal)
        loss = loss + value
    posterior = jnp.where(counted, jnp.exp(scores - marginal), 0.0)
    token_weight = -float(slots) * posterior
    weight[...] = posterior
    scaled[...] = token_weight * jnp.exp(mine[0, 0] - logsum)
    picked_grad[...] = token_weight * (1.0 - jnp.exp(log_probs))
    small_out[...] = jnp.broadcast_to(loss * (-1.0 / 4), small_out.shape)
    own_row = weight[pl.ds(own, 1), :]
    own_row = jnp.where(c == 0, own_row[:, :size], own_row[:, size:])
    small_out[1:2, :] = own_row * (-float(slots * length))

    def backward_block(k):
        target = target_rows(k)
        hit = picked_grad[pl.ds(k, 1), :]
        scale = scaled[pl.ds(k, 1), :]

        def make(j, carried):
            value = expo[cut_rows(j), token_lanes(k)].astype(jnp.float32)
            grad = jnp.where(row_numbers(j) == target, hit, -(value * scale))
            expo[cut_rows(j), token_lanes(k)] = grad.astype(BFLOAT)
            return carried

        lax.fori_loop(0, VOCAB_CUTS, make, 0)

        def to_rows(n, carried):
            cut_width = pl.ds(pl.multiple_of(n * 256, 256), 256)
            value = lax.dot_general(
                emb_t[cut_width, :],
                expo[:, token_lanes(k)],
                (((1,), (0,)), ((), ())),
                preferred_element_type=jnp.float32,
            ).astype(BFLOAT)
            part[k, 0, cut_width, :] = value[:, :size]
            part[k, 1, cut_width, :] = value[:, size:]
            return carried

        lax.fori_loop(0, width // 256, to_rows, 0)

    def dd_copy(k):
        return remote(part.at[k, 1 - c], sib_part.at[k], dd_send.at[k], dd_recv.at[k], sibling)

    def r1_copy(zz, j):
        f, _, first_peer, _, block = order(zz)
        return remote(
            sib_part.at[block(1 - f, j)], part_one.at[zz, j], r1_send.at[zz, j], r1_recv.at[zz, j],
            first_peer,
        )

    def r2_copy(zz):
        _, g, _, second_peer, _ = order(zz)
        return remote(part_one.at[zz, 1 - g], part_two.at[zz], r2_send.at[zz], r2_recv.at[zz], second_peer)

    def rz_copy(zz):
        return remote(part_two.at[zz], part_z.at[z], rz_send.at[zz], rz_recv.at[z], at(x, y, zz, c))

    def rz_arrival(zz):
        return remote(part_two.at[zz], part_z.at[zz], rz_send.at[zz], rz_recv.at[zz], at(x, y, zz, c))

    step = 64

    def add_into(target_ref, other_ref):
        @pl.loop(0, width // step)
        def _(n):
            rows_here = pl.ds(pl.multiple_of(n * step, step), step)
            target_ref[rows_here, :] = (
                target_ref[rows_here, :].astype(jnp.float32) + other_ref[rows_here, :].astype(jnp.float32)
            ).astype(BFLOAT)

    def group(n):
        return lax.rem(n, 2) * 2 + n // 2

    def chunk(q):
        j, n = q // 4, lax.rem(q, 4)
        columns = pl.ds(pl.multiple_of(n * 256, 256), 256)
        gemb_out[cut_rows(j), columns] = lax.dot_general(
            expo[cut_rows(j), :],
            held[:, columns],
            (((1,), (0,)), ((), ())),
            preferred_element_type=jnp.float32,
        ).astype(BFLOAT)

    @pl.loop(0, 28)
    def _(s):
        turn = s // 4
        edge = lax.rem(s, 4) == 0

        @pl.when(edge & (turn >= 1) & (turn < 5))
        def _():
            zz = group(turn - 1)

            @pl.loop(0, 4)
            def _(n):
                k = n * 4 + zz
                dd_copy(k).wait_recv()
                add_into(sib_part.at[k], part.at[k, c])

            for j in range(2):
                r1_copy(zz, j).start()

        @pl.when(edge & (turn >= 2) & (turn < 6))
        def _():
            zz = group(turn - 2)
            f, _, _, _, block = order(zz)
            for j in range(2):
                r1_copy(zz, j).wait_recv()
                add_into(part_one.at[zz, j], sib_part.at[block(f, j)])
            r2_copy(zz).start()

        @pl.when(edge & (turn >= 3))
        def _():
            zz = group(turn - 3)
            _, g, _, _, _ = order(zz)
            r2_copy(zz).wait_recv()
            add_into(part_two.at[zz], part_one.at[zz, g])

            @pl.when(zz != z)
            def _():
                rz_copy(zz).start()

        @pl.when(s < 16)
        def _():
            k = lax.rem(s, 4) * 4 + group(turn)
            backward_block(k)
            dd_copy(k).start()

        @pl.when(s >= 16)
        def _():
            chunk(s - 16)

    for d in (1, 2, 3):
        rz_arrival(lax.rem(z + d, 4)).wait_recv()

    @pl.loop(0, width // step)
    def _(n):
        rows_here = pl.ds(pl.multiple_of(n * step, step), step)
        value = part_two[z, rows_here, :].astype(jnp.float32)
        for d in (1, 2, 3):
            value = value + part_z[lax.rem(z + d, 4), rows_here, :].astype(jnp.float32)
        third_out[rows_here, :] = value

    for d in (1, 2, 3):
        along_copy(d).wait_send()
        rz_copy(lax.rem(z + d, 4)).wait_send()

    @pl.loop(0, 4)
    def _(zz):
        one_copy(zz).wait_send()
        for j in range(2):
            two_copy(zz, j).wait_send()
            r1_copy(zz, j).wait_send()
        r2_copy(zz).wait_send()

    @pl.loop(0, 16)
    def _(k):
        sib_copy(k).wait_send()
        dd_copy(k).wait_send()


def vocabulary_head(third_low, targets, log_prior, usable, embedding, slots, length):
    size, width = third_low.shape
    vocab_here = embedding.shape[0]
    rows = 16 * VOCAB_CUTS * -(-vocab_here // (4 * 16 * VOCAB_CUTS))
    start = jnp.minimum(lax.axis_index("pb") * rows, vocab_here - rows)
    emb = lax.dynamic_slice_in_dim(embedding, start, rows)
    aux = jnp.zeros((8, size), jnp.float32)
    aux = aux.at[0].set(targets.astype(jnp.float32))
    aux = aux.at[1].set(jnp.repeat(log_prior, length))
    aux = aux.at[2].set(jnp.repeat(usable.astype(jnp.float32), length))
    dma = pltpu.SemaphoreType.DMA
    vmem = pl.BlockSpec(memory_space=pltpu.VMEM)
    stat = (3, 16, 2 * size)
    f32 = jnp.float32
    block = (width, size)
    small, gemb, third = pl.pallas_call(
        functools.partial(head_kernel, slots, length, vocab_here),
        out_shape=(
            jax.ShapeDtypeStruct((8, size), f32),
            jax.ShapeDtypeStruct((rows, width), BFLOAT),
            jax.ShapeDtypeStruct((width, size), f32),
        ),
        in_specs=[vmem] * 4,
        out_specs=(vmem,) * 3,
        scratch_shapes=[
            pltpu.VMEM((32 * size, width), BFLOAT),
            pltpu.VMEM((2, 2, 4, 8, 2 * size), f32),
            pltpu.VMEM((rows, 2 * size), f32),
            pltpu.VMEM((rows, 32 * size), BFLOAT),
            pltpu.VMEM((16, 2) + block, BFLOAT),
            pltpu.VMEM((16,) + block, BFLOAT),
            pltpu.VMEM((4, 2) + block, BFLOAT),
            pltpu.VMEM((4,) + block, BFLOAT),
            pltpu.VMEM((4,) + block, BFLOAT),
            pltpu.VMEM((4,) + stat, f32),
            pltpu.VMEM((3,) + stat, f32),
            pltpu.VMEM((4,) + stat, f32),
        ]
        + [pltpu.VMEM((16, 2 * size), f32)] * 5
        + [dma((2,))]
        + [dma((3,))] * 2
        + [dma((4,))] * 2
        + [dma((4, 2))] * 2
        + [dma((16,))] * 2
        + [dma((3,))] * 8
        + [dma((16,))] * 2
        + [dma((4, 2))] * 2
        + [dma((4,))] * 4,
        compiler_params=pltpu.CompilerParams(
            collective_id=2, has_side_effects=True, vmem_limit_bytes=60 * 2**20
        ),
        name="vocabulary_head",
    )(third_low, aux, emb, emb.T)
    return small, gemb, third


def merged(part, axis, combine):
    gathered = jax.tree.map(lambda a: lax.all_gather(a, axis), part)

    def take(source):
        return jax.tree.map(lambda a: lax.dynamic_index_in_dim(a, source, 0, False), gathered)

    return lax.fori_loop(
        1, lax.axis_size(axis), lambda source, state: combine(state, take(source)), take(0)
    )


def matmul(matrix_left, matrix_right):
    return lax.dot_general(
        matrix_left,
        matrix_right,
        (((matrix_left.ndim - 1,), (0,)), ((), ())),
        preferred_element_type=jnp.float32,
    )


def matmul_back(matrix_left, matrix_right):
    return lax.dot_general(
        matrix_left,
        matrix_right,
        (((matrix_left.ndim - 1,), (1,)), ((), ())),
        preferred_element_type=jnp.float32,
    )


def outer_sum(matrix_left, matrix_right):
    flat_left = matrix_left.reshape(-1, matrix_left.shape[-1])
    flat_right = matrix_right.reshape(-1, matrix_right.shape[-1])
    return lax.dot_general(
        flat_left, flat_right, (((0,), (0,)), ((), ())), preferred_element_type=jnp.float32
    )


def split_heads(values):
    return values.reshape(values.shape[0], values.shape[1], HEADS, HEAD_DIM)


def join_heads(values):
    return values.reshape(values.shape[0], values.shape[1], HEADS * HEAD_DIM)


def exact_gelu(values):
    return jax.nn.gelu(values, approximate=False)


def norm_forward(values, gain_row, shift_row):
    centre = values - jnp.mean(values, -1, keepdims=True)
    inverse = lax.rsqrt(jnp.mean(centre * centre, -1, keepdims=True) + EPSILON)
    normed = centre * inverse
    return (normed * gain_row.astype(jnp.float32) + shift_row.astype(jnp.float32), normed, inverse)


def norm_backward(upstream, normed, inverse, gain_row):
    scaled = upstream * gain_row.astype(jnp.float32)
    mean_scaled = jnp.mean(scaled, -1, keepdims=True)
    along_normed = jnp.mean(scaled * normed, -1, keepdims=True)
    grad_values = inverse * (scaled - mean_scaled - normed * along_normed)
    model_width = upstream.shape[-1]
    grad_gain = jnp.sum((upstream * normed).reshape(-1, model_width), 0)
    grad_shift = jnp.sum(upstream.reshape(-1, model_width), 0)
    return (grad_values, grad_gain, grad_shift)


def score_block(queries, key_rows, causal):
    scores = jnp.einsum(
        "nqhd,nkhd->nhqk", queries, key_rows, preferred_element_type=jnp.float32
    ) * (1.0 / math.sqrt(HEAD_DIM))
    if causal:
        length = queries.shape[1]
        allowed = lax.broadcasted_iota(jnp.int32, (length, length), 0) >= lax.broadcasted_iota(
            jnp.int32, (length, length), 1
        )
        scores = jnp.where(allowed, scores, NEGATIVE)
    return scores


def attend(queries, key_rows, values, causal):
    scores = score_block(queries, key_rows, causal)
    highest = jnp.max(scores, -1, keepdims=True)
    totals = jnp.sum(jnp.exp(scores - highest), -1, keepdims=True)
    logsum = highest + jnp.log(totals)
    probs_low = jnp.exp(scores - logsum).astype(BFLOAT)
    context = jnp.einsum(
        "nhqk,nkhd->nqhd", probs_low, values, preferred_element_type=jnp.float32
    ).astype(BFLOAT)
    return (join_heads(context), logsum)


def attend_back(grad_context, queries, key_rows, values, logsum, causal):
    score_scale = 1.0 / math.sqrt(HEAD_DIM)
    probs_full = jnp.exp(score_block(queries, key_rows, causal) - logsum)
    grad_heads = split_heads(grad_context)
    grad_probs = jnp.einsum(
        "nqhd,nkhd->nhqk", grad_heads, values, preferred_element_type=jnp.float32
    )
    grad_values = jnp.einsum(
        "nhqk,nqhd->nkhd", probs_full.astype(BFLOAT), grad_heads, preferred_element_type=jnp.float32
    ).astype(BFLOAT)
    grad_scores = (
        probs_full * (grad_probs - jnp.sum(probs_full * grad_probs, -1, keepdims=True))
    ).astype(BFLOAT)
    grad_queries = (
        jnp.einsum("nhqk,nkhd->nqhd", grad_scores, key_rows, preferred_element_type=jnp.float32)
        * score_scale
    ).astype(BFLOAT)
    grad_keys = (
        jnp.einsum("nhqk,nqhd->nkhd", grad_scores, queries, preferred_element_type=jnp.float32)
        * score_scale
    ).astype(BFLOAT)
    return (join_heads(grad_queries), join_heads(grad_keys), join_heads(grad_values))


def layer_forward(inputs, encoded, weights):
    (
        packed_weight,
        output_weight,
        query_weight,
        memory_weight,
        cross_weight,
        expand_weight,
        reduce_weight,
        gains,
        shifts,
    ) = weights
    model_width = inputs.shape[-1]
    packed = matmul(inputs, packed_weight).astype(BFLOAT)
    context, self_logsum = attend(
        split_heads(packed[..., :model_width]),
        split_heads(packed[..., model_width : 2 * model_width]),
        split_heads(packed[..., 2 * model_width :]),
        True,
    )
    first_norm, first_normed, first_inverse = norm_forward(
        inputs.astype(jnp.float32) + matmul(context, output_weight), gains[0], shifts[0]
    )
    first_low = first_norm.astype(BFLOAT)
    cross_queries = matmul(first_low, query_weight).astype(BFLOAT)
    memory_pairs = matmul(encoded, memory_weight).astype(BFLOAT)
    cross_context, cross_logsum = attend(
        split_heads(cross_queries),
        split_heads(memory_pairs[..., :model_width]),
        split_heads(memory_pairs[..., model_width:]),
        False,
    )
    second, second_normed, second_inverse = norm_forward(
        first_norm + matmul(cross_context, cross_weight), gains[1], shifts[1]
    )
    second_low = second.astype(BFLOAT)
    inner_pre = matmul(second_low, expand_weight)
    active = exact_gelu(inner_pre).astype(BFLOAT)
    third_norm, third_normed, third_inverse = norm_forward(
        second + matmul(active, reduce_weight), gains[2], shifts[2]
    )
    stored = (
        packed,
        context,
        self_logsum,
        first_normed,
        first_inverse,
        first_low,
        cross_queries,
        memory_pairs,
        cross_context,
        cross_logsum,
        second_normed,
        second_inverse,
        second_low,
        inner_pre,
        active,
        third_normed,
        third_inverse,
    )
    return (third_norm.astype(BFLOAT), stored)


def layer_backward(grad_third, inputs, encoded, weights, stored):
    (
        packed_weight,
        output_weight,
        query_weight,
        memory_weight,
        cross_weight,
        expand_weight,
        reduce_weight,
        gains,
        shifts,
    ) = weights
    (
        packed,
        context,
        self_logsum,
        first_normed,
        first_inverse,
        first_low,
        cross_queries,
        memory_pairs,
        cross_context,
        cross_logsum,
        second_normed,
        second_inverse,
        second_low,
        inner_pre,
        active,
        third_normed,
        third_inverse,
    ) = stored
    model_width = inputs.shape[-1]
    grad_res3, gain_three, shift_three = norm_backward(
        grad_third, third_normed, third_inverse, gains[2]
    )
    grad_output = grad_res3.astype(BFLOAT)
    grad_reduce = outer_sum(active, grad_output)
    grad_active = matmul_back(grad_output, reduce_weight)
    _, gelu_pull = jax.vjp(exact_gelu, inner_pre)
    grad_inner = gelu_pull(grad_active)[0].astype(BFLOAT)
    grad_expand = outer_sum(second_low, grad_inner)
    grad_second = grad_res3 + matmul_back(grad_inner, expand_weight)
    grad_res2, gain_two, shift_two = norm_backward(
        grad_second, second_normed, second_inverse, gains[1]
    )
    grad_mixed = grad_res2.astype(BFLOAT)
    grad_cross_weight = outer_sum(cross_context, grad_mixed)
    grad_cross_context = matmul_back(grad_mixed, cross_weight).astype(BFLOAT)
    grad_cross_queries, grad_memory_keys, grad_memory_values = attend_back(
        grad_cross_context,
        split_heads(cross_queries),
        split_heads(memory_pairs[..., :model_width]),
        split_heads(memory_pairs[..., model_width:]),
        cross_logsum,
        False,
    )
    grad_query_weight = outer_sum(first_low, grad_cross_queries)
    grad_first = grad_res2 + matmul_back(grad_cross_queries, query_weight)
    grad_pairs = jnp.concatenate([grad_memory_keys, grad_memory_values], -1)
    grad_memory_weight = outer_sum(encoded, grad_pairs)
    grad_encoded = matmul_back(grad_pairs, memory_weight)
    grad_res1, gain_one, shift_one = norm_backward(
        grad_first, first_normed, first_inverse, gains[0]
    )
    grad_merged = grad_res1.astype(BFLOAT)
    grad_output_weight = outer_sum(context, grad_merged)
    grad_context = matmul_back(grad_merged, output_weight).astype(BFLOAT)
    grad_queries, grad_keys, grad_values = attend_back(
        grad_context,
        split_heads(packed[..., :model_width]),
        split_heads(packed[..., model_width : 2 * model_width]),
        split_heads(packed[..., 2 * model_width :]),
        self_logsum,
        True,
    )
    grad_packed = jnp.concatenate([grad_queries, grad_keys, grad_values], -1)
    grad_packed_weight = outer_sum(inputs, grad_packed)
    grad_inputs = grad_res1 + matmul_back(grad_packed, packed_weight)
    grad_gains = jnp.stack([gain_one, gain_two, gain_three])
    grad_shifts = jnp.stack([shift_one, shift_two, shift_three])
    return (
        grad_inputs,
        grad_encoded,
        (
            grad_packed_weight,
            grad_output_weight,
            grad_query_weight,
            grad_memory_weight,
            grad_cross_weight,
            grad_expand,
            grad_reduce,
            grad_gains,
            grad_shifts,
        ),
    )


def combine_scores(former, latter):
    highest = jnp.maximum(former[0], latter[0])
    totals = former[1] * jnp.exp(former[0] - highest) + latter[1] * jnp.exp(latter[0] - highest)
    return (highest, totals, former[2] + latter[2])


def combine_pairs(former, latter):
    highest = jnp.maximum(former[0], latter[0])
    totals = former[1] * jnp.exp(former[0] - highest) + latter[1] * jnp.exp(latter[0] - highest)
    return (highest, totals)


def per_device(
    decoder_states,
    encoder_memory,
    target_tokens,
    log_prior,
    slot_counts,
    slot_mask,
    self_packed,
    self_output,
    cross_query,
    cross_memory,
    cross_output,
    feed_expand,
    feed_reduce,
    embedding,
    norm_gains,
    norm_shifts,
):
    weights = (
        lax.all_gather(self_packed, "pa", axis=0, tiled=True),
        lax.all_gather(self_output, "pa", axis=0, tiled=True),
        lax.all_gather(cross_query, "pa", axis=0, tiled=True),
        lax.all_gather(cross_memory, "pa", axis=0, tiled=True),
        lax.all_gather(cross_output, "pa", axis=0, tiled=True),
        lax.all_gather(feed_expand, "pa", axis=0, tiled=True),
        lax.all_gather(feed_reduce, "pa", axis=0, tiled=True),
        lax.all_gather(norm_gains, "pa", axis=1, tiled=True),
        lax.all_gather(norm_shifts, "pa", axis=1, tiled=True),
    )
    questions, slots_here, length, model_width = decoder_states.shape
    mem_length = encoder_memory.shape[2]
    batch_size = questions * slots_here
    inputs = decoder_states.reshape(batch_size, length, model_width)
    encoded = encoder_memory.reshape(batch_size, mem_length, model_width)
    third_low, stored = layer_forward(inputs, encoded, weights)
    tokens_here = batch_size * length
    rows_all, tokens_all = (
        lax.all_gather(third_low.reshape(tokens_here, model_width), "pa", axis=0, tiled=True),
        lax.all_gather(target_tokens.reshape(tokens_here), "pa", axis=0, tiled=True),
    )
    total_rows = rows_all.shape[0]
    block_rows = min(total_rows, 2048)
    block_count = total_rows // block_rows
    vocab_start = lax.axis_index("pa") * embedding.shape[0]
    row_blocks = rows_all.reshape(block_count, block_rows, model_width)
    token_blocks = tokens_all.reshape(block_count, block_rows)

    def vocab_logits(hidden_rows, token_rows):
        logits = matmul_back(hidden_rows, embedding)
        column = lax.broadcasted_iota(jnp.int32, logits.shape, 1) + vocab_start
        return (logits, column == token_rows[:, None])

    def vocab_partial(pieces):
        logits, chosen = vocab_logits(pieces[0], pieces[1])
        highest = jnp.max(logits, -1)
        totals = jnp.sum(jnp.exp(logits - highest[:, None]), -1)
        picked = jnp.sum(jnp.where(chosen, logits, 0.0), -1)
        return (highest, totals, picked)

    highest, totals, picked = lax.map(vocab_partial, (row_blocks, token_blocks))
    highest, totals, picked = merged(
        (highest.reshape(total_rows), totals.reshape(total_rows), picked.reshape(total_rows)),
        "pa",
        combine_scores,
    )
    row_logsum = highest + jnp.log(totals)
    own_start = lax.axis_index("pa") * tokens_here
    own_logsum = lax.dynamic_slice_in_dim(row_logsum, own_start, tokens_here)
    own_picked = lax.dynamic_slice_in_dim(picked, own_start, tokens_here)
    log_probs = (own_picked - own_logsum).reshape(questions, slots_here, length)
    scores = log_prior + jnp.mean(log_probs, -1)
    slot_index = lax.axis_index("pa") * slots_here + lax.broadcasted_iota(
        jnp.int32, (questions, slots_here), 1
    )
    usable = (slot_mask == 1) & (slot_index < slot_counts[:, None])
    masked = jnp.where(usable, scores, NEGATIVE)
    local_high = jnp.max(masked, -1)
    local_total = jnp.sum(jnp.where(usable, jnp.exp(masked - local_high[:, None]), 0.0), -1)
    slot_high, slot_total = merged((local_high, local_total), "pa", combine_pairs)
    marginal = slot_high + jnp.log(slot_total)
    posterior = jnp.where(usable, jnp.exp(scores - marginal[:, None]), 0.0)
    loss_value = -lax.psum(jnp.sum(marginal), "pb") / (questions * lax.axis_size("pb"))
    slot_number = slots_here * lax.axis_size("pa")
    grad_prior = -(slot_number * length) * posterior
    token_grad = jnp.broadcast_to(
        (-slot_number * posterior)[:, :, None], (questions, slots_here, length)
    ).reshape(tokens_here)
    weights_all = lax.all_gather(token_grad, "pa", axis=0, tiled=True)

    def vocab_grads(accumulated, pieces):
        hidden_rows, token_rows, logsum_rows, weight_rows = pieces
        logits, chosen = vocab_logits(hidden_rows, token_rows)
        softmax_rows = jnp.exp(logits - logsum_rows[:, None])
        grad_logits = (weight_rows[:, None] * (jnp.where(chosen, 1.0, 0.0) - softmax_rows)).astype(
            BFLOAT
        )
        return (accumulated + outer_sum(grad_logits, hidden_rows), matmul(grad_logits, embedding))

    grad_embed, grad_rows = lax.scan(
        vocab_grads,
        jnp.zeros(embedding.shape, jnp.float32),
        (
            row_blocks,
            token_blocks,
            row_logsum.reshape(block_count, block_rows),
            weights_all.reshape(block_count, block_rows),
        ),
    )
    grad_third = lax.psum_scatter(
        grad_rows.reshape(total_rows, model_width).astype(BFLOAT),
        "pa",
        scatter_dimension=0,
        tiled=True,
    ).astype(jnp.float32).reshape(batch_size, length, model_width)
    grad_inputs, grad_encoded, grads = layer_backward(grad_third, inputs, encoded, weights, stored)
    shares = (
        lax.psum_scatter(grads[0].astype(BFLOAT), "pa", scatter_dimension=0, tiled=True),
        lax.psum_scatter(grads[1].astype(BFLOAT), "pa", scatter_dimension=0, tiled=True),
        lax.psum_scatter(grads[2].astype(BFLOAT), "pa", scatter_dimension=0, tiled=True),
        lax.psum_scatter(grads[3].astype(BFLOAT), "pa", scatter_dimension=0, tiled=True),
        lax.psum_scatter(grads[4].astype(BFLOAT), "pa", scatter_dimension=0, tiled=True),
        lax.psum_scatter(grads[5].astype(BFLOAT), "pa", scatter_dimension=0, tiled=True),
        lax.psum_scatter(grads[6].astype(BFLOAT), "pa", scatter_dimension=0, tiled=True),
        lax.psum_scatter(grads[7], "pa", scatter_dimension=1, tiled=True),
        lax.psum_scatter(grads[8], "pa", scatter_dimension=1, tiled=True),
    )
    outputs = lax.psum(
        (
            shares[0],
            shares[1],
            shares[2],
            shares[3],
            shares[4],
            shares[5],
            shares[6],
            shares[7],
            shares[8],
            grad_embed.astype(BFLOAT),
        ),
        "pb",
    )
    outputs = tuple(part.astype(jnp.float32) for part in outputs)
    return (
        loss_value,
        grad_inputs.reshape(decoder_states.shape),
        grad_encoded.reshape(encoder_memory.shape),
        grad_prior,
        outputs[0],
        outputs[1],
        outputs[2],
        outputs[3],
        outputs[4],
        outputs[5],
        outputs[6],
        outputs[9],
        outputs[7],
        outputs[8],
    )


def per_device_kernels(
    decoder_states,
    encoder_memory,
    target_tokens,
    log_prior,
    slot_counts,
    slot_mask,
    self_packed,
    self_output,
    cross_query,
    cross_memory,
    cross_output,
    feed_expand,
    feed_reduce,
    embedding,
    norm_gains,
    norm_shifts,
):
    shards = (
        self_packed,
        self_output,
        cross_query,
        cross_memory,
        cross_output,
        feed_expand,
        feed_reduce,
    )
    norm_rows = jnp.concatenate(
        [norm_gains, norm_shifts, jnp.zeros((2, norm_gains.shape[1]), BFLOAT)]
    ).astype(jnp.float32)
    matrices, norms = gather_weights(shards, norm_rows)
    weights = matrices + (norms[:3], norms[3:6])
    _, slots_here, length, model_width = decoder_states.shape
    slots = slots_here * lax.axis_size("pa")
    inputs = decoder_states[0]
    encoded = encoder_memory[0]
    third_low, stored = layer_forward(inputs, encoded, weights)
    slot_index = lax.axis_index("pa") * slots_here + jnp.arange(slots_here)
    usable = (slot_mask[0] == 1) & (slot_index < slot_counts[0])
    small, grad_embed, grad_third = vocabulary_head(
        third_low.reshape(slots_here * length, model_width),
        target_tokens.reshape(slots_here * length),
        log_prior[0],
        usable,
        embedding,
        slots,
        length,
    )
    loss_value = small[0, 0]
    grad_prior = small[1].reshape(1, slots_here, length)[:, :, 0]
    pieces = lax.all_gather(grad_embed, "pb", axis=0)
    repeated = 4 * grad_embed.shape[0] - embedding.shape[0]
    grad_embed = jnp.concatenate(
        [pieces[0], pieces[1], pieces[2], pieces[3][repeated:]]
    ).astype(jnp.float32)
    grad_third = grad_third.T.reshape(slots_here, length, model_width)
    grad_inputs, grad_encoded, grads = layer_backward(grad_third, inputs, encoded, weights, stored)
    low_grads = tuple(grad.astype(BFLOAT) for grad in grads[:7])
    norm_grads = jnp.concatenate([grads[7], grads[8], jnp.zeros((2, model_width), jnp.float32)])
    shares, norm_sums = reduce_grads(low_grads, norm_grads)
    norm_here = norm_gains.shape[1]
    norm_sums = lax.dynamic_slice_in_dim(
        norm_sums, lax.axis_index("pa") * norm_here, norm_here, axis=1
    )
    return (
        loss_value,
        grad_inputs.reshape(decoder_states.shape),
        grad_encoded.reshape(encoder_memory.shape),
        grad_prior,
    ) + shares + (grad_embed, norm_sums[:3], norm_sums[3:6])


def solution(mesh):
    own_kernels = mesh.shape["pb"] == 4 and mesh.shape["pa"] == 8
    return jax.shard_map(
        per_device_kernels if own_kernels else per_device,
        mesh=mesh,
        in_specs=(
            P("pb", "pa", None, None),
            P("pb", "pa", None, None),
            P("pb", "pa", None),
            P("pb", "pa"),
            P("pb"),
            P("pb", "pa"),
            P("pa", None),
            P("pa", None),
            P("pa", None),
            P("pa", None),
            P("pa", None),
            P("pa", None),
            P("pa", None),
            P("pa", None),
            P(None, "pa"),
            P(None, "pa"),
        ),
        out_specs=(
            P(),
            P("pb", "pa", None, None),
            P("pb", "pa", None, None),
            P("pb", "pa"),
            P("pa", None),
            P("pa", None),
            P("pa", None),
            P("pa", None),
            P("pa", None),
            P("pa", None),
            P("pa", None),
            P("pa", None),
            P(None, "pa"),
            P(None, "pa"),
        ),
        check_vma=False,
    )
```

```python
import functools
import math

import jax
import jax.numpy as jnp
from jax import lax
from jax.experimental import pallas as pl
from jax.experimental.pallas import tpu as pltpu
from jax.sharding import PartitionSpec as P

HEADS = 16
HEAD_DIM = 64


EPSILON = 1e-05
NEGATIVE = -1e30
BFLOAT = jnp.bfloat16
MESH = pl.DeviceIdType.MESH
TILE = 1024
ROWS = 128
WEIGHT_UNITS = (3, 1, 1, 2, 1, 4, 4)
UNITS = tuple((w, k) for w, n in enumerate(WEIGHT_UNITS) for k in range(n))
REDUCE_WEIGHT = 6


def whereami():
    pb = lax.axis_index("pb")
    pa = lax.axis_index("pa")
    return lax.rem(pb, 2), pb // 2, pa // 2, lax.rem(pa, 2)


def greet(peers):
    barrier = pltpu.get_barrier_semaphore()
    for peer in peers:
        pl.semaphore_signal(barrier, inc=1, device_id=peer, device_id_type=MESH)
    pl.semaphore_wait(barrier, len(peers))


def at(x, y, z, c):
    return (y * 2 + x, z * 2 + c)


def neighbours(x, y, z, c):
    return [at(1 - x, y, z, c), at(x, 1 - y, z, c), at(x, y, z, 1 - c)] + [
        at(x, y, lax.rem(z + d, 4), c) for d in (1, 2, 3)
    ]


def shard_view(ref, unit, start, size):
    weight, block = unit
    if weight == REDUCE_WEIGHT:
        return ref.at[pl.ds(block * ROWS + start, size), :]
    return ref.at[pl.ds(start, size), pl.ds(block * TILE, TILE)]


def full_view(ref, unit, place, core, start, size):
    weight, block = unit
    if weight == REDUCE_WEIGHT:
        return ref.at[place, core, block, pl.ds(start, size), :]
    return ref.at[place, core, pl.ds(start, size), pl.ds(block * TILE, TILE)]


Z_FULL = (9, 14)


LAGS = (0, 2, 4, 6, 8, 10)
SIBLING_WINDOW = 2


def reduce_kernel(*refs):
    grads, norm, outs, norm_out = refs[:7], refs[7], refs[8:15], refs[15]
    (
        own, got, one, two, line, done, norm_here, norm_there, norm_line,
        own_sem, d_send, d_recv, one_send, one_recv, two_send, two_recv,
        z_send, z_recv, ag_send, ag_recv, ah_send, ah_recv, out_sem,
        n_send, n_recv, nz_send, nz_recv,
    ) = refs[16:]
    x, y, z, c = whereami()
    greet(neighbours(x, y, z, c))
    count = len(UNITS)
    every = slice(None)

    def sibling_copy(u):
        return pltpu.make_async_remote_copy(
            src_ref=full_view(grads[UNITS[u][0]], UNITS[u], every, 1 - c, 0, ROWS),
            dst_ref=got.at[u],
            send_sem=d_send.at[u],
            recv_sem=d_recv.at[u],
            device_id=at(x, y, z, 1 - c),
            device_id_type=MESH,
        )

    def own_copy(u):
        return pltpu.make_async_copy(
            full_view(grads[UNITS[u][0]], UNITS[u], every, c, 0, ROWS),
            own.at[u % 2],
            own_sem.at[u % 2],
        )

    for u in range(SIBLING_WINDOW):
        sibling_copy(u).start()
    own_copy(0).start()

    def place(u):
        even = lax.rem(u, 2) == 0
        a = jnp.where(even, x, y)
        b = jnp.where(even, y, x)
        x_peer = y * 2 + (1 - x)
        y_peer = (1 - y) * 2 + x
        a_peer = (jnp.where(even, x_peer, y_peer), z * 2 + c)
        b_peer = (jnp.where(even, y_peer, x_peer), z * 2 + c)
        return a, b, a_peer, b_peer

    def remote(src, dst, send, recv, peer):
        return pltpu.make_async_remote_copy(
            src_ref=src, dst_ref=dst, send_sem=send, recv_sem=recv, device_id=peer, device_id_type=MESH
        )

    def one_copy(u):
        a, _, a_peer, _ = place(u)
        return remote(
            got.at[u, :, pl.ds(pl.multiple_of(64 * (1 - a), 64), 64), :],
            one.at[u], one_send.at[u], one_recv.at[u], a_peer,
        )

    def two_copy(u):
        _, b, _, b_peer = place(u)
        return remote(
            one.at[u, :, pl.ds(pl.multiple_of(32 * (1 - b), 32), 32), :],
            two.at[u], two_send.at[u], two_recv.at[u], b_peer,
        )

    def line_copy(u, d):
        other = lax.rem(z + d, 4)
        return remote(
            two.at[u, other], line.at[u, d - 1], z_send.at[u, d - 1], z_recv.at[u, d - 1],
            at(x, y, other, c),
        )

    def ag_copy(u):
        a, b, _, b_peer = place(u)
        part = done.at[u, pl.ds(pl.multiple_of(64 * a + 32 * b, 32), 32), :]
        return remote(part, part, ag_send.at[u], ag_recv.at[u], b_peer)

    def ah_copy(u):
        a, _, a_peer, _ = place(u)
        part = done.at[u, pl.ds(pl.multiple_of(64 * a, 64), 64), :]
        return remote(part, part, ah_send.at[u], ah_recv.at[u], a_peer)

    norm_peers = (at(x, y, z, 1 - c), at(1 - x, y, z, c), at(x, 1 - y, z, c))

    def norm_copy(n):
        return remote(norm_here.at[n], norm_there.at[n], n_send.at[n], n_recv.at[n], norm_peers[n])

    def norm_line_copy(d):
        return remote(
            norm_here.at[3], norm_line.at[d - 1], nz_send.at[d - 1], nz_recv.at[d - 1],
            at(x, y, lax.rem(z + d, 4), c),
        )

    norm_here[0] = norm[...]
    norm_copy(0).start()

    def out_copy(u):
        return pltpu.make_async_copy(
            done.at[u], shard_view(outs[UNITS[u][0]], UNITS[u], 0, ROWS), out_sem.at[u]
        )

    def total(*parts):
        out = parts[0].astype(jnp.float32)
        for part in parts[1:]:
            out = out + part.astype(jnp.float32)
        return out.astype(BFLOAT)

    @pl.loop(0, count + LAGS[-1])
    def _(i):
        u0 = i
        for k in range(SIBLING_WINDOW, count):
            @pl.when(i + SIBLING_WINDOW == k)
            def _():
                sibling_copy(k).start()

        for k in range(1, count):
            @pl.when(i + 1 == k)
            def _():
                own_copy(k).start()

        @pl.when(i < count)
        def _():
            for k in range(count):
                @pl.when(i == k)
                def _():
                    own_copy(k).wait()
                    sibling_copy(k).wait_recv()

            slot = lax.rem(u0, 2)

            @pl.loop(0, 32)
            def _(j):
                zz, r = j // 8, pl.multiple_of(lax.rem(j, 8) * 16, 16)
                got[u0, zz, pl.ds(r, 16), :] = total(
                    got[u0, zz, pl.ds(r, 16), :], own[slot, zz, pl.ds(r, 16), :]
                )

            one_copy(u0).start()

        for n in range(3):
            @pl.when(i == 2 + 2 * n)
            def _():
                norm_copy(n).wait_recv()
                norm_here[n + 1] = norm_here[n] + norm_there[n]
                if n < 2:
                    norm_copy(n + 1).start()
                else:
                    for d in (1, 2, 3):
                        norm_line_copy(d).start()

        @pl.when(i == 9)
        def _():
            for d in (1, 2, 3):
                norm_line_copy(d).wait_recv()
            norm_out[...] = ((norm_here[3] + norm_line[0]) + norm_line[1]) + norm_line[2]

        u1 = i - LAGS[1]

        @pl.when((u1 >= 0) & (u1 < count))
        def _():
            one_copy(u1).wait_recv()
            a, _, _, _ = place(u1)

            @pl.loop(0, 16)
            def _(j):
                zz, r = j // 4, pl.multiple_of(lax.rem(j, 4) * 16, 16)
                one[u1, zz, pl.ds(r, 16), :] = total(
                    one[u1, zz, pl.ds(r, 16), :],
                    got[u1, zz, pl.ds(pl.multiple_of(64 * a + r, 16), 16), :],
                )

            two_copy(u1).start()

        u2 = i - LAGS[2]

        @pl.when((u2 >= 0) & (u2 < count))
        def _():
            two_copy(u2).wait_recv()
            _, b, _, _ = place(u2)

            @pl.loop(0, 8)
            def _(j):
                zz, r = j // 2, pl.multiple_of(lax.rem(j, 2) * 16, 16)
                two[u2, zz, pl.ds(r, 16), :] = total(
                    two[u2, zz, pl.ds(r, 16), :],
                    one[u2, zz, pl.ds(pl.multiple_of(32 * b + r, 16), 16), :],
                )

            for d in (1, 2, 3):
                line_copy(u2, d).start()

        u3 = i - LAGS[3]

        @pl.when((u3 >= 0) & (u3 < count))
        def _():
            for d in (1, 2, 3):
                line_copy(u3, d).wait_recv()
            a, b, _, _ = place(u3)

            @pl.loop(0, 2)
            def _(j):
                r = pl.multiple_of(j * 16, 16)
                done[u3, pl.ds(pl.multiple_of(64 * a + 32 * b + r, 16), 16), :] = total(
                    two[u3, z, pl.ds(r, 16), :],
                    line[u3, 0, pl.ds(r, 16), :],
                    line[u3, 1, pl.ds(r, 16), :],
                    line[u3, 2, pl.ds(r, 16), :],
                )

            ag_copy(u3).start()

        u4 = i - LAGS[4]

        @pl.when((u4 >= 0) & (u4 < count))
        def _():
            ag_copy(u4).wait_recv()
            ah_copy(u4).start()

        u5 = i - LAGS[5]

        @pl.when((u5 >= 0) & (u5 < count))
        def _():
            ah_copy(u5).wait_recv()
            for k in range(count):
                @pl.when(u5 == k)
                def _():
                    out_copy(k).start()

    for u in range(count):
        sibling_copy(u).wait_send()

    @pl.loop(0, count)
    def _(u):
        one_copy(u).wait_send()
        two_copy(u).wait_send()
        for d in (1, 2, 3):
            line_copy(u, d).wait_send()
        ag_copy(u).wait_send()
        ah_copy(u).wait_send()

    for u in range(count):
        out_copy(u).wait()
    for n in range(3):
        norm_copy(n).wait_send()
        norm_line_copy(n + 1).wait_send()


def reduce_grads(grads, norm):
    count = len(UNITS)
    views = []
    shapes = []
    for w, grad in enumerate(grads):
        rows, columns = grad.shape[0] // 8, grad.shape[1]
        shapes.append((rows, columns))
        if w == REDUCE_WEIGHT:
            views.append(grad.reshape(4, 2, rows // ROWS, ROWS, columns))
        else:
            views.append(grad.reshape(4, 2, rows, columns))
    sems = pltpu.SemaphoreType.DMA((count,))
    every = pl.BlockSpec(memory_space=pl.ANY)
    vmem = pl.BlockSpec(memory_space=pltpu.VMEM)
    *shares, norm_sum = pl.pallas_call(
        reduce_kernel,
        out_shape=tuple(jax.ShapeDtypeStruct(shape, BFLOAT) for shape in shapes)
        + (jax.ShapeDtypeStruct(norm.shape, norm.dtype),),
        in_specs=[every] * 7 + [vmem],
        out_specs=(every,) * 7 + (vmem,),
        scratch_shapes=[
            pltpu.VMEM((2, 4, ROWS, TILE), BFLOAT),
            pltpu.VMEM((count, 4, ROWS, TILE), BFLOAT),
            pltpu.VMEM((count, 4, 64, TILE), BFLOAT),
            pltpu.VMEM((count, 4, 32, TILE), BFLOAT),
            pltpu.VMEM((count, 3, 32, TILE), BFLOAT),
            pltpu.VMEM((count, ROWS, TILE), BFLOAT),
            pltpu.VMEM((4,) + norm.shape, norm.dtype),
            pltpu.VMEM((3,) + norm.shape, norm.dtype),
            pltpu.VMEM((3,) + norm.shape, norm.dtype),
            pltpu.SemaphoreType.DMA((2,)),
            sems, sems, sems, sems, sems, sems,
            pltpu.SemaphoreType.DMA((count, 3)),
            pltpu.SemaphoreType.DMA((count, 3)),
            sems, sems, sems, sems, sems,
        ]
        + [pltpu.SemaphoreType.DMA((3,))] * 4,
        compiler_params=pltpu.CompilerParams(
            collective_id=1, has_side_effects=True, vmem_limit_bytes=48 * 2**20
        ),
        name="reduce_grads",
    )(*views, norm)
    return tuple(share.astype(jnp.float32) for share in shares), norm_sum
GATHER_WINDOW = 4
LAG_TWO, LAG_SIBLING, LAG_LOAD, LAG_USE = 1, 2, 4, 5
SLOTS_IN_FLIGHT = 3


def dot_nn(left, right):
    return lax.dot_general(left, right, (((1,), (0,)), ((), ())), preferred_element_type=jnp.float32)


def dot_nt(left, right):
    return lax.dot_general(left, right, (((1,), (1,)), ((), ())), preferred_element_type=jnp.float32)


def dot_tn(left, right):
    return lax.dot_general(left, right, (((0,), (0,)), ((), ())), preferred_element_type=jnp.float32)


def stack_heads(pair):
    lane = lax.broadcasted_iota(jnp.int32, pair.shape, 1)
    zero = jnp.zeros_like(pair)
    return jnp.concatenate(
        [jnp.where(lane < HEAD_DIM, pair, zero), jnp.where(lane < HEAD_DIM, zero, pair)], 0
    )


def unstack_heads(stacked):
    rows = stacked.shape[0] // 2
    lane = lax.broadcasted_iota(jnp.int32, (rows, stacked.shape[1]), 1)
    return jnp.where(lane < HEAD_DIM, stacked[:rows], stacked[rows:])


def pair_scores(queries, keys, causal):
    scores = dot_nt(queries, keys) * (1.0 / math.sqrt(HEAD_DIM))
    if causal:
        length = keys.shape[0]
        row = lax.rem(lax.broadcasted_iota(jnp.int32, scores.shape, 0), length)
        column = lax.broadcasted_iota(jnp.int32, scores.shape, 1)
        scores = jnp.where(row >= column, scores, NEGATIVE)
    highest = jnp.max(scores, -1, keepdims=True)
    total = jnp.sum(jnp.exp(scores - highest), -1, keepdims=True)
    return jnp.exp(scores - (highest + jnp.log(total)))


def attend_pair(queries, keys, values, causal):
    probs = pair_scores(stack_heads(queries), keys, causal).astype(BFLOAT)
    return unstack_heads(dot_nn(probs, values)).astype(BFLOAT)


def normalise(values, gain, shift):
    centre = values - jnp.mean(values, -1, keepdims=True)
    inverse = lax.rsqrt(jnp.mean(centre * centre, -1, keepdims=True) + EPSILON)
    normed = centre * inverse
    return normed * gain + shift, normed, inverse


def forward_kernel(length, mem_length, *refs):
    shards, norm, states, encoded = refs[:7], refs[7], refs[8], refs[9]
    fulls = refs[10:17]
    (
        norm_full, packed, context, first_normed, first_inverse, first_low, cross_queries, pairs,
        cross_context, second_normed, second_inverse, second_low, inner, active, third_normed,
        third_inverse, third_low,
    ) = refs[17:34]
    wbuf, residual = refs[34:36]
    (
        local_sem, z_send, z_recv, one_send, one_recv, two_send, two_recv, d_send, d_recv,
        norm_sem, nz_send, nz_recv, nd_send, nd_recv, load_sem,
    ) = refs[36:]
    x, y, z, c = whereami()
    greet(neighbours(x, y, z, c))
    every = slice(None)
    tokens, width = states.shape
    slots_here = tokens // length

    def copies(u):
        unit = UNITS[u]
        shard, full = shards[unit[0]], fulls[unit[0]]
        wide = u in Z_FULL
        a, b = (x, y) if u % 2 == 0 else (y, x)
        first_peer = at(x, 1 - y, z, c) if u % 2 == 0 else at(1 - x, y, z, c)
        second_peer = at(1 - x, y, z, c) if u % 2 == 0 else at(x, 1 - y, z, c)
        quarter = pl.multiple_of(64 * a + 32 * b, 32)
        half = pl.multiple_of(64 * a, 64)
        rows = (0, ROWS) if wide else (quarter, 32)
        local = pltpu.make_async_copy(
            shard_view(shard, unit, *rows), full_view(full, unit, z, c, *rows), local_sem.at[u]
        )
        along = [
            pltpu.make_async_remote_copy(
                src_ref=shard_view(shard, unit, *rows),
                dst_ref=full_view(full, unit, z, c, *rows),
                send_sem=z_send.at[u, d - 1],
                recv_sem=z_recv.at[u, d - 1],
                device_id=at(x, y, lax.rem(z + d, 4), c),
                device_id_type=MESH,
            )
            for d in (1, 2, 3)
        ]

        def cross(start, size, sends, recvs, peer):
            part = full_view(full, unit, every, c, start, size)
            return pltpu.make_async_remote_copy(
                src_ref=part,
                dst_ref=part,
                send_sem=sends.at[u],
                recv_sem=recvs.at[u],
                device_id=peer,
                device_id_type=MESH,
            )

        first = None if wide else cross(quarter, 32, one_send, one_recv, first_peer)
        second = None if wide else cross(half, 64, two_send, two_recv, second_peer)
        sibling = cross(0, ROWS, d_send, d_recv, at(x, y, z, 1 - c))
        load = pltpu.make_async_copy(
            full_view(full, unit, every, every, 0, ROWS),
            wbuf.at[u % SLOTS_IN_FLIGHT],
            load_sem.at[u % SLOTS_IN_FLIGHT],
        )
        return local, along, first, second, sibling, load

    def norm_copy(src, dst, send, recv, peer):
        return pltpu.make_async_remote_copy(
            src_ref=src, dst_ref=dst, send_sem=send, recv_sem=recv, device_id=peer, device_id_type=MESH
        )

    norm_local = pltpu.make_async_copy(norm, norm_full.at[z, c], norm_sem)
    norm_along = [
        norm_copy(
            norm, norm_full.at[z, c], nz_send.at[d - 1], nz_recv.at[d - 1], at(x, y, lax.rem(z + d, 4), c)
        )
        for d in (1, 2, 3)
    ]
    norm_sibling = norm_copy(
        norm_full.at[:, c], norm_full.at[:, c], nd_send, nd_recv, at(x, y, z, 1 - c)
    )
    norm_local.start()
    for copy in norm_along:
        copy.start()

    def norm_row(n):
        return jnp.concatenate(
            [norm_full[p // 2, p % 2, n : n + 1, :] for p in range(8)], 1
        )

    def times(left_ref, u, write):
        slot = u % SLOTS_IN_FLIGHT

        @pl.loop(0, 4)
        def _(n):
            columns = pl.ds(pl.multiple_of(n * 256, 256), 256)
            right = wbuf[slot, :, :, :, columns].reshape(TILE, 256)
            write(columns, n, dot_nn(left_ref[...], right))

    def block_columns(k, n):
        return pl.ds(pl.multiple_of(k * TILE + n * 256, 256), 256)

    def attention(queries, keys, key_start, value_start, key_length, out, causal):
        @pl.loop(0, slots_here * (width // 128))
        def _(n):
            slot, group = n // (width // 128), lax.rem(n, width // 128)
            lanes = pl.ds(pl.multiple_of(group * 128, 128), 128)
            key_lanes = pl.ds(pl.multiple_of(key_start + group * 128, 128), 128)
            value_lanes = pl.ds(pl.multiple_of(value_start + group * 128, 128), 128)
            query_rows = pl.ds(pl.multiple_of(slot * length, length), length)
            key_rows = pl.ds(pl.multiple_of(slot * key_length, key_length), key_length)
            out[query_rows, lanes] = attend_pair(
                queries[query_rows, lanes], keys[key_rows, key_lanes], keys[key_rows, value_lanes], causal
            )

    def finish_norm(n, value, normed_ref, inverse_ref, low_ref):
        out, normed, inverse = normalise(value, norm_row(n), norm_row(n + 3))
        normed_ref[...] = normed
        inverse_ref[...] = jnp.broadcast_to(inverse, inverse_ref.shape)
        low_ref[...] = out.astype(BFLOAT)
        return out

    def use(u):
        weight, k = UNITS[u]
        if weight == 0:
            def write(columns, n, value):
                packed[:, block_columns(k, n)] = value.astype(BFLOAT)

            times(states, u, write)
            if k == 2:
                attention(packed, packed, width, 2 * width, length, context, True)
        elif weight == 1:
            def write(columns, n, value):
                residual[:, columns] = states[:, columns].astype(jnp.float32) + value

            times(context, u, write)
            residual[...] = finish_norm(0, residual[...], first_normed, first_inverse, first_low)
        elif weight == 2:
            def write(columns, n, value):
                cross_queries[:, columns] = value.astype(BFLOAT)

            times(first_low, u, write)
        elif weight == 3:
            slot = u % SLOTS_IN_FLIGHT

            @pl.loop(0, 16)
            def _(n):
                m, n = n // 4, lax.rem(n, 4)
                columns = pl.ds(pl.multiple_of(n * 256, 256), 256)
                part = encoded.shape[0] // 4
                rows_here = pl.ds(pl.multiple_of(m * part, part), part)
                right = wbuf[slot, :, :, :, columns].reshape(TILE, 256)
                pairs[rows_here, block_columns(k, n)] = dot_nn(encoded[rows_here, :], right).astype(BFLOAT)

            if k == 1:
                attention(cross_queries, pairs, 0, width, mem_length, cross_context, False)
        elif weight == 4:
            def write(columns, n, value):
                residual[:, columns] = residual[:, columns] + value

            times(cross_context, u, write)
            residual[...] = finish_norm(1, residual[...], second_normed, second_inverse, second_low)
        elif weight == 5:
            def write(columns, n, value):
                inner[:, block_columns(k, n)] = value
                gate = 0.5 * (1.0 + lax.erf(value * math.sqrt(0.5)))
                active[:, block_columns(k, n)] = (value * gate).astype(BFLOAT)

            times(second_low, u, write)
        else:
            slot = u % SLOTS_IN_FLIGHT
            blocks = active.shape[1] // (8 * ROWS)
            left = jnp.concatenate(
                [active[:, (p * blocks + k) * ROWS : (p * blocks + k + 1) * ROWS] for p in range(8)], 1
            )

            @pl.loop(0, 4)
            def _(n):
                columns = pl.ds(pl.multiple_of(n * 256, 256), 256)
                right = wbuf[slot, :, :, :, columns].reshape(TILE, 256)
                residual[:, columns] = residual[:, columns] + dot_nn(left, right)

            if k == blocks - 1:
                finish_norm(2, residual[...], third_normed, third_inverse, third_low)

    count = len(UNITS)
    every_copy = [copies(u) for u in range(count)]
    for local, along, _, _, _, _ in every_copy[:GATHER_WINDOW]:
        local.start()
        for copy in along:
            copy.start()
    for i in range(count + LAG_USE):
        if i + GATHER_WINDOW < count:
            local, along = every_copy[i + GATHER_WINDOW][:2]
            local.start()
            for copy in along:
                copy.start()
        if i < count:
            local, along, first = every_copy[i][:3]
            local.wait()
            for copy in along:
                copy.wait_recv()
            if first is not None:
                first.start()
        if 0 <= i - LAG_TWO < count:
            first, second = every_copy[i - LAG_TWO][2:4]
            if first is not None:
                first.wait_recv()
                second.start()
        if 0 <= i - LAG_SIBLING < count:
            second, sibling = every_copy[i - LAG_SIBLING][3:5]
            if second is not None:
                second.wait_recv()
            sibling.start()
        if i == 2:
            norm_local.wait()
            for copy in norm_along:
                copy.wait()
            norm_sibling.start()
        if i == 4:
            norm_sibling.wait()
        if 0 <= i - LAG_LOAD < count:
            sibling, load = every_copy[i - LAG_LOAD][4:]
            sibling.wait_recv()
            load.start()
        if 0 <= i - LAG_USE < count:
            every_copy[i - LAG_USE][5].wait()
            use(i - LAG_USE)
    for _, along, first, second, sibling, _ in every_copy:
        for copy in along:
            copy.wait_send()
        if first is not None:
            first.wait_send()
            second.wait_send()
        sibling.wait_send()


def forward_layer(weights, norm, states, encoded, length):
    count = len(UNITS)
    shapes = []
    for w, weight in enumerate(weights):
        if w == REDUCE_WEIGHT:
            shapes.append((4, 2, weight.shape[0] // ROWS, ROWS, weight.shape[1]))
        else:
            shapes.append((4, 2) + weight.shape)
    tokens, width = states.shape
    mem_tokens = encoded.shape[0]
    mem_length = mem_tokens // (tokens // length)
    units = weights[5].shape[1]
    f32 = jnp.float32
    kept = [
        ((4, 2) + norm.shape, f32),
        ((tokens, 3 * width), BFLOAT),
        ((tokens, width), BFLOAT),
        ((tokens, width), f32),
        ((tokens, 128), f32),
        ((tokens, width), BFLOAT),
        ((tokens, width), BFLOAT),
        ((mem_tokens, 2 * width), BFLOAT),
        ((tokens, width), BFLOAT),
        ((tokens, width), f32),
        ((tokens, 128), f32),
        ((tokens, width), BFLOAT),
        ((tokens, units), f32),
        ((tokens, units), BFLOAT),
        ((tokens, width), f32),
        ((tokens, 128), f32),
        ((tokens, width), BFLOAT),
    ]
    every = pl.BlockSpec(memory_space=pl.ANY)
    vmem = pl.BlockSpec(memory_space=pltpu.VMEM)
    dma = pltpu.SemaphoreType.DMA
    results = pl.pallas_call(
        functools.partial(forward_kernel, length, mem_length),
        out_shape=tuple(jax.ShapeDtypeStruct(shape, BFLOAT) for shape in shapes)
        + tuple(jax.ShapeDtypeStruct(shape, kind) for shape, kind in kept),
        in_specs=[every] * 8 + [vmem] * 2,
        out_specs=(every,) * 7 + (vmem,) * len(kept),
        scratch_shapes=[
            pltpu.VMEM((SLOTS_IN_FLIGHT, 4, 2, ROWS, TILE), BFLOAT),
            pltpu.VMEM((tokens, width), f32),
            dma((count,)),
            dma((count, 3)),
            dma((count, 3)),
        ]
        + [dma((count,))] * 6
        + [dma]
        + [dma((3,))] * 2
        + [dma] * 2
        + [dma((SLOTS_IN_FLIGHT,))],
        compiler_params=pltpu.CompilerParams(
            collective_id=0, has_side_effects=True, vmem_limit_bytes=48 * 2**20
        ),
        name="forward_layer",
    )(*weights, norm, states, encoded)
    fulls = tuple(full.reshape(-1, full.shape[-1]) for full in results[:7])
    norm_full = results[7].reshape(8, norm.shape[0], norm.shape[1]).transpose(1, 0, 2)
    return fulls, norm_full.reshape(norm.shape[0], -1), results[8:]


VOCAB_CUTS = 3


def head_kernel(slots, length, vocab_here, *refs):
    hid, aux, emb_all = refs[:3]
    small_out, gemb_out, third_out = refs[3:6]
    (
        emb, emb_t, held, marks, logit, expo, part, sib_part, part_one, part_two, part_z,
        mine, theirs, lined, prior, usable, weight, scaled, picked_grad,
    ) = refs[6:25]
    (
        local_sem, z_send, z_recv, one_send, one_recv, two_send, two_recv, sib_send, sib_recv,
        ax_send, ax_recv, axz_send, axz_recv, st_send, st_recv, stz_send, stz_recv,
        dd_send, dd_recv, r1_send, r1_recv, r2_send, r2_recv, rz_send, rz_recv,
    ) = refs[25:]
    x, y, z, c = whereami()
    pb, pa = y * 2 + x, z * 2 + c
    size = hid.shape[0]
    pair = 2 * size
    width = hid.shape[1]
    rows = emb.shape[0]
    cut = rows // VOCAB_CUTS
    start = pl.multiple_of(pb * rows, 16)
    last = vocab_here - 3 * rows
    valid = jnp.where(pb == 3, last, rows)
    base = pa * vocab_here + start
    own = pb * 4 + z

    def remote(src, dst, send, recv, peer):
        return pltpu.make_async_remote_copy(
            src_ref=src, dst_ref=dst, send_sem=send, recv_sem=recv, device_id=peer, device_id_type=MESH
        )

    sibling = at(x, y, z, 1 - c)
    x_peer, y_peer = at(1 - x, y, z, c), at(x, 1 - y, z, c)

    def spot(k, core):
        return held.at[pl.ds(pl.multiple_of((k * 2 + core) * size, size), size), :]

    greet(neighbours(x, y, z, c))
    own_copy = pltpu.make_async_copy(hid, spot(own, c), local_sem.at[0])
    own_copy.start()
    lanes = pl.ds(pl.multiple_of(c * size, size), size)
    aux_copy = pltpu.make_async_copy(aux, marks.at[y, x, z, :, lanes], local_sem.at[1])
    aux_copy.start()
    emb_copy = pltpu.make_async_copy(
        emb_all.at[pl.ds(start, last), :], emb.at[pl.ds(0, last), :], local_sem.at[2]
    )
    rest_copy = pltpu.make_async_copy(
        emb_all.at[pl.ds(pl.multiple_of(jnp.minimum(start + last, vocab_here - (rows - last)), 16), rows - last), :],
        emb.at[pl.ds(last, rows - last), :],
        local_sem.at[3],
    )
    emb_copy.start()
    rest_copy.start()
    own_copy.wait()

    def along_copy(d):
        other = lax.rem(z + d, 4)
        return remote(hid, spot(own, c), z_send.at[d - 1], z_recv.at[d - 1], at(x, y, other, c))

    def sib_copy(k):
        return remote(spot(k, c), spot(k, c), sib_send.at[k], sib_recv.at[k], sibling)

    def order(zz):
        x_first = zz < 2
        f = jnp.where(x_first, x, y)
        g = jnp.where(x_first, y, x)
        first_peer = (jnp.where(x_first, y * 2 + 1 - x, (1 - y) * 2 + x), pa)
        second_peer = (jnp.where(x_first, (1 - y) * 2 + x, y * 2 + 1 - x), pa)

        def block(first, second):
            return jnp.where(x_first, second * 2 + first, first * 2 + second) * 4 + zz

        return f, g, first_peer, second_peer, block

    def one_copy(zz):
        f, g, first_peer, _, block = order(zz)
        return remote(
            spot(block(f, g), c), spot(block(f, g), c), one_send.at[zz], one_recv.at[zz], first_peer
        )

    def two_copy(zz, j):
        f, g, _, second_peer, block = order(zz)
        k = block(f if j == 0 else 1 - f, g)
        return remote(spot(k, c), spot(k, c), two_send.at[zz, j], two_recv.at[zz, j], second_peer)

    for d in (1, 2, 3):
        along_copy(d).start()
    sib_copy(own).start()
    one_copy(z).start()

    aux_copy.wait()
    steps = (
        (marks.at[y, x, z, :, lanes], sibling),
        (marks.at[y, x, z], x_peer),
        (marks.at[y, :, z], y_peer),
    )
    for n, (block_ref, peer) in enumerate(steps):
        copy = remote(block_ref, block_ref, ax_send.at[n], ax_recv.at[n], peer)
        copy.start()
        copy.wait()

    def mark_copy(d):
        block_ref = marks.at[:, :, z]
        other = lax.rem(z + d, 4)
        return remote(block_ref, block_ref, axz_send.at[d - 1], axz_recv.at[d - 1], at(x, y, other, c))

    for d in (1, 2, 3):
        mark_copy(d).start()
    for d in (1, 2, 3):
        mark_copy(d).wait()

    emb_copy.wait()
    rest_copy.wait()
    full_cuts = rows // 128

    @pl.loop(0, full_cuts)
    def _(n):
        here = pl.ds(pl.multiple_of(n * 128, 128), 128)
        emb_t[:, here] = emb[here, :].T

    if rows % 128:
        emb_t[:, full_cuts * 128 :] = emb[full_cuts * 128 :, :].T

    def target_rows(k):
        ypart, xpart, zpart = k // 8, lax.rem(k // 4, 2), lax.rem(k, 4)
        target = marks[ypart, xpart, zpart, 0:1, :].astype(jnp.int32) - base
        return jnp.where(target < valid, target, -1)

    def row_numbers(j):
        return lax.broadcasted_iota(jnp.int32, (cut, pair), 0) + j * cut

    def cut_rows(j):
        return pl.ds(pl.multiple_of(j * cut, cut), cut)

    def token_lanes(k):
        return pl.ds(pl.multiple_of(k * pair, pair), pair)

    def forward_block(k):
        target = target_rows(k)
        block = held[token_lanes(k), :]

        def scan_logits(j, carried):
            highest, picked = carried
            value = lax.dot_general(
                emb[cut_rows(j), :], block, (((1,), (1,)), ((), ())), preferred_element_type=jnp.float32
            )
            number = row_numbers(j)
            value = jnp.where(number < valid, value, NEGATIVE)
            logit[cut_rows(j), :] = value
            return (
                jnp.maximum(highest, jnp.max(value, 0, keepdims=True)),
                picked + jnp.sum(jnp.where(number == target, value, 0.0), 0, keepdims=True),
            )

        highest, picked = lax.fori_loop(
            0,
            VOCAB_CUTS,
            scan_logits,
            (jnp.full((1, pair), NEGATIVE, jnp.float32), jnp.zeros((1, pair), jnp.float32)),
        )

        def scan_exp(j, total):
            value = jnp.exp(logit[cut_rows(j), :] - highest)
            expo[cut_rows(j), token_lanes(k)] = value.astype(BFLOAT)
            return total + jnp.sum(value, 0, keepdims=True)

        total = lax.fori_loop(0, VOCAB_CUTS, scan_exp, jnp.zeros((1, pair), jnp.float32))
        mine[0, 0, pl.ds(k, 1), :] = highest
        mine[0, 1, pl.ds(k, 1), :] = total
        mine[0, 2, pl.ds(k, 1), :] = picked

    @pl.loop(0, 16)
    def _(s):
        phase, t = s // 4, lax.rem(s, 4)
        zz = lax.rem(z - t + 4, 4)
        f, g, _, _, block = order(zz)
        k = jnp.where(
            phase == 0,
            block(f, g),
            jnp.where(
                phase == 1, block(1 - f, g), jnp.where(phase == 2, block(f, 1 - g), block(1 - f, 1 - g))
            ),
        )

        for d in (1, 2, 3):
            @pl.when(s == d)
            def _():
                along_copy(d).wait_recv()

        @pl.when((s > 0) & (phase == 0))
        def _():
            sib_copy(k).start()
            one_copy(zz).start()

        @pl.when(phase == 1)
        def _():
            one_copy(zz).wait_recv()
            sib_copy(k).start()
            for j in range(2):
                two_copy(zz, j).start()

        for j in range(2):
            @pl.when(phase == 2 + j)
            def _():
                two_copy(zz, j).wait_recv()
                sib_copy(k).start()

        sib_copy(k).wait_recv()
        forward_block(k)

    def joined(parts):
        highest = functools.reduce(jnp.maximum, [p[0] for p in parts])
        total = functools.reduce(jnp.add, [p[1] * jnp.exp(p[0] - highest) for p in parts])
        picked = functools.reduce(jnp.add, [p[2] for p in parts])
        return highest, total, picked

    def rows_of(ref, n):
        return ref[n, 0], ref[n, 1], ref[n, 2]

    for n, (peer, side) in enumerate(((sibling, c), (x_peer, x), (y_peer, y))):
        copy = remote(mine.at[n], theirs.at[n], st_send.at[n], st_recv.at[n], peer)
        copy.start()
        copy.wait()
        here, there = rows_of(mine, n), rows_of(theirs, n)
        early = tuple(jnp.where(side == 0, a, b) for a, b in zip(here, there))
        late = tuple(jnp.where(side == 0, b, a) for a, b in zip(here, there))
        for r, value in enumerate(joined((early, late))):
            mine[n + 1, r] = value

    def stat_copy(d):
        other = lax.rem(z + d, 4)
        return remote(mine.at[3], lined.at[z], stz_send.at[d - 1], stz_recv.at[d - 1], at(x, y, other, c))

    for d in (1, 2, 3):
        stat_copy(d).start()
    for r in range(3):
        lined[z, r] = mine[3, r]
    for d in (1, 2, 3):
        stat_copy(d).wait()
    highest, total, picked = joined([rows_of(lined, n) for n in range(4)])
    logsum = highest + jnp.log(total)
    log_probs = picked - logsum
    for k in range(16):
        prior[k : k + 1, :] = marks[k // 8, (k // 4) % 2, k % 4, 1:2, :]
        usable[k : k + 1, :] = marks[k // 8, (k // 4) % 2, k % 4, 2:3, :]
    lane = lax.broadcasted_iota(jnp.int32, (16, pair), 1) // length
    mean = jnp.zeros((16, pair), jnp.float32)
    for n in range(pair // length):
        inside = lane == n
        slot_sum = jnp.sum(jnp.where(inside, log_probs, 0.0), 1, keepdims=True)
        mean = jnp.where(inside, slot_sum * (1.0 / length), mean)
    scores = prior[...] + mean
    counted = usable[...] > 0.5
    masked = jnp.where(counted, scores, NEGATIVE)
    question = lax.broadcasted_iota(jnp.int32, (16, pair), 0) // 4
    marginal = jnp.zeros((16, pair), jnp.float32)
    loss = jnp.zeros((1, 1), jnp.float32)
    for n in range(4):
        inside = question == n
        high = jnp.max(
            jnp.max(jnp.where(inside, masked, NEGATIVE), 1, keepdims=True), 0, keepdims=True
        )
        terms = jnp.where(inside & counted, jnp.exp(masked - high), 0.0)
        mass = jnp.sum(jnp.sum(terms, 1, keepdims=True), 0, keepdims=True) * (1.0 / length)
        value = high + jnp.log(mass)
        marginal = jnp.where(inside, value, marginal)
        loss = loss + value
    posterior = jnp.where(counted, jnp.exp(scores - marginal), 0.0)
    token_weight = -float(slots) * posterior
    weight[...] = posterior
    scaled[...] = token_weight * jnp.exp(mine[0, 0] - logsum)
    picked_grad[...] = token_weight * (1.0 - jnp.exp(log_probs))
    small_out[...] = jnp.broadcast_to(loss * (-1.0 / 4), small_out.shape)
    own_row = weight[pl.ds(own, 1), :]
    own_row = jnp.where(c == 0, own_row[:, :size], own_row[:, size:])
    small_out[1:2, :] = own_row * (-float(slots * length))

    def backward_block(k):
        target = target_rows(k)
        hit = picked_grad[pl.ds(k, 1), :]
        scale = scaled[pl.ds(k, 1), :]

        def make(j, carried):
            value = expo[cut_rows(j), token_lanes(k)].astype(jnp.float32)
            grad = jnp.where(row_numbers(j) == target, hit, -(value * scale))
            expo[cut_rows(j), token_lanes(k)] = grad.astype(BFLOAT)
            return carried

        lax.fori_loop(0, VOCAB_CUTS, make, 0)

        def to_rows(n, carried):
            cut_width = pl.ds(pl.multiple_of(n * 256, 256), 256)
            value = lax.dot_general(
                emb_t[cut_width, :],
                expo[:, token_lanes(k)],
                (((1,), (0,)), ((), ())),
                preferred_element_type=jnp.float32,
            ).astype(BFLOAT)
            part[k, 0, cut_width, :] = value[:, :size]
            part[k, 1, cut_width, :] = value[:, size:]
            return carried

        lax.fori_loop(0, width // 256, to_rows, 0)

    def dd_copy(k):
        return remote(part.at[k, 1 - c], sib_part.at[k], dd_send.at[k], dd_recv.at[k], sibling)

    def r1_copy(zz, j):
        f, _, first_peer, _, block = order(zz)
        return remote(
            sib_part.at[block(1 - f, j)], part_one.at[zz, j], r1_send.at[zz, j], r1_recv.at[zz, j],
            first_peer,
        )

    def r2_copy(zz):
        _, g, _, second_peer, _ = order(zz)
        return remote(part_one.at[zz, 1 - g], part_two.at[zz], r2_send.at[zz], r2_recv.at[zz], second_peer)

    def rz_copy(zz):
        return remote(part_two.at[zz], part_z.at[z], rz_send.at[zz], rz_recv.at[z], at(x, y, zz, c))

    def rz_arrival(zz):
        return remote(part_two.at[zz], part_z.at[zz], rz_send.at[zz], rz_recv.at[zz], at(x, y, zz, c))

    step = 64

    def add_into(target_ref, other_ref):
        @pl.loop(0, width // step)
        def _(n):
            rows_here = pl.ds(pl.multiple_of(n * step, step), step)
            target_ref[rows_here, :] = (
                target_ref[rows_here, :].astype(jnp.float32) + other_ref[rows_here, :].astype(jnp.float32)
            ).astype(BFLOAT)

    def group(n):
        return lax.rem(n, 2) * 2 + n // 2

    def chunk(q):
        j, n = q // 4, lax.rem(q, 4)
        columns = pl.ds(pl.multiple_of(n * 256, 256), 256)
        gemb_out[cut_rows(j), columns] = lax.dot_general(
            expo[cut_rows(j), :],
            held[:, columns],
            (((1,), (0,)), ((), ())),
            preferred_element_type=jnp.float32,
        ).astype(BFLOAT)

    @pl.loop(0, 28)
    def _(s):
        turn = s // 4
        edge = lax.rem(s, 4) == 0

        @pl.when(edge & (turn >= 1) & (turn < 5))
        def _():
            zz = group(turn - 1)

            @pl.loop(0, 4)
            def _(n):
                k = n * 4 + zz
                dd_copy(k).wait_recv()
                add_into(sib_part.at[k], part.at[k, c])

            for j in range(2):
                r1_copy(zz, j).start()

        @pl.when(edge & (turn >= 2) & (turn < 6))
        def _():
            zz = group(turn - 2)
            f, _, _, _, block = order(zz)
            for j in range(2):
                r1_copy(zz, j).wait_recv()
                add_into(part_one.at[zz, j], sib_part.at[block(f, j)])
            r2_copy(zz).start()

        @pl.when(edge & (turn >= 3))
        def _():
            zz = group(turn - 3)
            _, g, _, _, _ = order(zz)
            r2_copy(zz).wait_recv()
            add_into(part_two.at[zz], part_one.at[zz, g])

            @pl.when(zz != z)
            def _():
                rz_copy(zz).start()

        @pl.when(s < 16)
        def _():
            k = lax.rem(s, 4) * 4 + group(turn)
            backward_block(k)
            dd_copy(k).start()

        @pl.when(s >= 16)
        def _():
            chunk(s - 16)

    for d in (1, 2, 3):
        rz_arrival(lax.rem(z + d, 4)).wait_recv()

    @pl.loop(0, width // step)
    def _(n):
        rows_here = pl.ds(pl.multiple_of(n * step, step), step)
        value = part_two[z, rows_here, :].astype(jnp.float32)
        for d in (1, 2, 3):
            value = value + part_z[lax.rem(z + d, 4), rows_here, :].astype(jnp.float32)
        third_out[rows_here, :] = value

    for d in (1, 2, 3):
        along_copy(d).wait_send()
        rz_copy(lax.rem(z + d, 4)).wait_send()

    @pl.loop(0, 4)
    def _(zz):
        one_copy(zz).wait_send()
        for j in range(2):
            two_copy(zz, j).wait_send()
            r1_copy(zz, j).wait_send()
        r2_copy(zz).wait_send()

    @pl.loop(0, 16)
    def _(k):
        sib_copy(k).wait_send()
        dd_copy(k).wait_send()


def vocabulary_head(third_low, targets, log_prior, usable, embedding, slots, length):
    size, width = third_low.shape
    vocab_here = embedding.shape[0]
    rows = 16 * VOCAB_CUTS * -(-vocab_here // (4 * 16 * VOCAB_CUTS))
    aux = jnp.zeros((8, size), jnp.float32)
    aux = aux.at[0].set(targets.astype(jnp.float32))
    aux = aux.at[1].set(jnp.repeat(log_prior, length))
    aux = aux.at[2].set(jnp.repeat(usable.astype(jnp.float32), length))
    dma = pltpu.SemaphoreType.DMA
    vmem = pl.BlockSpec(memory_space=pltpu.VMEM)
    stat = (3, 16, 2 * size)
    f32 = jnp.float32
    block = (width, size)
    small, gemb, third = pl.pallas_call(
        functools.partial(head_kernel, slots, length, vocab_here),
        out_shape=(
            jax.ShapeDtypeStruct((8, size), f32),
            jax.ShapeDtypeStruct((rows, width), BFLOAT),
            jax.ShapeDtypeStruct((width, size), f32),
        ),
        in_specs=[vmem, vmem, pl.BlockSpec(memory_space=pl.ANY)],
        out_specs=(vmem,) * 3,
        scratch_shapes=[
            pltpu.VMEM((rows, width), BFLOAT),
            pltpu.VMEM((width, rows), BFLOAT),
            pltpu.VMEM((32 * size, width), BFLOAT),
            pltpu.VMEM((2, 2, 4, 8, 2 * size), f32),
            pltpu.VMEM((rows, 2 * size), f32),
            pltpu.VMEM((rows, 32 * size), BFLOAT),
            pltpu.VMEM((16, 2) + block, BFLOAT),
            pltpu.VMEM((16,) + block, BFLOAT),
            pltpu.VMEM((4, 2) + block, BFLOAT),
            pltpu.VMEM((4,) + block, BFLOAT),
            pltpu.VMEM((4,) + block, BFLOAT),
            pltpu.VMEM((4,) + stat, f32),
            pltpu.VMEM((3,) + stat, f32),
            pltpu.VMEM((4,) + stat, f32),
        ]
        + [pltpu.VMEM((16, 2 * size), f32)] * 5
        + [dma((4,))]
        + [dma((3,))] * 2
        + [dma((4,))] * 2
        + [dma((4, 2))] * 2
        + [dma((16,))] * 2
        + [dma((3,))] * 8
        + [dma((16,))] * 2
        + [dma((4, 2))] * 2
        + [dma((4,))] * 4,
        compiler_params=pltpu.CompilerParams(
            collective_id=2, has_side_effects=True, vmem_limit_bytes=60 * 2**20
        ),
        name="vocabulary_head",
    )(third_low, aux, embedding)
    return small, gemb, third


def merged(part, axis, combine):
    gathered = jax.tree.map(lambda a: lax.all_gather(a, axis), part)

    def take(source):
        return jax.tree.map(lambda a: lax.dynamic_index_in_dim(a, source, 0, False), gathered)

    return lax.fori_loop(
        1, lax.axis_size(axis), lambda source, state: combine(state, take(source)), take(0)
    )


def matmul(matrix_left, matrix_right):
    return lax.dot_general(
        matrix_left,
        matrix_right,
        (((matrix_left.ndim - 1,), (0,)), ((), ())),
        preferred_element_type=jnp.float32,
    )


def matmul_back(matrix_left, matrix_right):
    return lax.dot_general(
        matrix_left,
        matrix_right,
        (((matrix_left.ndim - 1,), (1,)), ((), ())),
        preferred_element_type=jnp.float32,
    )


def outer_sum(matrix_left, matrix_right):
    flat_left = matrix_left.reshape(-1, matrix_left.shape[-1])
    flat_right = matrix_right.reshape(-1, matrix_right.shape[-1])
    return lax.dot_general(
        flat_left, flat_right, (((0,), (0,)), ((), ())), preferred_element_type=jnp.float32
    )


def split_heads(values):
    return values.reshape(values.shape[0], values.shape[1], HEADS, HEAD_DIM)


def join_heads(values):
    return values.reshape(values.shape[0], values.shape[1], HEADS * HEAD_DIM)


def exact_gelu(values):
    return jax.nn.gelu(values, approximate=False)


def norm_forward(values, gain_row, shift_row):
    centre = values - jnp.mean(values, -1, keepdims=True)
    inverse = lax.rsqrt(jnp.mean(centre * centre, -1, keepdims=True) + EPSILON)
    normed = centre * inverse
    return (normed * gain_row.astype(jnp.float32) + shift_row.astype(jnp.float32), normed, inverse)


def norm_backward(upstream, normed, inverse, gain_row):
    scaled = upstream * gain_row.astype(jnp.float32)
    mean_scaled = jnp.mean(scaled, -1, keepdims=True)
    along_normed = jnp.mean(scaled * normed, -1, keepdims=True)
    grad_values = inverse * (scaled - mean_scaled - normed * along_normed)
    model_width = upstream.shape[-1]
    grad_gain = jnp.sum((upstream * normed).reshape(-1, model_width), 0)
    grad_shift = jnp.sum(upstream.reshape(-1, model_width), 0)
    return (grad_values, grad_gain, grad_shift)


def score_block(queries, key_rows, causal):
    scores = jnp.einsum(
        "nqhd,nkhd->nhqk", queries, key_rows, preferred_element_type=jnp.float32
    ) * (1.0 / math.sqrt(HEAD_DIM))
    if causal:
        length = queries.shape[1]
        allowed = lax.broadcasted_iota(jnp.int32, (length, length), 0) >= lax.broadcasted_iota(
            jnp.int32, (length, length), 1
        )
        scores = jnp.where(allowed, scores, NEGATIVE)
    return scores


def attend(queries, key_rows, values, causal):
    scores = score_block(queries, key_rows, causal)
    highest = jnp.max(scores, -1, keepdims=True)
    totals = jnp.sum(jnp.exp(scores - highest), -1, keepdims=True)
    logsum = highest + jnp.log(totals)
    probs_low = jnp.exp(scores - logsum).astype(BFLOAT)
    context = jnp.einsum(
        "nhqk,nkhd->nqhd", probs_low, values, preferred_element_type=jnp.float32
    ).astype(BFLOAT)
    return (join_heads(context), logsum)


def attend_back(grad_context, queries, key_rows, values, logsum, causal):
    score_scale = 1.0 / math.sqrt(HEAD_DIM)
    probs_full = jnp.exp(score_block(queries, key_rows, causal) - logsum)
    grad_heads = split_heads(grad_context)
    grad_probs = jnp.einsum(
        "nqhd,nkhd->nhqk", grad_heads, values, preferred_element_type=jnp.float32
    )
    grad_values = jnp.einsum(
        "nhqk,nqhd->nkhd", probs_full.astype(BFLOAT), grad_heads, preferred_element_type=jnp.float32
    ).astype(BFLOAT)
    grad_scores = (
        probs_full * (grad_probs - jnp.sum(probs_full * grad_probs, -1, keepdims=True))
    ).astype(BFLOAT)
    grad_queries = (
        jnp.einsum("nhqk,nkhd->nqhd", grad_scores, key_rows, preferred_element_type=jnp.float32)
        * score_scale
    ).astype(BFLOAT)
    grad_keys = (
        jnp.einsum("nhqk,nqhd->nkhd", grad_scores, queries, preferred_element_type=jnp.float32)
        * score_scale
    ).astype(BFLOAT)
    return (join_heads(grad_queries), join_heads(grad_keys), join_heads(grad_values))


def layer_forward(inputs, encoded, weights):
    (
        packed_weight,
        output_weight,
        query_weight,
        memory_weight,
        cross_weight,
        expand_weight,
        reduce_weight,
        gains,
        shifts,
    ) = weights
    model_width = inputs.shape[-1]
    packed = matmul(inputs, packed_weight).astype(BFLOAT)
    context, self_logsum = attend(
        split_heads(packed[..., :model_width]),
        split_heads(packed[..., model_width : 2 * model_width]),
        split_heads(packed[..., 2 * model_width :]),
        True,
    )
    first_norm, first_normed, first_inverse = norm_forward(
        inputs.astype(jnp.float32) + matmul(context, output_weight), gains[0], shifts[0]
    )
    first_low = first_norm.astype(BFLOAT)
    cross_queries = matmul(first_low, query_weight).astype(BFLOAT)
    memory_pairs = matmul(encoded, memory_weight).astype(BFLOAT)
    cross_context, cross_logsum = attend(
        split_heads(cross_queries),
        split_heads(memory_pairs[..., :model_width]),
        split_heads(memory_pairs[..., model_width:]),
        False,
    )
    second, second_normed, second_inverse = norm_forward(
        first_norm + matmul(cross_context, cross_weight), gains[1], shifts[1]
    )
    second_low = second.astype(BFLOAT)
    inner_pre = matmul(second_low, expand_weight)
    active = exact_gelu(inner_pre).astype(BFLOAT)
    third_norm, third_normed, third_inverse = norm_forward(
        second + matmul(active, reduce_weight), gains[2], shifts[2]
    )
    stored = (
        packed,
        context,
        self_logsum,
        first_normed,
        first_inverse,
        first_low,
        cross_queries,
        memory_pairs,
        cross_context,
        cross_logsum,
        second_normed,
        second_inverse,
        second_low,
        inner_pre,
        active,
        third_normed,
        third_inverse,
    )
    return (third_norm.astype(BFLOAT), stored)


def layer_backward(grad_third, inputs, encoded, weights, stored):
    (
        packed_weight,
        output_weight,
        query_weight,
        memory_weight,
        cross_weight,
        expand_weight,
        reduce_weight,
        gains,
        shifts,
    ) = weights
    (
        packed,
        context,
        self_logsum,
        first_normed,
        first_inverse,
        first_low,
        cross_queries,
        memory_pairs,
        cross_context,
        cross_logsum,
        second_normed,
        second_inverse,
        second_low,
        inner_pre,
        active,
        third_normed,
        third_inverse,
    ) = stored
    model_width = inputs.shape[-1]
    grad_res3, gain_three, shift_three = norm_backward(
        grad_third, third_normed, third_inverse, gains[2]
    )
    grad_output = grad_res3.astype(BFLOAT)
    grad_reduce = outer_sum(active, grad_output)
    grad_active = matmul_back(grad_output, reduce_weight)
    _, gelu_pull = jax.vjp(exact_gelu, inner_pre)
    grad_inner = gelu_pull(grad_active)[0].astype(BFLOAT)
    grad_expand = outer_sum(second_low, grad_inner)
    grad_second = grad_res3 + matmul_back(grad_inner, expand_weight)
    grad_res2, gain_two, shift_two = norm_backward(
        grad_second, second_normed, second_inverse, gains[1]
    )
    grad_mixed = grad_res2.astype(BFLOAT)
    grad_cross_weight = outer_sum(cross_context, grad_mixed)
    grad_cross_context = matmul_back(grad_mixed, cross_weight).astype(BFLOAT)
    grad_cross_queries, grad_memory_keys, grad_memory_values = attend_back(
        grad_cross_context,
        split_heads(cross_queries),
        split_heads(memory_pairs[..., :model_width]),
        split_heads(memory_pairs[..., model_width:]),
        cross_logsum,
        False,
    )
    grad_query_weight = outer_sum(first_low, grad_cross_queries)
    grad_first = grad_res2 + matmul_back(grad_cross_queries, query_weight)
    grad_pairs = jnp.concatenate([grad_memory_keys, grad_memory_values], -1)
    grad_memory_weight = outer_sum(encoded, grad_pairs)
    grad_encoded = matmul_back(grad_pairs, memory_weight)
    grad_res1, gain_one, shift_one = norm_backward(
        grad_first, first_normed, first_inverse, gains[0]
    )
    grad_merged = grad_res1.astype(BFLOAT)
    grad_output_weight = outer_sum(context, grad_merged)
    grad_context = matmul_back(grad_merged, output_weight).astype(BFLOAT)
    grad_queries, grad_keys, grad_values = attend_back(
        grad_context,
        split_heads(packed[..., :model_width]),
        split_heads(packed[..., model_width : 2 * model_width]),
        split_heads(packed[..., 2 * model_width :]),
        self_logsum,
        True,
    )
    grad_packed = jnp.concatenate([grad_queries, grad_keys, grad_values], -1)
    grad_packed_weight = outer_sum(inputs, grad_packed)
    grad_inputs = grad_res1 + matmul_back(grad_packed, packed_weight)
    grad_gains = jnp.stack([gain_one, gain_two, gain_three])
    grad_shifts = jnp.stack([shift_one, shift_two, shift_three])
    return (
        grad_inputs,
        grad_encoded,
        (
            grad_packed_weight,
            grad_output_weight,
            grad_query_weight,
            grad_memory_weight,
            grad_cross_weight,
            grad_expand,
            grad_reduce,
            grad_gains,
            grad_shifts,
        ),
    )


def combine_scores(former, latter):
    highest = jnp.maximum(former[0], latter[0])
    totals = former[1] * jnp.exp(former[0] - highest) + latter[1] * jnp.exp(latter[0] - highest)
    return (highest, totals, former[2] + latter[2])


def combine_pairs(former, latter):
    highest = jnp.maximum(former[0], latter[0])
    totals = former[1] * jnp.exp(former[0] - highest) + latter[1] * jnp.exp(latter[0] - highest)
    return (highest, totals)


def per_device(
    decoder_states,
    encoder_memory,
    target_tokens,
    log_prior,
    slot_counts,
    slot_mask,
    self_packed,
    self_output,
    cross_query,
    cross_memory,
    cross_output,
    feed_expand,
    feed_reduce,
    embedding,
    norm_gains,
    norm_shifts,
):
    weights = (
        lax.all_gather(self_packed, "pa", axis=0, tiled=True),
        lax.all_gather(self_output, "pa", axis=0, tiled=True),
        lax.all_gather(cross_query, "pa", axis=0, tiled=True),
        lax.all_gather(cross_memory, "pa", axis=0, tiled=True),
        lax.all_gather(cross_output, "pa", axis=0, tiled=True),
        lax.all_gather(feed_expand, "pa", axis=0, tiled=True),
        lax.all_gather(feed_reduce, "pa", axis=0, tiled=True),
        lax.all_gather(norm_gains, "pa", axis=1, tiled=True),
        lax.all_gather(norm_shifts, "pa", axis=1, tiled=True),
    )
    questions, slots_here, length, model_width = decoder_states.shape
    mem_length = encoder_memory.shape[2]
    batch_size = questions * slots_here
    inputs = decoder_states.reshape(batch_size, length, model_width)
    encoded = encoder_memory.reshape(batch_size, mem_length, model_width)
    third_low, stored = layer_forward(inputs, encoded, weights)
    tokens_here = batch_size * length
    rows_all, tokens_all = (
        lax.all_gather(third_low.reshape(tokens_here, model_width), "pa", axis=0, tiled=True),
        lax.all_gather(target_tokens.reshape(tokens_here), "pa", axis=0, tiled=True),
    )
    total_rows = rows_all.shape[0]
    block_rows = min(total_rows, 2048)
    block_count = total_rows // block_rows
    vocab_start = lax.axis_index("pa") * embedding.shape[0]
    row_blocks = rows_all.reshape(block_count, block_rows, model_width)
    token_blocks = tokens_all.reshape(block_count, block_rows)

    def vocab_logits(hidden_rows, token_rows):
        logits = matmul_back(hidden_rows, embedding)
        column = lax.broadcasted_iota(jnp.int32, logits.shape, 1) + vocab_start
        return (logits, column == token_rows[:, None])

    def vocab_partial(pieces):
        logits, chosen = vocab_logits(pieces[0], pieces[1])
        highest = jnp.max(logits, -1)
        totals = jnp.sum(jnp.exp(logits - highest[:, None]), -1)
        picked = jnp.sum(jnp.where(chosen, logits, 0.0), -1)
        return (highest, totals, picked)

    highest, totals, picked = lax.map(vocab_partial, (row_blocks, token_blocks))
    highest, totals, picked = merged(
        (highest.reshape(total_rows), totals.reshape(total_rows), picked.reshape(total_rows)),
        "pa",
        combine_scores,
    )
    row_logsum = highest + jnp.log(totals)
    own_start = lax.axis_index("pa") * tokens_here
    own_logsum = lax.dynamic_slice_in_dim(row_logsum, own_start, tokens_here)
    own_picked = lax.dynamic_slice_in_dim(picked, own_start, tokens_here)
    log_probs = (own_picked - own_logsum).reshape(questions, slots_here, length)
    scores = log_prior + jnp.mean(log_probs, -1)
    slot_index = lax.axis_index("pa") * slots_here + lax.broadcasted_iota(
        jnp.int32, (questions, slots_here), 1
    )
    usable = (slot_mask == 1) & (slot_index < slot_counts[:, None])
    masked = jnp.where(usable, scores, NEGATIVE)
    local_high = jnp.max(masked, -1)
    local_total = jnp.sum(jnp.where(usable, jnp.exp(masked - local_high[:, None]), 0.0), -1)
    slot_high, slot_total = merged((local_high, local_total), "pa", combine_pairs)
    marginal = slot_high + jnp.log(slot_total)
    posterior = jnp.where(usable, jnp.exp(scores - marginal[:, None]), 0.0)
    loss_value = -lax.psum(jnp.sum(marginal), "pb") / (questions * lax.axis_size("pb"))
    slot_number = slots_here * lax.axis_size("pa")
    grad_prior = -(slot_number * length) * posterior
    token_grad = jnp.broadcast_to(
        (-slot_number * posterior)[:, :, None], (questions, slots_here, length)
    ).reshape(tokens_here)
    weights_all = lax.all_gather(token_grad, "pa", axis=0, tiled=True)

    def vocab_grads(accumulated, pieces):
        hidden_rows, token_rows, logsum_rows, weight_rows = pieces
        logits, chosen = vocab_logits(hidden_rows, token_rows)
        softmax_rows = jnp.exp(logits - logsum_rows[:, None])
        grad_logits = (weight_rows[:, None] * (jnp.where(chosen, 1.0, 0.0) - softmax_rows)).astype(
            BFLOAT
        )
        return (accumulated + outer_sum(grad_logits, hidden_rows), matmul(grad_logits, embedding))

    grad_embed, grad_rows = lax.scan(
        vocab_grads,
        jnp.zeros(embedding.shape, jnp.float32),
        (
            row_blocks,
            token_blocks,
            row_logsum.reshape(block_count, block_rows),
            weights_all.reshape(block_count, block_rows),
        ),
    )
    grad_third = lax.psum_scatter(
        grad_rows.reshape(total_rows, model_width).astype(BFLOAT),
        "pa",
        scatter_dimension=0,
        tiled=True,
    ).astype(jnp.float32).reshape(batch_size, length, model_width)
    grad_inputs, grad_encoded, grads = layer_backward(grad_third, inputs, encoded, weights, stored)
    shares = (
        lax.psum_scatter(grads[0].astype(BFLOAT), "pa", scatter_dimension=0, tiled=True),
        lax.psum_scatter(grads[1].astype(BFLOAT), "pa", scatter_dimension=0, tiled=True),
        lax.psum_scatter(grads[2].astype(BFLOAT), "pa", scatter_dimension=0, tiled=True),
        lax.psum_scatter(grads[3].astype(BFLOAT), "pa", scatter_dimension=0, tiled=True),
        lax.psum_scatter(grads[4].astype(BFLOAT), "pa", scatter_dimension=0, tiled=True),
        lax.psum_scatter(grads[5].astype(BFLOAT), "pa", scatter_dimension=0, tiled=True),
        lax.psum_scatter(grads[6].astype(BFLOAT), "pa", scatter_dimension=0, tiled=True),
        lax.psum_scatter(grads[7], "pa", scatter_dimension=1, tiled=True),
        lax.psum_scatter(grads[8], "pa", scatter_dimension=1, tiled=True),
    )
    outputs = lax.psum(
        (
            shares[0],
            shares[1],
            shares[2],
            shares[3],
            shares[4],
            shares[5],
            shares[6],
            shares[7],
            shares[8],
            grad_embed.astype(BFLOAT),
        ),
        "pb",
    )
    outputs = tuple(part.astype(jnp.float32) for part in outputs)
    return (
        loss_value,
        grad_inputs.reshape(decoder_states.shape),
        grad_encoded.reshape(encoder_memory.shape),
        grad_prior,
        outputs[0],
        outputs[1],
        outputs[2],
        outputs[3],
        outputs[4],
        outputs[5],
        outputs[6],
        outputs[9],
        outputs[7],
        outputs[8],
    )


def score_logsum(queries, key_rows, causal):
    scores = score_block(split_heads(queries), split_heads(key_rows), causal)
    highest = jnp.max(scores, -1, keepdims=True)
    return highest + jnp.log(jnp.sum(jnp.exp(scores - highest), -1, keepdims=True))


def per_device_kernels(
    decoder_states,
    encoder_memory,
    target_tokens,
    log_prior,
    slot_counts,
    slot_mask,
    self_packed,
    self_output,
    cross_query,
    cross_memory,
    cross_output,
    feed_expand,
    feed_reduce,
    embedding,
    norm_gains,
    norm_shifts,
):
    shards = (
        self_packed,
        self_output,
        cross_query,
        cross_memory,
        cross_output,
        feed_expand,
        feed_reduce,
    )
    norm_rows = jnp.concatenate(
        [norm_gains, norm_shifts, jnp.zeros((2, norm_gains.shape[1]), BFLOAT)]
    ).astype(jnp.float32)
    _, slots_here, length, model_width = decoder_states.shape
    slots = slots_here * lax.axis_size("pa")
    inputs = decoder_states[0]
    encoded = encoder_memory[0]
    matrices, norms, kept = forward_layer(
        shards,
        norm_rows,
        inputs.reshape(slots_here * length, model_width),
        encoded.reshape(-1, model_width),
        length,
    )
    weights = matrices + (norms[:3], norms[3:6])
    (
        packed, context, first_normed, first_inverse, first_low, cross_queries, pairs,
        cross_context, second_normed, second_inverse, second_low, inner, active, third_normed,
        third_inverse, third_low,
    ) = (part.reshape(slots_here, -1, part.shape[-1]) for part in kept)
    self_logsum = score_logsum(packed[..., :model_width], packed[..., model_width : 2 * model_width], True)
    cross_logsum = score_logsum(cross_queries, pairs[..., :model_width], False)
    stored = (
        packed, context, self_logsum, first_normed, first_inverse[..., :1], first_low, cross_queries,
        pairs, cross_context, cross_logsum, second_normed, second_inverse[..., :1], second_low, inner,
        active, third_normed, third_inverse[..., :1],
    )
    slot_index = lax.axis_index("pa") * slots_here + jnp.arange(slots_here)
    usable = (slot_mask[0] == 1) & (slot_index < slot_counts[0])
    small, grad_embed, grad_third = vocabulary_head(
        third_low.reshape(slots_here * length, model_width),
        target_tokens.reshape(slots_here * length),
        log_prior[0],
        usable,
        embedding,
        slots,
        length,
    )
    loss_value = small[0, 0]
    grad_prior = small[1].reshape(1, slots_here, length)[:, :, 0]
    pieces = lax.all_gather(grad_embed, "pb", axis=0)
    pieces = pieces.reshape(4 * grad_embed.shape[0], model_width)
    grad_embed = pieces[: embedding.shape[0]].astype(jnp.float32)
    grad_third = grad_third.T.reshape(slots_here, length, model_width)
    grad_inputs, grad_encoded, grads = layer_backward(grad_third, inputs, encoded, weights, stored)
    low_grads = tuple(grad.astype(BFLOAT) for grad in grads[:7])
    norm_grads = jnp.concatenate([grads[7], grads[8], jnp.zeros((2, model_width), jnp.float32)])
    shares, norm_sums = reduce_grads(low_grads, norm_grads)
    norm_here = norm_gains.shape[1]
    norm_sums = lax.dynamic_slice_in_dim(
        norm_sums, lax.axis_index("pa") * norm_here, norm_here, axis=1
    )
    return (
        loss_value,
        grad_inputs.reshape(decoder_states.shape),
        grad_encoded.reshape(encoder_memory.shape),
        grad_prior,
    ) + shares + (grad_embed, norm_sums[:3], norm_sums[3:6])


def solution(mesh):
    own_kernels = mesh.shape["pb"] == 4 and mesh.shape["pa"] == 8
    return jax.shard_map(
        per_device_kernels if own_kernels else per_device,
        mesh=mesh,
        in_specs=(
            P("pb", "pa", None, None),
            P("pb", "pa", None, None),
            P("pb", "pa", None),
            P("pb", "pa"),
            P("pb"),
            P("pb", "pa"),
            P("pa", None),
            P("pa", None),
            P("pa", None),
            P("pa", None),
            P("pa", None),
            P("pa", None),
            P("pa", None),
            P("pa", None),
            P(None, "pa"),
            P(None, "pa"),
        ),
        out_specs=(
            P(),
            P("pb", "pa", None, None),
            P("pb", "pa", None, None),
            P("pb", "pa"),
            P("pa", None),
            P("pa", None),
            P("pa", None),
            P("pa", None),
            P("pa", None),
            P("pa", None),
            P("pa", None),
            P("pa", None),
            P(None, "pa"),
            P(None, "pa"),
        ),
        check_vma=False,
    )
```

```python
import functools
import math

import jax
import jax.numpy as jnp
from jax import lax
from jax.experimental import pallas as pl
from jax.experimental.pallas import tpu as pltpu
from jax.sharding import PartitionSpec as P

HEADS = 16
HEAD_DIM = 64


EPSILON = 1e-05
NEGATIVE = -1e30
BFLOAT = jnp.bfloat16
MESH = pl.DeviceIdType.MESH
TILE = 1024
ROWS = 128
WEIGHT_UNITS = (3, 1, 1, 2, 1, 4, 4)
UNITS = tuple((w, k) for w, n in enumerate(WEIGHT_UNITS) for k in range(n))
REDUCE_WEIGHT = 6


def whereami():
    pb = lax.axis_index("pb")
    pa = lax.axis_index("pa")
    return lax.rem(pb, 2), pb // 2, pa // 2, lax.rem(pa, 2)


def greet(peers):
    barrier = pltpu.get_barrier_semaphore()
    for peer in peers:
        pl.semaphore_signal(barrier, inc=1, device_id=peer, device_id_type=MESH)
    pl.semaphore_wait(barrier, len(peers))


def at(x, y, z, c):
    return (y * 2 + x, z * 2 + c)


def neighbours(x, y, z, c):
    return [at(1 - x, y, z, c), at(x, 1 - y, z, c), at(x, y, z, 1 - c)] + [
        at(x, y, lax.rem(z + d, 4), c) for d in (1, 2, 3)
    ]


def shard_view(ref, unit, start, size):
    weight, block = unit
    if weight == REDUCE_WEIGHT:
        return ref.at[pl.ds(block * ROWS + start, size), :]
    return ref.at[pl.ds(start, size), pl.ds(block * TILE, TILE)]


def full_view(ref, unit, place, core, start, size):
    weight, block = unit
    if weight == REDUCE_WEIGHT:
        return ref.at[place, core, block, pl.ds(start, size), :]
    return ref.at[place, core, pl.ds(start, size), pl.ds(block * TILE, TILE)]


Z_FULL = (9, 14)


GATHER_WINDOW = 4
LAG_TWO, LAG_SIBLING, LAG_LOAD, LAG_USE = 1, 2, 4, 5
SLOTS_IN_FLIGHT = 3


def dot_nn(left, right):
    return lax.dot_general(left, right, (((1,), (0,)), ((), ())), preferred_element_type=jnp.float32)


def dot_nt(left, right):
    return lax.dot_general(left, right, (((1,), (1,)), ((), ())), preferred_element_type=jnp.float32)


def dot_tn(left, right):
    return lax.dot_general(left, right, (((0,), (0,)), ((), ())), preferred_element_type=jnp.float32)


def stack_heads(pair):
    lane = lax.broadcasted_iota(jnp.int32, pair.shape, 1)
    zero = jnp.zeros_like(pair)
    return jnp.concatenate(
        [jnp.where(lane < HEAD_DIM, pair, zero), jnp.where(lane < HEAD_DIM, zero, pair)], 0
    )


def unstack_heads(stacked):
    rows = stacked.shape[0] // 2
    lane = lax.broadcasted_iota(jnp.int32, (rows, stacked.shape[1]), 1)
    return jnp.where(lane < HEAD_DIM, stacked[:rows], stacked[rows:])


def pair_scores(queries, keys, causal):
    scores = dot_nt(queries, keys) * (1.0 / math.sqrt(HEAD_DIM))
    if causal:
        length = keys.shape[0]
        row = lax.rem(lax.broadcasted_iota(jnp.int32, scores.shape, 0), length)
        column = lax.broadcasted_iota(jnp.int32, scores.shape, 1)
        scores = jnp.where(row >= column, scores, NEGATIVE)
    highest = jnp.max(scores, -1, keepdims=True)
    total = jnp.sum(jnp.exp(scores - highest), -1, keepdims=True)
    return jnp.exp(scores - (highest + jnp.log(total)))


def attend_pair(queries, keys, values, causal):
    probs = pair_scores(stack_heads(queries), keys, causal).astype(BFLOAT)
    return unstack_heads(dot_nn(probs, values)).astype(BFLOAT)


def normalise(values, gain, shift):
    centre = values - jnp.mean(values, -1, keepdims=True)
    inverse = lax.rsqrt(jnp.mean(centre * centre, -1, keepdims=True) + EPSILON)
    normed = centre * inverse
    return normed * gain + shift, normed, inverse


def forward_kernel(length, mem_length, *refs):
    shards, norm, states, encoded = refs[:7], refs[7], refs[8], refs[9]
    fulls = refs[10:17]
    (
        norm_full, packed, context, first_normed, first_inverse, first_low, cross_queries, pairs,
        cross_context, second_normed, second_inverse, second_low, inner, active, third_normed,
        third_inverse, third_low,
    ) = refs[17:34]
    wbuf, residual = refs[34:36]
    (
        local_sem, z_send, z_recv, one_send, one_recv, two_send, two_recv, d_send, d_recv,
        norm_sem, nz_send, nz_recv, nd_send, nd_recv, load_sem,
    ) = refs[36:]
    x, y, z, c = whereami()
    greet(neighbours(x, y, z, c))
    every = slice(None)
    tokens, width = states.shape
    slots_here = tokens // length

    def copies(u):
        unit = UNITS[u]
        shard, full = shards[unit[0]], fulls[unit[0]]
        wide = u in Z_FULL
        a, b = (x, y) if u % 2 == 0 else (y, x)
        first_peer = at(x, 1 - y, z, c) if u % 2 == 0 else at(1 - x, y, z, c)
        second_peer = at(1 - x, y, z, c) if u % 2 == 0 else at(x, 1 - y, z, c)
        quarter = pl.multiple_of(64 * a + 32 * b, 32)
        half = pl.multiple_of(64 * a, 64)
        rows = (0, ROWS) if wide else (quarter, 32)
        local = pltpu.make_async_copy(
            shard_view(shard, unit, *rows), full_view(full, unit, z, c, *rows), local_sem.at[u]
        )
        along = [
            pltpu.make_async_remote_copy(
                src_ref=shard_view(shard, unit, *rows),
                dst_ref=full_view(full, unit, z, c, *rows),
                send_sem=z_send.at[u, d - 1],
                recv_sem=z_recv.at[u, d - 1],
                device_id=at(x, y, lax.rem(z + d, 4), c),
                device_id_type=MESH,
            )
            for d in (1, 2, 3)
        ]

        def cross(start, size, sends, recvs, peer):
            part = full_view(full, unit, every, c, start, size)
            return pltpu.make_async_remote_copy(
                src_ref=part,
                dst_ref=part,
                send_sem=sends.at[u],
                recv_sem=recvs.at[u],
                device_id=peer,
                device_id_type=MESH,
            )

        first = None if wide else cross(quarter, 32, one_send, one_recv, first_peer)
        second = None if wide else cross(half, 64, two_send, two_recv, second_peer)
        sibling = cross(0, ROWS, d_send, d_recv, at(x, y, z, 1 - c))
        load = pltpu.make_async_copy(
            full_view(full, unit, every, every, 0, ROWS),
            wbuf.at[u % SLOTS_IN_FLIGHT],
            load_sem.at[u % SLOTS_IN_FLIGHT],
        )
        return local, along, first, second, sibling, load

    def norm_copy(src, dst, send, recv, peer):
        return pltpu.make_async_remote_copy(
            src_ref=src, dst_ref=dst, send_sem=send, recv_sem=recv, device_id=peer, device_id_type=MESH
        )

    norm_local = pltpu.make_async_copy(norm, norm_full.at[z, c], norm_sem)
    norm_along = [
        norm_copy(
            norm, norm_full.at[z, c], nz_send.at[d - 1], nz_recv.at[d - 1], at(x, y, lax.rem(z + d, 4), c)
        )
        for d in (1, 2, 3)
    ]
    norm_sibling = norm_copy(
        norm_full.at[:, c], norm_full.at[:, c], nd_send, nd_recv, at(x, y, z, 1 - c)
    )
    norm_local.start()
    for copy in norm_along:
        copy.start()

    def norm_row(n):
        return jnp.concatenate(
            [norm_full[p // 2, p % 2, n : n + 1, :] for p in range(8)], 1
        )

    def times(left_ref, u, write):
        slot = u % SLOTS_IN_FLIGHT

        @pl.loop(0, 4)
        def _(n):
            columns = pl.ds(pl.multiple_of(n * 256, 256), 256)
            right = wbuf[slot, :, :, :, columns].reshape(TILE, 256)
            write(columns, n, dot_nn(left_ref[...], right))

    def block_columns(k, n):
        return pl.ds(pl.multiple_of(k * TILE + n * 256, 256), 256)

    def attention(queries, keys, key_start, value_start, key_length, out, causal):
        @pl.loop(0, slots_here * (width // 128))
        def _(n):
            slot, group = n // (width // 128), lax.rem(n, width // 128)
            lanes = pl.ds(pl.multiple_of(group * 128, 128), 128)
            key_lanes = pl.ds(pl.multiple_of(key_start + group * 128, 128), 128)
            value_lanes = pl.ds(pl.multiple_of(value_start + group * 128, 128), 128)
            query_rows = pl.ds(pl.multiple_of(slot * length, length), length)
            key_rows = pl.ds(pl.multiple_of(slot * key_length, key_length), key_length)
            out[query_rows, lanes] = attend_pair(
                queries[query_rows, lanes], keys[key_rows, key_lanes], keys[key_rows, value_lanes], causal
            )

    def finish_norm(n, value, normed_ref, inverse_ref, low_ref):
        out, normed, inverse = normalise(value, norm_row(n), norm_row(n + 3))
        normed_ref[...] = normed
        inverse_ref[...] = jnp.broadcast_to(inverse, inverse_ref.shape)
        low_ref[...] = out.astype(BFLOAT)
        return out

    def use(u):
        weight, k = UNITS[u]
        if weight == 0:
            def write(columns, n, value):
                packed[:, block_columns(k, n)] = value.astype(BFLOAT)

            times(states, u, write)
            if k == 2:
                attention(packed, packed, width, 2 * width, length, context, True)
        elif weight == 1:
            def write(columns, n, value):
                residual[:, columns] = states[:, columns].astype(jnp.float32) + value

            times(context, u, write)
            residual[...] = finish_norm(0, residual[...], first_normed, first_inverse, first_low)
        elif weight == 2:
            def write(columns, n, value):
                cross_queries[:, columns] = value.astype(BFLOAT)

            times(first_low, u, write)
        elif weight == 3:
            slot = u % SLOTS_IN_FLIGHT

            @pl.loop(0, 16)
            def _(n):
                m, n = n // 4, lax.rem(n, 4)
                columns = pl.ds(pl.multiple_of(n * 256, 256), 256)
                part = encoded.shape[0] // 4
                rows_here = pl.ds(pl.multiple_of(m * part, part), part)
                right = wbuf[slot, :, :, :, columns].reshape(TILE, 256)
                pairs[rows_here, block_columns(k, n)] = dot_nn(encoded[rows_here, :], right).astype(BFLOAT)

            if k == 1:
                attention(cross_queries, pairs, 0, width, mem_length, cross_context, False)
        elif weight == 4:
            def write(columns, n, value):
                residual[:, columns] = residual[:, columns] + value

            times(cross_context, u, write)
            residual[...] = finish_norm(1, residual[...], second_normed, second_inverse, second_low)
        elif weight == 5:
            def write(columns, n, value):
                inner[:, block_columns(k, n)] = value
                gate = 0.5 * (1.0 + lax.erf(value * math.sqrt(0.5)))
                active[:, block_columns(k, n)] = (value * gate).astype(BFLOAT)

            times(second_low, u, write)
        else:
            slot = u % SLOTS_IN_FLIGHT
            blocks = active.shape[1] // (8 * ROWS)
            left = jnp.concatenate(
                [active[:, (p * blocks + k) * ROWS : (p * blocks + k + 1) * ROWS] for p in range(8)], 1
            )

            @pl.loop(0, 4)
            def _(n):
                columns = pl.ds(pl.multiple_of(n * 256, 256), 256)
                right = wbuf[slot, :, :, :, columns].reshape(TILE, 256)
                residual[:, columns] = residual[:, columns] + dot_nn(left, right)

            if k == blocks - 1:
                finish_norm(2, residual[...], third_normed, third_inverse, third_low)

    count = len(UNITS)
    every_copy = [copies(u) for u in range(count)]
    for local, along, _, _, _, _ in every_copy[:GATHER_WINDOW]:
        local.start()
        for copy in along:
            copy.start()
    for i in range(count + LAG_USE):
        if i + GATHER_WINDOW < count:
            local, along = every_copy[i + GATHER_WINDOW][:2]
            local.start()
            for copy in along:
                copy.start()
        if i < count:
            local, along, first = every_copy[i][:3]
            local.wait()
            for copy in along:
                copy.wait_recv()
            if first is not None:
                first.start()
        if 0 <= i - LAG_TWO < count:
            first, second = every_copy[i - LAG_TWO][2:4]
            if first is not None:
                first.wait_recv()
                second.start()
        if 0 <= i - LAG_SIBLING < count:
            second, sibling = every_copy[i - LAG_SIBLING][3:5]
            if second is not None:
                second.wait_recv()
            sibling.start()
        if i == 2:
            norm_local.wait()
            for copy in norm_along:
                copy.wait()
            norm_sibling.start()
        if i == 4:
            norm_sibling.wait()
        if 0 <= i - LAG_LOAD < count:
            sibling, load = every_copy[i - LAG_LOAD][4:]
            sibling.wait_recv()
            load.start()
        if 0 <= i - LAG_USE < count:
            every_copy[i - LAG_USE][5].wait()
            use(i - LAG_USE)
    for _, along, first, second, sibling, _ in every_copy:
        for copy in along:
            copy.wait_send()
        if first is not None:
            first.wait_send()
            second.wait_send()
        sibling.wait_send()


def forward_layer(weights, norm, states, encoded, length):
    count = len(UNITS)
    shapes = []
    for w, weight in enumerate(weights):
        if w == REDUCE_WEIGHT:
            shapes.append((4, 2, weight.shape[0] // ROWS, ROWS, weight.shape[1]))
        else:
            shapes.append((4, 2) + weight.shape)
    tokens, width = states.shape
    mem_tokens = encoded.shape[0]
    mem_length = mem_tokens // (tokens // length)
    units = weights[5].shape[1]
    f32 = jnp.float32
    kept = [
        ((4, 2) + norm.shape, f32),
        ((tokens, 3 * width), BFLOAT),
        ((tokens, width), BFLOAT),
        ((tokens, width), f32),
        ((tokens, 128), f32),
        ((tokens, width), BFLOAT),
        ((tokens, width), BFLOAT),
        ((mem_tokens, 2 * width), BFLOAT),
        ((tokens, width), BFLOAT),
        ((tokens, width), f32),
        ((tokens, 128), f32),
        ((tokens, width), BFLOAT),
        ((tokens, units), f32),
        ((tokens, units), BFLOAT),
        ((tokens, width), f32),
        ((tokens, 128), f32),
        ((tokens, width), BFLOAT),
    ]
    every = pl.BlockSpec(memory_space=pl.ANY)
    vmem = pl.BlockSpec(memory_space=pltpu.VMEM)
    dma = pltpu.SemaphoreType.DMA
    results = pl.pallas_call(
        functools.partial(forward_kernel, length, mem_length),
        out_shape=tuple(jax.ShapeDtypeStruct(shape, BFLOAT) for shape in shapes)
        + tuple(jax.ShapeDtypeStruct(shape, kind) for shape, kind in kept),
        in_specs=[every] * 8 + [vmem] * 2,
        out_specs=(every,) * 7 + (vmem,) * len(kept),
        scratch_shapes=[
            pltpu.VMEM((SLOTS_IN_FLIGHT, 4, 2, ROWS, TILE), BFLOAT),
            pltpu.VMEM((tokens, width), f32),
            dma((count,)),
            dma((count, 3)),
            dma((count, 3)),
        ]
        + [dma((count,))] * 6
        + [dma]
        + [dma((3,))] * 2
        + [dma] * 2
        + [dma((SLOTS_IN_FLIGHT,))],
        compiler_params=pltpu.CompilerParams(
            collective_id=0, has_side_effects=True, vmem_limit_bytes=48 * 2**20
        ),
        name="forward_layer",
    )(*weights, norm, states, encoded)
    fulls = tuple(full.reshape(-1, full.shape[-1]) for full in results[:7])
    return fulls, results[7], results[8:]


SEQUENCE = tuple((6, k) for k in range(4)) + tuple((5, k) for k in range(4)) + (
    (4, 0), (2, 0), (3, 0), (3, 1), (1, 0), (0, 0), (0, 1), (0, 2),
)
LINE_FIRST = 5
LINE_LAGS = (12, 14, 16, 18, 20)
CROSS_LAGS = (2, 4, 6, 8, 10)
TURNS = 27
READS = tuple(read for k in range(4) for read in ((6, k), (5, k))) + (
    (4, 0), (2, 0), (1, 0), (0, 0), (0, 1), (0, 2), (3, 0), (3, 1),
)


def norm_back(upstream, normed, inverse, gain):
    scaled = upstream * gain
    mean_scaled = jnp.mean(scaled, -1, keepdims=True)
    along = jnp.mean(scaled * normed, -1, keepdims=True)
    return (
        inverse * (scaled - mean_scaled - normed * along),
        jnp.sum(upstream * normed, 0, keepdims=True),
        jnp.sum(upstream, 0, keepdims=True),
    )


def attend_pair_back(grad, queries, keys, values, causal):
    scale = 1.0 / math.sqrt(HEAD_DIM)
    queries, grad = stack_heads(queries), stack_heads(grad)
    probs = pair_scores(queries, keys, causal)
    grad_probs = dot_nt(grad, values)
    grad_values = dot_tn(probs.astype(BFLOAT), grad).astype(BFLOAT)
    grad_scores = (
        probs * (grad_probs - jnp.sum(probs * grad_probs, -1, keepdims=True))
    ).astype(BFLOAT)
    grad_queries = unstack_heads(dot_nn(grad_scores, keys) * scale).astype(BFLOAT)
    grad_keys = (dot_tn(grad_scores, queries) * scale).astype(BFLOAT)
    return grad_queries, grad_keys, grad_values


def backward_kernel(length, mem_length, *refs):
    weights = refs[:7]
    kept_hbm = refs[7:23]
    inner_hbm = refs[23]
    norm_full, grad_third = refs[24:26]
    outs = refs[26:33]
    norm_out, grad_states, grad_memory, landing = refs[33:37]
    kept = refs[37:53]
    (
        wbuf, inner, stage, got, zload, one_line, two_line, one, two, line, fin,
        resid, low, grad_low, grad_context, grad_queries, grad_packed, memory_part,
        norm_here, norm_there, norm_line,
    ) = refs[53:74]
    (
        kept_sem, w_sem, inner_sem, dd_send, dd_recv, z_send, z_recv, zload_sem,
        ra_send, ra_recv, rb_send, rb_recv, rz_send, rz_recv, ag_send, ag_recv, ah_send, ah_recv,
        fin_sem, memory_sem, n_send, n_recv, nz_send, nz_recv,
    ) = refs[74:]
    (
        packed, context, first_normed, first_inverse, first_low, cross_queries, pairs, cross_context,
        second_normed, second_inverse, second_low, active, third_normed, third_inverse, states, encoded,
    ) = kept
    x, y, z, c = whereami()
    greet(neighbours(x, y, z, c))
    tokens, width = states.shape
    slots_here = tokens // length
    count = len(SEQUENCE)
    blocks = active.shape[1] // (8 * ROWS)

    def keep_copy(n):
        return pltpu.make_async_copy(kept_hbm[n], kept[n], kept_sem.at[n])

    first_needed = (12, 13, 11, 10)
    for n in first_needed:
        keep_copy(n).start()
    for n in range(16):
        if n not in first_needed:
            keep_copy(n).start()

    def need(*names):
        for n in names:
            keep_copy(n).wait()

    def read_copy(n):
        weight, k = READS[n]
        if weight == REDUCE_WEIGHT:
            source = weights[weight].at[pl.ds(k * TILE, TILE), :]
        else:
            source = weights[weight].at[:, pl.ds(k * TILE, TILE)]
        return pltpu.make_async_copy(source, wbuf.at[n % 2], w_sem.at[n % 2])

    def inner_copy(k):
        return pltpu.make_async_copy(
            inner_hbm.at[:, pl.ds(k * TILE, TILE)], inner.at[k % 2], inner_sem.at[k % 2]
        )

    read_copy(0).start()
    read_copy(1).start()
    inner_copy(0).start()
    inner_copy(1).start()

    def remote(src, dst, send, recv, peer):
        return pltpu.make_async_remote_copy(
            src_ref=src, dst_ref=dst, send_sem=send, recv_sem=recv, device_id=peer, device_id_type=MESH
        )

    def norm_row(n):
        return jnp.concatenate([norm_full[p // 2, p % 2, n : n + 1, :] for p in range(8)], 1)

    def place(q):
        even = lax.rem(q, 2) == 0
        a = jnp.where(even, x, y)
        b = jnp.where(even, y, x)
        x_peer = y * 2 + (1 - x)
        y_peer = (1 - y) * 2 + x
        a_peer = (jnp.where(even, x_peer, y_peer), z * 2 + c)
        b_peer = (jnp.where(even, y_peer, x_peer), z * 2 + c)
        return a, b, a_peer, b_peer

    def piece(index, size):
        return pl.ds(pl.multiple_of(index * size, size), size)

    def total(*parts):
        out = parts[0].astype(jnp.float32)
        for part in parts[1:]:
            out = out + part.astype(jnp.float32)
        return out.astype(BFLOAT)

    def dd_copy(q):
        return remote(
            stage.at[lax.rem(q, 2), 1 - c], got.at[q], dd_send.at[q], dd_recv.at[q], at(x, y, z, 1 - c)
        )

    def line_copy(q, d):
        other = lax.rem(z + d, 4)
        return remote(
            got.at[q, other], landing.at[q, d - 1], z_send.at[q, d - 1], z_recv.at[q, d - 1],
            at(x, y, other, c),
        )

    def ra_line(q):
        a, _, a_peer, _ = place(q)
        return remote(got.at[q, z, piece(1 - a, 64), :], one_line.at[q], ra_send.at[q], ra_recv.at[q], a_peer)

    def rb_line(q):
        _, b, _, b_peer = place(q)
        return remote(one_line.at[q, piece(1 - b, 32), :], two_line.at[q], rb_send.at[q], rb_recv.at[q], b_peer)

    def ra_cross(q):
        a, _, a_peer, _ = place(q)
        return remote(
            got.at[q, :, piece(1 - a, 64), :], one.at[q - LINE_FIRST], ra_send.at[q], ra_recv.at[q], a_peer
        )

    def rb_cross(q):
        _, b, _, b_peer = place(q)
        return remote(
            one.at[q - LINE_FIRST, :, piece(1 - b, 32), :], two.at[q - LINE_FIRST],
            rb_send.at[q], rb_recv.at[q], b_peer,
        )

    def rz_cross(q, d):
        other = lax.rem(z + d, 4)
        n = q - LINE_FIRST
        return remote(
            two.at[n, other], line.at[n, d - 1], rz_send.at[n, d - 1], rz_recv.at[n, d - 1],
            at(x, y, other, c),
        )

    def out_view(q, start, size):
        return shard_view(outs[SEQUENCE[q][0]], SEQUENCE[q], start, size)

    def quarter_start(q):
        a, b, _, _ = place(q)
        return pl.multiple_of(64 * a + 32 * b, 32)

    def fin_copy(q):
        return pltpu.make_async_copy(fin.at[q], out_view(q, quarter_start(q), 32), fin_sem.at[q])

    def ag_copy(q):
        return remote(
            fin.at[q], out_view(q, quarter_start(q), 32), ag_send.at[q], ag_recv.at[q], place(q)[3]
        )

    def ah_copy(q):
        a, _, a_peer, _ = place(q)
        part = out_view(q, pl.multiple_of(64 * a, 64), 64)
        return remote(part, part, ah_send.at[q], ah_recv.at[q], a_peer)

    norm_peers = (at(x, y, z, 1 - c), at(1 - x, y, z, c), at(x, 1 - y, z, c))

    def norm_copy(n):
        return remote(norm_here.at[n], norm_there.at[n], n_send.at[n], n_recv.at[n], norm_peers[n])

    def norm_line_copy(d):
        return remote(
            norm_here.at[3], norm_line.at[d - 1], nz_send.at[d - 1], nz_recv.at[d - 1],
            at(x, y, lax.rem(z + d, 4), c),
        )

    def outer(q, left, start, step, right):
        slot = q % 2

        @pl.loop(0, 8)
        def _(p):
            lanes = pl.ds(pl.multiple_of(start + p * step, 128), 128)
            stage[slot, lax.rem(p, 2), p // 2] = dot_tn(left[:, lanes], right()).astype(BFLOAT)

    def back_times(left, n, write):
        slot = n % 2
        read_copy(n).wait()

        @pl.loop(0, 4)
        def _(m):
            write(piece(m, 256), dot_nt(left[...], wbuf[slot, piece(m, 256), :]))

        if n + 2 < len(READS):
            read_copy(n + 2).start()

    def add_resid(columns, value):
        resid[:, columns] = resid[:, columns] + value

    def finish_norm(n, normed, inverse):
        value, gain, shift = norm_back(resid[...], normed[...], inverse[:, 0:1], norm_row(n))
        resid[...] = value
        low[...] = value.astype(BFLOAT)
        norm_here[0, n : n + 1, :] = gain
        norm_here[0, n + 3 : n + 4, :] = shift

    def attention_back(queries, keys, key_start, value_start, key_length, out, out_keys, causal):
        @pl.loop(0, slots_here * (width // 128))
        def _(n):
            slot, group = n // (width // 128), lax.rem(n, width // 128)
            lanes = piece(group, 128)
            key_lanes = pl.ds(pl.multiple_of(key_start + group * 128, 128), 128)
            value_lanes = pl.ds(pl.multiple_of(value_start + group * 128, 128), 128)
            query_rows = piece(slot, length)
            key_rows = piece(slot, key_length)
            grad_query, grad_key, grad_value = attend_pair_back(
                grad_context[query_rows, lanes],
                queries[query_rows, lanes],
                keys[key_rows, key_lanes],
                keys[key_rows, value_lanes],
                causal,
            )
            out[query_rows, lanes] = grad_query
            out_keys[key_rows, key_lanes] = grad_key
            out_keys[key_rows, value_lanes] = grad_value

    def produce(q):
        weight, k = SEQUENCE[q]
        if q == 0:
            norm_here[0] = jnp.zeros_like(norm_here[0])
            for p in range(8):
                resid[:, p * 128 : (p + 1) * 128] = grad_third[p * 128 : (p + 1) * 128, :].T
            need(12, 13, 11)
            finish_norm(2, third_normed, third_inverse)
        if weight == 6:
            outer(q, active, k * ROWS, blocks * ROWS, lambda: low[...])
        elif weight == 5:
            if k == 0:
                need(10)
            inner_copy(k).wait()

            def write(columns, value):
                pre = inner[k % 2, :, columns]
                slope = 0.5 * (1.0 + lax.erf(pre * math.sqrt(0.5))) + pre * jnp.exp(
                    -0.5 * pre * pre
                ) * (1.0 / math.sqrt(2.0 * math.pi))
                grad_low[:, columns] = (value * slope).astype(BFLOAT)

            back_times(low, 2 * k, write)
            if k + 2 < 4:
                inner_copy(k + 2).start()
            outer(q, second_low, 0, ROWS, lambda: grad_low[...])
            back_times(grad_low, 2 * k + 1, add_resid)
        elif weight == 4:
            need(8, 9, 7)
            finish_norm(1, second_normed, second_inverse)
            outer(q, cross_context, 0, ROWS, lambda: low[...])

            def write(columns, value):
                grad_context[:, columns] = value.astype(BFLOAT)

            back_times(low, 8, write)
        elif weight == 2:
            need(5, 6, 4, 2, 3)
            attention_back(cross_queries, pairs, 0, width, mem_length, grad_queries, pairs, False)
            outer(q, first_low, 0, ROWS, lambda: grad_queries[...])
            back_times(grad_queries, 9, add_resid)
            finish_norm(0, first_normed, first_inverse)
        elif weight == 3:
            if k == 0:
                need(15)
            outer(q, encoded, 0, ROWS, lambda: pairs[:, pl.ds(k * TILE, TILE)])
        elif weight == 1:
            need(1, 0, 14)
            outer(q, context, 0, ROWS, lambda: low[...])

            def write(columns, value):
                grad_context[:, columns] = value.astype(BFLOAT)

            back_times(low, 10, write)
            attention_back(packed, packed, width, 2 * width, length, grad_packed, grad_packed, True)
        else:
            def part():
                return grad_packed[:, pl.ds(k * TILE, TILE)]

            outer(q, states, 0, ROWS, part)
            back_times(grad_packed.at[:, pl.ds(k * TILE, TILE)], 11 + k, add_resid)
            if k == 2:
                grad_states[...] = resid[...]

    memory_rows = encoded.shape[0] // 8

    def memory_copy(m):
        return pltpu.make_async_copy(
            memory_part.at[m % 2], grad_memory.at[pl.ds(m * memory_rows, memory_rows), :], memory_sem.at[m % 2]
        )

    def memory_chunk(m):
        if m == 0:
            read_copy(14).wait()
            read_copy(15).wait()
        if m >= 2:
            memory_copy(m - 2).wait()
        rows_here = pl.ds(m * memory_rows, memory_rows)

        @pl.loop(0, 4)
        def _(n):
            memory_part[m % 2, :, piece(n, 256)] = dot_nt(
                pairs[rows_here, :width], wbuf[0, piece(n, 256), :]
            ) + dot_nt(pairs[rows_here, width:], wbuf[1, piece(n, 256), :])

        memory_copy(m).start()

    def each(q, action):
        for k in range(count):
            @pl.when(q == k)
            def _():
                action(k)

    def finish_block(q):
        def action(k):
            fin_copy(k).start()
            ag_copy(k).start()

        each(q, action)

    step = 16

    @pl.loop(0, TURNS)
    def _(i):
        for q in range(count):
            @pl.when(i == q)
            def _():
                if q >= 2:
                    dd_copy(q - 2).wait_send()
                produce(q)
                dd_copy(q).start()

        for m in range(8):
            @pl.when(i == count + 1 + m)
            def _():
                memory_chunk(m)

        qs = i - 1

        @pl.when((qs >= 0) & (qs < count))
        def _():
            dd_copy(qs).wait_recv()
            slot = lax.rem(qs, 2)

            @pl.loop(0, 32)
            def _(j):
                zz, rows_here = j // 8, piece(lax.rem(j, 8), step)
                got[qs, zz, rows_here, :] = total(got[qs, zz, rows_here, :], stage[slot, c, zz, rows_here, :])

            @pl.when(qs < LINE_FIRST)
            def _():
                for d in (1, 2, 3):
                    line_copy(qs, d).start()

            @pl.when(qs >= LINE_FIRST)
            def _():
                ra_cross(qs).start()

        q0 = i - LINE_LAGS[0]

        @pl.when((q0 >= 0) & (q0 < LINE_FIRST))
        def _():
            for d in (1, 2, 3):
                line_copy(q0, d).wait_recv()
            load = pltpu.make_async_copy(landing.at[q0], zload, zload_sem)
            load.start()
            load.wait()

            @pl.loop(0, 8)
            def _(j):
                rows_here = piece(j, step)
                got[q0, z, rows_here, :] = total(
                    got[q0, z, rows_here, :], zload[0, rows_here, :], zload[1, rows_here, :],
                    zload[2, rows_here, :],
                )

            ra_line(q0).start()

        q1 = i - LINE_LAGS[1]

        @pl.when((q1 >= 0) & (q1 < LINE_FIRST))
        def _():
            ra_line(q1).wait_recv()
            a = place(q1)[0]

            @pl.loop(0, 4)
            def _(j):
                rows_here = piece(j, step)
                one_line[q1, rows_here, :] = total(
                    one_line[q1, rows_here, :],
                    got[q1, z, pl.ds(pl.multiple_of(64 * a + j * step, step), step), :],
                )

            rb_line(q1).start()

        q2 = i - LINE_LAGS[2]

        @pl.when((q2 >= 0) & (q2 < LINE_FIRST))
        def _():
            rb_line(q2).wait_recv()
            b = place(q2)[1]

            @pl.loop(0, 2)
            def _(j):
                rows_here = piece(j, step)
                fin[q2, rows_here, :] = total(
                    two_line[q2, rows_here, :],
                    one_line[q2, pl.ds(pl.multiple_of(32 * b + j * step, step), step), :],
                )

            finish_block(q2)

        p0 = i - CROSS_LAGS[0]

        @pl.when((p0 >= LINE_FIRST) & (p0 < count))
        def _():
            ra_cross(p0).wait_recv()
            a = place(p0)[0]

            @pl.loop(0, 16)
            def _(j):
                zz, r = j // 4, lax.rem(j, 4)
                rows_here = piece(r, step)
                one[p0 - LINE_FIRST, zz, rows_here, :] = total(
                    one[p0 - LINE_FIRST, zz, rows_here, :],
                    got[p0, zz, pl.ds(pl.multiple_of(64 * a + r * step, step), step), :],
                )

            rb_cross(p0).start()

        p1 = i - CROSS_LAGS[1]

        @pl.when((p1 >= LINE_FIRST) & (p1 < count))
        def _():
            rb_cross(p1).wait_recv()
            b = place(p1)[1]

            @pl.loop(0, 8)
            def _(j):
                zz, r = j // 2, lax.rem(j, 2)
                rows_here = piece(r, step)
                two[p1 - LINE_FIRST, zz, rows_here, :] = total(
                    two[p1 - LINE_FIRST, zz, rows_here, :],
                    one[p1 - LINE_FIRST, zz, pl.ds(pl.multiple_of(32 * b + r * step, step), step), :],
                )

            for d in (1, 2, 3):
                rz_cross(p1, d).start()

        p2 = i - CROSS_LAGS[2]

        @pl.when((p2 >= LINE_FIRST) & (p2 < count))
        def _():
            for d in (1, 2, 3):
                rz_cross(p2, d).wait_recv()
            n = p2 - LINE_FIRST

            @pl.loop(0, 2)
            def _(j):
                rows_here = piece(j, step)
                fin[p2, rows_here, :] = total(
                    two[n, z, rows_here, :], line[n, 0, rows_here, :], line[n, 1, rows_here, :],
                    line[n, 2, rows_here, :],
                )

            finish_block(p2)

        def pass_on(k):
            ag_copy(k).wait_recv()
            fin_copy(k).wait()
            ah_copy(k).start()

        for lags, low_q, high_q in ((LINE_LAGS, 0, LINE_FIRST), (CROSS_LAGS, LINE_FIRST, count)):
            q3 = i - lags[3]

            @pl.when((q3 >= low_q) & (q3 < high_q))
            def _():
                each(q3, pass_on)

            q4 = i - lags[4]

            @pl.when((q4 >= low_q) & (q4 < high_q))
            def _():
                each(q4, lambda k: ah_copy(k).wait_recv())

        @pl.when(i == count)
        def _():
            norm_copy(0).start()

        for n in range(3):
            @pl.when(i == count + 2 * (n + 1))
            def _():
                norm_copy(n).wait_recv()
                norm_here[n + 1] = norm_here[n] + norm_there[n]
                if n < 2:
                    norm_copy(n + 1).start()
                else:
                    for d in (1, 2, 3):
                        norm_line_copy(d).start()

        @pl.when(i == count + 8)
        def _():
            for d in (1, 2, 3):
                norm_line_copy(d).wait_recv()
            norm_out[...] = ((norm_here[3] + norm_line[0]) + norm_line[1]) + norm_line[2]

    memory_copy(6).wait()
    memory_copy(7).wait()
    dd_copy(count - 2).wait_send()
    dd_copy(count - 1).wait_send()

    @pl.loop(0, LINE_FIRST)
    def _(q):
        for d in (1, 2, 3):
            line_copy(q, d).wait_send()
        ra_line(q).wait_send()
        rb_line(q).wait_send()

    @pl.loop(LINE_FIRST, count)
    def _(q):
        ra_cross(q).wait_send()
        rb_cross(q).wait_send()
        for d in (1, 2, 3):
            rz_cross(q, d).wait_send()

    for q in range(count):
        ag_copy(q).wait_send()
        ah_copy(q).wait_send()
    for n in range(3):
        norm_copy(n).wait_send()
        norm_line_copy(n + 1).wait_send()


def backward_layer(weights, kept, inner, norm_full, grad_third, length):
    count = len(SEQUENCE)
    f32 = jnp.float32
    tokens, width = kept[14].shape
    mem_tokens = kept[15].shape[0]
    mem_length = mem_tokens // (tokens // length)
    shapes = [(weight.shape[0] // 8, weight.shape[1]) for weight in weights]
    every = pl.BlockSpec(memory_space=pl.ANY)
    vmem = pl.BlockSpec(memory_space=pltpu.VMEM)
    dma = pltpu.SemaphoreType.DMA
    sems = dma((count,))
    crossed = count - LINE_FIRST
    *shares, norm_sum, grad_states, grad_memory, _ = pl.pallas_call(
        functools.partial(backward_kernel, length, mem_length),
        out_shape=tuple(jax.ShapeDtypeStruct(shape, BFLOAT) for shape in shapes)
        + (
            jax.ShapeDtypeStruct((8, width), f32),
            jax.ShapeDtypeStruct((tokens, width), f32),
            jax.ShapeDtypeStruct((mem_tokens, width), f32),
            jax.ShapeDtypeStruct((LINE_FIRST, 3, ROWS, TILE), BFLOAT),
        ),
        in_specs=[every] * 24 + [vmem] * 2,
        out_specs=(every,) * 7 + (vmem, vmem, every, every),
        scratch_shapes=[pltpu.VMEM(part.shape, part.dtype) for part in kept]
        + [
            pltpu.VMEM((2, TILE, TILE), BFLOAT),
            pltpu.VMEM((2, tokens, TILE), f32),
            pltpu.VMEM((2, 2, 4, ROWS, TILE), BFLOAT),
            pltpu.VMEM((count, 4, ROWS, TILE), BFLOAT),
            pltpu.VMEM((3, ROWS, TILE), BFLOAT),
            pltpu.VMEM((LINE_FIRST, 64, TILE), BFLOAT),
            pltpu.VMEM((LINE_FIRST, 32, TILE), BFLOAT),
            pltpu.VMEM((crossed, 4, 64, TILE), BFLOAT),
            pltpu.VMEM((crossed, 4, 32, TILE), BFLOAT),
            pltpu.VMEM((crossed, 3, 32, TILE), BFLOAT),
            pltpu.VMEM((count, 32, TILE), BFLOAT),
            pltpu.VMEM((tokens, width), f32),
            pltpu.VMEM((tokens, width), BFLOAT),
            pltpu.VMEM((tokens, TILE), BFLOAT),
            pltpu.VMEM((tokens, width), BFLOAT),
            pltpu.VMEM((tokens, width), BFLOAT),
            pltpu.VMEM((tokens, 3 * width), BFLOAT),
            pltpu.VMEM((2, mem_tokens // 8, width), f32),
            pltpu.VMEM((4, 8, width), f32),
            pltpu.VMEM((3, 8, width), f32),
            pltpu.VMEM((3, 8, width), f32),
            dma((16,)), dma((2,)), dma((2,)), sems, sems,
            dma((LINE_FIRST, 3)), dma((LINE_FIRST, 3)), dma,
            sems, sems, sems, sems,
            dma((crossed, 3)), dma((crossed, 3)),
            sems, sems, sems, sems, sems, dma((2,)),
            dma((3,)), dma((3,)), dma((3,)), dma((3,)),
        ],
        compiler_params=pltpu.CompilerParams(
            collective_id=1, has_side_effects=True, vmem_limit_bytes=62 * 2**20
        ),
        name="backward_layer",
    )(*weights, *kept, inner, norm_full, grad_third)
    return tuple(share.astype(f32) for share in shares), norm_sum, grad_states, grad_memory


VOCAB_CUTS = 3


def head_kernel(slots, length, vocab_here, *refs):
    hid, aux, emb_all = refs[:3]
    small_out, gemb_out, third_out = refs[3:6]
    (
        emb, emb_t, held, marks, logit, expo, part, sib_part, part_one, part_two, part_z,
        mine, theirs, lined, prior, usable, weight, scaled, picked_grad,
    ) = refs[6:25]
    (
        local_sem, z_send, z_recv, one_send, one_recv, two_send, two_recv, sib_send, sib_recv,
        ax_send, ax_recv, axz_send, axz_recv, st_send, st_recv, stz_send, stz_recv,
        dd_send, dd_recv, r1_send, r1_recv, r2_send, r2_recv, rz_send, rz_recv,
    ) = refs[25:]
    x, y, z, c = whereami()
    pb, pa = y * 2 + x, z * 2 + c
    size = hid.shape[0]
    pair = 2 * size
    width = hid.shape[1]
    rows = emb.shape[0]
    cut = rows // VOCAB_CUTS
    start = pl.multiple_of(pb * rows, 16)
    last = vocab_here - 3 * rows
    valid = jnp.where(pb == 3, last, rows)
    base = pa * vocab_here + start
    own = pb * 4 + z

    def remote(src, dst, send, recv, peer):
        return pltpu.make_async_remote_copy(
            src_ref=src, dst_ref=dst, send_sem=send, recv_sem=recv, device_id=peer, device_id_type=MESH
        )

    sibling = at(x, y, z, 1 - c)
    x_peer, y_peer = at(1 - x, y, z, c), at(x, 1 - y, z, c)

    def spot(k, core):
        return held.at[pl.ds(pl.multiple_of((k * 2 + core) * size, size), size), :]

    greet(neighbours(x, y, z, c))
    own_copy = pltpu.make_async_copy(hid, spot(own, c), local_sem.at[0])
    own_copy.start()
    lanes = pl.ds(pl.multiple_of(c * size, size), size)
    aux_copy = pltpu.make_async_copy(aux, marks.at[y, x, z, :, lanes], local_sem.at[1])
    aux_copy.start()
    emb_copy = pltpu.make_async_copy(
        emb_all.at[pl.ds(start, last), :], emb.at[pl.ds(0, last), :], local_sem.at[2]
    )
    rest_copy = pltpu.make_async_copy(
        emb_all.at[pl.ds(pl.multiple_of(jnp.minimum(start + last, vocab_here - (rows - last)), 16), rows - last), :],
        emb.at[pl.ds(last, rows - last), :],
        local_sem.at[3],
    )
    emb_copy.start()
    rest_copy.start()
    own_copy.wait()

    def along_copy(d):
        other = lax.rem(z + d, 4)
        return remote(hid, spot(own, c), z_send.at[d - 1], z_recv.at[d - 1], at(x, y, other, c))

    def sib_copy(k):
        return remote(spot(k, c), spot(k, c), sib_send.at[k], sib_recv.at[k], sibling)

    def order(zz):
        x_first = zz < 2
        f = jnp.where(x_first, x, y)
        g = jnp.where(x_first, y, x)
        first_peer = (jnp.where(x_first, y * 2 + 1 - x, (1 - y) * 2 + x), pa)
        second_peer = (jnp.where(x_first, (1 - y) * 2 + x, y * 2 + 1 - x), pa)

        def block(first, second):
            return jnp.where(x_first, second * 2 + first, first * 2 + second) * 4 + zz

        return f, g, first_peer, second_peer, block

    def one_copy(zz):
        f, g, first_peer, _, block = order(zz)
        return remote(
            spot(block(f, g), c), spot(block(f, g), c), one_send.at[zz], one_recv.at[zz], first_peer
        )

    def two_copy(zz, j):
        f, g, _, second_peer, block = order(zz)
        k = block(f if j == 0 else 1 - f, g)
        return remote(spot(k, c), spot(k, c), two_send.at[zz, j], two_recv.at[zz, j], second_peer)

    for d in (1, 2, 3):
        along_copy(d).start()
    sib_copy(own).start()
    one_copy(z).start()

    aux_copy.wait()
    steps = (
        (marks.at[y, x, z, :, lanes], sibling),
        (marks.at[y, x, z], x_peer),
        (marks.at[y, :, z], y_peer),
    )
    for n, (block_ref, peer) in enumerate(steps):
        copy = remote(block_ref, block_ref, ax_send.at[n], ax_recv.at[n], peer)
        copy.start()
        copy.wait()

    def mark_copy(d):
        block_ref = marks.at[:, :, z]
        other = lax.rem(z + d, 4)
        return remote(block_ref, block_ref, axz_send.at[d - 1], axz_recv.at[d - 1], at(x, y, other, c))

    for d in (1, 2, 3):
        mark_copy(d).start()
    for d in (1, 2, 3):
        mark_copy(d).wait()

    emb_copy.wait()
    rest_copy.wait()
    full_cuts = rows // 128

    @pl.loop(0, full_cuts)
    def _(n):
        here = pl.ds(pl.multiple_of(n * 128, 128), 128)
        emb_t[:, here] = emb[here, :].T

    if rows % 128:
        emb_t[:, full_cuts * 128 :] = emb[full_cuts * 128 :, :].T

    def target_rows(k):
        ypart, xpart, zpart = k // 8, lax.rem(k // 4, 2), lax.rem(k, 4)
        target = marks[ypart, xpart, zpart, 0:1, :].astype(jnp.int32) - base
        return jnp.where(target < valid, target, -1)

    def row_numbers(j):
        return lax.broadcasted_iota(jnp.int32, (cut, pair), 0) + j * cut

    def cut_rows(j):
        return pl.ds(pl.multiple_of(j * cut, cut), cut)

    def token_lanes(k):
        return pl.ds(pl.multiple_of(k * pair, pair), pair)

    def forward_block(k):
        target = target_rows(k)
        block = held[token_lanes(k), :]

        def scan_logits(j, carried):
            highest, picked = carried
            value = lax.dot_general(
                emb[cut_rows(j), :], block, (((1,), (1,)), ((), ())), preferred_element_type=jnp.float32
            )
            number = row_numbers(j)
            value = jnp.where(number < valid, value, NEGATIVE)
            logit[cut_rows(j), :] = value
            return (
                jnp.maximum(highest, jnp.max(value, 0, keepdims=True)),
                picked + jnp.sum(jnp.where(number == target, value, 0.0), 0, keepdims=True),
            )

        highest, picked = lax.fori_loop(
            0,
            VOCAB_CUTS,
            scan_logits,
            (jnp.full((1, pair), NEGATIVE, jnp.float32), jnp.zeros((1, pair), jnp.float32)),
        )

        def scan_exp(j, total):
            value = jnp.exp(logit[cut_rows(j), :] - highest)
            expo[cut_rows(j), token_lanes(k)] = value.astype(BFLOAT)
            return total + jnp.sum(value, 0, keepdims=True)

        total = lax.fori_loop(0, VOCAB_CUTS, scan_exp, jnp.zeros((1, pair), jnp.float32))
        mine[0, 0, pl.ds(k, 1), :] = highest
        mine[0, 1, pl.ds(k, 1), :] = total
        mine[0, 2, pl.ds(k, 1), :] = picked

    @pl.loop(0, 16)
    def _(s):
        phase, t = s // 4, lax.rem(s, 4)
        zz = lax.rem(z - t + 4, 4)
        f, g, _, _, block = order(zz)
        k = jnp.where(
            phase == 0,
            block(f, g),
            jnp.where(
                phase == 1, block(1 - f, g), jnp.where(phase == 2, block(f, 1 - g), block(1 - f, 1 - g))
            ),
        )

        for d in (1, 2, 3):
            @pl.when(s == d)
            def _():
                along_copy(d).wait_recv()

        @pl.when((s > 0) & (phase == 0))
        def _():
            sib_copy(k).start()
            one_copy(zz).start()

        @pl.when(phase == 1)
        def _():
            one_copy(zz).wait_recv()
            sib_copy(k).start()
            for j in range(2):
                two_copy(zz, j).start()

        for j in range(2):
            @pl.when(phase == 2 + j)
            def _():
                two_copy(zz, j).wait_recv()
                sib_copy(k).start()

        sib_copy(k).wait_recv()
        forward_block(k)

    def joined(parts):
        highest = functools.reduce(jnp.maximum, [p[0] for p in parts])
        total = functools.reduce(jnp.add, [p[1] * jnp.exp(p[0] - highest) for p in parts])
        picked = functools.reduce(jnp.add, [p[2] for p in parts])
        return highest, total, picked

    def rows_of(ref, n):
        return ref[n, 0], ref[n, 1], ref[n, 2]

    for n, (peer, side) in enumerate(((sibling, c), (x_peer, x), (y_peer, y))):
        copy = remote(mine.at[n], theirs.at[n], st_send.at[n], st_recv.at[n], peer)
        copy.start()
        copy.wait()
        here, there = rows_of(mine, n), rows_of(theirs, n)
        early = tuple(jnp.where(side == 0, a, b) for a, b in zip(here, there))
        late = tuple(jnp.where(side == 0, b, a) for a, b in zip(here, there))
        for r, value in enumerate(joined((early, late))):
            mine[n + 1, r] = value

    def stat_copy(d):
        other = lax.rem(z + d, 4)
        return remote(mine.at[3], lined.at[z], stz_send.at[d - 1], stz_recv.at[d - 1], at(x, y, other, c))

    for d in (1, 2, 3):
        stat_copy(d).start()
    for r in range(3):
        lined[z, r] = mine[3, r]
    for d in (1, 2, 3):
        stat_copy(d).wait()
    highest, total, picked = joined([rows_of(lined, n) for n in range(4)])
    logsum = highest + jnp.log(total)
    log_probs = picked - logsum
    for k in range(16):
        prior[k : k + 1, :] = marks[k // 8, (k // 4) % 2, k % 4, 1:2, :]
        usable[k : k + 1, :] = marks[k // 8, (k // 4) % 2, k % 4, 2:3, :]
    lane = lax.broadcasted_iota(jnp.int32, (16, pair), 1) // length
    mean = jnp.zeros((16, pair), jnp.float32)
    for n in range(pair // length):
        inside = lane == n
        slot_sum = jnp.sum(jnp.where(inside, log_probs, 0.0), 1, keepdims=True)
        mean = jnp.where(inside, slot_sum * (1.0 / length), mean)
    scores = prior[...] + mean
    counted = usable[...] > 0.5
    masked = jnp.where(counted, scores, NEGATIVE)
    question = lax.broadcasted_iota(jnp.int32, (16, pair), 0) // 4
    marginal = jnp.zeros((16, pair), jnp.float32)
    loss = jnp.zeros((1, 1), jnp.float32)
    for n in range(4):
        inside = question == n
        high = jnp.max(
            jnp.max(jnp.where(inside, masked, NEGATIVE), 1, keepdims=True), 0, keepdims=True
        )
        terms = jnp.where(inside & counted, jnp.exp(masked - high), 0.0)
        mass = jnp.sum(jnp.sum(terms, 1, keepdims=True), 0, keepdims=True) * (1.0 / length)
        value = high + jnp.log(mass)
        marginal = jnp.where(inside, value, marginal)
        loss = loss + value
    posterior = jnp.where(counted, jnp.exp(scores - marginal), 0.0)
    token_weight = -float(slots) * posterior
    weight[...] = posterior
    scaled[...] = token_weight * jnp.exp(mine[0, 0] - logsum)
    picked_grad[...] = token_weight * (1.0 - jnp.exp(log_probs))
    small_out[...] = jnp.broadcast_to(loss * (-1.0 / 4), small_out.shape)
    own_row = weight[pl.ds(own, 1), :]
    own_row = jnp.where(c == 0, own_row[:, :size], own_row[:, size:])
    small_out[1:2, :] = own_row * (-float(slots * length))

    def backward_block(k):
        target = target_rows(k)
        hit = picked_grad[pl.ds(k, 1), :]
        scale = scaled[pl.ds(k, 1), :]

        def make(j, carried):
            value = expo[cut_rows(j), token_lanes(k)].astype(jnp.float32)
            grad = jnp.where(row_numbers(j) == target, hit, -(value * scale))
            expo[cut_rows(j), token_lanes(k)] = grad.astype(BFLOAT)
            return carried

        lax.fori_loop(0, VOCAB_CUTS, make, 0)

        def to_rows(n, carried):
            cut_width = pl.ds(pl.multiple_of(n * 256, 256), 256)
            value = lax.dot_general(
                emb_t[cut_width, :],
                expo[:, token_lanes(k)],
                (((1,), (0,)), ((), ())),
                preferred_element_type=jnp.float32,
            ).astype(BFLOAT)
            part[k, 0, cut_width, :] = value[:, :size]
            part[k, 1, cut_width, :] = value[:, size:]
            return carried

        lax.fori_loop(0, width // 256, to_rows, 0)

    def dd_copy(k):
        return remote(part.at[k, 1 - c], sib_part.at[k], dd_send.at[k], dd_recv.at[k], sibling)

    def r1_copy(zz, j):
        f, _, first_peer, _, block = order(zz)
        return remote(
            sib_part.at[block(1 - f, j)], part_one.at[zz, j], r1_send.at[zz, j], r1_recv.at[zz, j],
            first_peer,
        )

    def r2_copy(zz):
        _, g, _, second_peer, _ = order(zz)
        return remote(part_one.at[zz, 1 - g], part_two.at[zz], r2_send.at[zz], r2_recv.at[zz], second_peer)

    def rz_copy(zz):
        return remote(part_two.at[zz], part_z.at[z], rz_send.at[zz], rz_recv.at[z], at(x, y, zz, c))

    def rz_arrival(zz):
        return remote(part_two.at[zz], part_z.at[zz], rz_send.at[zz], rz_recv.at[zz], at(x, y, zz, c))

    step = 64

    def add_into(target_ref, other_ref):
        @pl.loop(0, width // step)
        def _(n):
            rows_here = pl.ds(pl.multiple_of(n * step, step), step)
            target_ref[rows_here, :] = (
                target_ref[rows_here, :].astype(jnp.float32) + other_ref[rows_here, :].astype(jnp.float32)
            ).astype(BFLOAT)

    def group(n):
        return lax.rem(n, 2) * 2 + n // 2

    def chunk(q):
        j, n = q // 4, lax.rem(q, 4)
        columns = pl.ds(pl.multiple_of(n * 256, 256), 256)
        gemb_out[cut_rows(j), columns] = lax.dot_general(
            expo[cut_rows(j), :],
            held[:, columns],
            (((1,), (0,)), ((), ())),
            preferred_element_type=jnp.float32,
        ).astype(BFLOAT)

    @pl.loop(0, 28)
    def _(s):
        turn = s // 4
        edge = lax.rem(s, 4) == 0

        @pl.when(edge & (turn >= 1) & (turn < 5))
        def _():
            zz = group(turn - 1)

            @pl.loop(0, 4)
            def _(n):
                k = n * 4 + zz
                dd_copy(k).wait_recv()
                add_into(sib_part.at[k], part.at[k, c])

            for j in range(2):
                r1_copy(zz, j).start()

        @pl.when(edge & (turn >= 2) & (turn < 6))
        def _():
            zz = group(turn - 2)
            f, _, _, _, block = order(zz)
            for j in range(2):
                r1_copy(zz, j).wait_recv()
                add_into(part_one.at[zz, j], sib_part.at[block(f, j)])
            r2_copy(zz).start()

        @pl.when(edge & (turn >= 3))
        def _():
            zz = group(turn - 3)
            _, g, _, _, _ = order(zz)
            r2_copy(zz).wait_recv()
            add_into(part_two.at[zz], part_one.at[zz, g])

            @pl.when(zz != z)
            def _():
                rz_copy(zz).start()

        @pl.when(s < 16)
        def _():
            k = lax.rem(s, 4) * 4 + group(turn)
            backward_block(k)
            dd_copy(k).start()

        @pl.when(s >= 16)
        def _():
            chunk(s - 16)

    for d in (1, 2, 3):
        rz_arrival(lax.rem(z + d, 4)).wait_recv()

    @pl.loop(0, width // step)
    def _(n):
        rows_here = pl.ds(pl.multiple_of(n * step, step), step)
        value = part_two[z, rows_here, :].astype(jnp.float32)
        for d in (1, 2, 3):
            value = value + part_z[lax.rem(z + d, 4), rows_here, :].astype(jnp.float32)
        third_out[rows_here, :] = value

    for d in (1, 2, 3):
        along_copy(d).wait_send()
        rz_copy(lax.rem(z + d, 4)).wait_send()

    @pl.loop(0, 4)
    def _(zz):
        one_copy(zz).wait_send()
        for j in range(2):
            two_copy(zz, j).wait_send()
            r1_copy(zz, j).wait_send()
        r2_copy(zz).wait_send()

    @pl.loop(0, 16)
    def _(k):
        sib_copy(k).wait_send()
        dd_copy(k).wait_send()


def vocabulary_head(third_low, targets, log_prior, usable, embedding, slots, length):
    size, width = third_low.shape
    vocab_here = embedding.shape[0]
    rows = 16 * VOCAB_CUTS * -(-vocab_here // (4 * 16 * VOCAB_CUTS))
    aux = jnp.zeros((8, size), jnp.float32)
    aux = aux.at[0].set(targets.astype(jnp.float32))
    aux = aux.at[1].set(jnp.repeat(log_prior, length))
    aux = aux.at[2].set(jnp.repeat(usable.astype(jnp.float32), length))
    dma = pltpu.SemaphoreType.DMA
    vmem = pl.BlockSpec(memory_space=pltpu.VMEM)
    stat = (3, 16, 2 * size)
    f32 = jnp.float32
    block = (width, size)
    small, gemb, third = pl.pallas_call(
        functools.partial(head_kernel, slots, length, vocab_here),
        out_shape=(
            jax.ShapeDtypeStruct((8, size), f32),
            jax.ShapeDtypeStruct((rows, width), BFLOAT),
            jax.ShapeDtypeStruct((width, size), f32),
        ),
        in_specs=[vmem, vmem, pl.BlockSpec(memory_space=pl.ANY)],
        out_specs=(vmem,) * 3,
        scratch_shapes=[
            pltpu.VMEM((rows, width), BFLOAT),
            pltpu.VMEM((width, rows), BFLOAT),
            pltpu.VMEM((32 * size, width), BFLOAT),
            pltpu.VMEM((2, 2, 4, 8, 2 * size), f32),
            pltpu.VMEM((rows, 2 * size), f32),
            pltpu.VMEM((rows, 32 * size), BFLOAT),
            pltpu.VMEM((16, 2) + block, BFLOAT),
            pltpu.VMEM((16,) + block, BFLOAT),
            pltpu.VMEM((4, 2) + block, BFLOAT),
            pltpu.VMEM((4,) + block, BFLOAT),
            pltpu.VMEM((4,) + block, BFLOAT),
            pltpu.VMEM((4,) + stat, f32),
            pltpu.VMEM((3,) + stat, f32),
            pltpu.VMEM((4,) + stat, f32),
        ]
        + [pltpu.VMEM((16, 2 * size), f32)] * 5
        + [dma((4,))]
        + [dma((3,))] * 2
        + [dma((4,))] * 2
        + [dma((4, 2))] * 2
        + [dma((16,))] * 2
        + [dma((3,))] * 8
        + [dma((16,))] * 2
        + [dma((4, 2))] * 2
        + [dma((4,))] * 4,
        compiler_params=pltpu.CompilerParams(
            collective_id=2, has_side_effects=True, vmem_limit_bytes=60 * 2**20
        ),
        name="vocabulary_head",
    )(third_low, aux, embedding)
    return small, gemb, third


def merged(part, axis, combine):
    gathered = jax.tree.map(lambda a: lax.all_gather(a, axis), part)

    def take(source):
        return jax.tree.map(lambda a: lax.dynamic_index_in_dim(a, source, 0, False), gathered)

    return lax.fori_loop(
        1, lax.axis_size(axis), lambda source, state: combine(state, take(source)), take(0)
    )


def matmul(matrix_left, matrix_right):
    return lax.dot_general(
        matrix_left,
        matrix_right,
        (((matrix_left.ndim - 1,), (0,)), ((), ())),
        preferred_element_type=jnp.float32,
    )


def matmul_back(matrix_left, matrix_right):
    return lax.dot_general(
        matrix_left,
        matrix_right,
        (((matrix_left.ndim - 1,), (1,)), ((), ())),
        preferred_element_type=jnp.float32,
    )


def outer_sum(matrix_left, matrix_right):
    flat_left = matrix_left.reshape(-1, matrix_left.shape[-1])
    flat_right = matrix_right.reshape(-1, matrix_right.shape[-1])
    return lax.dot_general(
        flat_left, flat_right, (((0,), (0,)), ((), ())), preferred_element_type=jnp.float32
    )


def split_heads(values):
    return values.reshape(values.shape[0], values.shape[1], HEADS, HEAD_DIM)


def join_heads(values):
    return values.reshape(values.shape[0], values.shape[1], HEADS * HEAD_DIM)


def exact_gelu(values):
    return jax.nn.gelu(values, approximate=False)


def norm_forward(values, gain_row, shift_row):
    centre = values - jnp.mean(values, -1, keepdims=True)
    inverse = lax.rsqrt(jnp.mean(centre * centre, -1, keepdims=True) + EPSILON)
    normed = centre * inverse
    return (normed * gain_row.astype(jnp.float32) + shift_row.astype(jnp.float32), normed, inverse)


def norm_backward(upstream, normed, inverse, gain_row):
    scaled = upstream * gain_row.astype(jnp.float32)
    mean_scaled = jnp.mean(scaled, -1, keepdims=True)
    along_normed = jnp.mean(scaled * normed, -1, keepdims=True)
    grad_values = inverse * (scaled - mean_scaled - normed * along_normed)
    model_width = upstream.shape[-1]
    grad_gain = jnp.sum((upstream * normed).reshape(-1, model_width), 0)
    grad_shift = jnp.sum(upstream.reshape(-1, model_width), 0)
    return (grad_values, grad_gain, grad_shift)


def score_block(queries, key_rows, causal):
    scores = jnp.einsum(
        "nqhd,nkhd->nhqk", queries, key_rows, preferred_element_type=jnp.float32
    ) * (1.0 / math.sqrt(HEAD_DIM))
    if causal:
        length = queries.shape[1]
        allowed = lax.broadcasted_iota(jnp.int32, (length, length), 0) >= lax.broadcasted_iota(
            jnp.int32, (length, length), 1
        )
        scores = jnp.where(allowed, scores, NEGATIVE)
    return scores


def attend(queries, key_rows, values, causal):
    scores = score_block(queries, key_rows, causal)
    highest = jnp.max(scores, -1, keepdims=True)
    totals = jnp.sum(jnp.exp(scores - highest), -1, keepdims=True)
    logsum = highest + jnp.log(totals)
    probs_low = jnp.exp(scores - logsum).astype(BFLOAT)
    context = jnp.einsum(
        "nhqk,nkhd->nqhd", probs_low, values, preferred_element_type=jnp.float32
    ).astype(BFLOAT)
    return (join_heads(context), logsum)


def attend_back(grad_context, queries, key_rows, values, logsum, causal):
    score_scale = 1.0 / math.sqrt(HEAD_DIM)
    probs_full = jnp.exp(score_block(queries, key_rows, causal) - logsum)
    grad_heads = split_heads(grad_context)
    grad_probs = jnp.einsum(
        "nqhd,nkhd->nhqk", grad_heads, values, preferred_element_type=jnp.float32
    )
    grad_values = jnp.einsum(
        "nhqk,nqhd->nkhd", probs_full.astype(BFLOAT), grad_heads, preferred_element_type=jnp.float32
    ).astype(BFLOAT)
    grad_scores = (
        probs_full * (grad_probs - jnp.sum(probs_full * grad_probs, -1, keepdims=True))
    ).astype(BFLOAT)
    grad_queries = (
        jnp.einsum("nhqk,nkhd->nqhd", grad_scores, key_rows, preferred_element_type=jnp.float32)
        * score_scale
    ).astype(BFLOAT)
    grad_keys = (
        jnp.einsum("nhqk,nqhd->nkhd", grad_scores, queries, preferred_element_type=jnp.float32)
        * score_scale
    ).astype(BFLOAT)
    return (join_heads(grad_queries), join_heads(grad_keys), join_heads(grad_values))


def layer_forward(inputs, encoded, weights):
    (
        packed_weight,
        output_weight,
        query_weight,
        memory_weight,
        cross_weight,
        expand_weight,
        reduce_weight,
        gains,
        shifts,
    ) = weights
    model_width = inputs.shape[-1]
    packed = matmul(inputs, packed_weight).astype(BFLOAT)
    context, self_logsum = attend(
        split_heads(packed[..., :model_width]),
        split_heads(packed[..., model_width : 2 * model_width]),
        split_heads(packed[..., 2 * model_width :]),
        True,
    )
    first_norm, first_normed, first_inverse = norm_forward(
        inputs.astype(jnp.float32) + matmul(context, output_weight), gains[0], shifts[0]
    )
    first_low = first_norm.astype(BFLOAT)
    cross_queries = matmul(first_low, query_weight).astype(BFLOAT)
    memory_pairs = matmul(encoded, memory_weight).astype(BFLOAT)
    cross_context, cross_logsum = attend(
        split_heads(cross_queries),
        split_heads(memory_pairs[..., :model_width]),
        split_heads(memory_pairs[..., model_width:]),
        False,
    )
    second, second_normed, second_inverse = norm_forward(
        first_norm + matmul(cross_context, cross_weight), gains[1], shifts[1]
    )
    second_low = second.astype(BFLOAT)
    inner_pre = matmul(second_low, expand_weight)
    active = exact_gelu(inner_pre).astype(BFLOAT)
    third_norm, third_normed, third_inverse = norm_forward(
        second + matmul(active, reduce_weight), gains[2], shifts[2]
    )
    stored = (
        packed,
        context,
        self_logsum,
        first_normed,
        first_inverse,
        first_low,
        cross_queries,
        memory_pairs,
        cross_context,
        cross_logsum,
        second_normed,
        second_inverse,
        second_low,
        inner_pre,
        active,
        third_normed,
        third_inverse,
    )
    return (third_norm.astype(BFLOAT), stored)


def layer_backward(grad_third, inputs, encoded, weights, stored):
    (
        packed_weight,
        output_weight,
        query_weight,
        memory_weight,
        cross_weight,
        expand_weight,
        reduce_weight,
        gains,
        shifts,
    ) = weights
    (
        packed,
        context,
        self_logsum,
        first_normed,
        first_inverse,
        first_low,
        cross_queries,
        memory_pairs,
        cross_context,
        cross_logsum,
        second_normed,
        second_inverse,
        second_low,
        inner_pre,
        active,
        third_normed,
        third_inverse,
    ) = stored
    model_width = inputs.shape[-1]
    grad_res3, gain_three, shift_three = norm_backward(
        grad_third, third_normed, third_inverse, gains[2]
    )
    grad_output = grad_res3.astype(BFLOAT)
    grad_reduce = outer_sum(active, grad_output)
    grad_active = matmul_back(grad_output, reduce_weight)
    _, gelu_pull = jax.vjp(exact_gelu, inner_pre)
    grad_inner = gelu_pull(grad_active)[0].astype(BFLOAT)
    grad_expand = outer_sum(second_low, grad_inner)
    grad_second = grad_res3 + matmul_back(grad_inner, expand_weight)
    grad_res2, gain_two, shift_two = norm_backward(
        grad_second, second_normed, second_inverse, gains[1]
    )
    grad_mixed = grad_res2.astype(BFLOAT)
    grad_cross_weight = outer_sum(cross_context, grad_mixed)
    grad_cross_context = matmul_back(grad_mixed, cross_weight).astype(BFLOAT)
    grad_cross_queries, grad_memory_keys, grad_memory_values = attend_back(
        grad_cross_context,
        split_heads(cross_queries),
        split_heads(memory_pairs[..., :model_width]),
        split_heads(memory_pairs[..., model_width:]),
        cross_logsum,
        False,
    )
    grad_query_weight = outer_sum(first_low, grad_cross_queries)
    grad_first = grad_res2 + matmul_back(grad_cross_queries, query_weight)
    grad_pairs = jnp.concatenate([grad_memory_keys, grad_memory_values], -1)
    grad_memory_weight = outer_sum(encoded, grad_pairs)
    grad_encoded = matmul_back(grad_pairs, memory_weight)
    grad_res1, gain_one, shift_one = norm_backward(
        grad_first, first_normed, first_inverse, gains[0]
    )
    grad_merged = grad_res1.astype(BFLOAT)
    grad_output_weight = outer_sum(context, grad_merged)
    grad_context = matmul_back(grad_merged, output_weight).astype(BFLOAT)
    grad_queries, grad_keys, grad_values = attend_back(
        grad_context,
        split_heads(packed[..., :model_width]),
        split_heads(packed[..., model_width : 2 * model_width]),
        split_heads(packed[..., 2 * model_width :]),
        self_logsum,
        True,
    )
    grad_packed = jnp.concatenate([grad_queries, grad_keys, grad_values], -1)
    grad_packed_weight = outer_sum(inputs, grad_packed)
    grad_inputs = grad_res1 + matmul_back(grad_packed, packed_weight)
    grad_gains = jnp.stack([gain_one, gain_two, gain_three])
    grad_shifts = jnp.stack([shift_one, shift_two, shift_three])
    return (
        grad_inputs,
        grad_encoded,
        (
            grad_packed_weight,
            grad_output_weight,
            grad_query_weight,
            grad_memory_weight,
            grad_cross_weight,
            grad_expand,
            grad_reduce,
            grad_gains,
            grad_shifts,
        ),
    )


def combine_scores(former, latter):
    highest = jnp.maximum(former[0], latter[0])
    totals = former[1] * jnp.exp(former[0] - highest) + latter[1] * jnp.exp(latter[0] - highest)
    return (highest, totals, former[2] + latter[2])


def combine_pairs(former, latter):
    highest = jnp.maximum(former[0], latter[0])
    totals = former[1] * jnp.exp(former[0] - highest) + latter[1] * jnp.exp(latter[0] - highest)
    return (highest, totals)


def per_device(
    decoder_states,
    encoder_memory,
    target_tokens,
    log_prior,
    slot_counts,
    slot_mask,
    self_packed,
    self_output,
    cross_query,
    cross_memory,
    cross_output,
    feed_expand,
    feed_reduce,
    embedding,
    norm_gains,
    norm_shifts,
):
    weights = (
        lax.all_gather(self_packed, "pa", axis=0, tiled=True),
        lax.all_gather(self_output, "pa", axis=0, tiled=True),
        lax.all_gather(cross_query, "pa", axis=0, tiled=True),
        lax.all_gather(cross_memory, "pa", axis=0, tiled=True),
        lax.all_gather(cross_output, "pa", axis=0, tiled=True),
        lax.all_gather(feed_expand, "pa", axis=0, tiled=True),
        lax.all_gather(feed_reduce, "pa", axis=0, tiled=True),
        lax.all_gather(norm_gains, "pa", axis=1, tiled=True),
        lax.all_gather(norm_shifts, "pa", axis=1, tiled=True),
    )
    questions, slots_here, length, model_width = decoder_states.shape
    mem_length = encoder_memory.shape[2]
    batch_size = questions * slots_here
    inputs = decoder_states.reshape(batch_size, length, model_width)
    encoded = encoder_memory.reshape(batch_size, mem_length, model_width)
    third_low, stored = layer_forward(inputs, encoded, weights)
    tokens_here = batch_size * length
    rows_all, tokens_all = (
        lax.all_gather(third_low.reshape(tokens_here, model_width), "pa", axis=0, tiled=True),
        lax.all_gather(target_tokens.reshape(tokens_here), "pa", axis=0, tiled=True),
    )
    total_rows = rows_all.shape[0]
    block_rows = min(total_rows, 2048)
    block_count = total_rows // block_rows
    vocab_start = lax.axis_index("pa") * embedding.shape[0]
    row_blocks = rows_all.reshape(block_count, block_rows, model_width)
    token_blocks = tokens_all.reshape(block_count, block_rows)

    def vocab_logits(hidden_rows, token_rows):
        logits = matmul_back(hidden_rows, embedding)
        column = lax.broadcasted_iota(jnp.int32, logits.shape, 1) + vocab_start
        return (logits, column == token_rows[:, None])

    def vocab_partial(pieces):
        logits, chosen = vocab_logits(pieces[0], pieces[1])
        highest = jnp.max(logits, -1)
        totals = jnp.sum(jnp.exp(logits - highest[:, None]), -1)
        picked = jnp.sum(jnp.where(chosen, logits, 0.0), -1)
        return (highest, totals, picked)

    highest, totals, picked = lax.map(vocab_partial, (row_blocks, token_blocks))
    highest, totals, picked = merged(
        (highest.reshape(total_rows), totals.reshape(total_rows), picked.reshape(total_rows)),
        "pa",
        combine_scores,
    )
    row_logsum = highest + jnp.log(totals)
    own_start = lax.axis_index("pa") * tokens_here
    own_logsum = lax.dynamic_slice_in_dim(row_logsum, own_start, tokens_here)
    own_picked = lax.dynamic_slice_in_dim(picked, own_start, tokens_here)
    log_probs = (own_picked - own_logsum).reshape(questions, slots_here, length)
    scores = log_prior + jnp.mean(log_probs, -1)
    slot_index = lax.axis_index("pa") * slots_here + lax.broadcasted_iota(
        jnp.int32, (questions, slots_here), 1
    )
    usable = (slot_mask == 1) & (slot_index < slot_counts[:, None])
    masked = jnp.where(usable, scores, NEGATIVE)
    local_high = jnp.max(masked, -1)
    local_total = jnp.sum(jnp.where(usable, jnp.exp(masked - local_high[:, None]), 0.0), -1)
    slot_high, slot_total = merged((local_high, local_total), "pa", combine_pairs)
    marginal = slot_high + jnp.log(slot_total)
    posterior = jnp.where(usable, jnp.exp(scores - marginal[:, None]), 0.0)
    loss_value = -lax.psum(jnp.sum(marginal), "pb") / (questions * lax.axis_size("pb"))
    slot_number = slots_here * lax.axis_size("pa")
    grad_prior = -(slot_number * length) * posterior
    token_grad = jnp.broadcast_to(
        (-slot_number * posterior)[:, :, None], (questions, slots_here, length)
    ).reshape(tokens_here)
    weights_all = lax.all_gather(token_grad, "pa", axis=0, tiled=True)

    def vocab_grads(accumulated, pieces):
        hidden_rows, token_rows, logsum_rows, weight_rows = pieces
        logits, chosen = vocab_logits(hidden_rows, token_rows)
        softmax_rows = jnp.exp(logits - logsum_rows[:, None])
        grad_logits = (weight_rows[:, None] * (jnp.where(chosen, 1.0, 0.0) - softmax_rows)).astype(
            BFLOAT
        )
        return (accumulated + outer_sum(grad_logits, hidden_rows), matmul(grad_logits, embedding))

    grad_embed, grad_rows = lax.scan(
        vocab_grads,
        jnp.zeros(embedding.shape, jnp.float32),
        (
            row_blocks,
            token_blocks,
            row_logsum.reshape(block_count, block_rows),
            weights_all.reshape(block_count, block_rows),
        ),
    )
    grad_third = lax.psum_scatter(
        grad_rows.reshape(total_rows, model_width).astype(BFLOAT),
        "pa",
        scatter_dimension=0,
        tiled=True,
    ).astype(jnp.float32).reshape(batch_size, length, model_width)
    grad_inputs, grad_encoded, grads = layer_backward(grad_third, inputs, encoded, weights, stored)
    shares = (
        lax.psum_scatter(grads[0].astype(BFLOAT), "pa", scatter_dimension=0, tiled=True),
        lax.psum_scatter(grads[1].astype(BFLOAT), "pa", scatter_dimension=0, tiled=True),
        lax.psum_scatter(grads[2].astype(BFLOAT), "pa", scatter_dimension=0, tiled=True),
        lax.psum_scatter(grads[3].astype(BFLOAT), "pa", scatter_dimension=0, tiled=True),
        lax.psum_scatter(grads[4].astype(BFLOAT), "pa", scatter_dimension=0, tiled=True),
        lax.psum_scatter(grads[5].astype(BFLOAT), "pa", scatter_dimension=0, tiled=True),
        lax.psum_scatter(grads[6].astype(BFLOAT), "pa", scatter_dimension=0, tiled=True),
        lax.psum_scatter(grads[7], "pa", scatter_dimension=1, tiled=True),
        lax.psum_scatter(grads[8], "pa", scatter_dimension=1, tiled=True),
    )
    outputs = lax.psum(
        (
            shares[0],
            shares[1],
            shares[2],
            shares[3],
            shares[4],
            shares[5],
            shares[6],
            shares[7],
            shares[8],
            grad_embed.astype(BFLOAT),
        ),
        "pb",
    )
    outputs = tuple(part.astype(jnp.float32) for part in outputs)
    return (
        loss_value,
        grad_inputs.reshape(decoder_states.shape),
        grad_encoded.reshape(encoder_memory.shape),
        grad_prior,
        outputs[0],
        outputs[1],
        outputs[2],
        outputs[3],
        outputs[4],
        outputs[5],
        outputs[6],
        outputs[9],
        outputs[7],
        outputs[8],
    )


def per_device_kernels(
    decoder_states,
    encoder_memory,
    target_tokens,
    log_prior,
    slot_counts,
    slot_mask,
    self_packed,
    self_output,
    cross_query,
    cross_memory,
    cross_output,
    feed_expand,
    feed_reduce,
    embedding,
    norm_gains,
    norm_shifts,
):
    shards = (
        self_packed,
        self_output,
        cross_query,
        cross_memory,
        cross_output,
        feed_expand,
        feed_reduce,
    )
    norm_rows = jnp.concatenate(
        [norm_gains, norm_shifts, jnp.zeros((2, norm_gains.shape[1]), BFLOAT)]
    ).astype(jnp.float32)
    _, slots_here, length, model_width = decoder_states.shape
    slots = slots_here * lax.axis_size("pa")
    states = decoder_states.reshape(slots_here * length, model_width)
    memory = encoder_memory.reshape(-1, model_width)
    matrices, norms, kept = forward_layer(shards, norm_rows, states, memory, length)
    slot_index = lax.axis_index("pa") * slots_here + jnp.arange(slots_here)
    usable = (slot_mask[0] == 1) & (slot_index < slot_counts[0])
    small, grad_embed, grad_third = vocabulary_head(
        kept[-1],
        target_tokens.reshape(slots_here * length),
        log_prior[0],
        usable,
        embedding,
        slots,
        length,
    )
    loss_value = small[0, 0]
    grad_prior = small[1].reshape(1, slots_here, length)[:, :, 0]
    pieces = lax.all_gather(grad_embed, "pb", axis=0)
    pieces = pieces.reshape(4 * grad_embed.shape[0], model_width)
    grad_embed = pieces[: embedding.shape[0]].astype(jnp.float32)
    shares, norm_sums, grad_inputs, grad_encoded = backward_layer(
        matrices,
        kept[:11] + kept[12:15] + (states, memory),
        kept[11],
        norms,
        grad_third,
        length,
    )
    norm_here = norm_gains.shape[1]
    norm_sums = lax.dynamic_slice_in_dim(
        norm_sums, lax.axis_index("pa") * norm_here, norm_here, axis=1
    )
    return (
        loss_value,
        grad_inputs.reshape(decoder_states.shape),
        grad_encoded.reshape(encoder_memory.shape),
        grad_prior,
    ) + shares + (grad_embed, norm_sums[:3], norm_sums[3:6])


def solution(mesh):
    own_kernels = mesh.shape["pb"] == 4 and mesh.shape["pa"] == 8
    return jax.shard_map(
        per_device_kernels if own_kernels else per_device,
        mesh=mesh,
        in_specs=(
            P("pb", "pa", None, None),
            P("pb", "pa", None, None),
            P("pb", "pa", None),
            P("pb", "pa"),
            P("pb"),
            P("pb", "pa"),
            P("pa", None),
            P("pa", None),
            P("pa", None),
            P("pa", None),
            P("pa", None),
            P("pa", None),
            P("pa", None),
            P("pa", None),
            P(None, "pa"),
            P(None, "pa"),
        ),
        out_specs=(
            P(),
            P("pb", "pa", None, None),
            P("pb", "pa", None, None),
            P("pb", "pa"),
            P("pa", None),
            P("pa", None),
            P("pa", None),
            P("pa", None),
            P("pa", None),
            P("pa", None),
            P("pa", None),
            P("pa", None),
            P(None, "pa"),
            P(None, "pa"),
        ),
        check_vma=False,
    )
```

```python
import functools
import math

import jax
import jax.numpy as jnp
from jax import lax
from jax.experimental import pallas as pl
from jax.experimental.pallas import tpu as pltpu
from jax.sharding import PartitionSpec as P

HEADS = 16
HEAD_DIM = 64


EPSILON = 1e-05
NEGATIVE = -1e30
BFLOAT = jnp.bfloat16
MESH = pl.DeviceIdType.MESH
TILE = 1024
ROWS = 128
WEIGHT_UNITS = (3, 1, 1, 2, 1, 4, 4)
UNITS = tuple((w, k) for w, n in enumerate(WEIGHT_UNITS) for k in range(n))
REDUCE_WEIGHT = 6


def whereami():
    pb = lax.axis_index("pb")
    pa = lax.axis_index("pa")
    return lax.rem(pb, 2), pb // 2, pa // 2, lax.rem(pa, 2)


def greet(peers):
    barrier = pltpu.get_barrier_semaphore()
    for peer in peers:
        pl.semaphore_signal(barrier, inc=1, device_id=peer, device_id_type=MESH)
    pl.semaphore_wait(barrier, len(peers))


def at(x, y, z, c):
    return (y * 2 + x, z * 2 + c)


def neighbours(x, y, z, c):
    return [at(1 - x, y, z, c), at(x, 1 - y, z, c), at(x, y, z, 1 - c)] + [
        at(x, y, lax.rem(z + d, 4), c) for d in (1, 2, 3)
    ]


def shard_view(ref, unit, start, size):
    weight, block = unit
    if weight == REDUCE_WEIGHT:
        return ref.at[pl.ds(block * ROWS + start, size), :]
    return ref.at[pl.ds(start, size), pl.ds(block * TILE, TILE)]


def full_view(ref, unit, place, core, start, size):
    weight, block = unit
    if weight == REDUCE_WEIGHT:
        return ref.at[place, core, block, pl.ds(start, size), :]
    return ref.at[place, core, pl.ds(start, size), pl.ds(block * TILE, TILE)]


Z_FULL = (9, 14)


GATHER_WINDOW = 4
LAG_TWO, LAG_SIBLING, LAG_LOAD, LAG_USE = 1, 2, 4, 5
SLOTS_IN_FLIGHT = 3


def dot_nn(left, right):
    return lax.dot_general(left, right, (((1,), (0,)), ((), ())), preferred_element_type=jnp.float32)


def dot_nt(left, right):
    return lax.dot_general(left, right, (((1,), (1,)), ((), ())), preferred_element_type=jnp.float32)


def dot_tn(left, right):
    return lax.dot_general(left, right, (((0,), (0,)), ((), ())), preferred_element_type=jnp.float32)


def stack_heads(pair):
    lane = lax.broadcasted_iota(jnp.int32, pair.shape, 1)
    zero = jnp.zeros_like(pair)
    return jnp.concatenate(
        [jnp.where(lane < HEAD_DIM, pair, zero), jnp.where(lane < HEAD_DIM, zero, pair)], 0
    )


def unstack_heads(stacked):
    rows = stacked.shape[0] // 2
    lane = lax.broadcasted_iota(jnp.int32, (rows, stacked.shape[1]), 1)
    return jnp.where(lane < HEAD_DIM, stacked[:rows], stacked[rows:])


def pair_scores(queries, keys, causal):
    scores = dot_nt(queries, keys) * (1.0 / math.sqrt(HEAD_DIM))
    if causal:
        length = keys.shape[0]
        row = lax.rem(lax.broadcasted_iota(jnp.int32, scores.shape, 0), length)
        column = lax.broadcasted_iota(jnp.int32, scores.shape, 1)
        scores = jnp.where(row >= column, scores, NEGATIVE)
    highest = jnp.max(scores, -1, keepdims=True)
    total = jnp.sum(jnp.exp(scores - highest), -1, keepdims=True)
    return jnp.exp(scores - (highest + jnp.log(total)))


def attend_pair(queries, keys, values, causal):
    probs = pair_scores(stack_heads(queries), keys, causal).astype(BFLOAT)
    return unstack_heads(dot_nn(probs, values)).astype(BFLOAT)


def normalise(values, gain, shift):
    centre = values - jnp.mean(values, -1, keepdims=True)
    inverse = lax.rsqrt(jnp.mean(centre * centre, -1, keepdims=True) + EPSILON)
    normed = centre * inverse
    return normed * gain + shift, normed, inverse


def forward_kernel(length, mem_length, *refs):
    shards, norm, aux, states_hbm, encoded_hbm = refs[:7], refs[7], refs[8], refs[9], refs[10]
    fulls, marks, kept_hbm = refs[11:18], refs[18], refs[19:36]
    (
        norm_full, packed, context, first_normed, first_inverse, first_low, cross_queries, pairs,
        cross_context, second_normed, second_inverse, second_low, inner, active, third_normed,
        third_inverse, third_low,
    ) = refs[36:53]
    wbuf, residual, states, encoded = refs[53:57]
    (
        local_sem, z_send, z_recv, one_send, one_recv, two_send, two_recv, d_send, d_recv,
        norm_sem, nz_send, nz_recv, nd_send, nd_recv, load_sem, ax_sem, ax_send, ax_recv,
        axz_send, axz_recv, kept_sem, input_sem,
    ) = refs[57:]
    x, y, z, c = whereami()
    greet(neighbours(x, y, z, c))
    every = slice(None)
    tokens, width = states_hbm.shape
    slots_here = tokens // length

    def copies(u):
        unit = UNITS[u]
        shard, full = shards[unit[0]], fulls[unit[0]]
        wide = u in Z_FULL
        a, b = (x, y) if u % 2 == 0 else (y, x)
        first_peer = at(x, 1 - y, z, c) if u % 2 == 0 else at(1 - x, y, z, c)
        second_peer = at(1 - x, y, z, c) if u % 2 == 0 else at(x, 1 - y, z, c)
        quarter = pl.multiple_of(64 * a + 32 * b, 32)
        half = pl.multiple_of(64 * a, 64)
        rows = (0, ROWS) if wide else (quarter, 32)
        local = pltpu.make_async_copy(
            shard_view(shard, unit, *rows), full_view(full, unit, z, c, *rows), local_sem.at[u]
        )
        along = [
            pltpu.make_async_remote_copy(
                src_ref=shard_view(shard, unit, *rows),
                dst_ref=full_view(full, unit, z, c, *rows),
                send_sem=z_send.at[u, d - 1],
                recv_sem=z_recv.at[u, d - 1],
                device_id=at(x, y, lax.rem(z + d, 4), c),
                device_id_type=MESH,
            )
            for d in (1, 2, 3)
        ]

        def cross(start, size, sends, recvs, peer):
            part = full_view(full, unit, every, c, start, size)
            return pltpu.make_async_remote_copy(
                src_ref=part,
                dst_ref=part,
                send_sem=sends.at[u],
                recv_sem=recvs.at[u],
                device_id=peer,
                device_id_type=MESH,
            )

        first = None if wide else cross(quarter, 32, one_send, one_recv, first_peer)
        second = None if wide else cross(half, 64, two_send, two_recv, second_peer)
        sibling = cross(0, ROWS, d_send, d_recv, at(x, y, z, 1 - c))
        load = pltpu.make_async_copy(
            full_view(full, unit, every, every, 0, ROWS),
            wbuf.at[u % SLOTS_IN_FLIGHT],
            load_sem.at[u % SLOTS_IN_FLIGHT],
        )
        return local, along, first, second, sibling, load

    def norm_copy(src, dst, send, recv, peer):
        return pltpu.make_async_remote_copy(
            src_ref=src, dst_ref=dst, send_sem=send, recv_sem=recv, device_id=peer, device_id_type=MESH
        )

    norm_local = pltpu.make_async_copy(norm, norm_full.at[z, c], norm_sem)
    norm_along = [
        norm_copy(
            norm, norm_full.at[z, c], nz_send.at[d - 1], nz_recv.at[d - 1], at(x, y, lax.rem(z + d, 4), c)
        )
        for d in (1, 2, 3)
    ]
    norm_sibling = norm_copy(
        norm_full.at[:, c], norm_full.at[:, c], nd_send, nd_recv, at(x, y, z, 1 - c)
    )
    norm_local.start()
    for copy in norm_along:
        copy.start()

    lanes = pl.ds(pl.multiple_of(c * tokens, tokens), tokens)
    aux_local = pltpu.make_async_copy(aux, marks.at[y, x, z, :, lanes], ax_sem)
    aux_local.start()
    aux_steps = [
        norm_copy(part, part, ax_send.at[n], ax_recv.at[n], peer)
        for n, (part, peer) in enumerate(
            (
                (marks.at[y, x, z, :, lanes], at(x, y, z, 1 - c)),
                (marks.at[y, x, z], at(1 - x, y, z, c)),
                (marks.at[y, :, z], at(x, 1 - y, z, c)),
            )
        )
    ]
    aux_along = [
        norm_copy(
            marks.at[:, :, z], marks.at[:, :, z], axz_send.at[d - 1], axz_recv.at[d - 1],
            at(x, y, lax.rem(z + d, 4), c),
        )
        for d in (1, 2, 3)
    ]

    kept = (
        norm_full, packed, context, first_normed, first_inverse, first_low, cross_queries, pairs,
        cross_context, second_normed, second_inverse, second_low, inner, active, third_normed,
        third_inverse, third_low,
    )

    def keep(*numbers):
        for n in numbers:
            pltpu.make_async_copy(kept[n], kept_hbm[n], kept_sem.at[n]).start()

    states_copy = pltpu.make_async_copy(states_hbm, states, input_sem.at[0])
    encoded_copy = pltpu.make_async_copy(encoded_hbm, encoded, input_sem.at[1])
    states_copy.start()
    encoded_copy.start()

    def norm_row(n):
        return jnp.concatenate(
            [norm_full[p // 2, p % 2, n : n + 1, :] for p in range(8)], 1
        )

    def times(left_ref, u, write):
        slot = u % SLOTS_IN_FLIGHT

        @pl.loop(0, 4)
        def _(n):
            columns = pl.ds(pl.multiple_of(n * 256, 256), 256)
            right = wbuf[slot, :, :, :, columns].reshape(TILE, 256)
            write(columns, n, dot_nn(left_ref[...], right))

    def block_columns(k, n):
        return pl.ds(pl.multiple_of(k * TILE + n * 256, 256), 256)

    def attention(queries, keys, key_start, value_start, key_length, out, causal):
        @pl.loop(0, slots_here * (width // 128))
        def _(n):
            slot, group = n // (width // 128), lax.rem(n, width // 128)
            lanes = pl.ds(pl.multiple_of(group * 128, 128), 128)
            key_lanes = pl.ds(pl.multiple_of(key_start + group * 128, 128), 128)
            value_lanes = pl.ds(pl.multiple_of(value_start + group * 128, 128), 128)
            query_rows = pl.ds(pl.multiple_of(slot * length, length), length)
            key_rows = pl.ds(pl.multiple_of(slot * key_length, key_length), key_length)
            out[query_rows, lanes] = attend_pair(
                queries[query_rows, lanes], keys[key_rows, key_lanes], keys[key_rows, value_lanes], causal
            )

    def finish_norm(n, value, normed_ref, inverse_ref, low_ref):
        out, normed, inverse = normalise(value, norm_row(n), norm_row(n + 3))
        normed_ref[...] = normed
        inverse_ref[...] = jnp.broadcast_to(inverse, inverse_ref.shape)
        low_ref[...] = out.astype(BFLOAT)
        return out

    def use(u):
        weight, k = UNITS[u]
        if weight == 0:
            def write(columns, n, value):
                packed[:, block_columns(k, n)] = value.astype(BFLOAT)

            times(states, u, write)
            if k == 2:
                attention(packed, packed, width, 2 * width, length, context, True)
                keep(1, 2)
        elif weight == 1:
            def write(columns, n, value):
                residual[:, columns] = states[:, columns].astype(jnp.float32) + value

            times(context, u, write)
            residual[...] = finish_norm(0, residual[...], first_normed, first_inverse, first_low)
            keep(3, 4, 5)
        elif weight == 2:
            def write(columns, n, value):
                cross_queries[:, columns] = value.astype(BFLOAT)

            times(first_low, u, write)
        elif weight == 3:
            slot = u % SLOTS_IN_FLIGHT

            @pl.loop(0, 16)
            def _(n):
                m, n = n // 4, lax.rem(n, 4)
                columns = pl.ds(pl.multiple_of(n * 256, 256), 256)
                part = encoded.shape[0] // 4
                rows_here = pl.ds(pl.multiple_of(m * part, part), part)
                right = wbuf[slot, :, :, :, columns].reshape(TILE, 256)
                pairs[rows_here, block_columns(k, n)] = dot_nn(encoded[rows_here, :], right).astype(BFLOAT)

            if k == 1:
                attention(cross_queries, pairs, 0, width, mem_length, cross_context, False)
                keep(6, 7, 8)
        elif weight == 4:
            def write(columns, n, value):
                residual[:, columns] = residual[:, columns] + value

            times(cross_context, u, write)
            residual[...] = finish_norm(1, residual[...], second_normed, second_inverse, second_low)
            keep(9, 10, 11)
        elif weight == 5:
            def write(columns, n, value):
                inner[:, block_columns(k, n)] = value
                gate = 0.5 * (1.0 + lax.erf(value * math.sqrt(0.5)))
                active[:, block_columns(k, n)] = (value * gate).astype(BFLOAT)

            times(second_low, u, write)
            if k == 3:
                keep(12, 13)
        else:
            slot = u % SLOTS_IN_FLIGHT
            blocks = active.shape[1] // (8 * ROWS)
            left = jnp.concatenate(
                [active[:, (p * blocks + k) * ROWS : (p * blocks + k + 1) * ROWS] for p in range(8)], 1
            )

            @pl.loop(0, 4)
            def _(n):
                columns = pl.ds(pl.multiple_of(n * 256, 256), 256)
                right = wbuf[slot, :, :, :, columns].reshape(TILE, 256)
                residual[:, columns] = residual[:, columns] + dot_nn(left, right)

            if k == blocks - 1:
                finish_norm(2, residual[...], third_normed, third_inverse, third_low)
                keep(14, 15, 16)

    count = len(UNITS)
    every_copy = [copies(u) for u in range(count)]
    for local, along, _, _, _, _ in every_copy[:GATHER_WINDOW]:
        local.start()
        for copy in along:
            copy.start()
    for i in range(count + LAG_USE):
        if i + GATHER_WINDOW < count:
            local, along = every_copy[i + GATHER_WINDOW][:2]
            local.start()
            for copy in along:
                copy.start()
        if i < count:
            local, along, first = every_copy[i][:3]
            local.wait()
            for copy in along:
                copy.wait_recv()
            if first is not None:
                first.start()
        if 0 <= i - LAG_TWO < count:
            first, second = every_copy[i - LAG_TWO][2:4]
            if first is not None:
                first.wait_recv()
                second.start()
        if 0 <= i - LAG_SIBLING < count:
            second, sibling = every_copy[i - LAG_SIBLING][3:5]
            if second is not None:
                second.wait_recv()
            sibling.start()
        if i == 2:
            norm_local.wait()
            for copy in norm_along:
                copy.wait()
            norm_sibling.start()
        if i == 4:
            norm_sibling.wait()
            keep(0)
            states_copy.wait()
            encoded_copy.wait()
        if 5 <= i < 9:
            if i == 5:
                aux_local.wait()
            else:
                aux_steps[i - 6].wait()
            for copy in aux_steps[i - 5 : i - 4] if i < 8 else aux_along:
                copy.start()
        if i == 9:
            for copy in aux_along:
                copy.wait()
        if 0 <= i - LAG_LOAD < count:
            sibling, load = every_copy[i - LAG_LOAD][4:]
            sibling.wait_recv()
            load.start()
        if 0 <= i - LAG_USE < count:
            every_copy[i - LAG_USE][5].wait()
            use(i - LAG_USE)
    for _, along, first, second, sibling, _ in every_copy:
        for copy in along:
            copy.wait_send()
        if first is not None:
            first.wait_send()
            second.wait_send()
        sibling.wait_send()
    for n in range(len(kept)):
        pltpu.make_async_copy(kept[n], kept_hbm[n], kept_sem.at[n]).wait()


def forward_layer(weights, norm, aux, states, encoded, length):
    count = len(UNITS)
    shapes = []
    for w, weight in enumerate(weights):
        if w == REDUCE_WEIGHT:
            shapes.append((4, 2, weight.shape[0] // ROWS, ROWS, weight.shape[1]))
        else:
            shapes.append((4, 2) + weight.shape)
    tokens, width = states.shape
    mem_tokens = encoded.shape[0]
    mem_length = mem_tokens // (tokens // length)
    units = weights[5].shape[1]
    f32 = jnp.float32
    kept = [
        ((4, 2) + norm.shape, f32),
        ((tokens, 3 * width), BFLOAT),
        ((tokens, width), BFLOAT),
        ((tokens, width), f32),
        ((tokens, 128), f32),
        ((tokens, width), BFLOAT),
        ((tokens, width), BFLOAT),
        ((mem_tokens, 2 * width), BFLOAT),
        ((tokens, width), BFLOAT),
        ((tokens, width), f32),
        ((tokens, 128), f32),
        ((tokens, width), BFLOAT),
        ((tokens, units), f32),
        ((tokens, units), BFLOAT),
        ((tokens, width), f32),
        ((tokens, 128), f32),
        ((tokens, width), BFLOAT),
    ]
    every = pl.BlockSpec(memory_space=pl.ANY)
    dma = pltpu.SemaphoreType.DMA
    results = pl.pallas_call(
        functools.partial(forward_kernel, length, mem_length),
        out_shape=tuple(jax.ShapeDtypeStruct(shape, BFLOAT) for shape in shapes)
        + (jax.ShapeDtypeStruct((2, 2, 4, aux.shape[0], 2 * tokens), f32),)
        + tuple(jax.ShapeDtypeStruct(shape, kind) for shape, kind in kept),
        in_specs=[every] * 11,
        out_specs=(every,) * (8 + len(kept)),
        scratch_shapes=[pltpu.VMEM(shape, kind) for shape, kind in kept]
        + [
            pltpu.VMEM((SLOTS_IN_FLIGHT, 4, 2, ROWS, TILE), BFLOAT),
            pltpu.VMEM((tokens, width), f32),
            pltpu.VMEM((tokens, width), BFLOAT),
            pltpu.VMEM((mem_tokens, width), BFLOAT),
            dma((count,)),
            dma((count, 3)),
            dma((count, 3)),
        ]
        + [dma((count,))] * 6
        + [dma]
        + [dma((3,))] * 2
        + [dma] * 2
        + [dma((SLOTS_IN_FLIGHT,))]
        + [dma]
        + [dma((3,))] * 4
        + [dma((len(kept),)), dma((2,))],
        compiler_params=pltpu.CompilerParams(
            collective_id=0, has_side_effects=True, vmem_limit_bytes=62 * 2**20
        ),
        name="forward_layer",
    )(*weights, norm, aux, states, encoded)
    fulls = tuple(full.reshape(-1, full.shape[-1]) for full in results[:7])
    return fulls, results[7], results[8], results[9:]


SEQUENCE = tuple((6, k) for k in range(4)) + tuple((5, k) for k in range(4)) + (
    (4, 0), (2, 0), (3, 0), (3, 1), (1, 0), (0, 0), (0, 1), (0, 2),
)
LINE_FIRST = 5
LINE_LAGS = (12, 14, 16, 18, 20)
CROSS_LAGS = (2, 4, 6, 8, 10)
TURNS = 27
READS = tuple(read for k in range(4) for read in ((6, k), (5, k))) + (
    (4, 0), (2, 0), (1, 0), (0, 0), (0, 1), (0, 2), (3, 0), (3, 1),
)


def norm_back(upstream, normed, inverse, gain):
    scaled = upstream * gain
    mean_scaled = jnp.mean(scaled, -1, keepdims=True)
    along = jnp.mean(scaled * normed, -1, keepdims=True)
    return (
        inverse * (scaled - mean_scaled - normed * along),
        jnp.sum(upstream * normed, 0, keepdims=True),
        jnp.sum(upstream, 0, keepdims=True),
    )


def attend_pair_back(grad, queries, keys, values, causal):
    scale = 1.0 / math.sqrt(HEAD_DIM)
    queries, grad = stack_heads(queries), stack_heads(grad)
    probs = pair_scores(queries, keys, causal)
    grad_probs = dot_nt(grad, values)
    grad_values = dot_tn(probs.astype(BFLOAT), grad).astype(BFLOAT)
    grad_scores = (
        probs * (grad_probs - jnp.sum(probs * grad_probs, -1, keepdims=True))
    ).astype(BFLOAT)
    grad_queries = unstack_heads(dot_nn(grad_scores, keys) * scale).astype(BFLOAT)
    grad_keys = (dot_tn(grad_scores, queries) * scale).astype(BFLOAT)
    return grad_queries, grad_keys, grad_values


def backward_kernel(length, mem_length, *refs):
    weights = refs[:7]
    kept_hbm = refs[7:23]
    inner_hbm = refs[23]
    norm_full, grad_third = refs[24:26]
    outs = refs[26:33]
    norm_out, grad_states, grad_memory, landing = refs[33:37]
    kept = refs[37:53]
    (
        wbuf, inner, stage, got, zload, one_line, two_line, one, two, line, fin,
        resid, low, grad_low, grad_context, grad_queries, grad_packed, memory_part,
        norm_here, norm_there, norm_line,
    ) = refs[53:74]
    (
        kept_sem, w_sem, inner_sem, dd_send, dd_recv, z_send, z_recv, zload_sem,
        ra_send, ra_recv, rb_send, rb_recv, rz_send, rz_recv, ag_send, ag_recv, ah_send, ah_recv,
        fin_sem, memory_sem, n_send, n_recv, nz_send, nz_recv,
    ) = refs[74:]
    (
        packed, context, first_normed, first_inverse, first_low, cross_queries, pairs, cross_context,
        second_normed, second_inverse, second_low, active, third_normed, third_inverse, states, encoded,
    ) = kept
    x, y, z, c = whereami()
    greet(neighbours(x, y, z, c))
    tokens, width = states.shape
    slots_here = tokens // length
    count = len(SEQUENCE)
    blocks = active.shape[1] // (8 * ROWS)

    def keep_copy(n):
        return pltpu.make_async_copy(kept_hbm[n], kept[n], kept_sem.at[n])

    first_needed = (12, 13, 11, 10)
    for n in first_needed:
        keep_copy(n).start()
    for n in range(16):
        if n not in first_needed:
            keep_copy(n).start()

    def need(*names):
        for n in names:
            keep_copy(n).wait()

    def read_copy(n):
        weight, k = READS[n]
        if weight == REDUCE_WEIGHT:
            source = weights[weight].at[pl.ds(k * TILE, TILE), :]
        else:
            source = weights[weight].at[:, pl.ds(k * TILE, TILE)]
        return pltpu.make_async_copy(source, wbuf.at[n % 2], w_sem.at[n % 2])

    def inner_copy(k):
        return pltpu.make_async_copy(
            inner_hbm.at[:, pl.ds(k * TILE, TILE)], inner.at[k % 2], inner_sem.at[k % 2]
        )

    read_copy(0).start()
    read_copy(1).start()
    inner_copy(0).start()
    inner_copy(1).start()

    def remote(src, dst, send, recv, peer):
        return pltpu.make_async_remote_copy(
            src_ref=src, dst_ref=dst, send_sem=send, recv_sem=recv, device_id=peer, device_id_type=MESH
        )

    def norm_row(n):
        return jnp.concatenate([norm_full[p // 2, p % 2, n : n + 1, :] for p in range(8)], 1)

    def place(q):
        even = lax.rem(q, 2) == 0
        a = jnp.where(even, x, y)
        b = jnp.where(even, y, x)
        x_peer = y * 2 + (1 - x)
        y_peer = (1 - y) * 2 + x
        a_peer = (jnp.where(even, x_peer, y_peer), z * 2 + c)
        b_peer = (jnp.where(even, y_peer, x_peer), z * 2 + c)
        return a, b, a_peer, b_peer

    def piece(index, size):
        return pl.ds(pl.multiple_of(index * size, size), size)

    def total(*parts):
        out = parts[0].astype(jnp.float32)
        for part in parts[1:]:
            out = out + part.astype(jnp.float32)
        return out.astype(BFLOAT)

    def dd_copy(q):
        return remote(
            stage.at[lax.rem(q, 2), 1 - c], got.at[q], dd_send.at[q], dd_recv.at[q], at(x, y, z, 1 - c)
        )

    def line_copy(q, d):
        other = lax.rem(z + d, 4)
        return remote(
            got.at[q, other], landing.at[q, d - 1], z_send.at[q, d - 1], z_recv.at[q, d - 1],
            at(x, y, other, c),
        )

    def ra_line(q):
        a, _, a_peer, _ = place(q)
        return remote(got.at[q, z, piece(1 - a, 64), :], one_line.at[q], ra_send.at[q], ra_recv.at[q], a_peer)

    def rb_line(q):
        _, b, _, b_peer = place(q)
        return remote(one_line.at[q, piece(1 - b, 32), :], two_line.at[q], rb_send.at[q], rb_recv.at[q], b_peer)

    def ra_cross(q):
        a, _, a_peer, _ = place(q)
        return remote(
            got.at[q, :, piece(1 - a, 64), :], one.at[q - LINE_FIRST], ra_send.at[q], ra_recv.at[q], a_peer
        )

    def rb_cross(q):
        _, b, _, b_peer = place(q)
        return remote(
            one.at[q - LINE_FIRST, :, piece(1 - b, 32), :], two.at[q - LINE_FIRST],
            rb_send.at[q], rb_recv.at[q], b_peer,
        )

    def rz_cross(q, d):
        other = lax.rem(z + d, 4)
        n = q - LINE_FIRST
        return remote(
            two.at[n, other], line.at[n, d - 1], rz_send.at[n, d - 1], rz_recv.at[n, d - 1],
            at(x, y, other, c),
        )

    def out_view(q, start, size):
        return shard_view(outs[SEQUENCE[q][0]], SEQUENCE[q], start, size)

    def quarter_start(q):
        a, b, _, _ = place(q)
        return pl.multiple_of(64 * a + 32 * b, 32)

    def fin_copy(q):
        return pltpu.make_async_copy(fin.at[q], out_view(q, quarter_start(q), 32), fin_sem.at[q])

    def ag_copy(q):
        return remote(
            fin.at[q], out_view(q, quarter_start(q), 32), ag_send.at[q], ag_recv.at[q], place(q)[3]
        )

    def ah_copy(q):
        a, _, a_peer, _ = place(q)
        part = out_view(q, pl.multiple_of(64 * a, 64), 64)
        return remote(part, part, ah_send.at[q], ah_recv.at[q], a_peer)

    norm_peers = (at(x, y, z, 1 - c), at(1 - x, y, z, c), at(x, 1 - y, z, c))

    def norm_copy(n):
        return remote(norm_here.at[n], norm_there.at[n], n_send.at[n], n_recv.at[n], norm_peers[n])

    def norm_line_copy(d):
        return remote(
            norm_here.at[3], norm_line.at[d - 1], nz_send.at[d - 1], nz_recv.at[d - 1],
            at(x, y, lax.rem(z + d, 4), c),
        )

    def outer(q, left, start, step, right):
        slot = q % 2

        @pl.loop(0, 8)
        def _(p):
            lanes = pl.ds(pl.multiple_of(start + p * step, 128), 128)
            stage[slot, lax.rem(p, 2), p // 2] = dot_tn(left[:, lanes], right()).astype(BFLOAT)

    def back_times(left, n, write):
        slot = n % 2
        read_copy(n).wait()

        @pl.loop(0, 4)
        def _(m):
            write(piece(m, 256), dot_nt(left[...], wbuf[slot, piece(m, 256), :]))

        if n + 2 < len(READS):
            read_copy(n + 2).start()

    def add_resid(columns, value):
        resid[:, columns] = resid[:, columns] + value

    def finish_norm(n, normed, inverse):
        value, gain, shift = norm_back(resid[...], normed[...], inverse[:, 0:1], norm_row(n))
        resid[...] = value
        low[...] = value.astype(BFLOAT)
        norm_here[0, n : n + 1, :] = gain
        norm_here[0, n + 3 : n + 4, :] = shift

    def attention_back(queries, keys, key_start, value_start, key_length, out, out_keys, causal):
        @pl.loop(0, slots_here * (width // 128))
        def _(n):
            slot, group = n // (width // 128), lax.rem(n, width // 128)
            lanes = piece(group, 128)
            key_lanes = pl.ds(pl.multiple_of(key_start + group * 128, 128), 128)
            value_lanes = pl.ds(pl.multiple_of(value_start + group * 128, 128), 128)
            query_rows = piece(slot, length)
            key_rows = piece(slot, key_length)
            grad_query, grad_key, grad_value = attend_pair_back(
                grad_context[query_rows, lanes],
                queries[query_rows, lanes],
                keys[key_rows, key_lanes],
                keys[key_rows, value_lanes],
                causal,
            )
            out[query_rows, lanes] = grad_query
            out_keys[key_rows, key_lanes] = grad_key
            out_keys[key_rows, value_lanes] = grad_value

    def produce(q):
        weight, k = SEQUENCE[q]
        if q == 0:
            norm_here[0] = jnp.zeros_like(norm_here[0])
            for p in range(8):
                resid[:, p * 128 : (p + 1) * 128] = grad_third[p * 128 : (p + 1) * 128, :].T
            need(12, 13, 11)
            finish_norm(2, third_normed, third_inverse)
        if weight == 6:
            outer(q, active, k * ROWS, blocks * ROWS, lambda: low[...])
        elif weight == 5:
            if k == 0:
                need(10)
            inner_copy(k).wait()

            def write(columns, value):
                pre = inner[k % 2, :, columns]
                slope = 0.5 * (1.0 + lax.erf(pre * math.sqrt(0.5))) + pre * jnp.exp(
                    -0.5 * pre * pre
                ) * (1.0 / math.sqrt(2.0 * math.pi))
                grad_low[:, columns] = (value * slope).astype(BFLOAT)

            back_times(low, 2 * k, write)
            if k + 2 < 4:
                inner_copy(k + 2).start()
            outer(q, second_low, 0, ROWS, lambda: grad_low[...])
            back_times(grad_low, 2 * k + 1, add_resid)
        elif weight == 4:
            need(8, 9, 7)
            finish_norm(1, second_normed, second_inverse)
            outer(q, cross_context, 0, ROWS, lambda: low[...])

            def write(columns, value):
                grad_context[:, columns] = value.astype(BFLOAT)

            back_times(low, 8, write)
        elif weight == 2:
            need(5, 6, 4, 2, 3)
            attention_back(cross_queries, pairs, 0, width, mem_length, grad_queries, pairs, False)
            outer(q, first_low, 0, ROWS, lambda: grad_queries[...])
            back_times(grad_queries, 9, add_resid)
            finish_norm(0, first_normed, first_inverse)
        elif weight == 3:
            if k == 0:
                need(15)
            outer(q, encoded, 0, ROWS, lambda: pairs[:, pl.ds(k * TILE, TILE)])
        elif weight == 1:
            need(1, 0, 14)
            outer(q, context, 0, ROWS, lambda: low[...])

            def write(columns, value):
                grad_context[:, columns] = value.astype(BFLOAT)

            back_times(low, 10, write)
            attention_back(packed, packed, width, 2 * width, length, grad_packed, grad_packed, True)
        else:
            def part():
                return grad_packed[:, pl.ds(k * TILE, TILE)]

            outer(q, states, 0, ROWS, part)
            back_times(grad_packed.at[:, pl.ds(k * TILE, TILE)], 11 + k, add_resid)
            if k == 2:
                grad_states[...] = resid[...]

    memory_rows = encoded.shape[0] // 8

    def memory_copy(m):
        return pltpu.make_async_copy(
            memory_part.at[m % 2], grad_memory.at[pl.ds(m * memory_rows, memory_rows), :], memory_sem.at[m % 2]
        )

    def memory_chunk(m):
        if m == 0:
            read_copy(14).wait()
            read_copy(15).wait()
        if m >= 2:
            memory_copy(m - 2).wait()
        rows_here = pl.ds(m * memory_rows, memory_rows)

        @pl.loop(0, 4)
        def _(n):
            memory_part[m % 2, :, piece(n, 256)] = dot_nt(
                pairs[rows_here, :width], wbuf[0, piece(n, 256), :]
            ) + dot_nt(pairs[rows_here, width:], wbuf[1, piece(n, 256), :])

        memory_copy(m).start()

    def each(q, action):
        for k in range(count):
            @pl.when(q == k)
            def _():
                action(k)

    def finish_block(q):
        def action(k):
            fin_copy(k).start()
            ag_copy(k).start()

        each(q, action)

    step = 16

    @pl.loop(0, TURNS)
    def _(i):
        for q in range(count):
            @pl.when(i == q)
            def _():
                if q >= 2:
                    dd_copy(q - 2).wait_send()
                produce(q)
                dd_copy(q).start()

        for m in range(8):
            @pl.when(i == count + 1 + m)
            def _():
                memory_chunk(m)

        qs = i - 1

        @pl.when((qs >= 0) & (qs < count))
        def _():
            dd_copy(qs).wait_recv()
            slot = lax.rem(qs, 2)

            @pl.loop(0, 32)
            def _(j):
                zz, rows_here = j // 8, piece(lax.rem(j, 8), step)
                got[qs, zz, rows_here, :] = total(got[qs, zz, rows_here, :], stage[slot, c, zz, rows_here, :])

            @pl.when(qs < LINE_FIRST)
            def _():
                for d in (1, 2, 3):
                    line_copy(qs, d).start()

            @pl.when(qs >= LINE_FIRST)
            def _():
                ra_cross(qs).start()

        q0 = i - LINE_LAGS[0]

        @pl.when((q0 >= 0) & (q0 < LINE_FIRST))
        def _():
            for d in (1, 2, 3):
                line_copy(q0, d).wait_recv()
            load = pltpu.make_async_copy(landing.at[q0], zload, zload_sem)
            load.start()
            load.wait()

            @pl.loop(0, 8)
            def _(j):
                rows_here = piece(j, step)
                got[q0, z, rows_here, :] = total(
                    got[q0, z, rows_here, :], zload[0, rows_here, :], zload[1, rows_here, :],
                    zload[2, rows_here, :],
                )

            ra_line(q0).start()

        q1 = i - LINE_LAGS[1]

        @pl.when((q1 >= 0) & (q1 < LINE_FIRST))
        def _():
            ra_line(q1).wait_recv()
            a = place(q1)[0]

            @pl.loop(0, 4)
            def _(j):
                rows_here = piece(j, step)
                one_line[q1, rows_here, :] = total(
                    one_line[q1, rows_here, :],
                    got[q1, z, pl.ds(pl.multiple_of(64 * a + j * step, step), step), :],
                )

            rb_line(q1).start()

        q2 = i - LINE_LAGS[2]

        @pl.when((q2 >= 0) & (q2 < LINE_FIRST))
        def _():
            rb_line(q2).wait_recv()
            b = place(q2)[1]

            @pl.loop(0, 2)
            def _(j):
                rows_here = piece(j, step)
                fin[q2, rows_here, :] = total(
                    two_line[q2, rows_here, :],
                    one_line[q2, pl.ds(pl.multiple_of(32 * b + j * step, step), step), :],
                )

            finish_block(q2)

        p0 = i - CROSS_LAGS[0]

        @pl.when((p0 >= LINE_FIRST) & (p0 < count))
        def _():
            ra_cross(p0).wait_recv()
            a = place(p0)[0]

            @pl.loop(0, 16)
            def _(j):
                zz, r = j // 4, lax.rem(j, 4)
                rows_here = piece(r, step)
                one[p0 - LINE_FIRST, zz, rows_here, :] = total(
                    one[p0 - LINE_FIRST, zz, rows_here, :],
                    got[p0, zz, pl.ds(pl.multiple_of(64 * a + r * step, step), step), :],
                )

            rb_cross(p0).start()

        p1 = i - CROSS_LAGS[1]

        @pl.when((p1 >= LINE_FIRST) & (p1 < count))
        def _():
            rb_cross(p1).wait_recv()
            b = place(p1)[1]

            @pl.loop(0, 8)
            def _(j):
                zz, r = j // 2, lax.rem(j, 2)
                rows_here = piece(r, step)
                two[p1 - LINE_FIRST, zz, rows_here, :] = total(
                    two[p1 - LINE_FIRST, zz, rows_here, :],
                    one[p1 - LINE_FIRST, zz, pl.ds(pl.multiple_of(32 * b + r * step, step), step), :],
                )

            for d in (1, 2, 3):
                rz_cross(p1, d).start()

        p2 = i - CROSS_LAGS[2]

        @pl.when((p2 >= LINE_FIRST) & (p2 < count))
        def _():
            for d in (1, 2, 3):
                rz_cross(p2, d).wait_recv()
            n = p2 - LINE_FIRST

            @pl.loop(0, 2)
            def _(j):
                rows_here = piece(j, step)
                fin[p2, rows_here, :] = total(
                    two[n, z, rows_here, :], line[n, 0, rows_here, :], line[n, 1, rows_here, :],
                    line[n, 2, rows_here, :],
                )

            finish_block(p2)

        def pass_on(k):
            ag_copy(k).wait_recv()
            fin_copy(k).wait()
            ah_copy(k).start()

        for lags, low_q, high_q in ((LINE_LAGS, 0, LINE_FIRST), (CROSS_LAGS, LINE_FIRST, count)):
            q3 = i - lags[3]

            @pl.when((q3 >= low_q) & (q3 < high_q))
            def _():
                each(q3, pass_on)

            q4 = i - lags[4]

            @pl.when((q4 >= low_q) & (q4 < high_q))
            def _():
                each(q4, lambda k: ah_copy(k).wait_recv())

        @pl.when(i == count)
        def _():
            norm_copy(0).start()

        for n in range(3):
            @pl.when(i == count + 2 * (n + 1))
            def _():
                norm_copy(n).wait_recv()
                norm_here[n + 1] = norm_here[n] + norm_there[n]
                if n < 2:
                    norm_copy(n + 1).start()
                else:
                    for d in (1, 2, 3):
                        norm_line_copy(d).start()

        @pl.when(i == count + 8)
        def _():
            for d in (1, 2, 3):
                norm_line_copy(d).wait_recv()
            norm_out[...] = ((norm_here[3] + norm_line[0]) + norm_line[1]) + norm_line[2]

    memory_copy(6).wait()
    memory_copy(7).wait()
    dd_copy(count - 2).wait_send()
    dd_copy(count - 1).wait_send()

    @pl.loop(0, LINE_FIRST)
    def _(q):
        for d in (1, 2, 3):
            line_copy(q, d).wait_send()
        ra_line(q).wait_send()
        rb_line(q).wait_send()

    @pl.loop(LINE_FIRST, count)
    def _(q):
        ra_cross(q).wait_send()
        rb_cross(q).wait_send()
        for d in (1, 2, 3):
            rz_cross(q, d).wait_send()

    for q in range(count):
        ag_copy(q).wait_send()
        ah_copy(q).wait_send()
    for n in range(3):
        norm_copy(n).wait_send()
        norm_line_copy(n + 1).wait_send()


def backward_layer(weights, kept, inner, norm_full, grad_third, length):
    count = len(SEQUENCE)
    f32 = jnp.float32
    tokens, width = kept[14].shape
    mem_tokens = kept[15].shape[0]
    mem_length = mem_tokens // (tokens // length)
    shapes = [(weight.shape[0] // 8, weight.shape[1]) for weight in weights]
    every = pl.BlockSpec(memory_space=pl.ANY)
    vmem = pl.BlockSpec(memory_space=pltpu.VMEM)
    dma = pltpu.SemaphoreType.DMA
    sems = dma((count,))
    crossed = count - LINE_FIRST
    *shares, norm_sum, grad_states, grad_memory, _ = pl.pallas_call(
        functools.partial(backward_kernel, length, mem_length),
        out_shape=tuple(jax.ShapeDtypeStruct(shape, BFLOAT) for shape in shapes)
        + (
            jax.ShapeDtypeStruct((8, width), f32),
            jax.ShapeDtypeStruct((tokens, width), f32),
            jax.ShapeDtypeStruct((mem_tokens, width), f32),
            jax.ShapeDtypeStruct((LINE_FIRST, 3, ROWS, TILE), BFLOAT),
        ),
        in_specs=[every] * 24 + [vmem] * 2,
        out_specs=(every,) * 7 + (vmem, vmem, every, every),
        scratch_shapes=[pltpu.VMEM(part.shape, part.dtype) for part in kept]
        + [
            pltpu.VMEM((2, TILE, TILE), BFLOAT),
            pltpu.VMEM((2, tokens, TILE), f32),
            pltpu.VMEM((2, 2, 4, ROWS, TILE), BFLOAT),
            pltpu.VMEM((count, 4, ROWS, TILE), BFLOAT),
            pltpu.VMEM((3, ROWS, TILE), BFLOAT),
            pltpu.VMEM((LINE_FIRST, 64, TILE), BFLOAT),
            pltpu.VMEM((LINE_FIRST, 32, TILE), BFLOAT),
            pltpu.VMEM((crossed, 4, 64, TILE), BFLOAT),
            pltpu.VMEM((crossed, 4, 32, TILE), BFLOAT),
            pltpu.VMEM((crossed, 3, 32, TILE), BFLOAT),
            pltpu.VMEM((count, 32, TILE), BFLOAT),
            pltpu.VMEM((tokens, width), f32),
            pltpu.VMEM((tokens, width), BFLOAT),
            pltpu.VMEM((tokens, TILE), BFLOAT),
            pltpu.VMEM((tokens, width), BFLOAT),
            pltpu.VMEM((tokens, width), BFLOAT),
            pltpu.VMEM((tokens, 3 * width), BFLOAT),
            pltpu.VMEM((2, mem_tokens // 8, width), f32),
            pltpu.VMEM((4, 8, width), f32),
            pltpu.VMEM((3, 8, width), f32),
            pltpu.VMEM((3, 8, width), f32),
            dma((16,)), dma((2,)), dma((2,)), sems, sems,
            dma((LINE_FIRST, 3)), dma((LINE_FIRST, 3)), dma,
            sems, sems, sems, sems,
            dma((crossed, 3)), dma((crossed, 3)),
            sems, sems, sems, sems, sems, dma((2,)),
            dma((3,)), dma((3,)), dma((3,)), dma((3,)),
        ],
        compiler_params=pltpu.CompilerParams(
            collective_id=1, has_side_effects=True, vmem_limit_bytes=62 * 2**20
        ),
        name="backward_layer",
    )(*weights, *kept, inner, norm_full, grad_third)
    return tuple(share.astype(f32) for share in shares), norm_sum, grad_states, grad_memory


VOCAB_CUTS = 3
ARRIVAL_PHASES = (0, 0, 1, 0, 1, 2, 3, 0, 1, 2, 3, 1, 2, 3, 2, 3)
ARRIVAL_TURNS = (0, 1, 0, 2, 1, 0, 0, 3, 2, 1, 1, 3, 2, 2, 3, 3)
NEAREST = ((0, 1, 2, 3), (1, 0, 1, 2), (2, 2, 3, 1), (3, 3, 0, 0))


def head_kernel(slots, length, vocab_here, *refs):
    hid, marks, emb_all = refs[:3]
    small_out, gemb_out, third_out = refs[3:6]
    (
        emb, emb_t, held, logit, expo, part, sib_part, part_one, part_two, part_z,
        mine, theirs, lined, prior, usable, weight, scaled, picked_grad,
    ) = refs[6:24]
    (
        local_sem, z_send, z_recv, one_send, one_recv, two_send, two_recv, sib_send, sib_recv,
        st_send, st_recv, stz_send, stz_recv,
        dd_send, dd_recv, r1_send, r1_recv, r2_send, r2_recv, rz_send, rz_recv,
    ) = refs[24:]
    x, y, z, c = whereami()
    pb, pa = y * 2 + x, z * 2 + c
    size = hid.shape[0]
    pair = 2 * size
    width = hid.shape[1]
    rows = emb.shape[0]
    cut = rows // VOCAB_CUTS
    start = pl.multiple_of(pb * rows, 16)
    last = vocab_here - 3 * rows
    valid = jnp.where(pb == 3, last, rows)
    base = pa * vocab_here + start
    own = pb * 4 + z

    def remote(src, dst, send, recv, peer):
        return pltpu.make_async_remote_copy(
            src_ref=src, dst_ref=dst, send_sem=send, recv_sem=recv, device_id=peer, device_id_type=MESH
        )

    sibling = at(x, y, z, 1 - c)
    x_peer, y_peer = at(1 - x, y, z, c), at(x, 1 - y, z, c)

    def spot(k, core):
        return held.at[pl.ds(pl.multiple_of((k * 2 + core) * size, size), size), :]

    greet(neighbours(x, y, z, c))
    own_copy = pltpu.make_async_copy(hid, spot(own, c), local_sem.at[0])
    own_copy.start()
    emb_copy = pltpu.make_async_copy(
        emb_all.at[pl.ds(start, last), :], emb.at[pl.ds(0, last), :], local_sem.at[2]
    )
    rest_copy = pltpu.make_async_copy(
        emb_all.at[pl.ds(pl.multiple_of(jnp.minimum(start + last, vocab_here - (rows - last)), 16), rows - last), :],
        emb.at[pl.ds(last, rows - last), :],
        local_sem.at[3],
    )
    emb_copy.start()
    rest_copy.start()
    own_copy.wait()

    def up_copy(origin):
        block = spot(pb * 4 + origin, c)
        return remote(block, block, z_send.at[0, origin], z_recv.at[origin], at(x, y, z + 1, c))

    def down_copy(origin):
        block = spot(pb * 4 + origin, c)
        return remote(block, block, z_send.at[1, origin], z_recv.at[origin], at(x, y, z - 1, c))

    def pass_along(origin, action):
        @pl.when((origin <= z) & (z < 3))
        def _():
            action(up_copy(origin))

        @pl.when((origin >= z) & (z > 0))
        def _():
            action(down_copy(origin))

    def sib_copy(k):
        return remote(spot(k, c), spot(k, c), sib_send.at[k], sib_recv.at[k], sibling)

    def order(zz):
        x_first = zz < 2
        f = jnp.where(x_first, x, y)
        g = jnp.where(x_first, y, x)
        first_peer = (jnp.where(x_first, y * 2 + 1 - x, (1 - y) * 2 + x), pa)
        second_peer = (jnp.where(x_first, (1 - y) * 2 + x, y * 2 + 1 - x), pa)

        def block(first, second):
            return jnp.where(x_first, second * 2 + first, first * 2 + second) * 4 + zz

        return f, g, first_peer, second_peer, block

    def one_copy(zz):
        f, g, first_peer, _, block = order(zz)
        return remote(
            spot(block(f, g), c), spot(block(f, g), c), one_send.at[zz], one_recv.at[zz], first_peer
        )

    def two_copy(zz, j):
        f, g, _, second_peer, block = order(zz)
        k = block(f if j == 0 else 1 - f, g)
        return remote(spot(k, c), spot(k, c), two_send.at[zz, j], two_recv.at[zz, j], second_peer)

    pass_along(z, lambda copy: copy.start())
    sib_copy(own).start()
    one_copy(z).start()

    emb_copy.wait()
    rest_copy.wait()
    full_cuts = rows // 128

    def target_rows(k):
        ypart, xpart, zpart = k // 8, lax.rem(k // 4, 2), lax.rem(k, 4)
        target = marks[ypart, xpart, zpart, 0:1, :].astype(jnp.int32) - base
        return jnp.where(target < valid, target, -1)

    def row_numbers(j):
        return lax.broadcasted_iota(jnp.int32, (cut, pair), 0) + j * cut

    def cut_rows(j):
        return pl.ds(pl.multiple_of(j * cut, cut), cut)

    def token_lanes(k):
        return pl.ds(pl.multiple_of(k * pair, pair), pair)

    def forward_block(k):
        target = target_rows(k)
        block = held[token_lanes(k), :]

        def scan_logits(j, carried):
            highest, picked = carried
            value = lax.dot_general(
                emb[cut_rows(j), :], block, (((1,), (1,)), ((), ())), preferred_element_type=jnp.float32
            )
            number = row_numbers(j)
            value = jnp.where(number < valid, value, NEGATIVE)
            logit[cut_rows(j), :] = value
            return (
                jnp.maximum(highest, jnp.max(value, 0, keepdims=True)),
                picked + jnp.sum(jnp.where(number == target, value, 0.0), 0, keepdims=True),
            )

        highest, picked = lax.fori_loop(
            0,
            VOCAB_CUTS,
            scan_logits,
            (jnp.full((1, pair), NEGATIVE, jnp.float32), jnp.zeros((1, pair), jnp.float32)),
        )

        def scan_exp(j, total):
            value = jnp.exp(logit[cut_rows(j), :] - highest)
            expo[cut_rows(j), token_lanes(k)] = value.astype(BFLOAT)
            return total + jnp.sum(value, 0, keepdims=True)

        total = lax.fori_loop(0, VOCAB_CUTS, scan_exp, jnp.zeros((1, pair), jnp.float32))
        mine[0, 0, pl.ds(k, 1), :] = highest
        mine[0, 1, pl.ds(k, 1), :] = total
        mine[0, 2, pl.ds(k, 1), :] = picked

    def listed(values, index):
        out = values[0]
        for n in range(1, len(values)):
            out = jnp.where(index == n, values[n], out)
        return out

    def step_block(s):
        phase = listed(ARRIVAL_PHASES, s)
        t = listed(ARRIVAL_TURNS, s)
        zz = listed([listed(row, z) for row in NEAREST], t)
        f, g, _, _, block = order(zz)
        k = listed((block(f, g), block(1 - f, g), block(f, 1 - g), block(1 - f, 1 - g)), phase)
        return phase, zz, k

    @pl.loop(0, 17)
    def _(s):
        phase, zz, k = step_block(s)

        @pl.when(s < full_cuts)
        def _():
            here = pl.ds(pl.multiple_of(s * 128, 128), 128)
            emb_t[:, here] = emb[here, :].T

        if rows % 128:
            @pl.when(s == full_cuts)
            def _():
                emb_t[:, full_cuts * 128 :] = emb[full_cuts * 128 :, :].T

        @pl.when((s > 0) & (s < 16) & (phase == 0))
        def _():
            up_copy(zz).wait_recv()
            pass_along(zz, lambda copy: copy.start())
            sib_copy(k).start()
            one_copy(zz).start()

        @pl.when((s < 16) & (phase == 1))
        def _():
            one_copy(zz).wait_recv()
            sib_copy(k).start()
            for j in range(2):
                two_copy(zz, j).start()

        for j in range(2):
            @pl.when((s < 16) & (phase == 2 + j))
            def _():
                two_copy(zz, j).wait_recv()
                sib_copy(k).start()

        @pl.when(s > 0)
        def _():
            former = step_block(s - 1)[2]
            sib_copy(former).wait_recv()
            forward_block(former)

    def joined(parts):
        highest = functools.reduce(jnp.maximum, [p[0] for p in parts])
        total = functools.reduce(jnp.add, [p[1] * jnp.exp(p[0] - highest) for p in parts])
        picked = functools.reduce(jnp.add, [p[2] for p in parts])
        return highest, total, picked

    def rows_of(ref, n):
        return ref[n, 0], ref[n, 1], ref[n, 2]

    for n, (peer, side) in enumerate(((sibling, c), (x_peer, x), (y_peer, y))):
        copy = remote(mine.at[n], theirs.at[n], st_send.at[n], st_recv.at[n], peer)
        copy.start()
        copy.wait()
        here, there = rows_of(mine, n), rows_of(theirs, n)
        early = tuple(jnp.where(side == 0, a, b) for a, b in zip(here, there))
        late = tuple(jnp.where(side == 0, b, a) for a, b in zip(here, there))
        for r, value in enumerate(joined((early, late))):
            mine[n + 1, r] = value

    def stat_copy(d):
        other = lax.rem(z + d, 4)
        return remote(mine.at[3], lined.at[z], stz_send.at[d - 1], stz_recv.at[d - 1], at(x, y, other, c))

    for d in (1, 2, 3):
        stat_copy(d).start()
    for r in range(3):
        lined[z, r] = mine[3, r]
    for d in (1, 2, 3):
        stat_copy(d).wait()
    highest, total, picked = joined([rows_of(lined, n) for n in range(4)])
    logsum = highest + jnp.log(total)
    log_probs = picked - logsum
    for k in range(16):
        prior[k : k + 1, :] = marks[k // 8, (k // 4) % 2, k % 4, 1:2, :]
        usable[k : k + 1, :] = marks[k // 8, (k // 4) % 2, k % 4, 2:3, :]
    lane = lax.broadcasted_iota(jnp.int32, (16, pair), 1) // length
    mean = jnp.zeros((16, pair), jnp.float32)
    for n in range(pair // length):
        inside = lane == n
        slot_sum = jnp.sum(jnp.where(inside, log_probs, 0.0), 1, keepdims=True)
        mean = jnp.where(inside, slot_sum * (1.0 / length), mean)
    scores = prior[...] + mean
    counted = usable[...] > 0.5
    masked = jnp.where(counted, scores, NEGATIVE)
    question = lax.broadcasted_iota(jnp.int32, (16, pair), 0) // 4
    marginal = jnp.zeros((16, pair), jnp.float32)
    loss = jnp.zeros((1, 1), jnp.float32)
    for n in range(4):
        inside = question == n
        high = jnp.max(
            jnp.max(jnp.where(inside, masked, NEGATIVE), 1, keepdims=True), 0, keepdims=True
        )
        terms = jnp.where(inside & counted, jnp.exp(masked - high), 0.0)
        mass = jnp.sum(jnp.sum(terms, 1, keepdims=True), 0, keepdims=True) * (1.0 / length)
        value = high + jnp.log(mass)
        marginal = jnp.where(inside, value, marginal)
        loss = loss + value
    posterior = jnp.where(counted, jnp.exp(scores - marginal), 0.0)
    token_weight = -float(slots) * posterior
    weight[...] = posterior
    scaled[...] = token_weight * jnp.exp(mine[0, 0] - logsum)
    picked_grad[...] = token_weight * (1.0 - jnp.exp(log_probs))
    small_out[...] = jnp.broadcast_to(loss * (-1.0 / 4), small_out.shape)
    own_row = weight[pl.ds(own, 1), :]
    own_row = jnp.where(c == 0, own_row[:, :size], own_row[:, size:])
    small_out[1:2, :] = own_row * (-float(slots * length))

    def backward_block(k):
        target = target_rows(k)
        hit = picked_grad[pl.ds(k, 1), :]
        scale = scaled[pl.ds(k, 1), :]

        def make(j, carried):
            value = expo[cut_rows(j), token_lanes(k)].astype(jnp.float32)
            grad = jnp.where(row_numbers(j) == target, hit, -(value * scale))
            expo[cut_rows(j), token_lanes(k)] = grad.astype(BFLOAT)
            return carried

        lax.fori_loop(0, VOCAB_CUTS, make, 0)

        def to_rows(n, carried):
            cut_width = pl.ds(pl.multiple_of(n * 256, 256), 256)
            value = lax.dot_general(
                emb_t[cut_width, :],
                expo[:, token_lanes(k)],
                (((1,), (0,)), ((), ())),
                preferred_element_type=jnp.float32,
            ).astype(BFLOAT)
            part[k, 0, cut_width, :] = value[:, :size]
            part[k, 1, cut_width, :] = value[:, size:]
            return carried

        lax.fori_loop(0, width // 256, to_rows, 0)

    def dd_copy(k):
        return remote(part.at[k, 1 - c], sib_part.at[k], dd_send.at[k], dd_recv.at[k], sibling)

    def r1_copy(zz, j):
        f, _, first_peer, _, block = order(zz)
        return remote(
            sib_part.at[block(1 - f, j)], part_one.at[zz, j], r1_send.at[zz, j], r1_recv.at[zz, j],
            first_peer,
        )

    def r2_copy(zz):
        _, g, _, second_peer, _ = order(zz)
        return remote(part_one.at[zz, 1 - g], part_two.at[zz], r2_send.at[zz], r2_recv.at[zz], second_peer)

    def rz_copy(zz):
        return remote(part_two.at[zz], part_z.at[z], rz_send.at[zz], rz_recv.at[z], at(x, y, zz, c))

    def rz_arrival(zz):
        return remote(part_two.at[zz], part_z.at[zz], rz_send.at[zz], rz_recv.at[zz], at(x, y, zz, c))

    step = 128

    def add_into(target_ref, other_ref):
        @pl.loop(0, width // step)
        def _(n):
            rows_here = pl.ds(pl.multiple_of(n * step, step), step)
            target_ref[rows_here, :] = (
                target_ref[rows_here, :].astype(jnp.float32) + other_ref[rows_here, :].astype(jnp.float32)
            ).astype(BFLOAT)

    def group(n):
        return lax.rem(n, 2) * 2 + n // 2

    def chunk(q):
        j, n = q // 4, lax.rem(q, 4)
        columns = pl.ds(pl.multiple_of(n * 256, 256), 256)
        gemb_out[cut_rows(j), columns] = lax.dot_general(
            expo[cut_rows(j), :],
            held[:, columns],
            (((1,), (0,)), ((), ())),
            preferred_element_type=jnp.float32,
        ).astype(BFLOAT)

    def grad_block(s):
        leaves = s < 8
        zz = group(lax.rem(s, 8) // 2)
        j = lax.rem(s, 2)
        f, _, _, _, block = order(zz)
        return leaves, zz, j, block(jnp.where(leaves, 1 - f, f), j)

    @pl.loop(0, 28)
    def _(s):
        @pl.when((s >= 2) & (s < 18))
        def _():
            leaves, zz, turn, k = grad_block(s - 2)
            dd_copy(k).wait_recv()
            add_into(sib_part.at[k], part.at[k, c])
            for j in range(2):
                @pl.when(leaves & (turn == j))
                def _():
                    r1_copy(zz, j).start()

        @pl.when((lax.rem(s, 2) == 1) & (s >= 11) & (s < 18))
        def _():
            zz = group((s - 11) // 2)
            f, _, _, _, block = order(zz)
            for j in range(2):
                r1_copy(zz, j).wait_recv()
                add_into(part_one.at[zz, j], sib_part.at[block(f, j)])
            r2_copy(zz).start()

        @pl.when((lax.rem(s, 2) == 0) & (s >= 16) & (s < 24))
        def _():
            zz = group((s - 16) // 2)
            _, g, _, _, _ = order(zz)
            r2_copy(zz).wait_recv()
            add_into(part_two.at[zz], part_one.at[zz, g])

            @pl.when(zz != z)
            def _():
                rz_copy(zz).start()

        @pl.when(s < 16)
        def _():
            k = grad_block(s)[3]
            backward_block(k)
            dd_copy(k).start()

        @pl.when(s >= 16)
        def _():
            chunk(s - 16)

    for d in (1, 2, 3):
        rz_arrival(lax.rem(z + d, 4)).wait_recv()

    @pl.loop(0, width // step)
    def _(n):
        rows_here = pl.ds(pl.multiple_of(n * step, step), step)
        value = part_two[z, rows_here, :].astype(jnp.float32)
        for d in (1, 2, 3):
            value = value + part_z[lax.rem(z + d, 4), rows_here, :].astype(jnp.float32)
        third_out[rows_here, :] = value

    for d in (1, 2, 3):
        rz_copy(lax.rem(z + d, 4)).wait_send()

    @pl.loop(0, 4)
    def _(zz):
        pass_along(zz, lambda copy: copy.wait_send())
        one_copy(zz).wait_send()
        for j in range(2):
            two_copy(zz, j).wait_send()
            r1_copy(zz, j).wait_send()
        r2_copy(zz).wait_send()

    @pl.loop(0, 16)
    def _(k):
        sib_copy(k).wait_send()
        dd_copy(k).wait_send()


def vocabulary_head(third_low, marks, embedding, slots, length):
    size, width = third_low.shape
    vocab_here = embedding.shape[0]
    rows = 16 * VOCAB_CUTS * -(-vocab_here // (4 * 16 * VOCAB_CUTS))
    dma = pltpu.SemaphoreType.DMA
    vmem = pl.BlockSpec(memory_space=pltpu.VMEM)
    stat = (3, 16, 2 * size)
    f32 = jnp.float32
    block = (width, size)
    small, gemb, third = pl.pallas_call(
        functools.partial(head_kernel, slots, length, vocab_here),
        out_shape=(
            jax.ShapeDtypeStruct((8, size), f32),
            jax.ShapeDtypeStruct((rows, width), BFLOAT),
            jax.ShapeDtypeStruct((width, size), f32),
        ),
        in_specs=[vmem, vmem, pl.BlockSpec(memory_space=pl.ANY)],
        out_specs=(vmem,) * 3,
        scratch_shapes=[
            pltpu.VMEM((rows, width), BFLOAT),
            pltpu.VMEM((width, rows), BFLOAT),
            pltpu.VMEM((32 * size, width), BFLOAT),
            pltpu.VMEM((rows, 2 * size), f32),
            pltpu.VMEM((rows, 32 * size), BFLOAT),
            pltpu.VMEM((16, 2) + block, BFLOAT),
            pltpu.VMEM((16,) + block, BFLOAT),
            pltpu.VMEM((4, 2) + block, BFLOAT),
            pltpu.VMEM((4,) + block, BFLOAT),
            pltpu.VMEM((4,) + block, BFLOAT),
            pltpu.VMEM((4,) + stat, f32),
            pltpu.VMEM((3,) + stat, f32),
            pltpu.VMEM((4,) + stat, f32),
        ]
        + [pltpu.VMEM((16, 2 * size), f32)] * 5
        + [dma((4,))]
        + [dma((2, 4)), dma((4,))]
        + [dma((4,))] * 2
        + [dma((4, 2))] * 2
        + [dma((16,))] * 2
        + [dma((3,))] * 4
        + [dma((16,))] * 2
        + [dma((4, 2))] * 2
        + [dma((4,))] * 4,
        compiler_params=pltpu.CompilerParams(
            collective_id=2, has_side_effects=True, vmem_limit_bytes=60 * 2**20
        ),
        name="vocabulary_head",
    )(third_low, marks, embedding)
    return small, gemb, third


def merged(part, axis, combine):
    gathered = jax.tree.map(lambda a: lax.all_gather(a, axis), part)

    def take(source):
        return jax.tree.map(lambda a: lax.dynamic_index_in_dim(a, source, 0, False), gathered)

    return lax.fori_loop(
        1, lax.axis_size(axis), lambda source, state: combine(state, take(source)), take(0)
    )


def matmul(matrix_left, matrix_right):
    return lax.dot_general(
        matrix_left,
        matrix_right,
        (((matrix_left.ndim - 1,), (0,)), ((), ())),
        preferred_element_type=jnp.float32,
    )


def matmul_back(matrix_left, matrix_right):
    return lax.dot_general(
        matrix_left,
        matrix_right,
        (((matrix_left.ndim - 1,), (1,)), ((), ())),
        preferred_element_type=jnp.float32,
    )


def outer_sum(matrix_left, matrix_right):
    flat_left = matrix_left.reshape(-1, matrix_left.shape[-1])
    flat_right = matrix_right.reshape(-1, matrix_right.shape[-1])
    return lax.dot_general(
        flat_left, flat_right, (((0,), (0,)), ((), ())), preferred_element_type=jnp.float32
    )


def split_heads(values):
    return values.reshape(values.shape[0], values.shape[1], HEADS, HEAD_DIM)


def join_heads(values):
    return values.reshape(values.shape[0], values.shape[1], HEADS * HEAD_DIM)


def exact_gelu(values):
    return jax.nn.gelu(values, approximate=False)


def norm_forward(values, gain_row, shift_row):
    centre = values - jnp.mean(values, -1, keepdims=True)
    inverse = lax.rsqrt(jnp.mean(centre * centre, -1, keepdims=True) + EPSILON)
    normed = centre * inverse
    return (normed * gain_row.astype(jnp.float32) + shift_row.astype(jnp.float32), normed, inverse)


def norm_backward(upstream, normed, inverse, gain_row):
    scaled = upstream * gain_row.astype(jnp.float32)
    mean_scaled = jnp.mean(scaled, -1, keepdims=True)
    along_normed = jnp.mean(scaled * normed, -1, keepdims=True)
    grad_values = inverse * (scaled - mean_scaled - normed * along_normed)
    model_width = upstream.shape[-1]
    grad_gain = jnp.sum((upstream * normed).reshape(-1, model_width), 0)
    grad_shift = jnp.sum(upstream.reshape(-1, model_width), 0)
    return (grad_values, grad_gain, grad_shift)


def score_block(queries, key_rows, causal):
    scores = jnp.einsum(
        "nqhd,nkhd->nhqk", queries, key_rows, preferred_element_type=jnp.float32
    ) * (1.0 / math.sqrt(HEAD_DIM))
    if causal:
        length = queries.shape[1]
        allowed = lax.broadcasted_iota(jnp.int32, (length, length), 0) >= lax.broadcasted_iota(
            jnp.int32, (length, length), 1
        )
        scores = jnp.where(allowed, scores, NEGATIVE)
    return scores


def attend(queries, key_rows, values, causal):
    scores = score_block(queries, key_rows, causal)
    highest = jnp.max(scores, -1, keepdims=True)
    totals = jnp.sum(jnp.exp(scores - highest), -1, keepdims=True)
    logsum = highest + jnp.log(totals)
    probs_low = jnp.exp(scores - logsum).astype(BFLOAT)
    context = jnp.einsum(
        "nhqk,nkhd->nqhd", probs_low, values, preferred_element_type=jnp.float32
    ).astype(BFLOAT)
    return (join_heads(context), logsum)


def attend_back(grad_context, queries, key_rows, values, logsum, causal):
    score_scale = 1.0 / math.sqrt(HEAD_DIM)
    probs_full = jnp.exp(score_block(queries, key_rows, causal) - logsum)
    grad_heads = split_heads(grad_context)
    grad_probs = jnp.einsum(
        "nqhd,nkhd->nhqk", grad_heads, values, preferred_element_type=jnp.float32
    )
    grad_values = jnp.einsum(
        "nhqk,nqhd->nkhd", probs_full.astype(BFLOAT), grad_heads, preferred_element_type=jnp.float32
    ).astype(BFLOAT)
    grad_scores = (
        probs_full * (grad_probs - jnp.sum(probs_full * grad_probs, -1, keepdims=True))
    ).astype(BFLOAT)
    grad_queries = (
        jnp.einsum("nhqk,nkhd->nqhd", grad_scores, key_rows, preferred_element_type=jnp.float32)
        * score_scale
    ).astype(BFLOAT)
    grad_keys = (
        jnp.einsum("nhqk,nqhd->nkhd", grad_scores, queries, preferred_element_type=jnp.float32)
        * score_scale
    ).astype(BFLOAT)
    return (join_heads(grad_queries), join_heads(grad_keys), join_heads(grad_values))


def layer_forward(inputs, encoded, weights):
    (
        packed_weight,
        output_weight,
        query_weight,
        memory_weight,
        cross_weight,
        expand_weight,
        reduce_weight,
        gains,
        shifts,
    ) = weights
    model_width = inputs.shape[-1]
    packed = matmul(inputs, packed_weight).astype(BFLOAT)
    context, self_logsum = attend(
        split_heads(packed[..., :model_width]),
        split_heads(packed[..., model_width : 2 * model_width]),
        split_heads(packed[..., 2 * model_width :]),
        True,
    )
    first_norm, first_normed, first_inverse = norm_forward(
        inputs.astype(jnp.float32) + matmul(context, output_weight), gains[0], shifts[0]
    )
    first_low = first_norm.astype(BFLOAT)
    cross_queries = matmul(first_low, query_weight).astype(BFLOAT)
    memory_pairs = matmul(encoded, memory_weight).astype(BFLOAT)
    cross_context, cross_logsum = attend(
        split_heads(cross_queries),
        split_heads(memory_pairs[..., :model_width]),
        split_heads(memory_pairs[..., model_width:]),
        False,
    )
    second, second_normed, second_inverse = norm_forward(
        first_norm + matmul(cross_context, cross_weight), gains[1], shifts[1]
    )
    second_low = second.astype(BFLOAT)
    inner_pre = matmul(second_low, expand_weight)
    active = exact_gelu(inner_pre).astype(BFLOAT)
    third_norm, third_normed, third_inverse = norm_forward(
        second + matmul(active, reduce_weight), gains[2], shifts[2]
    )
    stored = (
        packed,
        context,
        self_logsum,
        first_normed,
        first_inverse,
        first_low,
        cross_queries,
        memory_pairs,
        cross_context,
        cross_logsum,
        second_normed,
        second_inverse,
        second_low,
        inner_pre,
        active,
        third_normed,
        third_inverse,
    )
    return (third_norm.astype(BFLOAT), stored)


def layer_backward(grad_third, inputs, encoded, weights, stored):
    (
        packed_weight,
        output_weight,
        query_weight,
        memory_weight,
        cross_weight,
        expand_weight,
        reduce_weight,
        gains,
        shifts,
    ) = weights
    (
        packed,
        context,
        self_logsum,
        first_normed,
        first_inverse,
        first_low,
        cross_queries,
        memory_pairs,
        cross_context,
        cross_logsum,
        second_normed,
        second_inverse,
        second_low,
        inner_pre,
        active,
        third_normed,
        third_inverse,
    ) = stored
    model_width = inputs.shape[-1]
    grad_res3, gain_three, shift_three = norm_backward(
        grad_third, third_normed, third_inverse, gains[2]
    )
    grad_output = grad_res3.astype(BFLOAT)
    grad_reduce = outer_sum(active, grad_output)
    grad_active = matmul_back(grad_output, reduce_weight)
    _, gelu_pull = jax.vjp(exact_gelu, inner_pre)
    grad_inner = gelu_pull(grad_active)[0].astype(BFLOAT)
    grad_expand = outer_sum(second_low, grad_inner)
    grad_second = grad_res3 + matmul_back(grad_inner, expand_weight)
    grad_res2, gain_two, shift_two = norm_backward(
        grad_second, second_normed, second_inverse, gains[1]
    )
    grad_mixed = grad_res2.astype(BFLOAT)
    grad_cross_weight = outer_sum(cross_context, grad_mixed)
    grad_cross_context = matmul_back(grad_mixed, cross_weight).astype(BFLOAT)
    grad_cross_queries, grad_memory_keys, grad_memory_values = attend_back(
        grad_cross_context,
        split_heads(cross_queries),
        split_heads(memory_pairs[..., :model_width]),
        split_heads(memory_pairs[..., model_width:]),
        cross_logsum,
        False,
    )
    grad_query_weight = outer_sum(first_low, grad_cross_queries)
    grad_first = grad_res2 + matmul_back(grad_cross_queries, query_weight)
    grad_pairs = jnp.concatenate([grad_memory_keys, grad_memory_values], -1)
    grad_memory_weight = outer_sum(encoded, grad_pairs)
    grad_encoded = matmul_back(grad_pairs, memory_weight)
    grad_res1, gain_one, shift_one = norm_backward(
        grad_first, first_normed, first_inverse, gains[0]
    )
    grad_merged = grad_res1.astype(BFLOAT)
    grad_output_weight = outer_sum(context, grad_merged)
    grad_context = matmul_back(grad_merged, output_weight).astype(BFLOAT)
    grad_queries, grad_keys, grad_values = attend_back(
        grad_context,
        split_heads(packed[..., :model_width]),
        split_heads(packed[..., model_width : 2 * model_width]),
        split_heads(packed[..., 2 * model_width :]),
        self_logsum,
        True,
    )
    grad_packed = jnp.concatenate([grad_queries, grad_keys, grad_values], -1)
    grad_packed_weight = outer_sum(inputs, grad_packed)
    grad_inputs = grad_res1 + matmul_back(grad_packed, packed_weight)
    grad_gains = jnp.stack([gain_one, gain_two, gain_three])
    grad_shifts = jnp.stack([shift_one, shift_two, shift_three])
    return (
        grad_inputs,
        grad_encoded,
        (
            grad_packed_weight,
            grad_output_weight,
            grad_query_weight,
            grad_memory_weight,
            grad_cross_weight,
            grad_expand,
            grad_reduce,
            grad_gains,
            grad_shifts,
        ),
    )


def combine_scores(former, latter):
    highest = jnp.maximum(former[0], latter[0])
    totals = former[1] * jnp.exp(former[0] - highest) + latter[1] * jnp.exp(latter[0] - highest)
    return (highest, totals, former[2] + latter[2])


def combine_pairs(former, latter):
    highest = jnp.maximum(former[0], latter[0])
    totals = former[1] * jnp.exp(former[0] - highest) + latter[1] * jnp.exp(latter[0] - highest)
    return (highest, totals)


def per_device(
    decoder_states,
    encoder_memory,
    target_tokens,
    log_prior,
    slot_counts,
    slot_mask,
    self_packed,
    self_output,
    cross_query,
    cross_memory,
    cross_output,
    feed_expand,
    feed_reduce,
    embedding,
    norm_gains,
    norm_shifts,
):
    weights = (
        lax.all_gather(self_packed, "pa", axis=0, tiled=True),
        lax.all_gather(self_output, "pa", axis=0, tiled=True),
        lax.all_gather(cross_query, "pa", axis=0, tiled=True),
        lax.all_gather(cross_memory, "pa", axis=0, tiled=True),
        lax.all_gather(cross_output, "pa", axis=0, tiled=True),
        lax.all_gather(feed_expand, "pa", axis=0, tiled=True),
        lax.all_gather(feed_reduce, "pa", axis=0, tiled=True),
        lax.all_gather(norm_gains, "pa", axis=1, tiled=True),
        lax.all_gather(norm_shifts, "pa", axis=1, tiled=True),
    )
    questions, slots_here, length, model_width = decoder_states.shape
    mem_length = encoder_memory.shape[2]
    batch_size = questions * slots_here
    inputs = decoder_states.reshape(batch_size, length, model_width)
    encoded = encoder_memory.reshape(batch_size, mem_length, model_width)
    third_low, stored = layer_forward(inputs, encoded, weights)
    tokens_here = batch_size * length
    rows_all, tokens_all = (
        lax.all_gather(third_low.reshape(tokens_here, model_width), "pa", axis=0, tiled=True),
        lax.all_gather(target_tokens.reshape(tokens_here), "pa", axis=0, tiled=True),
    )
    total_rows = rows_all.shape[0]
    block_rows = min(total_rows, 2048)
    block_count = total_rows // block_rows
    vocab_start = lax.axis_index("pa") * embedding.shape[0]
    row_blocks = rows_all.reshape(block_count, block_rows, model_width)
    token_blocks = tokens_all.reshape(block_count, block_rows)

    def vocab_logits(hidden_rows, token_rows):
        logits = matmul_back(hidden_rows, embedding)
        column = lax.broadcasted_iota(jnp.int32, logits.shape, 1) + vocab_start
        return (logits, column == token_rows[:, None])

    def vocab_partial(pieces):
        logits, chosen = vocab_logits(pieces[0], pieces[1])
        highest = jnp.max(logits, -1)
        totals = jnp.sum(jnp.exp(logits - highest[:, None]), -1)
        picked = jnp.sum(jnp.where(chosen, logits, 0.0), -1)
        return (highest, totals, picked)

    highest, totals, picked = lax.map(vocab_partial, (row_blocks, token_blocks))
    highest, totals, picked = merged(
        (highest.reshape(total_rows), totals.reshape(total_rows), picked.reshape(total_rows)),
        "pa",
        combine_scores,
    )
    row_logsum = highest + jnp.log(totals)
    own_start = lax.axis_index("pa") * tokens_here
    own_logsum = lax.dynamic_slice_in_dim(row_logsum, own_start, tokens_here)
    own_picked = lax.dynamic_slice_in_dim(picked, own_start, tokens_here)
    log_probs = (own_picked - own_logsum).reshape(questions, slots_here, length)
    scores = log_prior + jnp.mean(log_probs, -1)
    slot_index = lax.axis_index("pa") * slots_here + lax.broadcasted_iota(
        jnp.int32, (questions, slots_here), 1
    )
    usable = (slot_mask == 1) & (slot_index < slot_counts[:, None])
    masked = jnp.where(usable, scores, NEGATIVE)
    local_high = jnp.max(masked, -1)
    local_total = jnp.sum(jnp.where(usable, jnp.exp(masked - local_high[:, None]), 0.0), -1)
    slot_high, slot_total = merged((local_high, local_total), "pa", combine_pairs)
    marginal = slot_high + jnp.log(slot_total)
    posterior = jnp.where(usable, jnp.exp(scores - marginal[:, None]), 0.0)
    loss_value = -lax.psum(jnp.sum(marginal), "pb") / (questions * lax.axis_size("pb"))
    slot_number = slots_here * lax.axis_size("pa")
    grad_prior = -(slot_number * length) * posterior
    token_grad = jnp.broadcast_to(
        (-slot_number * posterior)[:, :, None], (questions, slots_here, length)
    ).reshape(tokens_here)
    weights_all = lax.all_gather(token_grad, "pa", axis=0, tiled=True)

    def vocab_grads(accumulated, pieces):
        hidden_rows, token_rows, logsum_rows, weight_rows = pieces
        logits, chosen = vocab_logits(hidden_rows, token_rows)
        softmax_rows = jnp.exp(logits - logsum_rows[:, None])
        grad_logits = (weight_rows[:, None] * (jnp.where(chosen, 1.0, 0.0) - softmax_rows)).astype(
            BFLOAT
        )
        return (accumulated + outer_sum(grad_logits, hidden_rows), matmul(grad_logits, embedding))

    grad_embed, grad_rows = lax.scan(
        vocab_grads,
        jnp.zeros(embedding.shape, jnp.float32),
        (
            row_blocks,
            token_blocks,
            row_logsum.reshape(block_count, block_rows),
            weights_all.reshape(block_count, block_rows),
        ),
    )
    grad_third = lax.psum_scatter(
        grad_rows.reshape(total_rows, model_width).astype(BFLOAT),
        "pa",
        scatter_dimension=0,
        tiled=True,
    ).astype(jnp.float32).reshape(batch_size, length, model_width)
    grad_inputs, grad_encoded, grads = layer_backward(grad_third, inputs, encoded, weights, stored)
    shares = (
        lax.psum_scatter(grads[0].astype(BFLOAT), "pa", scatter_dimension=0, tiled=True),
        lax.psum_scatter(grads[1].astype(BFLOAT), "pa", scatter_dimension=0, tiled=True),
        lax.psum_scatter(grads[2].astype(BFLOAT), "pa", scatter_dimension=0, tiled=True),
        lax.psum_scatter(grads[3].astype(BFLOAT), "pa", scatter_dimension=0, tiled=True),
        lax.psum_scatter(grads[4].astype(BFLOAT), "pa", scatter_dimension=0, tiled=True),
        lax.psum_scatter(grads[5].astype(BFLOAT), "pa", scatter_dimension=0, tiled=True),
        lax.psum_scatter(grads[6].astype(BFLOAT), "pa", scatter_dimension=0, tiled=True),
        lax.psum_scatter(grads[7], "pa", scatter_dimension=1, tiled=True),
        lax.psum_scatter(grads[8], "pa", scatter_dimension=1, tiled=True),
    )
    outputs = lax.psum(
        (
            shares[0],
            shares[1],
            shares[2],
            shares[3],
            shares[4],
            shares[5],
            shares[6],
            shares[7],
            shares[8],
            grad_embed.astype(BFLOAT),
        ),
        "pb",
    )
    outputs = tuple(part.astype(jnp.float32) for part in outputs)
    return (
        loss_value,
        grad_inputs.reshape(decoder_states.shape),
        grad_encoded.reshape(encoder_memory.shape),
        grad_prior,
        outputs[0],
        outputs[1],
        outputs[2],
        outputs[3],
        outputs[4],
        outputs[5],
        outputs[6],
        outputs[9],
        outputs[7],
        outputs[8],
    )


def per_device_kernels(
    decoder_states,
    encoder_memory,
    target_tokens,
    log_prior,
    slot_counts,
    slot_mask,
    self_packed,
    self_output,
    cross_query,
    cross_memory,
    cross_output,
    feed_expand,
    feed_reduce,
    embedding,
    norm_gains,
    norm_shifts,
):
    shards = (
        self_packed,
        self_output,
        cross_query,
        cross_memory,
        cross_output,
        feed_expand,
        feed_reduce,
    )
    norm_rows = jnp.concatenate(
        [norm_gains, norm_shifts, jnp.zeros((2, norm_gains.shape[1]), BFLOAT)]
    ).astype(jnp.float32)
    _, slots_here, length, model_width = decoder_states.shape
    slots = slots_here * lax.axis_size("pa")
    states = decoder_states.reshape(slots_here * length, model_width)
    memory = encoder_memory.reshape(-1, model_width)
    slot_index = lax.axis_index("pa") * slots_here + jnp.arange(slots_here)
    usable = (slot_mask[0] == 1) & (slot_index < slot_counts[0])
    marks = jnp.concatenate(
        [
            target_tokens.reshape(1, slots_here * length).astype(jnp.float32),
            jnp.repeat(log_prior, length, axis=1),
            jnp.repeat(usable[None].astype(jnp.float32), length, axis=1),
            jnp.zeros((5, slots_here * length), jnp.float32),
        ]
    )
    matrices, marks, norms, kept = forward_layer(
        shards, norm_rows, marks, states, memory, length
    )
    small, grad_embed, grad_third = vocabulary_head(
        kept[-1], marks, embedding, slots, length
    )
    loss_value = small[0, 0]
    grad_prior = small[1].reshape(1, slots_here, length)[:, :, 0]
    pieces = lax.all_gather(grad_embed, "pb", axis=0)
    pieces = pieces.reshape(4 * grad_embed.shape[0], model_width)
    grad_embed = pieces[: embedding.shape[0]].astype(jnp.float32)
    shares, norm_sums, grad_inputs, grad_encoded = backward_layer(
        matrices,
        kept[:11] + kept[12:15] + (states, memory),
        kept[11],
        norms,
        grad_third,
        length,
    )
    norm_here = norm_gains.shape[1]
    norm_sums = lax.dynamic_slice_in_dim(
        norm_sums, lax.axis_index("pa") * norm_here, norm_here, axis=1
    )
    return (
        loss_value,
        grad_inputs.reshape(decoder_states.shape),
        grad_encoded.reshape(encoder_memory.shape),
        grad_prior,
    ) + shares + (grad_embed, norm_sums[:3], norm_sums[3:6])


def solution(mesh):
    own_kernels = mesh.shape["pb"] == 4 and mesh.shape["pa"] == 8
    return jax.shard_map(
        per_device_kernels if own_kernels else per_device,
        mesh=mesh,
        in_specs=(
            P("pb", "pa", None, None),
            P("pb", "pa", None, None),
            P("pb", "pa", None),
            P("pb", "pa"),
            P("pb"),
            P("pb", "pa"),
            P("pa", None),
            P("pa", None),
            P("pa", None),
            P("pa", None),
            P("pa", None),
            P("pa", None),
            P("pa", None),
            P("pa", None),
            P(None, "pa"),
            P(None, "pa"),
        ),
        out_specs=(
            P(),
            P("pb", "pa", None, None),
            P("pb", "pa", None, None),
            P("pb", "pa"),
            P("pa", None),
            P("pa", None),
            P("pa", None),
            P("pa", None),
            P("pa", None),
            P("pa", None),
            P("pa", None),
            P("pa", None),
            P(None, "pa"),
            P(None, "pa"),
        ),
        check_vma=False,
    )
```

```python
import functools
import math

import jax
import jax.numpy as jnp
from jax import lax
from jax.experimental import pallas as pl
from jax.experimental.pallas import tpu as pltpu
from jax.sharding import PartitionSpec as P

HEADS = 16
HEAD_DIM = 64


EPSILON = 1e-05
NEGATIVE = -1e30
BFLOAT = jnp.bfloat16
MESH = pl.DeviceIdType.MESH
TILE = 1024
ROWS = 128
WEIGHT_UNITS = (3, 1, 1, 2, 1, 4, 4)
UNITS = tuple((w, k) for w, n in enumerate(WEIGHT_UNITS) for k in range(n))
REDUCE_WEIGHT = 6


def whereami():
    pb = lax.axis_index("pb")
    pa = lax.axis_index("pa")
    return lax.rem(pb, 2), pb // 2, pa // 2, lax.rem(pa, 2)


def greet(peers):
    barrier = pltpu.get_barrier_semaphore()
    for peer in peers:
        pl.semaphore_signal(barrier, inc=1, device_id=peer, device_id_type=MESH)
    pl.semaphore_wait(barrier, len(peers))


def at(x, y, z, c):
    return (y * 2 + x, z * 2 + c)


def neighbours(x, y, z, c):
    return [at(1 - x, y, z, c), at(x, 1 - y, z, c), at(x, y, z, 1 - c)] + [
        at(x, y, lax.rem(z + d, 4), c) for d in (1, 2, 3)
    ]


def shard_view(ref, unit, start, size):
    weight, block = unit
    if weight == REDUCE_WEIGHT:
        return ref.at[pl.ds(block * ROWS + start, size), :]
    return ref.at[pl.ds(start, size), pl.ds(block * TILE, TILE)]


def full_view(ref, unit, place, core, start, size):
    weight, block = unit
    if weight == REDUCE_WEIGHT:
        return ref.at[place, core, block, pl.ds(start, size), :]
    return ref.at[place, core, pl.ds(start, size), pl.ds(block * TILE, TILE)]


Z_FULL = (9, 14)


HOP_LAG = 1
LAG_TWO, LAG_SIBLING, LAG_LOAD, LAG_USE = 3, 6, 8, 9
SLOTS_IN_FLIGHT = 3


def dot_nn(left, right):
    return lax.dot_general(left, right, (((1,), (0,)), ((), ())), preferred_element_type=jnp.float32)


def dot_nt(left, right):
    return lax.dot_general(left, right, (((1,), (1,)), ((), ())), preferred_element_type=jnp.float32)


def dot_tn(left, right):
    return lax.dot_general(left, right, (((0,), (0,)), ((), ())), preferred_element_type=jnp.float32)


def stack_heads(pair):
    lane = lax.broadcasted_iota(jnp.int32, pair.shape, 1)
    zero = jnp.zeros_like(pair)
    return jnp.concatenate(
        [jnp.where(lane < HEAD_DIM, pair, zero), jnp.where(lane < HEAD_DIM, zero, pair)], 0
    )


def unstack_heads(stacked):
    rows = stacked.shape[0] // 2
    lane = lax.broadcasted_iota(jnp.int32, (rows, stacked.shape[1]), 1)
    return jnp.where(lane < HEAD_DIM, stacked[:rows], stacked[rows:])


def pair_scores(queries, keys, causal):
    scores = dot_nt(queries, keys) * (1.0 / math.sqrt(HEAD_DIM))
    if causal:
        length = keys.shape[0]
        row = lax.rem(lax.broadcasted_iota(jnp.int32, scores.shape, 0), length)
        column = lax.broadcasted_iota(jnp.int32, scores.shape, 1)
        scores = jnp.where(row >= column, scores, NEGATIVE)
    highest = jnp.max(scores, -1, keepdims=True)
    total = jnp.sum(jnp.exp(scores - highest), -1, keepdims=True)
    return jnp.exp(scores - (highest + jnp.log(total)))


def attend_pair(queries, keys, values, causal):
    probs = pair_scores(stack_heads(queries), keys, causal).astype(BFLOAT)
    return unstack_heads(dot_nn(probs, values)).astype(BFLOAT)


def normalise(values, gain, shift):
    centre = values - jnp.mean(values, -1, keepdims=True)
    inverse = lax.rsqrt(jnp.mean(centre * centre, -1, keepdims=True) + EPSILON)
    normed = centre * inverse
    return normed * gain + shift, normed, inverse


def forward_kernel(length, mem_length, *refs):
    shards, norm, aux, states_hbm, encoded_hbm = refs[:7], refs[7], refs[8], refs[9], refs[10]
    fulls, marks, kept_hbm = refs[11:18], refs[18], refs[19:36]
    (
        norm_full, packed, context, first_normed, first_inverse, first_low, cross_queries, pairs,
        cross_context, second_normed, second_inverse, second_low, inner, active, third_normed,
        third_inverse, third_low,
    ) = refs[36:53]
    wbuf, residual, states, encoded = refs[53:57]
    (
        local_sem, z_send, z_recv, one_send, one_recv, two_send, two_recv, d_send, d_recv,
        norm_sem, nz_send, nz_recv, nd_send, nd_recv, load_sem, ax_sem, ax_send, ax_recv,
        axz_send, axz_recv, kept_sem, input_sem,
    ) = refs[57:]
    x, y, z, c = whereami()
    greet(neighbours(x, y, z, c))
    every = slice(None)
    tokens, width = states_hbm.shape
    slots_here = tokens // length

    def copies(u):
        unit = UNITS[u]
        shard, full = shards[unit[0]], fulls[unit[0]]
        wide = u in Z_FULL
        a, b = (x, y) if u % 2 == 0 else (y, x)
        first_peer = at(x, 1 - y, z, c) if u % 2 == 0 else at(1 - x, y, z, c)
        second_peer = at(1 - x, y, z, c) if u % 2 == 0 else at(x, 1 - y, z, c)
        quarter = pl.multiple_of(64 * a + 32 * b, 32)
        half = pl.multiple_of(64 * a, 64)
        rows = (0, ROWS) if wide else (quarter, 32)
        local = pltpu.make_async_copy(
            shard_view(shard, unit, *rows), full_view(full, unit, z, c, *rows), local_sem.at[u]
        )
        def along(origin, direction):
            block = full_view(full, unit, origin, c, *rows)
            return pltpu.make_async_remote_copy(
                src_ref=block,
                dst_ref=block,
                send_sem=z_send.at[u, (direction + 1) // 2, origin],
                recv_sem=z_recv.at[u, origin],
                device_id=at(x, y, z + direction, c),
                device_id_type=MESH,
            )

        def cross(start, size, sends, recvs, peer):
            part = full_view(full, unit, every, c, start, size)
            return pltpu.make_async_remote_copy(
                src_ref=part,
                dst_ref=part,
                send_sem=sends.at[u],
                recv_sem=recvs.at[u],
                device_id=peer,
                device_id_type=MESH,
            )

        first = None if wide else cross(quarter, 32, one_send, one_recv, first_peer)
        second = None if wide else cross(half, 64, two_send, two_recv, second_peer)
        sibling = cross(0, ROWS, d_send, d_recv, at(x, y, z, 1 - c))
        load = pltpu.make_async_copy(
            full_view(full, unit, every, every, 0, ROWS),
            wbuf.at[u % SLOTS_IN_FLIGHT],
            load_sem.at[u % SLOTS_IN_FLIGHT],
        )
        return local, along, first, second, sibling, load

    def norm_copy(src, dst, send, recv, peer):
        return pltpu.make_async_remote_copy(
            src_ref=src, dst_ref=dst, send_sem=send, recv_sem=recv, device_id=peer, device_id_type=MESH
        )

    norm_local = pltpu.make_async_copy(norm, norm_full.at[z, c], norm_sem)
    norm_along = [
        norm_copy(
            norm, norm_full.at[z, c], nz_send.at[d - 1], nz_recv.at[d - 1], at(x, y, lax.rem(z + d, 4), c)
        )
        for d in (1, 2, 3)
    ]
    norm_sibling = norm_copy(
        norm_full.at[:, c], norm_full.at[:, c], nd_send, nd_recv, at(x, y, z, 1 - c)
    )
    norm_local.start()
    for copy in norm_along:
        copy.start()

    lanes = pl.ds(pl.multiple_of(c * tokens, tokens), tokens)
    aux_local = pltpu.make_async_copy(aux, marks.at[y, x, z, :, lanes], ax_sem)
    aux_local.start()
    aux_steps = [
        norm_copy(part, part, ax_send.at[n], ax_recv.at[n], peer)
        for n, (part, peer) in enumerate(
            (
                (marks.at[y, x, z, :, lanes], at(x, y, z, 1 - c)),
                (marks.at[y, x, z], at(1 - x, y, z, c)),
                (marks.at[y, :, z], at(x, 1 - y, z, c)),
            )
        )
    ]
    aux_along = [
        norm_copy(
            marks.at[:, :, z], marks.at[:, :, z], axz_send.at[d - 1], axz_recv.at[d - 1],
            at(x, y, lax.rem(z + d, 4), c),
        )
        for d in (1, 2, 3)
    ]

    kept = (
        norm_full, packed, context, first_normed, first_inverse, first_low, cross_queries, pairs,
        cross_context, second_normed, second_inverse, second_low, inner, active, third_normed,
        third_inverse, third_low,
    )

    def keep(*numbers):
        for n in numbers:
            pltpu.make_async_copy(kept[n], kept_hbm[n], kept_sem.at[n]).start()

    states_copy = pltpu.make_async_copy(states_hbm, states, input_sem.at[0])
    encoded_copy = pltpu.make_async_copy(encoded_hbm, encoded, input_sem.at[1])
    states_copy.start()
    encoded_copy.start()

    def norm_row(n):
        return jnp.concatenate(
            [norm_full[p // 2, p % 2, n : n + 1, :] for p in range(8)], 1
        )

    def times(left_ref, u, write):
        slot = u % SLOTS_IN_FLIGHT

        @pl.loop(0, 4, unroll=True)
        def _(n):
            columns = pl.ds(pl.multiple_of(n * 256, 256), 256)
            right = wbuf[slot, :, :, :, columns].reshape(TILE, 256)
            write(columns, n, dot_nn(left_ref[...], right))

    def block_columns(k, n):
        return pl.ds(pl.multiple_of(k * TILE + n * 256, 256), 256)

    def attention(queries, keys, key_start, value_start, key_length, out, causal):
        @pl.loop(0, slots_here * (width // 128), unroll=2)
        def _(n):
            slot, group = n // (width // 128), lax.rem(n, width // 128)
            lanes = pl.ds(pl.multiple_of(group * 128, 128), 128)
            key_lanes = pl.ds(pl.multiple_of(key_start + group * 128, 128), 128)
            value_lanes = pl.ds(pl.multiple_of(value_start + group * 128, 128), 128)
            query_rows = pl.ds(pl.multiple_of(slot * length, length), length)
            key_rows = pl.ds(pl.multiple_of(slot * key_length, key_length), key_length)
            out[query_rows, lanes] = attend_pair(
                queries[query_rows, lanes], keys[key_rows, key_lanes], keys[key_rows, value_lanes], causal
            )

    def finish_norm(n, value, normed_ref, inverse_ref, low_ref):
        out, normed, inverse = normalise(value, norm_row(n), norm_row(n + 3))
        normed_ref[...] = normed
        inverse_ref[...] = jnp.broadcast_to(inverse, inverse_ref.shape)
        low_ref[...] = out.astype(BFLOAT)
        return out

    def use(u):
        weight, k = UNITS[u]
        if weight == 0:
            def write(columns, n, value):
                packed[:, block_columns(k, n)] = value.astype(BFLOAT)

            times(states, u, write)
            if k == 2:
                attention(packed, packed, width, 2 * width, length, context, True)
                keep(1, 2)
        elif weight == 1:
            def write(columns, n, value):
                residual[:, columns] = states[:, columns].astype(jnp.float32) + value

            times(context, u, write)
            residual[...] = finish_norm(0, residual[...], first_normed, first_inverse, first_low)
            keep(3, 4, 5)
        elif weight == 2:
            def write(columns, n, value):
                cross_queries[:, columns] = value.astype(BFLOAT)

            times(first_low, u, write)
        elif weight == 3:
            slot = u % SLOTS_IN_FLIGHT

            @pl.loop(0, 8)
            def _(n):
                m, n = n // 4, lax.rem(n, 4)
                columns = pl.ds(pl.multiple_of(n * 256, 256), 256)
                part = encoded.shape[0] // 2
                rows_here = pl.ds(pl.multiple_of(m * part, part), part)
                right = wbuf[slot, :, :, :, columns].reshape(TILE, 256)
                pairs[rows_here, block_columns(k, n)] = dot_nn(encoded[rows_here, :], right).astype(BFLOAT)

            if k == 1:
                attention(cross_queries, pairs, 0, width, mem_length, cross_context, False)
                keep(6, 7, 8)
        elif weight == 4:
            def write(columns, n, value):
                residual[:, columns] = residual[:, columns] + value

            times(cross_context, u, write)
            residual[...] = finish_norm(1, residual[...], second_normed, second_inverse, second_low)
            keep(9, 10, 11)
        elif weight == 5:
            def write(columns, n, value):
                inner[:, block_columns(k, n)] = value
                gate = 0.5 * (1.0 + lax.erf(value * math.sqrt(0.5)))
                active[:, block_columns(k, n)] = (value * gate).astype(BFLOAT)

            times(second_low, u, write)
            if k == 3:
                keep(12, 13)
        else:
            slot = u % SLOTS_IN_FLIGHT
            blocks = active.shape[1] // (8 * ROWS)
            left = jnp.concatenate(
                [active[:, (p * blocks + k) * ROWS : (p * blocks + k + 1) * ROWS] for p in range(8)], 1
            )

            @pl.loop(0, 4, unroll=True)
            def _(n):
                columns = pl.ds(pl.multiple_of(n * 256, 256), 256)
                right = wbuf[slot, :, :, :, columns].reshape(TILE, 256)
                residual[:, columns] = residual[:, columns] + dot_nn(left, right)

            if k == blocks - 1:
                finish_norm(2, residual[...], third_normed, third_inverse, third_low)
                keep(14, 15, 16)

    count = len(UNITS)
    every_copy = [copies(u) for u in range(count)]

    def hop(u, h):
        local, along = every_copy[u][:2]
        if h == 1:
            local.wait()
        for origin, there, edge, direction in (
            (z - (h - 1), z >= h - 1, z < 3, 1),
            (z + (h - 1), z + (h - 1) <= 3, z > 0, -1),
        ):
            @pl.when(there)
            def _():
                if h > 1:
                    along(origin, direction).wait_recv()
                if h < 4:
                    @pl.when(edge)
                    def _():
                        along(origin, direction).start()

    for copies_here in every_copy:
        copies_here[0].start()
    for h in range(1, 4):
        for u in range(HOP_LAG * (4 - h)):
            hop(u, h)
    for i in range(count + LAG_USE):
        for h in range(1, 5):
            u = i + HOP_LAG * (4 - h)
            if u < count:
                hop(u, h)
        if i < count:
            first = every_copy[i][2]
            if first is not None:
                first.start()
        if 0 <= i - LAG_TWO < count:
            first, second = every_copy[i - LAG_TWO][2:4]
            if first is not None:
                first.wait_recv()
                second.start()
        if 0 <= i - LAG_SIBLING < count:
            second, sibling = every_copy[i - LAG_SIBLING][3:5]
            if second is not None:
                second.wait_recv()
            sibling.start()
        if i == 2:
            norm_local.wait()
            for copy in norm_along:
                copy.wait()
            norm_sibling.start()
        if i == 4:
            norm_sibling.wait()
            keep(0)
            states_copy.wait()
            encoded_copy.wait()
        if 5 <= i < 9:
            if i == 5:
                aux_local.wait()
            else:
                aux_steps[i - 6].wait()
            for copy in aux_steps[i - 5 : i - 4] if i < 8 else aux_along:
                copy.start()
        if i == 9:
            for copy in aux_along:
                copy.wait()
        if 0 <= i - LAG_LOAD < count:
            sibling, load = every_copy[i - LAG_LOAD][4:]
            sibling.wait_recv()
            load.start()
        if 0 <= i - LAG_USE < count:
            every_copy[i - LAG_USE][5].wait()
            use(i - LAG_USE)
    for _, along, first, second, sibling, _ in every_copy:
        for origin in range(4):
            @pl.when((origin <= z) & (z < 3))
            def _():
                along(origin, 1).wait_send()

            @pl.when((origin >= z) & (z > 0))
            def _():
                along(origin, -1).wait_send()

        if first is not None:
            first.wait_send()
            second.wait_send()
        sibling.wait_send()
    for n in range(len(kept)):
        pltpu.make_async_copy(kept[n], kept_hbm[n], kept_sem.at[n]).wait()


def forward_layer(weights, norm, aux, states, encoded, length):
    count = len(UNITS)
    shapes = []
    for w, weight in enumerate(weights):
        if w == REDUCE_WEIGHT:
            shapes.append((4, 2, weight.shape[0] // ROWS, ROWS, weight.shape[1]))
        else:
            shapes.append((4, 2) + weight.shape)
    tokens, width = states.shape
    mem_tokens = encoded.shape[0]
    mem_length = mem_tokens // (tokens // length)
    units = weights[5].shape[1]
    f32 = jnp.float32
    kept = [
        ((4, 2) + norm.shape, f32),
        ((tokens, 3 * width), BFLOAT),
        ((tokens, width), BFLOAT),
        ((tokens, width), f32),
        ((tokens, 128), f32),
        ((tokens, width), BFLOAT),
        ((tokens, width), BFLOAT),
        ((mem_tokens, 2 * width), BFLOAT),
        ((tokens, width), BFLOAT),
        ((tokens, width), f32),
        ((tokens, 128), f32),
        ((tokens, width), BFLOAT),
        ((tokens, units), f32),
        ((tokens, units), BFLOAT),
        ((tokens, width), f32),
        ((tokens, 128), f32),
        ((tokens, width), BFLOAT),
    ]
    every = pl.BlockSpec(memory_space=pl.ANY)
    dma = pltpu.SemaphoreType.DMA
    results = pl.pallas_call(
        functools.partial(forward_kernel, length, mem_length),
        out_shape=tuple(jax.ShapeDtypeStruct(shape, BFLOAT) for shape in shapes)
        + (jax.ShapeDtypeStruct((2, 2, 4, aux.shape[0], 2 * tokens), f32),)
        + tuple(jax.ShapeDtypeStruct(shape, kind) for shape, kind in kept),
        in_specs=[every] * 11,
        out_specs=(every,) * (8 + len(kept)),
        scratch_shapes=[pltpu.VMEM(shape, kind) for shape, kind in kept]
        + [
            pltpu.VMEM((SLOTS_IN_FLIGHT, 4, 2, ROWS, TILE), BFLOAT),
            pltpu.VMEM((tokens, width), f32),
            pltpu.VMEM((tokens, width), BFLOAT),
            pltpu.VMEM((mem_tokens, width), BFLOAT),
            dma((count,)),
            dma((count, 2, 4)),
            dma((count, 4)),
        ]
        + [dma((count,))] * 6
        + [dma]
        + [dma((3,))] * 2
        + [dma] * 2
        + [dma((SLOTS_IN_FLIGHT,))]
        + [dma]
        + [dma((3,))] * 4
        + [dma((len(kept),)), dma((2,))],
        compiler_params=pltpu.CompilerParams(
            collective_id=0, has_side_effects=True, vmem_limit_bytes=62 * 2**20
        ),
        name="forward_layer",
    )(*weights, norm, aux, states, encoded)
    fulls = tuple(full.reshape(-1, full.shape[-1]) for full in results[:7])
    return fulls, results[7], results[8], results[9:]


SEQUENCE = tuple((6, k) for k in range(4)) + tuple((5, k) for k in range(4)) + (
    (4, 0), (2, 0), (3, 0), (3, 1), (1, 0), (0, 0), (0, 1), (0, 2),
)
LINE_FIRST = 9
HOP_LAGS = (4, 7, 10)
LINE_LAGS = (10, 12, 14, 16, 18)
CROSS_LAGS = (2, 4, 6, 8, 10)
TURNS = 27
READS = tuple(read for k in range(4) for read in ((6, k), (5, k))) + (
    (4, 0), (2, 0), (1, 0), (0, 0), (0, 1), (0, 2), (3, 0), (3, 1),
)


def norm_back(upstream, normed, inverse, gain):
    scaled = upstream * gain
    mean_scaled = jnp.mean(scaled, -1, keepdims=True)
    along = jnp.mean(scaled * normed, -1, keepdims=True)
    return (
        inverse * (scaled - mean_scaled - normed * along),
        jnp.sum(upstream * normed, 0, keepdims=True),
        jnp.sum(upstream, 0, keepdims=True),
    )


def attend_pair_back(grad, queries, keys, values, causal):
    scale = 1.0 / math.sqrt(HEAD_DIM)
    queries, grad = stack_heads(queries), stack_heads(grad)
    probs = pair_scores(queries, keys, causal)
    grad_probs = dot_nt(grad, values)
    grad_values = dot_tn(probs.astype(BFLOAT), grad).astype(BFLOAT)
    grad_scores = (
        probs * (grad_probs - jnp.sum(probs * grad_probs, -1, keepdims=True))
    ).astype(BFLOAT)
    grad_queries = unstack_heads(dot_nn(grad_scores, keys) * scale).astype(BFLOAT)
    grad_keys = (dot_tn(grad_scores, queries) * scale).astype(BFLOAT)
    return grad_queries, grad_keys, grad_values


def backward_kernel(length, mem_length, *refs):
    weights = refs[:7]
    kept_hbm = refs[7:23]
    inner_hbm = refs[23]
    norm_full, grad_third = refs[24:26]
    outs = refs[26:33]
    norm_out, grad_states, grad_memory, landing = refs[33:37]
    kept = refs[37:53]
    (
        wbuf, inner, stage, got, zload, one_line, two_line, one, two, line, fin,
        resid, low, grad_low, grad_context, grad_queries, grad_packed, memory_part,
        norm_here, norm_there, norm_line,
    ) = refs[53:74]
    (
        kept_sem, w_sem, inner_sem, dd_send, dd_recv, z_send, z_recv, zload_sem,
        ra_send, ra_recv, rb_send, rb_recv, rz_send, rz_recv, ag_send, ag_recv, ah_send, ah_recv,
        fin_sem, memory_sem, n_send, n_recv, nz_send, nz_recv,
    ) = refs[74:]
    (
        packed, context, first_normed, first_inverse, first_low, cross_queries, pairs, cross_context,
        second_normed, second_inverse, second_low, active, third_normed, third_inverse, states, encoded,
    ) = kept
    x, y, z, c = whereami()
    greet(neighbours(x, y, z, c))
    tokens, width = states.shape
    slots_here = tokens // length
    count = len(SEQUENCE)
    blocks = active.shape[1] // (8 * ROWS)

    def keep_copy(n):
        return pltpu.make_async_copy(kept_hbm[n], kept[n], kept_sem.at[n])

    first_needed = (12, 13, 11, 10)
    for n in first_needed:
        keep_copy(n).start()
    for n in range(16):
        if n not in first_needed:
            keep_copy(n).start()

    def need(*names):
        for n in names:
            keep_copy(n).wait()

    def read_copy(n):
        weight, k = READS[n]
        if weight == REDUCE_WEIGHT:
            source = weights[weight].at[pl.ds(k * TILE, TILE), :]
        else:
            source = weights[weight].at[:, pl.ds(k * TILE, TILE)]
        return pltpu.make_async_copy(source, wbuf.at[n % 2], w_sem.at[n % 2])

    def inner_copy(k):
        return pltpu.make_async_copy(
            inner_hbm.at[:, pl.ds(k * TILE, TILE)], inner.at[k % 2], inner_sem.at[k % 2]
        )

    read_copy(0).start()
    read_copy(1).start()
    inner_copy(0).start()
    inner_copy(1).start()

    def remote(src, dst, send, recv, peer):
        return pltpu.make_async_remote_copy(
            src_ref=src, dst_ref=dst, send_sem=send, recv_sem=recv, device_id=peer, device_id_type=MESH
        )

    def norm_row(n):
        return jnp.concatenate([norm_full[p // 2, p % 2, n : n + 1, :] for p in range(8)], 1)

    def place(q):
        even = lax.rem(q, 2) == 0
        a = jnp.where(even, x, y)
        b = jnp.where(even, y, x)
        x_peer = y * 2 + (1 - x)
        y_peer = (1 - y) * 2 + x
        a_peer = (jnp.where(even, x_peer, y_peer), z * 2 + c)
        b_peer = (jnp.where(even, y_peer, x_peer), z * 2 + c)
        return a, b, a_peer, b_peer

    def piece(index, size):
        return pl.ds(pl.multiple_of(index * size, size), size)

    def total(*parts):
        out = parts[0].astype(jnp.float32)
        for part in parts[1:]:
            out = out + part.astype(jnp.float32)
        return out.astype(BFLOAT)

    def dd_copy(q):
        return remote(
            stage.at[lax.rem(q, 2), 1 - c], got.at[q], dd_send.at[q], dd_recv.at[q], at(x, y, z, 1 - c)
        )

    def line_copy(q, side, h, dest, step):
        return remote(
            got.at[q, dest], landing.at[q, side, h - 1], z_send.at[q, side, h - 1],
            z_recv.at[q, side, h - 1], at(x, y, z + step, c),
        )

    def line_sides(h):
        return (
            (0, z + 4 - h, z <= h - 1, z >= 1, 1),
            (1, z - 4 + h, z >= 4 - h, z <= 2, -1),
        )

    def line_load(q, side, h):
        return pltpu.make_async_copy(landing.at[q, side, h - 2], zload.at[side], zload_sem.at[side])

    def line_hop(q, h):
        if h > 1:
            for side, dest, there, fed, step in line_sides(h):
                @pl.when(there & fed)
                def _():
                    line_copy(q, side, h - 1, dest, step).wait_recv()
                    line_load(q, side, h).start()

        for side, dest, there, fed, step in line_sides(h):
            if h > 1:
                @pl.when(there & fed)
                def _():
                    line_load(q, side, h).wait()

                    @pl.loop(0, 8)
                    def _(j):
                        rows_here = piece(j, 16)
                        got[q, dest, rows_here, :] = total(
                            got[q, dest, rows_here, :], zload[side, rows_here, :]
                        )

            if h < 4:
                @pl.when(there)
                def _():
                    line_copy(q, side, h, dest, step).start()

    def ra_line(q):
        a, _, a_peer, _ = place(q)
        return remote(got.at[q, z, piece(1 - a, 64), :], one_line.at[q], ra_send.at[q], ra_recv.at[q], a_peer)

    def rb_line(q):
        _, b, _, b_peer = place(q)
        return remote(one_line.at[q, piece(1 - b, 32), :], two_line.at[q], rb_send.at[q], rb_recv.at[q], b_peer)

    def ra_cross(q):
        a, _, a_peer, _ = place(q)
        return remote(
            got.at[q, :, piece(1 - a, 64), :], one.at[q - LINE_FIRST], ra_send.at[q], ra_recv.at[q], a_peer
        )

    def rb_cross(q):
        _, b, _, b_peer = place(q)
        return remote(
            one.at[q - LINE_FIRST, :, piece(1 - b, 32), :], two.at[q - LINE_FIRST],
            rb_send.at[q], rb_recv.at[q], b_peer,
        )

    def rz_cross(q, d):
        other = lax.rem(z + d, 4)
        n = q - LINE_FIRST
        return remote(
            two.at[n, other], line.at[n, d - 1], rz_send.at[n, d - 1], rz_recv.at[n, d - 1],
            at(x, y, other, c),
        )

    def out_view(q, start, size):
        return shard_view(outs[SEQUENCE[q][0]], SEQUENCE[q], start, size)

    def quarter_start(q):
        a, b, _, _ = place(q)
        return pl.multiple_of(64 * a + 32 * b, 32)

    def fin_copy(q):
        return pltpu.make_async_copy(fin.at[q], out_view(q, quarter_start(q), 32), fin_sem.at[q])

    def ag_copy(q):
        return remote(
            fin.at[q], out_view(q, quarter_start(q), 32), ag_send.at[q], ag_recv.at[q], place(q)[3]
        )

    def ah_copy(q):
        a, _, a_peer, _ = place(q)
        part = out_view(q, pl.multiple_of(64 * a, 64), 64)
        return remote(part, part, ah_send.at[q], ah_recv.at[q], a_peer)

    norm_peers = (at(x, y, z, 1 - c), at(1 - x, y, z, c), at(x, 1 - y, z, c))

    def norm_copy(n):
        return remote(norm_here.at[n], norm_there.at[n], n_send.at[n], n_recv.at[n], norm_peers[n])

    def norm_line_copy(d):
        return remote(
            norm_here.at[3], norm_line.at[d - 1], nz_send.at[d - 1], nz_recv.at[d - 1],
            at(x, y, lax.rem(z + d, 4), c),
        )

    def outer(q, left, start, step, right):
        slot = q % 2

        @pl.loop(0, 8, unroll=4)
        def _(p):
            lanes = pl.ds(pl.multiple_of(start + p * step, 128), 128)
            stage[slot, lax.rem(p, 2), p // 2] = dot_tn(left[:, lanes], right()).astype(BFLOAT)

    def back_times(left, n, write):
        slot = n % 2
        read_copy(n).wait()

        @pl.loop(0, 4, unroll=True)
        def _(m):
            write(piece(m, 256), dot_nt(left[...], wbuf[slot, piece(m, 256), :]))

        if n + 2 < len(READS):
            read_copy(n + 2).start()

    def add_resid(columns, value):
        resid[:, columns] = resid[:, columns] + value

    def finish_norm(n, normed, inverse):
        value, gain, shift = norm_back(resid[...], normed[...], inverse[:, 0:1], norm_row(n))
        resid[...] = value
        low[...] = value.astype(BFLOAT)
        norm_here[0, n : n + 1, :] = gain
        norm_here[0, n + 3 : n + 4, :] = shift

    def attention_back(queries, keys, key_start, value_start, key_length, out, out_keys, causal):
        @pl.loop(0, slots_here * (width // 128), unroll=2)
        def _(n):
            slot, group = n // (width // 128), lax.rem(n, width // 128)
            lanes = piece(group, 128)
            key_lanes = pl.ds(pl.multiple_of(key_start + group * 128, 128), 128)
            value_lanes = pl.ds(pl.multiple_of(value_start + group * 128, 128), 128)
            query_rows = piece(slot, length)
            key_rows = piece(slot, key_length)
            grad_query, grad_key, grad_value = attend_pair_back(
                grad_context[query_rows, lanes],
                queries[query_rows, lanes],
                keys[key_rows, key_lanes],
                keys[key_rows, value_lanes],
                causal,
            )
            out[query_rows, lanes] = grad_query
            out_keys[key_rows, key_lanes] = grad_key
            out_keys[key_rows, value_lanes] = grad_value

    def produce(q):
        weight, k = SEQUENCE[q]
        if q == 0:
            norm_here[0] = jnp.zeros_like(norm_here[0])
            for p in range(8):
                resid[:, p * 128 : (p + 1) * 128] = grad_third[p * 128 : (p + 1) * 128, :].T
            need(12, 13, 11)
            finish_norm(2, third_normed, third_inverse)
        if weight == 6:
            outer(q, active, k * ROWS, blocks * ROWS, lambda: low[...])
        elif weight == 5:
            if k == 0:
                need(10)
            inner_copy(k).wait()

            def write(columns, value):
                pre = inner[k % 2, :, columns]
                slope = 0.5 * (1.0 + lax.erf(pre * math.sqrt(0.5))) + pre * jnp.exp(
                    -0.5 * pre * pre
                ) * (1.0 / math.sqrt(2.0 * math.pi))
                grad_low[:, columns] = (value * slope).astype(BFLOAT)

            back_times(low, 2 * k, write)
            if k + 2 < 4:
                inner_copy(k + 2).start()
            outer(q, second_low, 0, ROWS, lambda: grad_low[...])
            back_times(grad_low, 2 * k + 1, add_resid)
        elif weight == 4:
            need(8, 9, 7)
            finish_norm(1, second_normed, second_inverse)
            outer(q, cross_context, 0, ROWS, lambda: low[...])

            def write(columns, value):
                grad_context[:, columns] = value.astype(BFLOAT)

            back_times(low, 8, write)
        elif weight == 2:
            need(5, 6, 4, 2, 3)
            attention_back(cross_queries, pairs, 0, width, mem_length, grad_queries, pairs, False)
            outer(q, first_low, 0, ROWS, lambda: grad_queries[...])
            back_times(grad_queries, 9, add_resid)
            finish_norm(0, first_normed, first_inverse)
        elif weight == 3:
            if k == 0:
                need(15)
            outer(q, encoded, 0, ROWS, lambda: pairs[:, pl.ds(k * TILE, TILE)])
        elif weight == 1:
            need(1, 0, 14)
            outer(q, context, 0, ROWS, lambda: low[...])

            def write(columns, value):
                grad_context[:, columns] = value.astype(BFLOAT)

            back_times(low, 10, write)
            attention_back(packed, packed, width, 2 * width, length, grad_packed, grad_packed, True)
        else:
            def part():
                return grad_packed[:, pl.ds(k * TILE, TILE)]

            outer(q, states, 0, ROWS, part)
            back_times(grad_packed.at[:, pl.ds(k * TILE, TILE)], 11 + k, add_resid)
            if k == 2:
                grad_states[...] = resid[...]

    half = encoded.shape[0] // 2

    def memory_copy(m):
        return pltpu.make_async_copy(
            memory_part.at[m % 2],
            grad_memory.at[pl.ds(m // 4 * half, half), pl.ds(m % 4 * 256, 256)],
            memory_sem.at[m % 2],
        )

    def memory_chunk(m):
        if m == 0:
            read_copy(14).wait()
            read_copy(15).wait()
        if m >= 2:
            memory_copy(m - 2).wait()
        rows_here, columns = pl.ds(m // 4 * half, half), pl.ds(m % 4 * 256, 256)
        memory_part[m % 2] = dot_nt(pairs[rows_here, :width], wbuf[0, columns, :]) + dot_nt(
            pairs[rows_here, width:], wbuf[1, columns, :]
        )
        memory_copy(m).start()

    def each(q, action):
        for k in range(count):
            @pl.when(q == k)
            def _():
                action(k)

    def finish_block(q):
        def action(k):
            fin_copy(k).start()
            ag_copy(k).start()

        each(q, action)

    step = 16

    @pl.loop(0, TURNS)
    def _(i):
        for q in range(count):
            @pl.when(i == q)
            def _():
                if q >= 2:
                    dd_copy(q - 2).wait_send()
                produce(q)
                dd_copy(q).start()

        for m in range(8):
            @pl.when(i == count + 1 + m)
            def _():
                memory_chunk(m)

        qs = i - 1

        @pl.when((qs >= 0) & (qs < count))
        def _():
            dd_copy(qs).wait_recv()
            slot = lax.rem(qs, 2)

            @pl.loop(0, 32)
            def _(j):
                zz, rows_here = j // 8, piece(lax.rem(j, 8), step)
                got[qs, zz, rows_here, :] = total(got[qs, zz, rows_here, :], stage[slot, c, zz, rows_here, :])

            @pl.when(qs < LINE_FIRST)
            def _():
                line_hop(qs, 1)

            @pl.when(qs >= LINE_FIRST)
            def _():
                ra_cross(qs).start()

        for h in (2, 3, 4):
            qh = i - HOP_LAGS[h - 2]

            @pl.when((qh >= 0) & (qh < LINE_FIRST))
            def _():
                line_hop(qh, h)
                if h == 4:
                    ra_line(qh).start()

        q1 = i - LINE_LAGS[1]

        @pl.when((q1 >= 0) & (q1 < LINE_FIRST))
        def _():
            ra_line(q1).wait_recv()
            a = place(q1)[0]

            @pl.loop(0, 4)
            def _(j):
                rows_here = piece(j, step)
                one_line[q1, rows_here, :] = total(
                    one_line[q1, rows_here, :],
                    got[q1, z, pl.ds(pl.multiple_of(64 * a + j * step, step), step), :],
                )

            rb_line(q1).start()

        q2 = i - LINE_LAGS[2]

        @pl.when((q2 >= 0) & (q2 < LINE_FIRST))
        def _():
            rb_line(q2).wait_recv()
            b = place(q2)[1]

            @pl.loop(0, 2)
            def _(j):
                rows_here = piece(j, step)
                fin[q2, rows_here, :] = total(
                    two_line[q2, rows_here, :],
                    one_line[q2, pl.ds(pl.multiple_of(32 * b + j * step, step), step), :],
                )

            finish_block(q2)

        p0 = i - CROSS_LAGS[0]

        @pl.when((p0 >= LINE_FIRST) & (p0 < count))
        def _():
            ra_cross(p0).wait_recv()
            a = place(p0)[0]

            @pl.loop(0, 16)
            def _(j):
                zz, r = j // 4, lax.rem(j, 4)
                rows_here = piece(r, step)
                one[p0 - LINE_FIRST, zz, rows_here, :] = total(
                    one[p0 - LINE_FIRST, zz, rows_here, :],
                    got[p0, zz, pl.ds(pl.multiple_of(64 * a + r * step, step), step), :],
                )

            rb_cross(p0).start()

        p1 = i - CROSS_LAGS[1]

        @pl.when((p1 >= LINE_FIRST) & (p1 < count))
        def _():
            rb_cross(p1).wait_recv()
            b = place(p1)[1]

            @pl.loop(0, 8)
            def _(j):
                zz, r = j // 2, lax.rem(j, 2)
                rows_here = piece(r, step)
                two[p1 - LINE_FIRST, zz, rows_here, :] = total(
                    two[p1 - LINE_FIRST, zz, rows_here, :],
                    one[p1 - LINE_FIRST, zz, pl.ds(pl.multiple_of(32 * b + r * step, step), step), :],
                )

            for d in (1, 2, 3):
                rz_cross(p1, d).start()

        p2 = i - CROSS_LAGS[2]

        @pl.when((p2 >= LINE_FIRST) & (p2 < count))
        def _():
            for d in (1, 2, 3):
                rz_cross(p2, d).wait_recv()
            n = p2 - LINE_FIRST

            @pl.loop(0, 2)
            def _(j):
                rows_here = piece(j, step)
                fin[p2, rows_here, :] = total(
                    two[n, z, rows_here, :], line[n, 0, rows_here, :], line[n, 1, rows_here, :],
                    line[n, 2, rows_here, :],
                )

            finish_block(p2)

        def pass_on(k):
            ag_copy(k).wait_recv()
            fin_copy(k).wait()
            ah_copy(k).start()

        for lags, low_q, high_q in ((LINE_LAGS, 0, LINE_FIRST), (CROSS_LAGS, LINE_FIRST, count)):
            q3 = i - lags[3]

            @pl.when((q3 >= low_q) & (q3 < high_q))
            def _():
                each(q3, pass_on)

            q4 = i - lags[4]

            @pl.when((q4 >= low_q) & (q4 < high_q))
            def _():
                each(q4, lambda k: ah_copy(k).wait_recv())

        @pl.when(i == count)
        def _():
            norm_copy(0).start()

        for n in range(3):
            @pl.when(i == count + 2 * (n + 1))
            def _():
                norm_copy(n).wait_recv()
                norm_here[n + 1] = norm_here[n] + norm_there[n]
                if n < 2:
                    norm_copy(n + 1).start()
                else:
                    for d in (1, 2, 3):
                        norm_line_copy(d).start()

        @pl.when(i == count + 8)
        def _():
            for d in (1, 2, 3):
                norm_line_copy(d).wait_recv()
            norm_out[...] = ((norm_here[3] + norm_line[0]) + norm_line[1]) + norm_line[2]

    memory_copy(6).wait()
    memory_copy(7).wait()
    dd_copy(count - 2).wait_send()
    dd_copy(count - 1).wait_send()

    @pl.loop(0, LINE_FIRST)
    def _(q):
        for h in (1, 2, 3):
            for side, dest, there, _, step in line_sides(h):
                @pl.when(there)
                def _():
                    line_copy(q, side, h, dest, step).wait_send()

        ra_line(q).wait_send()
        rb_line(q).wait_send()

    @pl.loop(LINE_FIRST, count)
    def _(q):
        ra_cross(q).wait_send()
        rb_cross(q).wait_send()
        for d in (1, 2, 3):
            rz_cross(q, d).wait_send()

    for q in range(count):
        ag_copy(q).wait_send()
        ah_copy(q).wait_send()
    for n in range(3):
        norm_copy(n).wait_send()
        norm_line_copy(n + 1).wait_send()


def backward_layer(weights, kept, inner, norm_full, grad_third, length):
    count = len(SEQUENCE)
    f32 = jnp.float32
    tokens, width = kept[14].shape
    mem_tokens = kept[15].shape[0]
    mem_length = mem_tokens // (tokens // length)
    shapes = [(weight.shape[0] // 8, weight.shape[1]) for weight in weights]
    every = pl.BlockSpec(memory_space=pl.ANY)
    vmem = pl.BlockSpec(memory_space=pltpu.VMEM)
    dma = pltpu.SemaphoreType.DMA
    sems = dma((count,))
    crossed = count - LINE_FIRST
    *shares, norm_sum, grad_states, grad_memory, _ = pl.pallas_call(
        functools.partial(backward_kernel, length, mem_length),
        out_shape=tuple(jax.ShapeDtypeStruct(shape, BFLOAT) for shape in shapes)
        + (
            jax.ShapeDtypeStruct((8, width), f32),
            jax.ShapeDtypeStruct((tokens, width), f32),
            jax.ShapeDtypeStruct((mem_tokens, width), f32),
            jax.ShapeDtypeStruct((LINE_FIRST, 2, 3, ROWS, TILE), BFLOAT),
        ),
        in_specs=[every] * 24 + [vmem] * 2,
        out_specs=(every,) * 7 + (vmem, vmem, every, every),
        scratch_shapes=[pltpu.VMEM(part.shape, part.dtype) for part in kept]
        + [
            pltpu.VMEM((2, TILE, TILE), BFLOAT),
            pltpu.VMEM((2, tokens, TILE), f32),
            pltpu.VMEM((2, 2, 4, ROWS, TILE), BFLOAT),
            pltpu.VMEM((count, 4, ROWS, TILE), BFLOAT),
            pltpu.VMEM((2, ROWS, TILE), BFLOAT),
            pltpu.VMEM((LINE_FIRST, 64, TILE), BFLOAT),
            pltpu.VMEM((LINE_FIRST, 32, TILE), BFLOAT),
            pltpu.VMEM((crossed, 4, 64, TILE), BFLOAT),
            pltpu.VMEM((crossed, 4, 32, TILE), BFLOAT),
            pltpu.VMEM((crossed, 3, 32, TILE), BFLOAT),
            pltpu.VMEM((count, 32, TILE), BFLOAT),
            pltpu.VMEM((tokens, width), f32),
            pltpu.VMEM((tokens, width), BFLOAT),
            pltpu.VMEM((tokens, TILE), BFLOAT),
            pltpu.VMEM((tokens, width), BFLOAT),
            pltpu.VMEM((tokens, width), BFLOAT),
            pltpu.VMEM((tokens, 3 * width), BFLOAT),
            pltpu.VMEM((2, mem_tokens // 2, 256), f32),
            pltpu.VMEM((4, 8, width), f32),
            pltpu.VMEM((3, 8, width), f32),
            pltpu.VMEM((3, 8, width), f32),
            dma((16,)), dma((2,)), dma((2,)), sems, sems,
            dma((LINE_FIRST, 2, 3)), dma((LINE_FIRST, 2, 3)), dma((2,)),
            sems, sems, sems, sems,
            dma((crossed, 3)), dma((crossed, 3)),
            sems, sems, sems, sems, sems, dma((2,)),
            dma((3,)), dma((3,)), dma((3,)), dma((3,)),
        ],
        compiler_params=pltpu.CompilerParams(
            collective_id=1, has_side_effects=True, vmem_limit_bytes=62 * 2**20
        ),
        name="backward_layer",
    )(*weights, *kept, inner, norm_full, grad_third)
    return tuple(share.astype(f32) for share in shares), norm_sum, grad_states, grad_memory


VOCAB_CUTS = 3
ARRIVAL_PHASES = (0, 0, 1, 0, 1, 2, 3, 0, 1, 2, 3, 1, 2, 3, 2, 3)
ARRIVAL_TURNS = (0, 1, 0, 2, 1, 0, 0, 3, 2, 1, 1, 3, 2, 2, 3, 3)
NEAREST = ((0, 1, 2, 3), (1, 0, 1, 2), (2, 2, 3, 1), (3, 3, 0, 0))


def head_kernel(slots, length, vocab_here, *refs):
    hid, marks, emb_all = refs[:3]
    small_out, gemb_out, third_out = refs[3:6]
    (
        emb, emb_t, held, logit, expo, part, sib_part, part_one, part_two, part_z,
        mine, theirs, lined, prior, usable, weight, scaled, picked_grad,
    ) = refs[6:24]
    (
        local_sem, z_send, z_recv, one_send, one_recv, two_send, two_recv, sib_send, sib_recv,
        st_send, st_recv, stz_send, stz_recv,
        dd_send, dd_recv, r1_send, r1_recv, r2_send, r2_recv, rz_send, rz_recv,
    ) = refs[24:]
    x, y, z, c = whereami()
    pb, pa = y * 2 + x, z * 2 + c
    size = hid.shape[0]
    pair = 2 * size
    width = hid.shape[1]
    rows = emb.shape[0]
    cut = rows // VOCAB_CUTS
    start = pl.multiple_of(pb * rows, 16)
    last = vocab_here - 3 * rows
    valid = jnp.where(pb == 3, last, rows)
    base = pa * vocab_here + start
    own = pb * 4 + z

    def remote(src, dst, send, recv, peer):
        return pltpu.make_async_remote_copy(
            src_ref=src, dst_ref=dst, send_sem=send, recv_sem=recv, device_id=peer, device_id_type=MESH
        )

    sibling = at(x, y, z, 1 - c)
    x_peer, y_peer = at(1 - x, y, z, c), at(x, 1 - y, z, c)

    def spot(k, core):
        return held.at[pl.ds(pl.multiple_of((k * 2 + core) * size, size), size), :]

    greet(neighbours(x, y, z, c))
    own_copy = pltpu.make_async_copy(hid, spot(own, c), local_sem.at[0])
    own_copy.start()
    emb_copy = pltpu.make_async_copy(
        emb_all.at[pl.ds(start, last), :], emb.at[pl.ds(0, last), :], local_sem.at[2]
    )
    rest_copy = pltpu.make_async_copy(
        emb_all.at[pl.ds(pl.multiple_of(jnp.minimum(start + last, vocab_here - (rows - last)), 16), rows - last), :],
        emb.at[pl.ds(last, rows - last), :],
        local_sem.at[3],
    )
    emb_copy.start()
    rest_copy.start()
    own_copy.wait()

    def up_copy(origin):
        block = spot(pb * 4 + origin, c)
        return remote(block, block, z_send.at[0, origin], z_recv.at[origin], at(x, y, z + 1, c))

    def down_copy(origin):
        block = spot(pb * 4 + origin, c)
        return remote(block, block, z_send.at[1, origin], z_recv.at[origin], at(x, y, z - 1, c))

    def pass_along(origin, action):
        @pl.when((origin <= z) & (z < 3))
        def _():
            action(up_copy(origin))

        @pl.when((origin >= z) & (z > 0))
        def _():
            action(down_copy(origin))

    def sib_copy(k):
        return remote(spot(k, c), spot(k, c), sib_send.at[k], sib_recv.at[k], sibling)

    def order(zz):
        x_first = zz < 2
        f = jnp.where(x_first, x, y)
        g = jnp.where(x_first, y, x)
        first_peer = (jnp.where(x_first, y * 2 + 1 - x, (1 - y) * 2 + x), pa)
        second_peer = (jnp.where(x_first, (1 - y) * 2 + x, y * 2 + 1 - x), pa)

        def block(first, second):
            return jnp.where(x_first, second * 2 + first, first * 2 + second) * 4 + zz

        return f, g, first_peer, second_peer, block

    def one_copy(zz):
        f, g, first_peer, _, block = order(zz)
        return remote(
            spot(block(f, g), c), spot(block(f, g), c), one_send.at[zz], one_recv.at[zz], first_peer
        )

    def two_copy(zz, j):
        f, g, _, second_peer, block = order(zz)
        k = block(f if j == 0 else 1 - f, g)
        return remote(spot(k, c), spot(k, c), two_send.at[zz, j], two_recv.at[zz, j], second_peer)

    pass_along(z, lambda copy: copy.start())
    sib_copy(own).start()
    one_copy(z).start()

    emb_copy.wait()
    rest_copy.wait()
    full_cuts = rows // 128

    def target_rows(k):
        ypart, xpart, zpart = k // 8, lax.rem(k // 4, 2), lax.rem(k, 4)
        target = marks[ypart, xpart, zpart, 0:1, :].astype(jnp.int32) - base
        return jnp.where(target < valid, target, -1)

    def row_numbers(j):
        return lax.broadcasted_iota(jnp.int32, (cut, pair), 0) + j * cut

    def cut_rows(j):
        return pl.ds(pl.multiple_of(j * cut, cut), cut)

    def token_lanes(k):
        return pl.ds(pl.multiple_of(k * pair, pair), pair)

    def forward_block(k):
        target = target_rows(k)
        block = held[token_lanes(k), :]

        def scan_logits(j, carried):
            highest, picked = carried
            value = lax.dot_general(
                emb[cut_rows(j), :], block, (((1,), (1,)), ((), ())), preferred_element_type=jnp.float32
            )
            number = row_numbers(j)
            value = jnp.where(number < valid, value, NEGATIVE)
            logit[cut_rows(j), :] = value
            return (
                jnp.maximum(highest, jnp.max(value, 0, keepdims=True)),
                picked + jnp.sum(jnp.where(number == target, value, 0.0), 0, keepdims=True),
            )

        highest, picked = lax.fori_loop(
            0,
            VOCAB_CUTS,
            scan_logits,
            (jnp.full((1, pair), NEGATIVE, jnp.float32), jnp.zeros((1, pair), jnp.float32)),
        )

        def scan_exp(j, total):
            value = jnp.exp(logit[cut_rows(j), :] - highest)
            expo[cut_rows(j), token_lanes(k)] = value.astype(BFLOAT)
            return total + jnp.sum(value, 0, keepdims=True)

        total = lax.fori_loop(0, VOCAB_CUTS, scan_exp, jnp.zeros((1, pair), jnp.float32))
        mine[0, 0, pl.ds(k, 1), :] = highest
        mine[0, 1, pl.ds(k, 1), :] = total
        mine[0, 2, pl.ds(k, 1), :] = picked

    def listed(values, index):
        out = values[0]
        for n in range(1, len(values)):
            out = jnp.where(index == n, values[n], out)
        return out

    def step_block(s):
        phase = listed(ARRIVAL_PHASES, s)
        t = listed(ARRIVAL_TURNS, s)
        zz = listed([listed(row, z) for row in NEAREST], t)
        f, g, _, _, block = order(zz)
        k = listed((block(f, g), block(1 - f, g), block(f, 1 - g), block(1 - f, 1 - g)), phase)
        return phase, zz, k

    @pl.loop(0, 17)
    def _(s):
        phase, zz, k = step_block(s)

        @pl.when(s < full_cuts)
        def _():
            here = pl.ds(pl.multiple_of(s * 128, 128), 128)
            emb_t[:, here] = emb[here, :].T

        if rows % 128:
            @pl.when(s == full_cuts)
            def _():
                emb_t[:, full_cuts * 128 :] = emb[full_cuts * 128 :, :].T

        @pl.when((s > 0) & (s < 16) & (phase == 0))
        def _():
            up_copy(zz).wait_recv()
            pass_along(zz, lambda copy: copy.start())
            sib_copy(k).start()
            one_copy(zz).start()

        @pl.when((s < 16) & (phase == 1))
        def _():
            one_copy(zz).wait_recv()
            sib_copy(k).start()
            for j in range(2):
                two_copy(zz, j).start()

        for j in range(2):
            @pl.when((s < 16) & (phase == 2 + j))
            def _():
                two_copy(zz, j).wait_recv()
                sib_copy(k).start()

        @pl.when(s > 0)
        def _():
            former = step_block(s - 1)[2]
            sib_copy(former).wait_recv()
            forward_block(former)

    def joined(parts):
        highest = functools.reduce(jnp.maximum, [p[0] for p in parts])
        total = functools.reduce(jnp.add, [p[1] * jnp.exp(p[0] - highest) for p in parts])
        picked = functools.reduce(jnp.add, [p[2] for p in parts])
        return highest, total, picked

    def rows_of(ref, n):
        return ref[n, 0], ref[n, 1], ref[n, 2]

    for n, (peer, side) in enumerate(((sibling, c), (x_peer, x), (y_peer, y))):
        copy = remote(mine.at[n], theirs.at[n], st_send.at[n], st_recv.at[n], peer)
        copy.start()
        copy.wait()
        here, there = rows_of(mine, n), rows_of(theirs, n)
        early = tuple(jnp.where(side == 0, a, b) for a, b in zip(here, there))
        late = tuple(jnp.where(side == 0, b, a) for a, b in zip(here, there))
        for r, value in enumerate(joined((early, late))):
            mine[n + 1, r] = value

    def stat_copy(d):
        other = lax.rem(z + d, 4)
        return remote(mine.at[3], lined.at[z], stz_send.at[d - 1], stz_recv.at[d - 1], at(x, y, other, c))

    for d in (1, 2, 3):
        stat_copy(d).start()
    for r in range(3):
        lined[z, r] = mine[3, r]
    for d in (1, 2, 3):
        stat_copy(d).wait()
    highest, total, picked = joined([rows_of(lined, n) for n in range(4)])
    logsum = highest + jnp.log(total)
    log_probs = picked - logsum
    for k in range(16):
        prior[k : k + 1, :] = marks[k // 8, (k // 4) % 2, k % 4, 1:2, :]
        usable[k : k + 1, :] = marks[k // 8, (k // 4) % 2, k % 4, 2:3, :]
    lane = lax.broadcasted_iota(jnp.int32, (16, pair), 1) // length
    mean = jnp.zeros((16, pair), jnp.float32)
    for n in range(pair // length):
        inside = lane == n
        slot_sum = jnp.sum(jnp.where(inside, log_probs, 0.0), 1, keepdims=True)
        mean = jnp.where(inside, slot_sum * (1.0 / length), mean)
    scores = prior[...] + mean
    counted = usable[...] > 0.5
    masked = jnp.where(counted, scores, NEGATIVE)
    question = lax.broadcasted_iota(jnp.int32, (16, pair), 0) // 4
    marginal = jnp.zeros((16, pair), jnp.float32)
    loss = jnp.zeros((1, 1), jnp.float32)
    for n in range(4):
        inside = question == n
        high = jnp.max(
            jnp.max(jnp.where(inside, masked, NEGATIVE), 1, keepdims=True), 0, keepdims=True
        )
        terms = jnp.where(inside & counted, jnp.exp(masked - high), 0.0)
        mass = jnp.sum(jnp.sum(terms, 1, keepdims=True), 0, keepdims=True) * (1.0 / length)
        value = high + jnp.log(mass)
        marginal = jnp.where(inside, value, marginal)
        loss = loss + value
    posterior = jnp.where(counted, jnp.exp(scores - marginal), 0.0)
    token_weight = -float(slots) * posterior
    weight[...] = posterior
    scaled[...] = token_weight * jnp.exp(mine[0, 0] - logsum)
    picked_grad[...] = token_weight * (1.0 - jnp.exp(log_probs))
    small_out[...] = jnp.broadcast_to(loss * (-1.0 / 4), small_out.shape)
    own_row = weight[pl.ds(own, 1), :]
    own_row = jnp.where(c == 0, own_row[:, :size], own_row[:, size:])
    small_out[1:2, :] = own_row * (-float(slots * length))

    def backward_block(k):
        target = target_rows(k)
        hit = picked_grad[pl.ds(k, 1), :]
        scale = scaled[pl.ds(k, 1), :]

        def make(j, carried):
            value = expo[cut_rows(j), token_lanes(k)].astype(jnp.float32)
            grad = jnp.where(row_numbers(j) == target, hit, -(value * scale))
            expo[cut_rows(j), token_lanes(k)] = grad.astype(BFLOAT)
            return carried

        lax.fori_loop(0, VOCAB_CUTS, make, 0)

        def to_rows(n, carried):
            cut_width = pl.ds(pl.multiple_of(n * 256, 256), 256)
            value = lax.dot_general(
                emb_t[cut_width, :],
                expo[:, token_lanes(k)],
                (((1,), (0,)), ((), ())),
                preferred_element_type=jnp.float32,
            ).astype(BFLOAT)
            part[k, 0, cut_width, :] = value[:, :size]
            part[k, 1, cut_width, :] = value[:, size:]
            return carried

        lax.fori_loop(0, width // 256, to_rows, 0)

    def dd_copy(k):
        return remote(part.at[k, 1 - c], sib_part.at[k], dd_send.at[k], dd_recv.at[k], sibling)

    def r1_copy(zz, j):
        f, _, first_peer, _, block = order(zz)
        return remote(
            sib_part.at[block(1 - f, j)], part_one.at[zz, j], r1_send.at[zz, j], r1_recv.at[zz, j],
            first_peer,
        )

    def r2_copy(zz):
        _, g, _, second_peer, _ = order(zz)
        return remote(part_one.at[zz, 1 - g], part_two.at[zz], r2_send.at[zz], r2_recv.at[zz], second_peer)

    def rz_copy(zz):
        return remote(part_two.at[zz], part_z.at[z], rz_send.at[zz], rz_recv.at[z], at(x, y, zz, c))

    def rz_arrival(zz):
        return remote(part_two.at[zz], part_z.at[zz], rz_send.at[zz], rz_recv.at[zz], at(x, y, zz, c))

    step = 128

    def add_into(target_ref, other_ref):
        @pl.loop(0, width // step)
        def _(n):
            rows_here = pl.ds(pl.multiple_of(n * step, step), step)
            target_ref[rows_here, :] = (
                target_ref[rows_here, :].astype(jnp.float32) + other_ref[rows_here, :].astype(jnp.float32)
            ).astype(BFLOAT)

    def group(n):
        return lax.rem(n, 2) * 2 + n // 2

    def chunk(q):
        j, n = q // 4, lax.rem(q, 4)
        columns = pl.ds(pl.multiple_of(n * 256, 256), 256)
        gemb_out[cut_rows(j), columns] = lax.dot_general(
            expo[cut_rows(j), :],
            held[:, columns],
            (((1,), (0,)), ((), ())),
            preferred_element_type=jnp.float32,
        ).astype(BFLOAT)

    def grad_block(s):
        leaves = s < 8
        zz = group(lax.rem(s, 8) // 2)
        j = lax.rem(s, 2)
        f, _, _, _, block = order(zz)
        return leaves, zz, j, block(jnp.where(leaves, 1 - f, f), j)

    @pl.loop(0, 28)
    def _(s):
        @pl.when((s >= 2) & (s < 18))
        def _():
            leaves, zz, turn, k = grad_block(s - 2)
            dd_copy(k).wait_recv()
            add_into(sib_part.at[k], part.at[k, c])
            for j in range(2):
                @pl.when(leaves & (turn == j))
                def _():
                    r1_copy(zz, j).start()

        @pl.when((lax.rem(s, 2) == 1) & (s >= 11) & (s < 18))
        def _():
            zz = group((s - 11) // 2)
            f, _, _, _, block = order(zz)
            for j in range(2):
                r1_copy(zz, j).wait_recv()
                add_into(part_one.at[zz, j], sib_part.at[block(f, j)])
            r2_copy(zz).start()

        @pl.when((lax.rem(s, 2) == 0) & (s >= 16) & (s < 24))
        def _():
            zz = group((s - 16) // 2)
            _, g, _, _, _ = order(zz)
            r2_copy(zz).wait_recv()
            add_into(part_two.at[zz], part_one.at[zz, g])

            @pl.when(zz != z)
            def _():
                rz_copy(zz).start()

        @pl.when(s < 16)
        def _():
            k = grad_block(s)[3]
            backward_block(k)
            dd_copy(k).start()

        @pl.when(s >= 16)
        def _():
            chunk(s - 16)

    for d in (1, 2, 3):
        rz_arrival(lax.rem(z + d, 4)).wait_recv()

    @pl.loop(0, width // step)
    def _(n):
        rows_here = pl.ds(pl.multiple_of(n * step, step), step)
        value = part_two[z, rows_here, :].astype(jnp.float32)
        for d in (1, 2, 3):
            value = value + part_z[lax.rem(z + d, 4), rows_here, :].astype(jnp.float32)
        third_out[rows_here, :] = value

    for d in (1, 2, 3):
        rz_copy(lax.rem(z + d, 4)).wait_send()

    @pl.loop(0, 4)
    def _(zz):
        pass_along(zz, lambda copy: copy.wait_send())
        one_copy(zz).wait_send()
        for j in range(2):
            two_copy(zz, j).wait_send()
            r1_copy(zz, j).wait_send()
        r2_copy(zz).wait_send()

    @pl.loop(0, 16)
    def _(k):
        sib_copy(k).wait_send()
        dd_copy(k).wait_send()


def vocabulary_head(third_low, marks, embedding, slots, length):
    size, width = third_low.shape
    vocab_here = embedding.shape[0]
    rows = 16 * VOCAB_CUTS * -(-vocab_here // (4 * 16 * VOCAB_CUTS))
    dma = pltpu.SemaphoreType.DMA
    vmem = pl.BlockSpec(memory_space=pltpu.VMEM)
    stat = (3, 16, 2 * size)
    f32 = jnp.float32
    block = (width, size)
    small, gemb, third = pl.pallas_call(
        functools.partial(head_kernel, slots, length, vocab_here),
        out_shape=(
            jax.ShapeDtypeStruct((8, size), f32),
            jax.ShapeDtypeStruct((rows, width), BFLOAT),
            jax.ShapeDtypeStruct((width, size), f32),
        ),
        in_specs=[vmem, vmem, pl.BlockSpec(memory_space=pl.ANY)],
        out_specs=(vmem,) * 3,
        scratch_shapes=[
            pltpu.VMEM((rows, width), BFLOAT),
            pltpu.VMEM((width, rows), BFLOAT),
            pltpu.VMEM((32 * size, width), BFLOAT),
            pltpu.VMEM((rows, 2 * size), f32),
            pltpu.VMEM((rows, 32 * size), BFLOAT),
            pltpu.VMEM((16, 2) + block, BFLOAT),
            pltpu.VMEM((16,) + block, BFLOAT),
            pltpu.VMEM((4, 2) + block, BFLOAT),
            pltpu.VMEM((4,) + block, BFLOAT),
            pltpu.VMEM((4,) + block, BFLOAT),
            pltpu.VMEM((4,) + stat, f32),
            pltpu.VMEM((3,) + stat, f32),
            pltpu.VMEM((4,) + stat, f32),
        ]
        + [pltpu.VMEM((16, 2 * size), f32)] * 5
        + [dma((4,))]
        + [dma((2, 4)), dma((4,))]
        + [dma((4,))] * 2
        + [dma((4, 2))] * 2
        + [dma((16,))] * 2
        + [dma((3,))] * 4
        + [dma((16,))] * 2
        + [dma((4, 2))] * 2
        + [dma((4,))] * 4,
        compiler_params=pltpu.CompilerParams(
            collective_id=2, has_side_effects=True, vmem_limit_bytes=60 * 2**20
        ),
        name="vocabulary_head",
    )(third_low, marks, embedding)
    return small, gemb, third


def merged(part, axis, combine):
    gathered = jax.tree.map(lambda a: lax.all_gather(a, axis), part)

    def take(source):
        return jax.tree.map(lambda a: lax.dynamic_index_in_dim(a, source, 0, False), gathered)

    return lax.fori_loop(
        1, lax.axis_size(axis), lambda source, state: combine(state, take(source)), take(0)
    )


def matmul(matrix_left, matrix_right):
    return lax.dot_general(
        matrix_left,
        matrix_right,
        (((matrix_left.ndim - 1,), (0,)), ((), ())),
        preferred_element_type=jnp.float32,
    )


def matmul_back(matrix_left, matrix_right):
    return lax.dot_general(
        matrix_left,
        matrix_right,
        (((matrix_left.ndim - 1,), (1,)), ((), ())),
        preferred_element_type=jnp.float32,
    )


def outer_sum(matrix_left, matrix_right):
    flat_left = matrix_left.reshape(-1, matrix_left.shape[-1])
    flat_right = matrix_right.reshape(-1, matrix_right.shape[-1])
    return lax.dot_general(
        flat_left, flat_right, (((0,), (0,)), ((), ())), preferred_element_type=jnp.float32
    )


def split_heads(values):
    return values.reshape(values.shape[0], values.shape[1], HEADS, HEAD_DIM)


def join_heads(values):
    return values.reshape(values.shape[0], values.shape[1], HEADS * HEAD_DIM)


def exact_gelu(values):
    return jax.nn.gelu(values, approximate=False)


def norm_forward(values, gain_row, shift_row):
    centre = values - jnp.mean(values, -1, keepdims=True)
    inverse = lax.rsqrt(jnp.mean(centre * centre, -1, keepdims=True) + EPSILON)
    normed = centre * inverse
    return (normed * gain_row.astype(jnp.float32) + shift_row.astype(jnp.float32), normed, inverse)


def norm_backward(upstream, normed, inverse, gain_row):
    scaled = upstream * gain_row.astype(jnp.float32)
    mean_scaled = jnp.mean(scaled, -1, keepdims=True)
    along_normed = jnp.mean(scaled * normed, -1, keepdims=True)
    grad_values = inverse * (scaled - mean_scaled - normed * along_normed)
    model_width = upstream.shape[-1]
    grad_gain = jnp.sum((upstream * normed).reshape(-1, model_width), 0)
    grad_shift = jnp.sum(upstream.reshape(-1, model_width), 0)
    return (grad_values, grad_gain, grad_shift)


def score_block(queries, key_rows, causal):
    scores = jnp.einsum(
        "nqhd,nkhd->nhqk", queries, key_rows, preferred_element_type=jnp.float32
    ) * (1.0 / math.sqrt(HEAD_DIM))
    if causal:
        length = queries.shape[1]
        allowed = lax.broadcasted_iota(jnp.int32, (length, length), 0) >= lax.broadcasted_iota(
            jnp.int32, (length, length), 1
        )
        scores = jnp.where(allowed, scores, NEGATIVE)
    return scores


def attend(queries, key_rows, values, causal):
    scores = score_block(queries, key_rows, causal)
    highest = jnp.max(scores, -1, keepdims=True)
    totals = jnp.sum(jnp.exp(scores - highest), -1, keepdims=True)
    logsum = highest + jnp.log(totals)
    probs_low = jnp.exp(scores - logsum).astype(BFLOAT)
    context = jnp.einsum(
        "nhqk,nkhd->nqhd", probs_low, values, preferred_element_type=jnp.float32
    ).astype(BFLOAT)
    return (join_heads(context), logsum)


def attend_back(grad_context, queries, key_rows, values, logsum, causal):
    score_scale = 1.0 / math.sqrt(HEAD_DIM)
    probs_full = jnp.exp(score_block(queries, key_rows, causal) - logsum)
    grad_heads = split_heads(grad_context)
    grad_probs = jnp.einsum(
        "nqhd,nkhd->nhqk", grad_heads, values, preferred_element_type=jnp.float32
    )
    grad_values = jnp.einsum(
        "nhqk,nqhd->nkhd", probs_full.astype(BFLOAT), grad_heads, preferred_element_type=jnp.float32
    ).astype(BFLOAT)
    grad_scores = (
        probs_full * (grad_probs - jnp.sum(probs_full * grad_probs, -1, keepdims=True))
    ).astype(BFLOAT)
    grad_queries = (
        jnp.einsum("nhqk,nkhd->nqhd", grad_scores, key_rows, preferred_element_type=jnp.float32)
        * score_scale
    ).astype(BFLOAT)
    grad_keys = (
        jnp.einsum("nhqk,nqhd->nkhd", grad_scores, queries, preferred_element_type=jnp.float32)
        * score_scale
    ).astype(BFLOAT)
    return (join_heads(grad_queries), join_heads(grad_keys), join_heads(grad_values))


def layer_forward(inputs, encoded, weights):
    (
        packed_weight,
        output_weight,
        query_weight,
        memory_weight,
        cross_weight,
        expand_weight,
        reduce_weight,
        gains,
        shifts,
    ) = weights
    model_width = inputs.shape[-1]
    packed = matmul(inputs, packed_weight).astype(BFLOAT)
    context, self_logsum = attend(
        split_heads(packed[..., :model_width]),
        split_heads(packed[..., model_width : 2 * model_width]),
        split_heads(packed[..., 2 * model_width :]),
        True,
    )
    first_norm, first_normed, first_inverse = norm_forward(
        inputs.astype(jnp.float32) + matmul(context, output_weight), gains[0], shifts[0]
    )
    first_low = first_norm.astype(BFLOAT)
    cross_queries = matmul(first_low, query_weight).astype(BFLOAT)
    memory_pairs = matmul(encoded, memory_weight).astype(BFLOAT)
    cross_context, cross_logsum = attend(
        split_heads(cross_queries),
        split_heads(memory_pairs[..., :model_width]),
        split_heads(memory_pairs[..., model_width:]),
        False,
    )
    second, second_normed, second_inverse = norm_forward(
        first_norm + matmul(cross_context, cross_weight), gains[1], shifts[1]
    )
    second_low = second.astype(BFLOAT)
    inner_pre = matmul(second_low, expand_weight)
    active = exact_gelu(inner_pre).astype(BFLOAT)
    third_norm, third_normed, third_inverse = norm_forward(
        second + matmul(active, reduce_weight), gains[2], shifts[2]
    )
    stored = (
        packed,
        context,
        self_logsum,
        first_normed,
        first_inverse,
        first_low,
        cross_queries,
        memory_pairs,
        cross_context,
        cross_logsum,
        second_normed,
        second_inverse,
        second_low,
        inner_pre,
        active,
        third_normed,
        third_inverse,
    )
    return (third_norm.astype(BFLOAT), stored)


def layer_backward(grad_third, inputs, encoded, weights, stored):
    (
        packed_weight,
        output_weight,
        query_weight,
        memory_weight,
        cross_weight,
        expand_weight,
        reduce_weight,
        gains,
        shifts,
    ) = weights
    (
        packed,
        context,
        self_logsum,
        first_normed,
        first_inverse,
        first_low,
        cross_queries,
        memory_pairs,
        cross_context,
        cross_logsum,
        second_normed,
        second_inverse,
        second_low,
        inner_pre,
        active,
        third_normed,
        third_inverse,
    ) = stored
    model_width = inputs.shape[-1]
    grad_res3, gain_three, shift_three = norm_backward(
        grad_third, third_normed, third_inverse, gains[2]
    )
    grad_output = grad_res3.astype(BFLOAT)
    grad_reduce = outer_sum(active, grad_output)
    grad_active = matmul_back(grad_output, reduce_weight)
    _, gelu_pull = jax.vjp(exact_gelu, inner_pre)
    grad_inner = gelu_pull(grad_active)[0].astype(BFLOAT)
    grad_expand = outer_sum(second_low, grad_inner)
    grad_second = grad_res3 + matmul_back(grad_inner, expand_weight)
    grad_res2, gain_two, shift_two = norm_backward(
        grad_second, second_normed, second_inverse, gains[1]
    )
    grad_mixed = grad_res2.astype(BFLOAT)
    grad_cross_weight = outer_sum(cross_context, grad_mixed)
    grad_cross_context = matmul_back(grad_mixed, cross_weight).astype(BFLOAT)
    grad_cross_queries, grad_memory_keys, grad_memory_values = attend_back(
        grad_cross_context,
        split_heads(cross_queries),
        split_heads(memory_pairs[..., :model_width]),
        split_heads(memory_pairs[..., model_width:]),
        cross_logsum,
        False,
    )
    grad_query_weight = outer_sum(first_low, grad_cross_queries)
    grad_first = grad_res2 + matmul_back(grad_cross_queries, query_weight)
    grad_pairs = jnp.concatenate([grad_memory_keys, grad_memory_values], -1)
    grad_memory_weight = outer_sum(encoded, grad_pairs)
    grad_encoded = matmul_back(grad_pairs, memory_weight)
    grad_res1, gain_one, shift_one = norm_backward(
        grad_first, first_normed, first_inverse, gains[0]
    )
    grad_merged = grad_res1.astype(BFLOAT)
    grad_output_weight = outer_sum(context, grad_merged)
    grad_context = matmul_back(grad_merged, output_weight).astype(BFLOAT)
    grad_queries, grad_keys, grad_values = attend_back(
        grad_context,
        split_heads(packed[..., :model_width]),
        split_heads(packed[..., model_width : 2 * model_width]),
        split_heads(packed[..., 2 * model_width :]),
        self_logsum,
        True,
    )
    grad_packed = jnp.concatenate([grad_queries, grad_keys, grad_values], -1)
    grad_packed_weight = outer_sum(inputs, grad_packed)
    grad_inputs = grad_res1 + matmul_back(grad_packed, packed_weight)
    grad_gains = jnp.stack([gain_one, gain_two, gain_three])
    grad_shifts = jnp.stack([shift_one, shift_two, shift_three])
    return (
        grad_inputs,
        grad_encoded,
        (
            grad_packed_weight,
            grad_output_weight,
            grad_query_weight,
            grad_memory_weight,
            grad_cross_weight,
            grad_expand,
            grad_reduce,
            grad_gains,
            grad_shifts,
        ),
    )


def combine_scores(former, latter):
    highest = jnp.maximum(former[0], latter[0])
    totals = former[1] * jnp.exp(former[0] - highest) + latter[1] * jnp.exp(latter[0] - highest)
    return (highest, totals, former[2] + latter[2])


def combine_pairs(former, latter):
    highest = jnp.maximum(former[0], latter[0])
    totals = former[1] * jnp.exp(former[0] - highest) + latter[1] * jnp.exp(latter[0] - highest)
    return (highest, totals)


def per_device(
    decoder_states,
    encoder_memory,
    target_tokens,
    log_prior,
    slot_counts,
    slot_mask,
    self_packed,
    self_output,
    cross_query,
    cross_memory,
    cross_output,
    feed_expand,
    feed_reduce,
    embedding,
    norm_gains,
    norm_shifts,
):
    weights = (
        lax.all_gather(self_packed, "pa", axis=0, tiled=True),
        lax.all_gather(self_output, "pa", axis=0, tiled=True),
        lax.all_gather(cross_query, "pa", axis=0, tiled=True),
        lax.all_gather(cross_memory, "pa", axis=0, tiled=True),
        lax.all_gather(cross_output, "pa", axis=0, tiled=True),
        lax.all_gather(feed_expand, "pa", axis=0, tiled=True),
        lax.all_gather(feed_reduce, "pa", axis=0, tiled=True),
        lax.all_gather(norm_gains, "pa", axis=1, tiled=True),
        lax.all_gather(norm_shifts, "pa", axis=1, tiled=True),
    )
    questions, slots_here, length, model_width = decoder_states.shape
    mem_length = encoder_memory.shape[2]
    batch_size = questions * slots_here
    inputs = decoder_states.reshape(batch_size, length, model_width)
    encoded = encoder_memory.reshape(batch_size, mem_length, model_width)
    third_low, stored = layer_forward(inputs, encoded, weights)
    tokens_here = batch_size * length
    rows_all, tokens_all = (
        lax.all_gather(third_low.reshape(tokens_here, model_width), "pa", axis=0, tiled=True),
        lax.all_gather(target_tokens.reshape(tokens_here), "pa", axis=0, tiled=True),
    )
    total_rows = rows_all.shape[0]
    block_rows = min(total_rows, 2048)
    block_count = total_rows // block_rows
    vocab_start = lax.axis_index("pa") * embedding.shape[0]
    row_blocks = rows_all.reshape(block_count, block_rows, model_width)
    token_blocks = tokens_all.reshape(block_count, block_rows)

    def vocab_logits(hidden_rows, token_rows):
        logits = matmul_back(hidden_rows, embedding)
        column = lax.broadcasted_iota(jnp.int32, logits.shape, 1) + vocab_start
        return (logits, column == token_rows[:, None])

    def vocab_partial(pieces):
        logits, chosen = vocab_logits(pieces[0], pieces[1])
        highest = jnp.max(logits, -1)
        totals = jnp.sum(jnp.exp(logits - highest[:, None]), -1)
        picked = jnp.sum(jnp.where(chosen, logits, 0.0), -1)
        return (highest, totals, picked)

    highest, totals, picked = lax.map(vocab_partial, (row_blocks, token_blocks))
    highest, totals, picked = merged(
        (highest.reshape(total_rows), totals.reshape(total_rows), picked.reshape(total_rows)),
        "pa",
        combine_scores,
    )
    row_logsum = highest + jnp.log(totals)
    own_start = lax.axis_index("pa") * tokens_here
    own_logsum = lax.dynamic_slice_in_dim(row_logsum, own_start, tokens_here)
    own_picked = lax.dynamic_slice_in_dim(picked, own_start, tokens_here)
    log_probs = (own_picked - own_logsum).reshape(questions, slots_here, length)
    scores = log_prior + jnp.mean(log_probs, -1)
    slot_index = lax.axis_index("pa") * slots_here + lax.broadcasted_iota(
        jnp.int32, (questions, slots_here), 1
    )
    usable = (slot_mask == 1) & (slot_index < slot_counts[:, None])
    masked = jnp.where(usable, scores, NEGATIVE)
    local_high = jnp.max(masked, -1)
    local_total = jnp.sum(jnp.where(usable, jnp.exp(masked - local_high[:, None]), 0.0), -1)
    slot_high, slot_total = merged((local_high, local_total), "pa", combine_pairs)
    marginal = slot_high + jnp.log(slot_total)
    posterior = jnp.where(usable, jnp.exp(scores - marginal[:, None]), 0.0)
    loss_value = -lax.psum(jnp.sum(marginal), "pb") / (questions * lax.axis_size("pb"))
    slot_number = slots_here * lax.axis_size("pa")
    grad_prior = -(slot_number * length) * posterior
    token_grad = jnp.broadcast_to(
        (-slot_number * posterior)[:, :, None], (questions, slots_here, length)
    ).reshape(tokens_here)
    weights_all = lax.all_gather(token_grad, "pa", axis=0, tiled=True)

    def vocab_grads(accumulated, pieces):
        hidden_rows, token_rows, logsum_rows, weight_rows = pieces
        logits, chosen = vocab_logits(hidden_rows, token_rows)
        softmax_rows = jnp.exp(logits - logsum_rows[:, None])
        grad_logits = (weight_rows[:, None] * (jnp.where(chosen, 1.0, 0.0) - softmax_rows)).astype(
            BFLOAT
        )
        return (accumulated + outer_sum(grad_logits, hidden_rows), matmul(grad_logits, embedding))

    grad_embed, grad_rows = lax.scan(
        vocab_grads,
        jnp.zeros(embedding.shape, jnp.float32),
        (
            row_blocks,
            token_blocks,
            row_logsum.reshape(block_count, block_rows),
            weights_all.reshape(block_count, block_rows),
        ),
    )
    grad_third = lax.psum_scatter(
        grad_rows.reshape(total_rows, model_width).astype(BFLOAT),
        "pa",
        scatter_dimension=0,
        tiled=True,
    ).astype(jnp.float32).reshape(batch_size, length, model_width)
    grad_inputs, grad_encoded, grads = layer_backward(grad_third, inputs, encoded, weights, stored)
    shares = (
        lax.psum_scatter(grads[0].astype(BFLOAT), "pa", scatter_dimension=0, tiled=True),
        lax.psum_scatter(grads[1].astype(BFLOAT), "pa", scatter_dimension=0, tiled=True),
        lax.psum_scatter(grads[2].astype(BFLOAT), "pa", scatter_dimension=0, tiled=True),
        lax.psum_scatter(grads[3].astype(BFLOAT), "pa", scatter_dimension=0, tiled=True),
        lax.psum_scatter(grads[4].astype(BFLOAT), "pa", scatter_dimension=0, tiled=True),
        lax.psum_scatter(grads[5].astype(BFLOAT), "pa", scatter_dimension=0, tiled=True),
        lax.psum_scatter(grads[6].astype(BFLOAT), "pa", scatter_dimension=0, tiled=True),
        lax.psum_scatter(grads[7], "pa", scatter_dimension=1, tiled=True),
        lax.psum_scatter(grads[8], "pa", scatter_dimension=1, tiled=True),
    )
    outputs = lax.psum(
        (
            shares[0],
            shares[1],
            shares[2],
            shares[3],
            shares[4],
            shares[5],
            shares[6],
            shares[7],
            shares[8],
            grad_embed.astype(BFLOAT),
        ),
        "pb",
    )
    outputs = tuple(part.astype(jnp.float32) for part in outputs)
    return (
        loss_value,
        grad_inputs.reshape(decoder_states.shape),
        grad_encoded.reshape(encoder_memory.shape),
        grad_prior,
        outputs[0],
        outputs[1],
        outputs[2],
        outputs[3],
        outputs[4],
        outputs[5],
        outputs[6],
        outputs[9],
        outputs[7],
        outputs[8],
    )


def per_device_kernels(
    decoder_states,
    encoder_memory,
    target_tokens,
    log_prior,
    slot_counts,
    slot_mask,
    self_packed,
    self_output,
    cross_query,
    cross_memory,
    cross_output,
    feed_expand,
    feed_reduce,
    embedding,
    norm_gains,
    norm_shifts,
):
    shards = (
        self_packed,
        self_output,
        cross_query,
        cross_memory,
        cross_output,
        feed_expand,
        feed_reduce,
    )
    norm_rows = jnp.concatenate(
        [norm_gains, norm_shifts, jnp.zeros((2, norm_gains.shape[1]), BFLOAT)]
    ).astype(jnp.float32)
    _, slots_here, length, model_width = decoder_states.shape
    slots = slots_here * lax.axis_size("pa")
    states = decoder_states.reshape(slots_here * length, model_width)
    memory = encoder_memory.reshape(-1, model_width)
    slot_index = lax.axis_index("pa") * slots_here + jnp.arange(slots_here)
    usable = (slot_mask[0] == 1) & (slot_index < slot_counts[0])
    marks = jnp.concatenate(
        [
            target_tokens.reshape(1, slots_here * length).astype(jnp.float32),
            jnp.repeat(log_prior, length, axis=1),
            jnp.repeat(usable[None].astype(jnp.float32), length, axis=1),
            jnp.zeros((5, slots_here * length), jnp.float32),
        ]
    )
    matrices, marks, norms, kept = forward_layer(
        shards, norm_rows, marks, states, memory, length
    )
    small, grad_embed, grad_third = vocabulary_head(
        kept[-1], marks, embedding, slots, length
    )
    loss_value = small[0, 0]
    grad_prior = small[1].reshape(1, slots_here, length)[:, :, 0]
    pieces = lax.all_gather(grad_embed, "pb", axis=0)
    pieces = pieces.reshape(4 * grad_embed.shape[0], model_width)
    grad_embed = pieces[: embedding.shape[0]].astype(jnp.float32)
    shares, norm_sums, grad_inputs, grad_encoded = backward_layer(
        matrices,
        kept[:11] + kept[12:15] + (states, memory),
        kept[11],
        norms,
        grad_third,
        length,
    )
    norm_here = norm_gains.shape[1]
    norm_sums = lax.dynamic_slice_in_dim(
        norm_sums, lax.axis_index("pa") * norm_here, norm_here, axis=1
    )
    return (
        loss_value,
        grad_inputs.reshape(decoder_states.shape),
        grad_encoded.reshape(encoder_memory.shape),
        grad_prior,
    ) + shares + (grad_embed, norm_sums[:3], norm_sums[3:6])


def solution(mesh):
    own_kernels = mesh.shape["pb"] == 4 and mesh.shape["pa"] == 8
    return jax.shard_map(
        per_device_kernels if own_kernels else per_device,
        mesh=mesh,
        in_specs=(
            P("pb", "pa", None, None),
            P("pb", "pa", None, None),
            P("pb", "pa", None),
            P("pb", "pa"),
            P("pb"),
            P("pb", "pa"),
            P("pa", None),
            P("pa", None),
            P("pa", None),
            P("pa", None),
            P("pa", None),
            P("pa", None),
            P("pa", None),
            P("pa", None),
            P(None, "pa"),
            P(None, "pa"),
        ),
        out_specs=(
            P(),
            P("pb", "pa", None, None),
            P("pb", "pa", None, None),
            P("pb", "pa"),
            P("pa", None),
            P("pa", None),
            P("pa", None),
            P("pa", None),
            P("pa", None),
            P("pa", None),
            P("pa", None),
            P("pa", None),
            P(None, "pa"),
            P(None, "pa"),
        ),
        check_vma=False,
    )
```

```python
import functools
import math

import jax
import jax.numpy as jnp
from jax import lax
from jax.experimental import pallas as pl
from jax.experimental.pallas import tpu as pltpu
from jax.sharding import PartitionSpec as P

HEADS = 16
HEAD_DIM = 64


EPSILON = 1e-05
NEGATIVE = -1e30
BFLOAT = jnp.bfloat16
MESH = pl.DeviceIdType.MESH
TILE = 1024
ROWS = 128
WEIGHT_UNITS = (3, 1, 1, 2, 1, 4, 4)
UNITS = tuple((w, k) for w, n in enumerate(WEIGHT_UNITS) for k in range(n))
REDUCE_WEIGHT = 6


def whereami():
    pb = lax.axis_index("pb")
    pa = lax.axis_index("pa")
    return lax.rem(pb, 2), pb // 2, pa // 2, lax.rem(pa, 2)


def greet(peers):
    barrier = pltpu.get_barrier_semaphore()
    for peer in peers:
        pl.semaphore_signal(barrier, inc=1, device_id=peer, device_id_type=MESH)
    pl.semaphore_wait(barrier, len(peers))


def at(x, y, z, c):
    return (y * 2 + x, z * 2 + c)


def neighbours(x, y, z, c):
    return [at(1 - x, y, z, c), at(x, 1 - y, z, c), at(x, y, z, 1 - c)] + [
        at(x, y, lax.rem(z + d, 4), c) for d in (1, 2, 3)
    ]


def shard_view(ref, unit, start, size):
    weight, block = unit
    if weight == REDUCE_WEIGHT:
        return ref.at[pl.ds(block * ROWS + start, size), :]
    return ref.at[pl.ds(start, size), pl.ds(block * TILE, TILE)]


def full_view(ref, unit, place, core, start, size):
    weight, block = unit
    if weight == REDUCE_WEIGHT:
        return ref.at[place, core, block, pl.ds(start, size), :]
    return ref.at[place, core, pl.ds(start, size), pl.ds(block * TILE, TILE)]


Z_FULL = (13, 14, 15)


HOP_LAG = 1
LAG_TWO, LAG_SIBLING, LAG_LOAD, LAG_USE = 3, 6, 8, 9
SLOTS_IN_FLIGHT = 3


def dot_nn(left, right):
    return lax.dot_general(left, right, (((1,), (0,)), ((), ())), preferred_element_type=jnp.float32)


def dot_nt(left, right):
    return lax.dot_general(left, right, (((1,), (1,)), ((), ())), preferred_element_type=jnp.float32)


def dot_tn(left, right):
    return lax.dot_general(left, right, (((0,), (0,)), ((), ())), preferred_element_type=jnp.float32)


def stack_heads(pair):
    lane = lax.broadcasted_iota(jnp.int32, pair.shape, 1)
    zero = jnp.zeros_like(pair)
    return jnp.concatenate(
        [jnp.where(lane < HEAD_DIM, pair, zero), jnp.where(lane < HEAD_DIM, zero, pair)], 0
    )


def unstack_heads(stacked):
    rows = stacked.shape[0] // 2
    lane = lax.broadcasted_iota(jnp.int32, (rows, stacked.shape[1]), 1)
    return jnp.where(lane < HEAD_DIM, stacked[:rows], stacked[rows:])


def pair_scores(queries, keys, causal):
    scores = dot_nt(queries, keys) * (1.0 / math.sqrt(HEAD_DIM))
    if causal:
        length = keys.shape[0]
        row = lax.rem(lax.broadcasted_iota(jnp.int32, scores.shape, 0), length)
        column = lax.broadcasted_iota(jnp.int32, scores.shape, 1)
        scores = jnp.where(row >= column, scores, NEGATIVE)
    highest = jnp.max(scores, -1, keepdims=True)
    total = jnp.sum(jnp.exp(scores - highest), -1, keepdims=True)
    return jnp.exp(scores - (highest + jnp.log(total)))


def attend_pair(queries, keys, values, causal):
    probs = pair_scores(stack_heads(queries), keys, causal).astype(BFLOAT)
    return unstack_heads(dot_nn(probs, values)).astype(BFLOAT)


def normalise(values, gain, shift):
    centre = values - jnp.mean(values, -1, keepdims=True)
    inverse = lax.rsqrt(jnp.mean(centre * centre, -1, keepdims=True) + EPSILON)
    normed = centre * inverse
    return normed * gain + shift, normed, inverse


def forward_kernel(length, mem_length, *refs):
    shards, norm, aux, states_hbm, encoded_hbm = refs[:7], refs[7], refs[8], refs[9], refs[10]
    fulls, marks, kept_hbm = refs[11:18], refs[18], refs[19:36]
    (
        norm_full, packed, context, first_normed, first_inverse, first_low, cross_queries, pairs,
        cross_context, second_normed, second_inverse, second_low, inner, active, third_normed,
        third_inverse, third_low,
    ) = refs[36:53]
    wbuf, residual, states, encoded = refs[53:57]
    (
        local_sem, z_send, z_recv, one_send, one_recv, two_send, two_recv, d_send, d_recv,
        norm_sem, nz_send, nz_recv, nd_send, nd_recv, load_sem, ax_sem, ax_send, ax_recv,
        axz_send, axz_recv, kept_sem, input_sem,
    ) = refs[57:]
    x, y, z, c = whereami()
    greet(neighbours(x, y, z, c))
    every = slice(None)
    tokens, width = states_hbm.shape
    slots_here = tokens // length

    def copies(u):
        unit = UNITS[u]
        shard, full = shards[unit[0]], fulls[unit[0]]
        wide = u in Z_FULL
        a, b = (x, y) if u % 2 == 0 else (y, x)
        first_peer = at(x, 1 - y, z, c) if u % 2 == 0 else at(1 - x, y, z, c)
        second_peer = at(1 - x, y, z, c) if u % 2 == 0 else at(x, 1 - y, z, c)
        quarter = pl.multiple_of(64 * a + 32 * b, 32)
        half = pl.multiple_of(64 * a, 64)
        rows = (0, ROWS) if wide else (quarter, 32)
        local = pltpu.make_async_copy(
            shard_view(shard, unit, *rows), full_view(full, unit, z, c, *rows), local_sem.at[u]
        )
        def along(origin, direction):
            block = full_view(full, unit, origin, c, *rows)
            return pltpu.make_async_remote_copy(
                src_ref=block,
                dst_ref=block,
                send_sem=z_send.at[u, (direction + 1) // 2, origin],
                recv_sem=z_recv.at[u, origin],
                device_id=at(x, y, z + direction, c),
                device_id_type=MESH,
            )

        def cross(start, size, sends, recvs, peer):
            part = full_view(full, unit, every, c, start, size)
            return pltpu.make_async_remote_copy(
                src_ref=part,
                dst_ref=part,
                send_sem=sends.at[u],
                recv_sem=recvs.at[u],
                device_id=peer,
                device_id_type=MESH,
            )

        first = None if wide else cross(quarter, 32, one_send, one_recv, first_peer)
        second = None if wide else cross(half, 64, two_send, two_recv, second_peer)
        sibling = cross(0, ROWS, d_send, d_recv, at(x, y, z, 1 - c))
        load = pltpu.make_async_copy(
            full_view(full, unit, every, every, 0, ROWS),
            wbuf.at[u % SLOTS_IN_FLIGHT],
            load_sem.at[u % SLOTS_IN_FLIGHT],
        )
        return local, along, first, second, sibling, load

    def norm_copy(src, dst, send, recv, peer):
        return pltpu.make_async_remote_copy(
            src_ref=src, dst_ref=dst, send_sem=send, recv_sem=recv, device_id=peer, device_id_type=MESH
        )

    norm_local = pltpu.make_async_copy(norm, norm_full.at[z, c], norm_sem)
    norm_along = [
        norm_copy(
            norm, norm_full.at[z, c], nz_send.at[d - 1], nz_recv.at[d - 1], at(x, y, lax.rem(z + d, 4), c)
        )
        for d in (1, 2, 3)
    ]
    norm_sibling = norm_copy(
        norm_full.at[:, c], norm_full.at[:, c], nd_send, nd_recv, at(x, y, z, 1 - c)
    )
    norm_local.start()
    for copy in norm_along:
        copy.start()

    lanes = pl.ds(pl.multiple_of(c * tokens, tokens), tokens)
    aux_local = pltpu.make_async_copy(aux, marks.at[y, x, z, :, lanes], ax_sem)
    aux_local.start()
    aux_steps = [
        norm_copy(part, part, ax_send.at[n], ax_recv.at[n], peer)
        for n, (part, peer) in enumerate(
            (
                (marks.at[y, x, z, :, lanes], at(x, y, z, 1 - c)),
                (marks.at[y, x, z], at(1 - x, y, z, c)),
                (marks.at[y, :, z], at(x, 1 - y, z, c)),
            )
        )
    ]
    aux_along = [
        norm_copy(
            marks.at[:, :, z], marks.at[:, :, z], axz_send.at[d - 1], axz_recv.at[d - 1],
            at(x, y, lax.rem(z + d, 4), c),
        )
        for d in (1, 2, 3)
    ]

    kept = (
        norm_full, packed, context, first_normed, first_inverse, first_low, cross_queries, pairs,
        cross_context, second_normed, second_inverse, second_low, inner, active, third_normed,
        third_inverse, third_low,
    )

    def keep(*numbers):
        for n in numbers:
            pltpu.make_async_copy(kept[n], kept_hbm[n], kept_sem.at[n]).start()

    states_copy = pltpu.make_async_copy(states_hbm, states, input_sem.at[0])
    encoded_copy = pltpu.make_async_copy(encoded_hbm, encoded, input_sem.at[1])
    states_copy.start()
    encoded_copy.start()

    def norm_row(n):
        return jnp.concatenate(
            [norm_full[p // 2, p % 2, n : n + 1, :] for p in range(8)], 1
        )

    def times(left_ref, u, write):
        slot = u % SLOTS_IN_FLIGHT

        @pl.loop(0, 4, unroll=True)
        def _(n):
            columns = pl.ds(pl.multiple_of(n * 256, 256), 256)
            right = wbuf[slot, :, :, :, columns].reshape(TILE, 256)
            write(columns, n, dot_nn(left_ref[...], right))

    def block_columns(k, n):
        return pl.ds(pl.multiple_of(k * TILE + n * 256, 256), 256)

    def attention(queries, keys, key_start, value_start, key_length, out, causal):
        @pl.loop(0, slots_here * (width // 128), unroll=2)
        def _(n):
            slot, group = n // (width // 128), lax.rem(n, width // 128)
            lanes = pl.ds(pl.multiple_of(group * 128, 128), 128)
            key_lanes = pl.ds(pl.multiple_of(key_start + group * 128, 128), 128)
            value_lanes = pl.ds(pl.multiple_of(value_start + group * 128, 128), 128)
            query_rows = pl.ds(pl.multiple_of(slot * length, length), length)
            key_rows = pl.ds(pl.multiple_of(slot * key_length, key_length), key_length)
            out[query_rows, lanes] = attend_pair(
                queries[query_rows, lanes], keys[key_rows, key_lanes], keys[key_rows, value_lanes], causal
            )

    def finish_norm(n, value, normed_ref, inverse_ref, low_ref):
        out, normed, inverse = normalise(value, norm_row(n), norm_row(n + 3))
        normed_ref[...] = normed
        inverse_ref[...] = jnp.broadcast_to(inverse, inverse_ref.shape)
        low_ref[...] = out.astype(BFLOAT)
        return out

    def use(u):
        weight, k = UNITS[u]
        if weight == 0:
            def write(columns, n, value):
                packed[:, block_columns(k, n)] = value.astype(BFLOAT)

            times(states, u, write)
            if k == 2:
                attention(packed, packed, width, 2 * width, length, context, True)
                keep(1, 2)
        elif weight == 1:
            def write(columns, n, value):
                residual[:, columns] = states[:, columns].astype(jnp.float32) + value

            times(context, u, write)
            residual[...] = finish_norm(0, residual[...], first_normed, first_inverse, first_low)
            keep(3, 4, 5)
        elif weight == 2:
            def write(columns, n, value):
                cross_queries[:, columns] = value.astype(BFLOAT)

            times(first_low, u, write)
        elif weight == 3:
            slot = u % SLOTS_IN_FLIGHT

            @pl.loop(0, 8)
            def _(n):
                m, n = n // 4, lax.rem(n, 4)
                columns = pl.ds(pl.multiple_of(n * 256, 256), 256)
                part = encoded.shape[0] // 2
                rows_here = pl.ds(pl.multiple_of(m * part, part), part)
                right = wbuf[slot, :, :, :, columns].reshape(TILE, 256)
                pairs[rows_here, block_columns(k, n)] = dot_nn(encoded[rows_here, :], right).astype(BFLOAT)

            if k == 1:
                attention(cross_queries, pairs, 0, width, mem_length, cross_context, False)
                keep(6, 7, 8)
        elif weight == 4:
            def write(columns, n, value):
                residual[:, columns] = residual[:, columns] + value

            times(cross_context, u, write)
            residual[...] = finish_norm(1, residual[...], second_normed, second_inverse, second_low)
            keep(9, 10, 11)
        elif weight == 5:
            def write(columns, n, value):
                inner[:, block_columns(k, n)] = value
                gate = 0.5 * (1.0 + lax.erf(value * math.sqrt(0.5)))
                active[:, block_columns(k, n)] = (value * gate).astype(BFLOAT)

            times(second_low, u, write)
            if k == 3:
                keep(12, 13)
        else:
            slot = u % SLOTS_IN_FLIGHT
            blocks = active.shape[1] // (8 * ROWS)
            left = jnp.concatenate(
                [active[:, (p * blocks + k) * ROWS : (p * blocks + k + 1) * ROWS] for p in range(8)], 1
            )

            @pl.loop(0, 4, unroll=True)
            def _(n):
                columns = pl.ds(pl.multiple_of(n * 256, 256), 256)
                right = wbuf[slot, :, :, :, columns].reshape(TILE, 256)
                residual[:, columns] = residual[:, columns] + dot_nn(left, right)

            if k == blocks - 1:
                finish_norm(2, residual[...], third_normed, third_inverse, third_low)
                keep(14, 15, 16)

    count = len(UNITS)
    every_copy = [copies(u) for u in range(count)]

    def hop(u, h):
        local, along = every_copy[u][:2]
        if h == 1:
            local.wait()
        for origin, there, edge, direction in (
            (z - (h - 1), z >= h - 1, z < 3, 1),
            (z + (h - 1), z + (h - 1) <= 3, z > 0, -1),
        ):
            @pl.when(there)
            def _():
                if h > 1:
                    along(origin, direction).wait_recv()
                if h < 4:
                    @pl.when(edge)
                    def _():
                        along(origin, direction).start()

    for copies_here in every_copy:
        copies_here[0].start()
    for h in range(1, 4):
        for u in range(HOP_LAG * (4 - h)):
            hop(u, h)
    for i in range(count + LAG_USE):
        for h in range(1, 5):
            u = i + HOP_LAG * (4 - h)
            if u < count:
                hop(u, h)
        if i < count:
            first = every_copy[i][2]
            if first is not None:
                first.start()
        if 0 <= i - LAG_TWO < count:
            first, second = every_copy[i - LAG_TWO][2:4]
            if first is not None:
                first.wait_recv()
                second.start()
        if 0 <= i - LAG_SIBLING < count:
            second, sibling = every_copy[i - LAG_SIBLING][3:5]
            if second is not None:
                second.wait_recv()
            sibling.start()
        if i == 2:
            norm_local.wait()
            for copy in norm_along:
                copy.wait()
            norm_sibling.start()
        if i == 4:
            norm_sibling.wait()
            keep(0)
            states_copy.wait()
            encoded_copy.wait()
        if 5 <= i < 9:
            if i == 5:
                aux_local.wait()
            else:
                aux_steps[i - 6].wait()
            for copy in aux_steps[i - 5 : i - 4] if i < 8 else aux_along:
                copy.start()
        if i == 9:
            for copy in aux_along:
                copy.wait()
        if 0 <= i - LAG_LOAD < count:
            sibling, load = every_copy[i - LAG_LOAD][4:]
            sibling.wait_recv()
            load.start()
        if 0 <= i - LAG_USE < count:
            every_copy[i - LAG_USE][5].wait()
            use(i - LAG_USE)
    for _, along, first, second, sibling, _ in every_copy:
        for origin in range(4):
            @pl.when((origin <= z) & (z < 3))
            def _():
                along(origin, 1).wait_send()

            @pl.when((origin >= z) & (z > 0))
            def _():
                along(origin, -1).wait_send()

        if first is not None:
            first.wait_send()
            second.wait_send()
        sibling.wait_send()
    for n in range(len(kept)):
        pltpu.make_async_copy(kept[n], kept_hbm[n], kept_sem.at[n]).wait()


def forward_layer(weights, norm, aux, states, encoded, length):
    count = len(UNITS)
    shapes = []
    for w, weight in enumerate(weights):
        if w == REDUCE_WEIGHT:
            shapes.append((4, 2, weight.shape[0] // ROWS, ROWS, weight.shape[1]))
        else:
            shapes.append((4, 2) + weight.shape)
    tokens, width = states.shape
    mem_tokens = encoded.shape[0]
    mem_length = mem_tokens // (tokens // length)
    units = weights[5].shape[1]
    f32 = jnp.float32
    kept = [
        ((4, 2) + norm.shape, f32),
        ((tokens, 3 * width), BFLOAT),
        ((tokens, width), BFLOAT),
        ((tokens, width), f32),
        ((tokens, 128), f32),
        ((tokens, width), BFLOAT),
        ((tokens, width), BFLOAT),
        ((mem_tokens, 2 * width), BFLOAT),
        ((tokens, width), BFLOAT),
        ((tokens, width), f32),
        ((tokens, 128), f32),
        ((tokens, width), BFLOAT),
        ((tokens, units), f32),
        ((tokens, units), BFLOAT),
        ((tokens, width), f32),
        ((tokens, 128), f32),
        ((tokens, width), BFLOAT),
    ]
    every = pl.BlockSpec(memory_space=pl.ANY)
    dma = pltpu.SemaphoreType.DMA
    results = pl.pallas_call(
        functools.partial(forward_kernel, length, mem_length),
        out_shape=tuple(jax.ShapeDtypeStruct(shape, BFLOAT) for shape in shapes)
        + (jax.ShapeDtypeStruct((2, 2, 4, aux.shape[0], 2 * tokens), f32),)
        + tuple(jax.ShapeDtypeStruct(shape, kind) for shape, kind in kept),
        in_specs=[every] * 11,
        out_specs=(every,) * (8 + len(kept)),
        scratch_shapes=[pltpu.VMEM(shape, kind) for shape, kind in kept]
        + [
            pltpu.VMEM((SLOTS_IN_FLIGHT, 4, 2, ROWS, TILE), BFLOAT),
            pltpu.VMEM((tokens, width), f32),
            pltpu.VMEM((tokens, width), BFLOAT),
            pltpu.VMEM((mem_tokens, width), BFLOAT),
            dma((count,)),
            dma((count, 2, 4)),
            dma((count, 4)),
        ]
        + [dma((count,))] * 6
        + [dma]
        + [dma((3,))] * 2
        + [dma] * 2
        + [dma((SLOTS_IN_FLIGHT,))]
        + [dma]
        + [dma((3,))] * 4
        + [dma((len(kept),)), dma((2,))],
        compiler_params=pltpu.CompilerParams(
            collective_id=0, has_side_effects=True, vmem_limit_bytes=62 * 2**20
        ),
        name="forward_layer",
    )(*weights, norm, aux, states, encoded)
    fulls = tuple(full.reshape(-1, full.shape[-1]) for full in results[:7])
    return fulls, results[7], results[8], results[9:]


SEQUENCE = tuple((6, k) for k in range(4)) + tuple((5, k) for k in range(4)) + (
    (4, 0), (2, 0), (3, 0), (3, 1), (1, 0), (0, 0), (0, 1), (0, 2),
)
LINE_FIRST = 9
HOP_LAGS = (4, 7, 10)
LINE_LAGS = (10, 12, 14, 16, 18)
CROSS_LAGS = (2, 4, 6, 8, 10)
TURNS = 27
GATHER_TURNS = (4, 8)
READS = tuple(read for k in range(4) for read in ((6, k), (5, k))) + (
    (4, 0), (2, 0), (1, 0), (0, 0), (0, 1), (0, 2), (3, 0), (3, 1),
)


def norm_back(upstream, normed, inverse, gain):
    scaled = upstream * gain
    mean_scaled = jnp.mean(scaled, -1, keepdims=True)
    along = jnp.mean(scaled * normed, -1, keepdims=True)
    return (
        inverse * (scaled - mean_scaled - normed * along),
        jnp.sum(upstream * normed, 0, keepdims=True),
        jnp.sum(upstream, 0, keepdims=True),
    )


def attend_pair_back(grad, queries, keys, values, causal):
    scale = 1.0 / math.sqrt(HEAD_DIM)
    queries, grad = stack_heads(queries), stack_heads(grad)
    probs = pair_scores(queries, keys, causal)
    grad_probs = dot_nt(grad, values)
    grad_values = dot_tn(probs.astype(BFLOAT), grad).astype(BFLOAT)
    grad_scores = (
        probs * (grad_probs - jnp.sum(probs * grad_probs, -1, keepdims=True))
    ).astype(BFLOAT)
    grad_queries = unstack_heads(dot_nn(grad_scores, keys) * scale).astype(BFLOAT)
    grad_keys = (dot_tn(grad_scores, queries) * scale).astype(BFLOAT)
    return grad_queries, grad_keys, grad_values


def backward_kernel(length, mem_length, *refs):
    weights = refs[:7]
    kept_hbm = refs[7:23]
    inner_hbm = refs[23]
    norm_full, grad_third, gemb = refs[24:27]
    outs = refs[27:34]
    norm_out, grad_states, grad_memory, pieces, landing = refs[34:39]
    kept = refs[39:55]
    (
        wbuf, inner, stage, got, zload, one_line, two_line, one, two, line, fin,
        resid, low, grad_low, grad_context, grad_queries, grad_packed, memory_part,
        norm_here, norm_there, norm_line,
    ) = refs[55:76]
    (
        kept_sem, w_sem, inner_sem, dd_send, dd_recv, z_send, z_recv, zload_sem,
        ra_send, ra_recv, rb_send, rb_recv, rz_send, rz_recv, ag_send, ag_recv, ah_send, ah_recv,
        fin_sem, memory_sem, n_send, n_recv, nz_send, nz_recv, gemb_sem, ga_send, ga_recv,
        gb_send, gb_recv,
    ) = refs[76:]
    (
        packed, context, first_normed, first_inverse, first_low, cross_queries, pairs, cross_context,
        second_normed, second_inverse, second_low, active, third_normed, third_inverse, states, encoded,
    ) = kept
    x, y, z, c = whereami()
    greet(neighbours(x, y, z, c))
    tokens, width = states.shape
    slots_here = tokens // length
    count = len(SEQUENCE)
    blocks = active.shape[1] // (8 * ROWS)

    def keep_copy(n):
        return pltpu.make_async_copy(kept_hbm[n], kept[n], kept_sem.at[n])

    first_needed = (12, 13, 11, 10)
    for n in first_needed:
        keep_copy(n).start()
    for n in range(16):
        if n not in first_needed:
            keep_copy(n).start()

    def need(*names):
        for n in names:
            keep_copy(n).wait()

    def read_copy(n):
        weight, k = READS[n]
        if weight == REDUCE_WEIGHT:
            source = weights[weight].at[pl.ds(k * TILE, TILE), :]
        else:
            source = weights[weight].at[:, pl.ds(k * TILE, TILE)]
        return pltpu.make_async_copy(source, wbuf.at[n % 2], w_sem.at[n % 2])

    def inner_copy(k):
        return pltpu.make_async_copy(
            inner_hbm.at[:, pl.ds(k * TILE, TILE)], inner.at[k % 2], inner_sem.at[k % 2]
        )

    read_copy(0).start()
    read_copy(1).start()
    inner_copy(0).start()
    inner_copy(1).start()

    def remote(src, dst, send, recv, peer):
        return pltpu.make_async_remote_copy(
            src_ref=src, dst_ref=dst, send_sem=send, recv_sem=recv, device_id=peer, device_id_type=MESH
        )

    def norm_row(n):
        return jnp.concatenate([norm_full[p // 2, p % 2, n : n + 1, :] for p in range(8)], 1)

    def place(q):
        even = lax.rem(q, 2) == 0
        a = jnp.where(even, x, y)
        b = jnp.where(even, y, x)
        x_peer = y * 2 + (1 - x)
        y_peer = (1 - y) * 2 + x
        a_peer = (jnp.where(even, x_peer, y_peer), z * 2 + c)
        b_peer = (jnp.where(even, y_peer, x_peer), z * 2 + c)
        return a, b, a_peer, b_peer

    def piece(index, size):
        return pl.ds(pl.multiple_of(index * size, size), size)

    def total(*parts):
        out = parts[0].astype(jnp.float32)
        for part in parts[1:]:
            out = out + part.astype(jnp.float32)
        return out.astype(BFLOAT)

    pb = y * 2 + x
    pb_x, pb_y = y * 2 + 1 - x, (1 - y) * 2 + x
    vocab_rows = gemb.shape[0]
    cut = 16 * (vocab_rows // 64)
    cuts = [(n * cut, cut if n < 3 else vocab_rows - 3 * cut) for n in range(4)]

    def gather_one(n):
        rows_here = pl.ds(*cuts[n])
        peer = at(1 - x, y, z, c) if n < 2 else at(x, 1 - y, z, c)
        return remote(gemb.at[rows_here, :], pieces.at[pb, rows_here, :], ga_send.at[n], ga_recv.at[n], peer)

    def gather_two(n, j):
        rows_here = pl.ds(*cuts[n])
        peer = at(x, 1 - y, z, c) if n < 2 else at(1 - x, y, z, c)
        origin = pb if j == 0 else (pb_x if n < 2 else pb_y)
        source = gemb.at[rows_here, :] if j == 0 else pieces.at[origin, rows_here, :]
        return remote(source, pieces.at[origin, rows_here, :], gb_send.at[n, j], gb_recv.at[n, j], peer)

    gemb_copy = pltpu.make_async_copy(gemb, pieces.at[pb], gemb_sem)
    for n in (0, 2, 1, 3):
        gather_one(n).start()
    gemb_copy.start()

    def dd_copy(q):
        return remote(
            stage.at[lax.rem(q, 2), 1 - c], got.at[q], dd_send.at[q], dd_recv.at[q], at(x, y, z, 1 - c)
        )

    def line_copy(q, side, h, dest, step):
        return remote(
            got.at[q, dest], landing.at[q, side, h - 1], z_send.at[q, side, h - 1],
            z_recv.at[q, side, h - 1], at(x, y, z + step, c),
        )

    def line_sides(h):
        return (
            (0, z + 4 - h, z <= h - 1, z >= 1, 1),
            (1, z - 4 + h, z >= 4 - h, z <= 2, -1),
        )

    def line_load(q, side, h):
        return pltpu.make_async_copy(landing.at[q, side, h - 2], zload.at[side], zload_sem.at[side])

    def line_hop(q, h):
        if h > 1:
            for side, dest, there, fed, step in line_sides(h):
                @pl.when(there & fed)
                def _():
                    line_copy(q, side, h - 1, dest, step).wait_recv()
                    line_load(q, side, h).start()

        for side, dest, there, fed, step in line_sides(h):
            if h > 1:
                @pl.when(there & fed)
                def _():
                    line_load(q, side, h).wait()

                    @pl.loop(0, 8)
                    def _(j):
                        rows_here = piece(j, 16)
                        got[q, dest, rows_here, :] = total(
                            got[q, dest, rows_here, :], zload[side, rows_here, :]
                        )

            if h < 4:
                @pl.when(there)
                def _():
                    line_copy(q, side, h, dest, step).start()

    def ra_line(q):
        a, _, a_peer, _ = place(q)
        return remote(got.at[q, z, piece(1 - a, 64), :], one_line.at[q], ra_send.at[q], ra_recv.at[q], a_peer)

    def rb_line(q):
        _, b, _, b_peer = place(q)
        return remote(one_line.at[q, piece(1 - b, 32), :], two_line.at[q], rb_send.at[q], rb_recv.at[q], b_peer)

    def ra_cross(q):
        a, _, a_peer, _ = place(q)
        return remote(
            got.at[q, :, piece(1 - a, 64), :], one.at[q - LINE_FIRST], ra_send.at[q], ra_recv.at[q], a_peer
        )

    def rb_cross(q):
        _, b, _, b_peer = place(q)
        return remote(
            one.at[q - LINE_FIRST, :, piece(1 - b, 32), :], two.at[q - LINE_FIRST],
            rb_send.at[q], rb_recv.at[q], b_peer,
        )

    def rz_cross(q, d):
        other = lax.rem(z + d, 4)
        n = q - LINE_FIRST
        return remote(
            two.at[n, other], line.at[n, d - 1], rz_send.at[n, d - 1], rz_recv.at[n, d - 1],
            at(x, y, other, c),
        )

    def out_view(q, start, size):
        return shard_view(outs[SEQUENCE[q][0]], SEQUENCE[q], start, size)

    def quarter_start(q):
        a, b, _, _ = place(q)
        return pl.multiple_of(64 * a + 32 * b, 32)

    def fin_copy(q):
        return pltpu.make_async_copy(fin.at[q], out_view(q, quarter_start(q), 32), fin_sem.at[q])

    def ag_copy(q):
        return remote(
            fin.at[q], out_view(q, quarter_start(q), 32), ag_send.at[q], ag_recv.at[q], place(q)[3]
        )

    def ah_copy(q):
        a, _, a_peer, _ = place(q)
        part = out_view(q, pl.multiple_of(64 * a, 64), 64)
        return remote(part, part, ah_send.at[q], ah_recv.at[q], a_peer)

    norm_peers = (at(x, y, z, 1 - c), at(1 - x, y, z, c), at(x, 1 - y, z, c))

    def norm_copy(n):
        return remote(norm_here.at[n], norm_there.at[n], n_send.at[n], n_recv.at[n], norm_peers[n])

    def norm_line_copy(d):
        return remote(
            norm_here.at[3], norm_line.at[d - 1], nz_send.at[d - 1], nz_recv.at[d - 1],
            at(x, y, lax.rem(z + d, 4), c),
        )

    def outer(q, left, start, step, right):
        slot = q % 2

        @pl.loop(0, 8, unroll=4)
        def _(p):
            lanes = pl.ds(pl.multiple_of(start + p * step, 128), 128)
            stage[slot, lax.rem(p, 2), p // 2] = dot_tn(left[:, lanes], right()).astype(BFLOAT)

    def back_times(left, n, write):
        slot = n % 2
        read_copy(n).wait()

        @pl.loop(0, 4, unroll=True)
        def _(m):
            write(piece(m, 256), dot_nt(left[...], wbuf[slot, piece(m, 256), :]))

        if n + 2 < len(READS):
            read_copy(n + 2).start()

    def add_resid(columns, value):
        resid[:, columns] = resid[:, columns] + value

    def finish_norm(n, normed, inverse):
        value, gain, shift = norm_back(resid[...], normed[...], inverse[:, 0:1], norm_row(n))
        resid[...] = value
        low[...] = value.astype(BFLOAT)
        norm_here[0, n : n + 1, :] = gain
        norm_here[0, n + 3 : n + 4, :] = shift

    def attention_back(queries, keys, key_start, value_start, key_length, out, out_keys, causal):
        @pl.loop(0, slots_here * (width // 128), unroll=2)
        def _(n):
            slot, group = n // (width // 128), lax.rem(n, width // 128)
            lanes = piece(group, 128)
            key_lanes = pl.ds(pl.multiple_of(key_start + group * 128, 128), 128)
            value_lanes = pl.ds(pl.multiple_of(value_start + group * 128, 128), 128)
            query_rows = piece(slot, length)
            key_rows = piece(slot, key_length)
            grad_query, grad_key, grad_value = attend_pair_back(
                grad_context[query_rows, lanes],
                queries[query_rows, lanes],
                keys[key_rows, key_lanes],
                keys[key_rows, value_lanes],
                causal,
            )
            out[query_rows, lanes] = grad_query
            out_keys[key_rows, key_lanes] = grad_key
            out_keys[key_rows, value_lanes] = grad_value

    def produce(q):
        weight, k = SEQUENCE[q]
        if q == 0:
            norm_here[0] = jnp.zeros_like(norm_here[0])
            for p in range(8):
                resid[:, p * 128 : (p + 1) * 128] = grad_third[p * 128 : (p + 1) * 128, :].T
            need(12, 13, 11)
            finish_norm(2, third_normed, third_inverse)
        if weight == 6:
            outer(q, active, k * ROWS, blocks * ROWS, lambda: low[...])
        elif weight == 5:
            if k == 0:
                need(10)
            inner_copy(k).wait()

            def write(columns, value):
                pre = inner[k % 2, :, columns]
                slope = 0.5 * (1.0 + lax.erf(pre * math.sqrt(0.5))) + pre * jnp.exp(
                    -0.5 * pre * pre
                ) * (1.0 / math.sqrt(2.0 * math.pi))
                grad_low[:, columns] = (value * slope).astype(BFLOAT)

            back_times(low, 2 * k, write)
            if k + 2 < 4:
                inner_copy(k + 2).start()
            outer(q, second_low, 0, ROWS, lambda: grad_low[...])
            back_times(grad_low, 2 * k + 1, add_resid)
        elif weight == 4:
            need(8, 9, 7)
            finish_norm(1, second_normed, second_inverse)
            outer(q, cross_context, 0, ROWS, lambda: low[...])

            def write(columns, value):
                grad_context[:, columns] = value.astype(BFLOAT)

            back_times(low, 8, write)
        elif weight == 2:
            need(5, 6, 4, 2, 3)
            attention_back(cross_queries, pairs, 0, width, mem_length, grad_queries, pairs, False)
            outer(q, first_low, 0, ROWS, lambda: grad_queries[...])
            back_times(grad_queries, 9, add_resid)
            finish_norm(0, first_normed, first_inverse)
        elif weight == 3:
            if k == 0:
                need(15)
            outer(q, encoded, 0, ROWS, lambda: pairs[:, pl.ds(k * TILE, TILE)])
        elif weight == 1:
            need(1, 0, 14)
            outer(q, context, 0, ROWS, lambda: low[...])

            def write(columns, value):
                grad_context[:, columns] = value.astype(BFLOAT)

            back_times(low, 10, write)
            attention_back(packed, packed, width, 2 * width, length, grad_packed, grad_packed, True)
        else:
            def part():
                return grad_packed[:, pl.ds(k * TILE, TILE)]

            outer(q, states, 0, ROWS, part)
            back_times(grad_packed.at[:, pl.ds(k * TILE, TILE)], 11 + k, add_resid)
            if k == 2:
                grad_states[...] = resid[...]

    half = encoded.shape[0] // 2

    def memory_copy(m):
        return pltpu.make_async_copy(
            memory_part.at[m % 2],
            grad_memory.at[pl.ds(m // 4 * half, half), pl.ds(m % 4 * 256, 256)],
            memory_sem.at[m % 2],
        )

    def memory_chunk(m):
        if m == 0:
            read_copy(14).wait()
            read_copy(15).wait()
        if m >= 2:
            memory_copy(m - 2).wait()
        rows_here, columns = pl.ds(m // 4 * half, half), pl.ds(m % 4 * 256, 256)
        memory_part[m % 2] = dot_nt(pairs[rows_here, :width], wbuf[0, columns, :]) + dot_nt(
            pairs[rows_here, width:], wbuf[1, columns, :]
        )
        memory_copy(m).start()

    def each(q, action):
        for k in range(count):
            @pl.when(q == k)
            def _():
                action(k)

    def finish_block(q):
        def action(k):
            fin_copy(k).start()
            ag_copy(k).start()

        each(q, action)

    step = 16

    @pl.loop(0, TURNS)
    def _(i):
        for q in range(count):
            @pl.when(i == q)
            def _():
                if q >= 2:
                    dd_copy(q - 2).wait_send()
                produce(q)
                dd_copy(q).start()

        for n, turn in enumerate(GATHER_TURNS):
            @pl.when(i == turn)
            def _():
                for part in (n, n + 2):
                    gather_two(part, 0).start()
                    gather_one(part).wait_recv()
                    gather_two(part, 1).start()

        for m in range(8):
            @pl.when(i == count + 1 + m)
            def _():
                memory_chunk(m)

        qs = i - 1

        @pl.when((qs >= 0) & (qs < count))
        def _():
            dd_copy(qs).wait_recv()
            slot = lax.rem(qs, 2)

            @pl.loop(0, 32)
            def _(j):
                zz, rows_here = j // 8, piece(lax.rem(j, 8), step)
                got[qs, zz, rows_here, :] = total(got[qs, zz, rows_here, :], stage[slot, c, zz, rows_here, :])

            @pl.when(qs < LINE_FIRST)
            def _():
                line_hop(qs, 1)

            @pl.when(qs >= LINE_FIRST)
            def _():
                ra_cross(qs).start()

        for h in (2, 3, 4):
            qh = i - HOP_LAGS[h - 2]

            @pl.when((qh >= 0) & (qh < LINE_FIRST))
            def _():
                line_hop(qh, h)
                if h == 4:
                    ra_line(qh).start()

        q1 = i - LINE_LAGS[1]

        @pl.when((q1 >= 0) & (q1 < LINE_FIRST))
        def _():
            ra_line(q1).wait_recv()
            a = place(q1)[0]

            @pl.loop(0, 4)
            def _(j):
                rows_here = piece(j, step)
                one_line[q1, rows_here, :] = total(
                    one_line[q1, rows_here, :],
                    got[q1, z, pl.ds(pl.multiple_of(64 * a + j * step, step), step), :],
                )

            rb_line(q1).start()

        q2 = i - LINE_LAGS[2]

        @pl.when((q2 >= 0) & (q2 < LINE_FIRST))
        def _():
            rb_line(q2).wait_recv()
            b = place(q2)[1]

            @pl.loop(0, 2)
            def _(j):
                rows_here = piece(j, step)
                fin[q2, rows_here, :] = total(
                    two_line[q2, rows_here, :],
                    one_line[q2, pl.ds(pl.multiple_of(32 * b + j * step, step), step), :],
                )

            finish_block(q2)

        p0 = i - CROSS_LAGS[0]

        @pl.when((p0 >= LINE_FIRST) & (p0 < count))
        def _():
            ra_cross(p0).wait_recv()
            a = place(p0)[0]

            @pl.loop(0, 16)
            def _(j):
                zz, r = j // 4, lax.rem(j, 4)
                rows_here = piece(r, step)
                one[p0 - LINE_FIRST, zz, rows_here, :] = total(
                    one[p0 - LINE_FIRST, zz, rows_here, :],
                    got[p0, zz, pl.ds(pl.multiple_of(64 * a + r * step, step), step), :],
                )

            rb_cross(p0).start()

        p1 = i - CROSS_LAGS[1]

        @pl.when((p1 >= LINE_FIRST) & (p1 < count))
        def _():
            rb_cross(p1).wait_recv()
            b = place(p1)[1]

            @pl.loop(0, 8)
            def _(j):
                zz, r = j // 2, lax.rem(j, 2)
                rows_here = piece(r, step)
                two[p1 - LINE_FIRST, zz, rows_here, :] = total(
                    two[p1 - LINE_FIRST, zz, rows_here, :],
                    one[p1 - LINE_FIRST, zz, pl.ds(pl.multiple_of(32 * b + r * step, step), step), :],
                )

            for d in (1, 2, 3):
                rz_cross(p1, d).start()

        p2 = i - CROSS_LAGS[2]

        @pl.when((p2 >= LINE_FIRST) & (p2 < count))
        def _():
            for d in (1, 2, 3):
                rz_cross(p2, d).wait_recv()
            n = p2 - LINE_FIRST

            @pl.loop(0, 2)
            def _(j):
                rows_here = piece(j, step)
                fin[p2, rows_here, :] = total(
                    two[n, z, rows_here, :], line[n, 0, rows_here, :], line[n, 1, rows_here, :],
                    line[n, 2, rows_here, :],
                )

            finish_block(p2)

        def pass_on(k):
            ag_copy(k).wait_recv()
            fin_copy(k).wait()
            ah_copy(k).start()

        for lags, low_q, high_q in ((LINE_LAGS, 0, LINE_FIRST), (CROSS_LAGS, LINE_FIRST, count)):
            q3 = i - lags[3]

            @pl.when((q3 >= low_q) & (q3 < high_q))
            def _():
                each(q3, pass_on)

            q4 = i - lags[4]

            @pl.when((q4 >= low_q) & (q4 < high_q))
            def _():
                each(q4, lambda k: ah_copy(k).wait_recv())

        @pl.when(i == count)
        def _():
            norm_copy(0).start()

        for n in range(3):
            @pl.when(i == count + 2 * (n + 1))
            def _():
                norm_copy(n).wait_recv()
                norm_here[n + 1] = norm_here[n] + norm_there[n]
                if n < 2:
                    norm_copy(n + 1).start()
                else:
                    for d in (1, 2, 3):
                        norm_line_copy(d).start()

        @pl.when(i == count + 8)
        def _():
            for d in (1, 2, 3):
                norm_line_copy(d).wait_recv()
            norm_out[...] = ((norm_here[3] + norm_line[0]) + norm_line[1]) + norm_line[2]

    gemb_copy.wait()
    for n in range(4):
        gather_one(n).wait_send()
        for j in range(2):
            gather_two(n, j).wait()
    memory_copy(6).wait()
    memory_copy(7).wait()
    dd_copy(count - 2).wait_send()
    dd_copy(count - 1).wait_send()

    @pl.loop(0, LINE_FIRST)
    def _(q):
        for h in (1, 2, 3):
            for side, dest, there, _, step in line_sides(h):
                @pl.when(there)
                def _():
                    line_copy(q, side, h, dest, step).wait_send()

        ra_line(q).wait_send()
        rb_line(q).wait_send()

    @pl.loop(LINE_FIRST, count)
    def _(q):
        ra_cross(q).wait_send()
        rb_cross(q).wait_send()
        for d in (1, 2, 3):
            rz_cross(q, d).wait_send()

    for q in range(count):
        ag_copy(q).wait_send()
        ah_copy(q).wait_send()
    for n in range(3):
        norm_copy(n).wait_send()
        norm_line_copy(n + 1).wait_send()


def backward_layer(weights, kept, inner, norm_full, grad_third, gemb, length):
    count = len(SEQUENCE)
    f32 = jnp.float32
    tokens, width = kept[14].shape
    mem_tokens = kept[15].shape[0]
    mem_length = mem_tokens // (tokens // length)
    shapes = [(weight.shape[0] // 8, weight.shape[1]) for weight in weights]
    every = pl.BlockSpec(memory_space=pl.ANY)
    vmem = pl.BlockSpec(memory_space=pltpu.VMEM)
    dma = pltpu.SemaphoreType.DMA
    sems = dma((count,))
    crossed = count - LINE_FIRST
    *shares, norm_sum, grad_states, grad_memory, pieces, _ = pl.pallas_call(
        functools.partial(backward_kernel, length, mem_length),
        out_shape=tuple(jax.ShapeDtypeStruct(shape, BFLOAT) for shape in shapes)
        + (
            jax.ShapeDtypeStruct((8, width), f32),
            jax.ShapeDtypeStruct((tokens, width), f32),
            jax.ShapeDtypeStruct((mem_tokens, width), f32),
            jax.ShapeDtypeStruct((4,) + gemb.shape, BFLOAT),
            jax.ShapeDtypeStruct((LINE_FIRST, 2, 3, ROWS, TILE), BFLOAT),
        ),
        in_specs=[every] * 24 + [vmem] * 2 + [every],
        out_specs=(every,) * 7 + (vmem, vmem, every, every, every),
        scratch_shapes=[pltpu.VMEM(part.shape, part.dtype) for part in kept]
        + [
            pltpu.VMEM((2, TILE, TILE), BFLOAT),
            pltpu.VMEM((2, tokens, TILE), f32),
            pltpu.VMEM((2, 2, 4, ROWS, TILE), BFLOAT),
            pltpu.VMEM((count, 4, ROWS, TILE), BFLOAT),
            pltpu.VMEM((2, ROWS, TILE), BFLOAT),
            pltpu.VMEM((LINE_FIRST, 64, TILE), BFLOAT),
            pltpu.VMEM((LINE_FIRST, 32, TILE), BFLOAT),
            pltpu.VMEM((crossed, 4, 64, TILE), BFLOAT),
            pltpu.VMEM((crossed, 4, 32, TILE), BFLOAT),
            pltpu.VMEM((crossed, 3, 32, TILE), BFLOAT),
            pltpu.VMEM((count, 32, TILE), BFLOAT),
            pltpu.VMEM((tokens, width), f32),
            pltpu.VMEM((tokens, width), BFLOAT),
            pltpu.VMEM((tokens, TILE), BFLOAT),
            pltpu.VMEM((tokens, width), BFLOAT),
            pltpu.VMEM((tokens, width), BFLOAT),
            pltpu.VMEM((tokens, 3 * width), BFLOAT),
            pltpu.VMEM((2, mem_tokens // 2, 256), f32),
            pltpu.VMEM((4, 8, width), f32),
            pltpu.VMEM((3, 8, width), f32),
            pltpu.VMEM((3, 8, width), f32),
            dma((16,)), dma((2,)), dma((2,)), sems, sems,
            dma((LINE_FIRST, 2, 3)), dma((LINE_FIRST, 2, 3)), dma((2,)),
            sems, sems, sems, sems,
            dma((crossed, 3)), dma((crossed, 3)),
            sems, sems, sems, sems, sems, dma((2,)),
            dma((3,)), dma((3,)), dma((3,)), dma((3,)),
            dma, dma((4,)), dma((4,)), dma((4, 2)), dma((4, 2)),
        ],
        compiler_params=pltpu.CompilerParams(
            collective_id=1, has_side_effects=True, vmem_limit_bytes=62 * 2**20
        ),
        name="backward_layer",
    )(*weights, *kept, inner, norm_full, grad_third, gemb)
    return shares, norm_sum, grad_states, grad_memory, pieces


WIDE_ROWS = 512
WIDE_SLOTS = 4


def widen_kernel(embed_rows, *refs):
    parts, pieces, norms = refs[:7], refs[7], refs[8]
    outs, embed_out, gains_out, shifts_out = refs[9:16], refs[16], refs[17], refs[18]
    low, wide = refs[19:26], refs[26:33]
    embed_low, embed_wide, norm_here = refs[33:36]
    in_sem, out_sem, embed_in, embed_out_sem, norm_sem = refs[36:]
    here = norm_here.shape[1]
    norm_copy = pltpu.make_async_copy(
        norms.at[:, pl.ds(pl.multiple_of(lax.axis_index("pa") * here, here), here)], norm_here, norm_sem
    )
    norm_copy.start()
    full = embed_rows // WIDE_ROWS
    rest = embed_rows - full * WIDE_ROWS

    def load(n, rows):
        return pltpu.make_async_copy(
            pieces.at[pl.ds(n * WIDE_ROWS, rows), :],
            embed_low.at[n % WIDE_SLOTS, pl.ds(0, rows), :],
            embed_in.at[n % WIDE_SLOTS],
        )

    def store(n, rows):
        return pltpu.make_async_copy(
            embed_wide.at[n % WIDE_SLOTS, pl.ds(0, rows), :],
            embed_out.at[pl.ds(n * WIDE_ROWS, rows), :],
            embed_out_sem.at[n % WIDE_SLOTS],
        )

    sizes = [WIDE_ROWS] * full + [rest] * (rest > 0)
    for n in range(WIDE_SLOTS):
        load(n, sizes[n]).start()
    for n in range(7):
        pltpu.make_async_copy(parts[n], low[n], in_sem.at[n]).start()
    for n, rows in enumerate(sizes):
        load(n, rows).wait()
        if n >= WIDE_SLOTS:
            store(n - WIDE_SLOTS, sizes[n - WIDE_SLOTS]).wait()

        @pl.loop(0, rows // 16, unroll=4)
        def _(j):
            part = pl.ds(pl.multiple_of(j * 16, 16), 16)
            embed_wide[n % WIDE_SLOTS, part, :] = embed_low[n % WIDE_SLOTS, part, :].astype(jnp.float32)

        store(n, rows).start()
        if n + WIDE_SLOTS < len(sizes):
            load(n + WIDE_SLOTS, sizes[n + WIDE_SLOTS]).start()
    for n in range(7):
        pltpu.make_async_copy(parts[n], low[n], in_sem.at[n]).wait()

        @pl.loop(0, low[n].shape[0] // 16)
        def _(j):
            part = pl.ds(pl.multiple_of(j * 16, 16), 16)
            wide[n][part, :] = low[n][part, :].astype(jnp.float32)

        pltpu.make_async_copy(wide[n], outs[n], out_sem.at[n]).start()
    norm_copy.wait()
    gains_out[...] = norm_here[0:3, :]
    shifts_out[...] = norm_here[3:6, :]
    for n in range(len(sizes) - WIDE_SLOTS, len(sizes)):
        store(n, sizes[n]).wait()
    for n in range(7):
        pltpu.make_async_copy(wide[n], outs[n], out_sem.at[n]).wait()


def widen(parts, pieces, norms, embed_rows, norm_here):
    every = pl.BlockSpec(memory_space=pl.ANY)
    vmem = pl.BlockSpec(memory_space=pltpu.VMEM)
    f32 = jnp.float32
    width = pieces.shape[1]
    dma = pltpu.SemaphoreType.DMA
    results = pl.pallas_call(
        functools.partial(widen_kernel, embed_rows),
        out_shape=tuple(jax.ShapeDtypeStruct(part.shape, f32) for part in parts)
        + (jax.ShapeDtypeStruct((embed_rows, width), f32),)
        + (jax.ShapeDtypeStruct((3, norm_here), f32),) * 2,
        in_specs=[every] * 9,
        out_specs=(every,) * 8 + (vmem,) * 2,
        scratch_shapes=[pltpu.VMEM(part.shape, BFLOAT) for part in parts]
        + [pltpu.VMEM(part.shape, f32) for part in parts]
        + [
            pltpu.VMEM((WIDE_SLOTS, WIDE_ROWS, width), BFLOAT),
            pltpu.VMEM((WIDE_SLOTS, WIDE_ROWS, width), f32),
            pltpu.VMEM((8, norm_here), f32),
            dma((7,)),
            dma((7,)),
            dma((WIDE_SLOTS,)),
            dma((WIDE_SLOTS,)),
            dma,
        ],
        compiler_params=pltpu.CompilerParams(vmem_limit_bytes=60 * 2**20),
        name="widen",
    )(*parts, pieces, norms)
    return results[:7], results[7], results[8], results[9]


VOCAB_CUTS = 3
ARRIVAL_PHASES = (0, 0, 1, 0, 1, 2, 3, 0, 1, 2, 3, 1, 2, 3, 2, 3)
ARRIVAL_TURNS = (0, 1, 0, 2, 1, 0, 0, 3, 2, 1, 1, 3, 2, 2, 3, 3)
NEAREST = ((0, 1, 2, 3), (1, 0, 1, 2), (2, 2, 3, 1), (3, 3, 0, 0))


def head_kernel(slots, length, vocab_here, *refs):
    hid, marks, emb_all = refs[:3]
    small_out, gemb_out, third_out = refs[3:6]
    (
        emb, emb_t, held, logit, expo, part, sib_part, part_one, part_two, part_z,
        mine, theirs, lined, prior, usable, weight, scaled, picked_grad,
    ) = refs[6:24]
    (
        local_sem, z_send, z_recv, one_send, one_recv, two_send, two_recv, sib_send, sib_recv,
        st_send, st_recv, stz_send, stz_recv,
        dd_send, dd_recv, r1_send, r1_recv, r2_send, r2_recv, rz_send, rz_recv,
    ) = refs[24:]
    x, y, z, c = whereami()
    pb, pa = y * 2 + x, z * 2 + c
    size = hid.shape[0]
    pair = 2 * size
    width = hid.shape[1]
    rows = emb.shape[0]
    cut = rows // VOCAB_CUTS
    start = pl.multiple_of(pb * rows, 16)
    last = vocab_here - 3 * rows
    valid = jnp.where(pb == 3, last, rows)
    base = pa * vocab_here + start
    own = pb * 4 + z

    def remote(src, dst, send, recv, peer):
        return pltpu.make_async_remote_copy(
            src_ref=src, dst_ref=dst, send_sem=send, recv_sem=recv, device_id=peer, device_id_type=MESH
        )

    sibling = at(x, y, z, 1 - c)
    x_peer, y_peer = at(1 - x, y, z, c), at(x, 1 - y, z, c)

    def spot(k, core):
        return held.at[pl.ds(pl.multiple_of((k * 2 + core) * size, size), size), :]

    greet(neighbours(x, y, z, c))
    own_copy = pltpu.make_async_copy(hid, spot(own, c), local_sem.at[0])
    own_copy.start()
    emb_copy = pltpu.make_async_copy(
        emb_all.at[pl.ds(start, last), :], emb.at[pl.ds(0, last), :], local_sem.at[2]
    )
    rest_copy = pltpu.make_async_copy(
        emb_all.at[pl.ds(pl.multiple_of(jnp.minimum(start + last, vocab_here - (rows - last)), 16), rows - last), :],
        emb.at[pl.ds(last, rows - last), :],
        local_sem.at[3],
    )
    emb_copy.start()
    rest_copy.start()
    own_copy.wait()

    def up_copy(origin):
        block = spot(pb * 4 + origin, c)
        return remote(block, block, z_send.at[0, origin], z_recv.at[origin], at(x, y, z + 1, c))

    def down_copy(origin):
        block = spot(pb * 4 + origin, c)
        return remote(block, block, z_send.at[1, origin], z_recv.at[origin], at(x, y, z - 1, c))

    def pass_along(origin, action):
        @pl.when((origin <= z) & (z < 3))
        def _():
            action(up_copy(origin))

        @pl.when((origin >= z) & (z > 0))
        def _():
            action(down_copy(origin))

    def sib_copy(k):
        return remote(spot(k, c), spot(k, c), sib_send.at[k], sib_recv.at[k], sibling)

    def order(zz):
        x_first = zz < 2
        f = jnp.where(x_first, x, y)
        g = jnp.where(x_first, y, x)
        first_peer = (jnp.where(x_first, y * 2 + 1 - x, (1 - y) * 2 + x), pa)
        second_peer = (jnp.where(x_first, (1 - y) * 2 + x, y * 2 + 1 - x), pa)

        def block(first, second):
            return jnp.where(x_first, second * 2 + first, first * 2 + second) * 4 + zz

        return f, g, first_peer, second_peer, block

    def one_copy(zz):
        f, g, first_peer, _, block = order(zz)
        return remote(
            spot(block(f, g), c), spot(block(f, g), c), one_send.at[zz], one_recv.at[zz], first_peer
        )

    def two_copy(zz, j):
        f, g, _, second_peer, block = order(zz)
        k = block(f if j == 0 else 1 - f, g)
        return remote(spot(k, c), spot(k, c), two_send.at[zz, j], two_recv.at[zz, j], second_peer)

    pass_along(z, lambda copy: copy.start())
    sib_copy(own).start()
    one_copy(z).start()

    emb_copy.wait()
    rest_copy.wait()
    full_cuts = rows // 128

    def target_rows(k):
        ypart, xpart, zpart = k // 8, lax.rem(k // 4, 2), lax.rem(k, 4)
        target = marks[ypart, xpart, zpart, 0:1, :].astype(jnp.int32) - base
        return jnp.where(target < valid, target, -1)

    def row_numbers(j):
        return lax.broadcasted_iota(jnp.int32, (cut, pair), 0) + j * cut

    def cut_rows(j):
        return pl.ds(pl.multiple_of(j * cut, cut), cut)

    def token_lanes(k):
        return pl.ds(pl.multiple_of(k * pair, pair), pair)

    def forward_block(k):
        target = target_rows(k)
        block = held[token_lanes(k), :]

        def scan_logits(j, carried):
            highest, picked = carried
            value = lax.dot_general(
                emb[cut_rows(j), :], block, (((1,), (1,)), ((), ())), preferred_element_type=jnp.float32
            )
            number = row_numbers(j)
            value = jnp.where(number < valid, value, NEGATIVE)
            logit[cut_rows(j), :] = value
            return (
                jnp.maximum(highest, jnp.max(value, 0, keepdims=True)),
                picked + jnp.sum(jnp.where(number == target, value, 0.0), 0, keepdims=True),
            )

        highest, picked = lax.fori_loop(
            0,
            VOCAB_CUTS,
            scan_logits,
            (jnp.full((1, pair), NEGATIVE, jnp.float32), jnp.zeros((1, pair), jnp.float32)),
            unroll=True,
        )

        def scan_exp(j, total):
            value = jnp.exp(logit[cut_rows(j), :] - highest)
            expo[cut_rows(j), token_lanes(k)] = value.astype(BFLOAT)
            return total + jnp.sum(value, 0, keepdims=True)

        total = lax.fori_loop(
            0, VOCAB_CUTS, scan_exp, jnp.zeros((1, pair), jnp.float32), unroll=True
        )
        mine[0, 0, pl.ds(k, 1), :] = highest
        mine[0, 1, pl.ds(k, 1), :] = total
        mine[0, 2, pl.ds(k, 1), :] = picked

    def listed(values, index):
        out = values[0]
        for n in range(1, len(values)):
            out = jnp.where(index == n, values[n], out)
        return out

    def step_block(s):
        phase = listed(ARRIVAL_PHASES, s)
        t = listed(ARRIVAL_TURNS, s)
        zz = listed([listed(row, z) for row in NEAREST], t)
        f, g, _, _, block = order(zz)
        k = listed((block(f, g), block(1 - f, g), block(f, 1 - g), block(1 - f, 1 - g)), phase)
        return phase, zz, k

    @pl.loop(0, 17)
    def _(s):
        phase, zz, k = step_block(s)

        @pl.when(s < full_cuts)
        def _():
            here = pl.ds(pl.multiple_of(s * 128, 128), 128)
            emb_t[:, here] = emb[here, :].T

        if rows % 128:
            @pl.when(s == full_cuts)
            def _():
                emb_t[:, full_cuts * 128 :] = emb[full_cuts * 128 :, :].T

        @pl.when((s > 0) & (s < 16) & (phase == 0))
        def _():
            up_copy(zz).wait_recv()
            pass_along(zz, lambda copy: copy.start())
            sib_copy(k).start()
            one_copy(zz).start()

        @pl.when((s < 16) & (phase == 1))
        def _():
            one_copy(zz).wait_recv()
            sib_copy(k).start()
            for j in range(2):
                two_copy(zz, j).start()

        for j in range(2):
            @pl.when((s < 16) & (phase == 2 + j))
            def _():
                two_copy(zz, j).wait_recv()
                sib_copy(k).start()

        @pl.when(s > 0)
        def _():
            former = step_block(s - 1)[2]
            sib_copy(former).wait_recv()
            forward_block(former)

    def joined(parts):
        highest = functools.reduce(jnp.maximum, [p[0] for p in parts])
        total = functools.reduce(jnp.add, [p[1] * jnp.exp(p[0] - highest) for p in parts])
        picked = functools.reduce(jnp.add, [p[2] for p in parts])
        return highest, total, picked

    def rows_of(ref, n):
        return ref[n, 0], ref[n, 1], ref[n, 2]

    for n, (peer, side) in enumerate(((sibling, c), (x_peer, x), (y_peer, y))):
        copy = remote(mine.at[n], theirs.at[n], st_send.at[n], st_recv.at[n], peer)
        copy.start()
        copy.wait()
        here, there = rows_of(mine, n), rows_of(theirs, n)
        early = tuple(jnp.where(side == 0, a, b) for a, b in zip(here, there))
        late = tuple(jnp.where(side == 0, b, a) for a, b in zip(here, there))
        for r, value in enumerate(joined((early, late))):
            mine[n + 1, r] = value

    def stat_copy(d):
        other = lax.rem(z + d, 4)
        return remote(mine.at[3], lined.at[z], stz_send.at[d - 1], stz_recv.at[d - 1], at(x, y, other, c))

    for d in (1, 2, 3):
        stat_copy(d).start()
    for r in range(3):
        lined[z, r] = mine[3, r]
    for d in (1, 2, 3):
        stat_copy(d).wait()
    highest, total, picked = joined([rows_of(lined, n) for n in range(4)])
    logsum = highest + jnp.log(total)
    log_probs = picked - logsum
    for k in range(16):
        prior[k : k + 1, :] = marks[k // 8, (k // 4) % 2, k % 4, 1:2, :]
        usable[k : k + 1, :] = marks[k // 8, (k // 4) % 2, k % 4, 2:3, :]
    lane = lax.broadcasted_iota(jnp.int32, (16, pair), 1) // length
    mean = jnp.zeros((16, pair), jnp.float32)
    for n in range(pair // length):
        inside = lane == n
        slot_sum = jnp.sum(jnp.where(inside, log_probs, 0.0), 1, keepdims=True)
        mean = jnp.where(inside, slot_sum * (1.0 / length), mean)
    scores = prior[...] + mean
    counted = usable[...] > 0.5
    masked = jnp.where(counted, scores, NEGATIVE)
    question = lax.broadcasted_iota(jnp.int32, (16, pair), 0) // 4
    marginal = jnp.zeros((16, pair), jnp.float32)
    loss = jnp.zeros((1, 1), jnp.float32)
    for n in range(4):
        inside = question == n
        high = jnp.max(
            jnp.max(jnp.where(inside, masked, NEGATIVE), 1, keepdims=True), 0, keepdims=True
        )
        terms = jnp.where(inside & counted, jnp.exp(masked - high), 0.0)
        mass = jnp.sum(jnp.sum(terms, 1, keepdims=True), 0, keepdims=True) * (1.0 / length)
        value = high + jnp.log(mass)
        marginal = jnp.where(inside, value, marginal)
        loss = loss + value
    posterior = jnp.where(counted, jnp.exp(scores - marginal), 0.0)
    token_weight = -float(slots) * posterior
    weight[...] = posterior
    scaled[...] = token_weight * jnp.exp(mine[0, 0] - logsum)
    picked_grad[...] = token_weight * (1.0 - jnp.exp(log_probs))
    small_out[...] = jnp.broadcast_to(loss * (-1.0 / 4), small_out.shape)
    own_row = weight[pl.ds(own, 1), :]
    own_row = jnp.where(c == 0, own_row[:, :size], own_row[:, size:])
    small_out[1:2, :] = own_row * (-float(slots * length))

    def backward_block(k):
        target = target_rows(k)
        hit = picked_grad[pl.ds(k, 1), :]
        scale = scaled[pl.ds(k, 1), :]

        def make(j, carried):
            value = expo[cut_rows(j), token_lanes(k)].astype(jnp.float32)
            grad = jnp.where(row_numbers(j) == target, hit, -(value * scale))
            expo[cut_rows(j), token_lanes(k)] = grad.astype(BFLOAT)
            return carried

        lax.fori_loop(0, VOCAB_CUTS, make, 0, unroll=True)

        def to_rows(n, carried):
            cut_width = pl.ds(pl.multiple_of(n * 256, 256), 256)
            value = lax.dot_general(
                emb_t[cut_width, :],
                expo[:, token_lanes(k)],
                (((1,), (0,)), ((), ())),
                preferred_element_type=jnp.float32,
            ).astype(BFLOAT)
            part[k, 0, cut_width, :] = value[:, :size]
            part[k, 1, cut_width, :] = value[:, size:]
            return carried

        lax.fori_loop(0, width // 256, to_rows, 0, unroll=True)

    def dd_copy(k):
        return remote(part.at[k, 1 - c], sib_part.at[k], dd_send.at[k], dd_recv.at[k], sibling)

    def r1_copy(zz, j):
        f, _, first_peer, _, block = order(zz)
        return remote(
            sib_part.at[block(1 - f, j)], part_one.at[zz, j], r1_send.at[zz, j], r1_recv.at[zz, j],
            first_peer,
        )

    def r2_copy(zz):
        _, g, _, second_peer, _ = order(zz)
        return remote(part_one.at[zz, 1 - g], part_two.at[zz], r2_send.at[zz], r2_recv.at[zz], second_peer)

    def rz_copy(zz):
        return remote(part_two.at[zz], part_z.at[z], rz_send.at[zz], rz_recv.at[z], at(x, y, zz, c))

    def rz_arrival(zz):
        return remote(part_two.at[zz], part_z.at[zz], rz_send.at[zz], rz_recv.at[zz], at(x, y, zz, c))

    step = 128

    def add_into(target_ref, other_ref):
        @pl.loop(0, width // step)
        def _(n):
            rows_here = pl.ds(pl.multiple_of(n * step, step), step)
            target_ref[rows_here, :] = (
                target_ref[rows_here, :].astype(jnp.float32) + other_ref[rows_here, :].astype(jnp.float32)
            ).astype(BFLOAT)

    def group(n):
        return lax.rem(n, 2) * 2 + n // 2

    def chunk(q):
        j, n = q // 4, lax.rem(q, 4)
        columns = pl.ds(pl.multiple_of(n * 256, 256), 256)
        gemb_out[cut_rows(j), columns] = lax.dot_general(
            expo[cut_rows(j), :],
            held[:, columns],
            (((1,), (0,)), ((), ())),
            preferred_element_type=jnp.float32,
        ).astype(BFLOAT)

    def grad_block(s):
        leaves = s < 8
        zz = group(lax.rem(s, 8) // 2)
        j = lax.rem(s, 2)
        f, _, _, _, block = order(zz)
        return leaves, zz, j, block(jnp.where(leaves, 1 - f, f), j)

    @pl.loop(0, 28)
    def _(s):
        @pl.when((s >= 2) & (s < 18))
        def _():
            leaves, zz, turn, k = grad_block(s - 2)
            dd_copy(k).wait_recv()
            add_into(sib_part.at[k], part.at[k, c])
            for j in range(2):
                @pl.when(leaves & (turn == j))
                def _():
                    r1_copy(zz, j).start()

        @pl.when((lax.rem(s, 2) == 1) & (s >= 11) & (s < 18))
        def _():
            zz = group((s - 11) // 2)
            f, _, _, _, block = order(zz)
            for j in range(2):
                r1_copy(zz, j).wait_recv()
                add_into(part_one.at[zz, j], sib_part.at[block(f, j)])
            r2_copy(zz).start()

        @pl.when((lax.rem(s, 2) == 0) & (s >= 16) & (s < 24))
        def _():
            zz = group((s - 16) // 2)
            _, g, _, _, _ = order(zz)
            r2_copy(zz).wait_recv()
            add_into(part_two.at[zz], part_one.at[zz, g])

            @pl.when(zz != z)
            def _():
                rz_copy(zz).start()

        @pl.when(s < 16)
        def _():
            k = grad_block(s)[3]
            backward_block(k)
            dd_copy(k).start()

        @pl.when(s >= 16)
        def _():
            chunk(s - 16)

    for d in (1, 2, 3):
        rz_arrival(lax.rem(z + d, 4)).wait_recv()

    @pl.loop(0, width // step)
    def _(n):
        rows_here = pl.ds(pl.multiple_of(n * step, step), step)
        value = part_two[z, rows_here, :].astype(jnp.float32)
        for d in (1, 2, 3):
            value = value + part_z[lax.rem(z + d, 4), rows_here, :].astype(jnp.float32)
        third_out[rows_here, :] = value

    for d in (1, 2, 3):
        rz_copy(lax.rem(z + d, 4)).wait_send()

    @pl.loop(0, 4)
    def _(zz):
        pass_along(zz, lambda copy: copy.wait_send())
        one_copy(zz).wait_send()
        for j in range(2):
            two_copy(zz, j).wait_send()
            r1_copy(zz, j).wait_send()
        r2_copy(zz).wait_send()

    @pl.loop(0, 16)
    def _(k):
        sib_copy(k).wait_send()
        dd_copy(k).wait_send()


def vocabulary_head(third_low, marks, embedding, slots, length):
    size, width = third_low.shape
    vocab_here = embedding.shape[0]
    rows = 16 * VOCAB_CUTS * -(-vocab_here // (4 * 16 * VOCAB_CUTS))
    dma = pltpu.SemaphoreType.DMA
    vmem = pl.BlockSpec(memory_space=pltpu.VMEM)
    stat = (3, 16, 2 * size)
    f32 = jnp.float32
    block = (width, size)
    small, gemb, third = pl.pallas_call(
        functools.partial(head_kernel, slots, length, vocab_here),
        out_shape=(
            jax.ShapeDtypeStruct((8, size), f32),
            jax.ShapeDtypeStruct((rows, width), BFLOAT),
            jax.ShapeDtypeStruct((width, size), f32),
        ),
        in_specs=[vmem, vmem, pl.BlockSpec(memory_space=pl.ANY)],
        out_specs=(vmem,) * 3,
        scratch_shapes=[
            pltpu.VMEM((rows, width), BFLOAT),
            pltpu.VMEM((width, rows), BFLOAT),
            pltpu.VMEM((32 * size, width), BFLOAT),
            pltpu.VMEM((rows, 2 * size), f32),
            pltpu.VMEM((rows, 32 * size), BFLOAT),
            pltpu.VMEM((16, 2) + block, BFLOAT),
            pltpu.VMEM((16,) + block, BFLOAT),
            pltpu.VMEM((4, 2) + block, BFLOAT),
            pltpu.VMEM((4,) + block, BFLOAT),
            pltpu.VMEM((4,) + block, BFLOAT),
            pltpu.VMEM((4,) + stat, f32),
            pltpu.VMEM((3,) + stat, f32),
            pltpu.VMEM((4,) + stat, f32),
        ]
        + [pltpu.VMEM((16, 2 * size), f32)] * 5
        + [dma((4,))]
        + [dma((2, 4)), dma((4,))]
        + [dma((4,))] * 2
        + [dma((4, 2))] * 2
        + [dma((16,))] * 2
        + [dma((3,))] * 4
        + [dma((16,))] * 2
        + [dma((4, 2))] * 2
        + [dma((4,))] * 4,
        compiler_params=pltpu.CompilerParams(
            collective_id=2, has_side_effects=True, vmem_limit_bytes=60 * 2**20
        ),
        name="vocabulary_head",
    )(third_low, marks, embedding)
    return small, gemb, third


def merged(part, axis, combine):
    gathered = jax.tree.map(lambda a: lax.all_gather(a, axis), part)

    def take(source):
        return jax.tree.map(lambda a: lax.dynamic_index_in_dim(a, source, 0, False), gathered)

    return lax.fori_loop(
        1, lax.axis_size(axis), lambda source, state: combine(state, take(source)), take(0)
    )


def matmul(matrix_left, matrix_right):
    return lax.dot_general(
        matrix_left,
        matrix_right,
        (((matrix_left.ndim - 1,), (0,)), ((), ())),
        preferred_element_type=jnp.float32,
    )


def matmul_back(matrix_left, matrix_right):
    return lax.dot_general(
        matrix_left,
        matrix_right,
        (((matrix_left.ndim - 1,), (1,)), ((), ())),
        preferred_element_type=jnp.float32,
    )


def outer_sum(matrix_left, matrix_right):
    flat_left = matrix_left.reshape(-1, matrix_left.shape[-1])
    flat_right = matrix_right.reshape(-1, matrix_right.shape[-1])
    return lax.dot_general(
        flat_left, flat_right, (((0,), (0,)), ((), ())), preferred_element_type=jnp.float32
    )


def split_heads(values):
    return values.reshape(values.shape[0], values.shape[1], HEADS, HEAD_DIM)


def join_heads(values):
    return values.reshape(values.shape[0], values.shape[1], HEADS * HEAD_DIM)


def exact_gelu(values):
    return jax.nn.gelu(values, approximate=False)


def norm_forward(values, gain_row, shift_row):
    centre = values - jnp.mean(values, -1, keepdims=True)
    inverse = lax.rsqrt(jnp.mean(centre * centre, -1, keepdims=True) + EPSILON)
    normed = centre * inverse
    return (normed * gain_row.astype(jnp.float32) + shift_row.astype(jnp.float32), normed, inverse)


def norm_backward(upstream, normed, inverse, gain_row):
    scaled = upstream * gain_row.astype(jnp.float32)
    mean_scaled = jnp.mean(scaled, -1, keepdims=True)
    along_normed = jnp.mean(scaled * normed, -1, keepdims=True)
    grad_values = inverse * (scaled - mean_scaled - normed * along_normed)
    model_width = upstream.shape[-1]
    grad_gain = jnp.sum((upstream * normed).reshape(-1, model_width), 0)
    grad_shift = jnp.sum(upstream.reshape(-1, model_width), 0)
    return (grad_values, grad_gain, grad_shift)


def score_block(queries, key_rows, causal):
    scores = jnp.einsum(
        "nqhd,nkhd->nhqk", queries, key_rows, preferred_element_type=jnp.float32
    ) * (1.0 / math.sqrt(HEAD_DIM))
    if causal:
        length = queries.shape[1]
        allowed = lax.broadcasted_iota(jnp.int32, (length, length), 0) >= lax.broadcasted_iota(
            jnp.int32, (length, length), 1
        )
        scores = jnp.where(allowed, scores, NEGATIVE)
    return scores


def attend(queries, key_rows, values, causal):
    scores = score_block(queries, key_rows, causal)
    highest = jnp.max(scores, -1, keepdims=True)
    totals = jnp.sum(jnp.exp(scores - highest), -1, keepdims=True)
    logsum = highest + jnp.log(totals)
    probs_low = jnp.exp(scores - logsum).astype(BFLOAT)
    context = jnp.einsum(
        "nhqk,nkhd->nqhd", probs_low, values, preferred_element_type=jnp.float32
    ).astype(BFLOAT)
    return (join_heads(context), logsum)


def attend_back(grad_context, queries, key_rows, values, logsum, causal):
    score_scale = 1.0 / math.sqrt(HEAD_DIM)
    probs_full = jnp.exp(score_block(queries, key_rows, causal) - logsum)
    grad_heads = split_heads(grad_context)
    grad_probs = jnp.einsum(
        "nqhd,nkhd->nhqk", grad_heads, values, preferred_element_type=jnp.float32
    )
    grad_values = jnp.einsum(
        "nhqk,nqhd->nkhd", probs_full.astype(BFLOAT), grad_heads, preferred_element_type=jnp.float32
    ).astype(BFLOAT)
    grad_scores = (
        probs_full * (grad_probs - jnp.sum(probs_full * grad_probs, -1, keepdims=True))
    ).astype(BFLOAT)
    grad_queries = (
        jnp.einsum("nhqk,nkhd->nqhd", grad_scores, key_rows, preferred_element_type=jnp.float32)
        * score_scale
    ).astype(BFLOAT)
    grad_keys = (
        jnp.einsum("nhqk,nqhd->nkhd", grad_scores, queries, preferred_element_type=jnp.float32)
        * score_scale
    ).astype(BFLOAT)
    return (join_heads(grad_queries), join_heads(grad_keys), join_heads(grad_values))


def layer_forward(inputs, encoded, weights):
    (
        packed_weight,
        output_weight,
        query_weight,
        memory_weight,
        cross_weight,
        expand_weight,
        reduce_weight,
        gains,
        shifts,
    ) = weights
    model_width = inputs.shape[-1]
    packed = matmul(inputs, packed_weight).astype(BFLOAT)
    context, self_logsum = attend(
        split_heads(packed[..., :model_width]),
        split_heads(packed[..., model_width : 2 * model_width]),
        split_heads(packed[..., 2 * model_width :]),
        True,
    )
    first_norm, first_normed, first_inverse = norm_forward(
        inputs.astype(jnp.float32) + matmul(context, output_weight), gains[0], shifts[0]
    )
    first_low = first_norm.astype(BFLOAT)
    cross_queries = matmul(first_low, query_weight).astype(BFLOAT)
    memory_pairs = matmul(encoded, memory_weight).astype(BFLOAT)
    cross_context, cross_logsum = attend(
        split_heads(cross_queries),
        split_heads(memory_pairs[..., :model_width]),
        split_heads(memory_pairs[..., model_width:]),
        False,
    )
    second, second_normed, second_inverse = norm_forward(
        first_norm + matmul(cross_context, cross_weight), gains[1], shifts[1]
    )
    second_low = second.astype(BFLOAT)
    inner_pre = matmul(second_low, expand_weight)
    active = exact_gelu(inner_pre).astype(BFLOAT)
    third_norm, third_normed, third_inverse = norm_forward(
        second + matmul(active, reduce_weight), gains[2], shifts[2]
    )
    stored = (
        packed,
        context,
        self_logsum,
        first_normed,
        first_inverse,
        first_low,
        cross_queries,
        memory_pairs,
        cross_context,
        cross_logsum,
        second_normed,
        second_inverse,
        second_low,
        inner_pre,
        active,
        third_normed,
        third_inverse,
    )
    return (third_norm.astype(BFLOAT), stored)


def layer_backward(grad_third, inputs, encoded, weights, stored):
    (
        packed_weight,
        output_weight,
        query_weight,
        memory_weight,
        cross_weight,
        expand_weight,
        reduce_weight,
        gains,
        shifts,
    ) = weights
    (
        packed,
        context,
        self_logsum,
        first_normed,
        first_inverse,
        first_low,
        cross_queries,
        memory_pairs,
        cross_context,
        cross_logsum,
        second_normed,
        second_inverse,
        second_low,
        inner_pre,
        active,
        third_normed,
        third_inverse,
    ) = stored
    model_width = inputs.shape[-1]
    grad_res3, gain_three, shift_three = norm_backward(
        grad_third, third_normed, third_inverse, gains[2]
    )
    grad_output = grad_res3.astype(BFLOAT)
    grad_reduce = outer_sum(active, grad_output)
    grad_active = matmul_back(grad_output, reduce_weight)
    _, gelu_pull = jax.vjp(exact_gelu, inner_pre)
    grad_inner = gelu_pull(grad_active)[0].astype(BFLOAT)
    grad_expand = outer_sum(second_low, grad_inner)
    grad_second = grad_res3 + matmul_back(grad_inner, expand_weight)
    grad_res2, gain_two, shift_two = norm_backward(
        grad_second, second_normed, second_inverse, gains[1]
    )
    grad_mixed = grad_res2.astype(BFLOAT)
    grad_cross_weight = outer_sum(cross_context, grad_mixed)
    grad_cross_context = matmul_back(grad_mixed, cross_weight).astype(BFLOAT)
    grad_cross_queries, grad_memory_keys, grad_memory_values = attend_back(
        grad_cross_context,
        split_heads(cross_queries),
        split_heads(memory_pairs[..., :model_width]),
        split_heads(memory_pairs[..., model_width:]),
        cross_logsum,
        False,
    )
    grad_query_weight = outer_sum(first_low, grad_cross_queries)
    grad_first = grad_res2 + matmul_back(grad_cross_queries, query_weight)
    grad_pairs = jnp.concatenate([grad_memory_keys, grad_memory_values], -1)
    grad_memory_weight = outer_sum(encoded, grad_pairs)
    grad_encoded = matmul_back(grad_pairs, memory_weight)
    grad_res1, gain_one, shift_one = norm_backward(
        grad_first, first_normed, first_inverse, gains[0]
    )
    grad_merged = grad_res1.astype(BFLOAT)
    grad_output_weight = outer_sum(context, grad_merged)
    grad_context = matmul_back(grad_merged, output_weight).astype(BFLOAT)
    grad_queries, grad_keys, grad_values = attend_back(
        grad_context,
        split_heads(packed[..., :model_width]),
        split_heads(packed[..., model_width : 2 * model_width]),
        split_heads(packed[..., 2 * model_width :]),
        self_logsum,
        True,
    )
    grad_packed = jnp.concatenate([grad_queries, grad_keys, grad_values], -1)
    grad_packed_weight = outer_sum(inputs, grad_packed)
    grad_inputs = grad_res1 + matmul_back(grad_packed, packed_weight)
    grad_gains = jnp.stack([gain_one, gain_two, gain_three])
    grad_shifts = jnp.stack([shift_one, shift_two, shift_three])
    return (
        grad_inputs,
        grad_encoded,
        (
            grad_packed_weight,
            grad_output_weight,
            grad_query_weight,
            grad_memory_weight,
            grad_cross_weight,
            grad_expand,
            grad_reduce,
            grad_gains,
            grad_shifts,
        ),
    )


def combine_scores(former, latter):
    highest = jnp.maximum(former[0], latter[0])
    totals = former[1] * jnp.exp(former[0] - highest) + latter[1] * jnp.exp(latter[0] - highest)
    return (highest, totals, former[2] + latter[2])


def combine_pairs(former, latter):
    highest = jnp.maximum(former[0], latter[0])
    totals = former[1] * jnp.exp(former[0] - highest) + latter[1] * jnp.exp(latter[0] - highest)
    return (highest, totals)


def per_device(
    decoder_states,
    encoder_memory,
    target_tokens,
    log_prior,
    slot_counts,
    slot_mask,
    self_packed,
    self_output,
    cross_query,
    cross_memory,
    cross_output,
    feed_expand,
    feed_reduce,
    embedding,
    norm_gains,
    norm_shifts,
):
    weights = (
        lax.all_gather(self_packed, "pa", axis=0, tiled=True),
        lax.all_gather(self_output, "pa", axis=0, tiled=True),
        lax.all_gather(cross_query, "pa", axis=0, tiled=True),
        lax.all_gather(cross_memory, "pa", axis=0, tiled=True),
        lax.all_gather(cross_output, "pa", axis=0, tiled=True),
        lax.all_gather(feed_expand, "pa", axis=0, tiled=True),
        lax.all_gather(feed_reduce, "pa", axis=0, tiled=True),
        lax.all_gather(norm_gains, "pa", axis=1, tiled=True),
        lax.all_gather(norm_shifts, "pa", axis=1, tiled=True),
    )
    questions, slots_here, length, model_width = decoder_states.shape
    mem_length = encoder_memory.shape[2]
    batch_size = questions * slots_here
    inputs = decoder_states.reshape(batch_size, length, model_width)
    encoded = encoder_memory.reshape(batch_size, mem_length, model_width)
    third_low, stored = layer_forward(inputs, encoded, weights)
    tokens_here = batch_size * length
    rows_all, tokens_all = (
        lax.all_gather(third_low.reshape(tokens_here, model_width), "pa", axis=0, tiled=True),
        lax.all_gather(target_tokens.reshape(tokens_here), "pa", axis=0, tiled=True),
    )
    total_rows = rows_all.shape[0]
    block_rows = min(total_rows, 2048)
    block_count = total_rows // block_rows
    vocab_start = lax.axis_index("pa") * embedding.shape[0]
    row_blocks = rows_all.reshape(block_count, block_rows, model_width)
    token_blocks = tokens_all.reshape(block_count, block_rows)

    def vocab_logits(hidden_rows, token_rows):
        logits = matmul_back(hidden_rows, embedding)
        column = lax.broadcasted_iota(jnp.int32, logits.shape, 1) + vocab_start
        return (logits, column == token_rows[:, None])

    def vocab_partial(pieces):
        logits, chosen = vocab_logits(pieces[0], pieces[1])
        highest = jnp.max(logits, -1)
        totals = jnp.sum(jnp.exp(logits - highest[:, None]), -1)
        picked = jnp.sum(jnp.where(chosen, logits, 0.0), -1)
        return (highest, totals, picked)

    highest, totals, picked = lax.map(vocab_partial, (row_blocks, token_blocks))
    highest, totals, picked = merged(
        (highest.reshape(total_rows), totals.reshape(total_rows), picked.reshape(total_rows)),
        "pa",
        combine_scores,
    )
    row_logsum = highest + jnp.log(totals)
    own_start = lax.axis_index("pa") * tokens_here
    own_logsum = lax.dynamic_slice_in_dim(row_logsum, own_start, tokens_here)
    own_picked = lax.dynamic_slice_in_dim(picked, own_start, tokens_here)
    log_probs = (own_picked - own_logsum).reshape(questions, slots_here, length)
    scores = log_prior + jnp.mean(log_probs, -1)
    slot_index = lax.axis_index("pa") * slots_here + lax.broadcasted_iota(
        jnp.int32, (questions, slots_here), 1
    )
    usable = (slot_mask == 1) & (slot_index < slot_counts[:, None])
    masked = jnp.where(usable, scores, NEGATIVE)
    local_high = jnp.max(masked, -1)
    local_total = jnp.sum(jnp.where(usable, jnp.exp(masked - local_high[:, None]), 0.0), -1)
    slot_high, slot_total = merged((local_high, local_total), "pa", combine_pairs)
    marginal = slot_high + jnp.log(slot_total)
    posterior = jnp.where(usable, jnp.exp(scores - marginal[:, None]), 0.0)
    loss_value = -lax.psum(jnp.sum(marginal), "pb") / (questions * lax.axis_size("pb"))
    slot_number = slots_here * lax.axis_size("pa")
    grad_prior = -(slot_number * length) * posterior
    token_grad = jnp.broadcast_to(
        (-slot_number * posterior)[:, :, None], (questions, slots_here, length)
    ).reshape(tokens_here)
    weights_all = lax.all_gather(token_grad, "pa", axis=0, tiled=True)

    def vocab_grads(accumulated, pieces):
        hidden_rows, token_rows, logsum_rows, weight_rows = pieces
        logits, chosen = vocab_logits(hidden_rows, token_rows)
        softmax_rows = jnp.exp(logits - logsum_rows[:, None])
        grad_logits = (weight_rows[:, None] * (jnp.where(chosen, 1.0, 0.0) - softmax_rows)).astype(
            BFLOAT
        )
        return (accumulated + outer_sum(grad_logits, hidden_rows), matmul(grad_logits, embedding))

    grad_embed, grad_rows = lax.scan(
        vocab_grads,
        jnp.zeros(embedding.shape, jnp.float32),
        (
            row_blocks,
            token_blocks,
            row_logsum.reshape(block_count, block_rows),
            weights_all.reshape(block_count, block_rows),
        ),
    )
    grad_third = lax.psum_scatter(
        grad_rows.reshape(total_rows, model_width).astype(BFLOAT),
        "pa",
        scatter_dimension=0,
        tiled=True,
    ).astype(jnp.float32).reshape(batch_size, length, model_width)
    grad_inputs, grad_encoded, grads = layer_backward(grad_third, inputs, encoded, weights, stored)
    shares = (
        lax.psum_scatter(grads[0].astype(BFLOAT), "pa", scatter_dimension=0, tiled=True),
        lax.psum_scatter(grads[1].astype(BFLOAT), "pa", scatter_dimension=0, tiled=True),
        lax.psum_scatter(grads[2].astype(BFLOAT), "pa", scatter_dimension=0, tiled=True),
        lax.psum_scatter(grads[3].astype(BFLOAT), "pa", scatter_dimension=0, tiled=True),
        lax.psum_scatter(grads[4].astype(BFLOAT), "pa", scatter_dimension=0, tiled=True),
        lax.psum_scatter(grads[5].astype(BFLOAT), "pa", scatter_dimension=0, tiled=True),
        lax.psum_scatter(grads[6].astype(BFLOAT), "pa", scatter_dimension=0, tiled=True),
        lax.psum_scatter(grads[7], "pa", scatter_dimension=1, tiled=True),
        lax.psum_scatter(grads[8], "pa", scatter_dimension=1, tiled=True),
    )
    outputs = lax.psum(
        (
            shares[0],
            shares[1],
            shares[2],
            shares[3],
            shares[4],
            shares[5],
            shares[6],
            shares[7],
            shares[8],
            grad_embed.astype(BFLOAT),
        ),
        "pb",
    )
    outputs = tuple(part.astype(jnp.float32) for part in outputs)
    return (
        loss_value,
        grad_inputs.reshape(decoder_states.shape),
        grad_encoded.reshape(encoder_memory.shape),
        grad_prior,
        outputs[0],
        outputs[1],
        outputs[2],
        outputs[3],
        outputs[4],
        outputs[5],
        outputs[6],
        outputs[9],
        outputs[7],
        outputs[8],
    )


def per_device_kernels(
    decoder_states,
    encoder_memory,
    target_tokens,
    log_prior,
    slot_counts,
    slot_mask,
    self_packed,
    self_output,
    cross_query,
    cross_memory,
    cross_output,
    feed_expand,
    feed_reduce,
    embedding,
    norm_gains,
    norm_shifts,
):
    shards = (
        self_packed,
        self_output,
        cross_query,
        cross_memory,
        cross_output,
        feed_expand,
        feed_reduce,
    )
    norm_rows = jnp.concatenate(
        [norm_gains, norm_shifts, jnp.zeros((2, norm_gains.shape[1]), BFLOAT)]
    ).astype(jnp.float32)
    _, slots_here, length, model_width = decoder_states.shape
    slots = slots_here * lax.axis_size("pa")
    states = decoder_states.reshape(slots_here * length, model_width)
    memory = encoder_memory.reshape(-1, model_width)
    slot_index = lax.axis_index("pa") * slots_here + jnp.arange(slots_here)
    usable = (slot_mask[0] == 1) & (slot_index < slot_counts[0])
    marks = jnp.concatenate(
        [
            target_tokens.reshape(1, slots_here * length).astype(jnp.float32),
            jnp.repeat(log_prior, length, axis=1),
            jnp.repeat(usable[None].astype(jnp.float32), length, axis=1),
            jnp.zeros((5, slots_here * length), jnp.float32),
        ]
    )
    matrices, marks, norms, kept = forward_layer(
        shards, norm_rows, marks, states, memory, length
    )
    small, grad_embed, grad_third = vocabulary_head(
        kept[-1], marks, embedding, slots, length
    )
    loss_value = small[0, 0]
    grad_prior = small[1].reshape(1, slots_here, length)[:, :, 0]
    shares, norm_sums, grad_inputs, grad_encoded, pieces = backward_layer(
        matrices,
        kept[:11] + kept[12:15] + (states, memory),
        kept[11],
        norms,
        grad_third,
        grad_embed,
        length,
    )
    pieces = pieces.reshape(4 * grad_embed.shape[0], model_width)
    shares, grad_embed, grad_gains, grad_shifts = widen(
        shares, pieces, norm_sums, embedding.shape[0], norm_gains.shape[1]
    )
    return (
        loss_value,
        grad_inputs.reshape(decoder_states.shape),
        grad_encoded.reshape(encoder_memory.shape),
        grad_prior,
    ) + tuple(shares) + (grad_embed, grad_gains, grad_shifts)


def solution(mesh):
    own_kernels = mesh.shape["pb"] == 4 and mesh.shape["pa"] == 8
    return jax.shard_map(
        per_device_kernels if own_kernels else per_device,
        mesh=mesh,
        in_specs=(
            P("pb", "pa", None, None),
            P("pb", "pa", None, None),
            P("pb", "pa", None),
            P("pb", "pa"),
            P("pb"),
            P("pb", "pa"),
            P("pa", None),
            P("pa", None),
            P("pa", None),
            P("pa", None),
            P("pa", None),
            P("pa", None),
            P("pa", None),
            P("pa", None),
            P(None, "pa"),
            P(None, "pa"),
        ),
        out_specs=(
            P(),
            P("pb", "pa", None, None),
            P("pb", "pa", None, None),
            P("pb", "pa"),
            P("pa", None),
            P("pa", None),
            P("pa", None),
            P("pa", None),
            P("pa", None),
            P("pa", None),
            P("pa", None),
            P("pa", None),
            P(None, "pa"),
            P(None, "pa"),
        ),
        check_vma=False,
    )
```

```python
import functools
import math

import jax
import jax.numpy as jnp
from jax import lax
from jax.experimental import pallas as pl
from jax.experimental.pallas import tpu as pltpu
from jax.sharding import PartitionSpec as P

HEADS = 16
HEAD_DIM = 64


EPSILON = 1e-05
NEGATIVE = -1e30
BFLOAT = jnp.bfloat16
MESH = pl.DeviceIdType.MESH
TILE = 1024
ROWS = 128
WEIGHT_UNITS = (3, 1, 1, 2, 1, 4, 4)
UNITS = tuple((w, k) for w, n in enumerate(WEIGHT_UNITS) for k in range(n))
REDUCE_WEIGHT = 6


def whereami():
    pb = lax.axis_index("pb")
    pa = lax.axis_index("pa")
    return lax.rem(pb, 2), pb // 2, pa // 2, lax.rem(pa, 2)


def greet(peers):
    barrier = pltpu.get_barrier_semaphore()
    for peer in peers:
        pl.semaphore_signal(barrier, inc=1, device_id=peer, device_id_type=MESH)
    pl.semaphore_wait(barrier, len(peers))


def at(x, y, z, c):
    return (y * 2 + x, z * 2 + c)


def neighbours(x, y, z, c):
    return [at(1 - x, y, z, c), at(x, 1 - y, z, c), at(x, y, z, 1 - c)] + [
        at(x, y, lax.rem(z + d, 4), c) for d in (1, 2, 3)
    ]


def shard_view(ref, unit, start, size):
    weight, block = unit
    if weight == REDUCE_WEIGHT:
        return ref.at[pl.ds(block * ROWS + start, size), :]
    return ref.at[pl.ds(start, size), pl.ds(block * TILE, TILE)]


def full_view(ref, unit, place, core, start, size):
    weight, block = unit
    if weight == REDUCE_WEIGHT:
        return ref.at[place, core, block, pl.ds(start, size), :]
    return ref.at[place, core, pl.ds(start, size), pl.ds(block * TILE, TILE)]


Z_FULL = (13, 14, 15)


HOP_LAG = 1
LAG_TWO, LAG_SIBLING, LAG_LOAD, LAG_USE = 3, 6, 8, 9
SLOTS_IN_FLIGHT = 3


def dot_nn(left, right):
    return lax.dot_general(left, right, (((1,), (0,)), ((), ())), preferred_element_type=jnp.float32)


def dot_nt(left, right):
    return lax.dot_general(left, right, (((1,), (1,)), ((), ())), preferred_element_type=jnp.float32)


def dot_tn(left, right):
    return lax.dot_general(left, right, (((0,), (0,)), ((), ())), preferred_element_type=jnp.float32)


def stack_heads(pair):
    lane = lax.broadcasted_iota(jnp.int32, pair.shape, 1)
    zero = jnp.zeros_like(pair)
    return jnp.concatenate(
        [jnp.where(lane < HEAD_DIM, pair, zero), jnp.where(lane < HEAD_DIM, zero, pair)], 0
    )


def unstack_heads(stacked):
    rows = stacked.shape[0] // 2
    lane = lax.broadcasted_iota(jnp.int32, (rows, stacked.shape[1]), 1)
    return jnp.where(lane < HEAD_DIM, stacked[:rows], stacked[rows:])


def pair_scores(queries, keys, causal):
    scores = dot_nt(queries, keys) * (1.0 / math.sqrt(HEAD_DIM))
    if causal:
        length = keys.shape[0]
        row = lax.rem(lax.broadcasted_iota(jnp.int32, scores.shape, 0), length)
        column = lax.broadcasted_iota(jnp.int32, scores.shape, 1)
        scores = jnp.where(row >= column, scores, NEGATIVE)
    highest = jnp.max(scores, -1, keepdims=True)
    total = jnp.sum(jnp.exp(scores - highest), -1, keepdims=True)
    return jnp.exp(scores - (highest + jnp.log(total)))


def attend_pair(queries, keys, values, causal):
    probs = pair_scores(stack_heads(queries), keys, causal).astype(BFLOAT)
    return unstack_heads(dot_nn(probs, values)).astype(BFLOAT)


def normalise(values, gain, shift):
    centre = values - jnp.mean(values, -1, keepdims=True)
    inverse = lax.rsqrt(jnp.mean(centre * centre, -1, keepdims=True) + EPSILON)
    normed = centre * inverse
    return normed * gain + shift, normed, inverse


def forward_kernel(length, mem_length, *refs):
    shards, norm, aux, states_hbm, encoded_hbm = refs[:7], refs[7], refs[8], refs[9], refs[10]
    fulls, marks, kept_hbm = refs[11:18], refs[18], refs[19:36]
    (
        norm_full, packed, context, first_normed, first_inverse, first_low, cross_queries, pairs,
        cross_context, second_normed, second_inverse, second_low, inner, active, third_normed,
        third_inverse, third_low,
    ) = refs[36:53]
    wbuf, residual, states, encoded = refs[53:57]
    (
        local_sem, z_send, z_recv, one_send, one_recv, two_send, two_recv, d_send, d_recv,
        norm_sem, nz_send, nz_recv, nd_send, nd_recv, load_sem, ax_sem, ax_send, ax_recv,
        axz_send, axz_recv, kept_sem, input_sem,
    ) = refs[57:]
    x, y, z, c = whereami()
    greet(neighbours(x, y, z, c))
    every = slice(None)
    tokens, width = states_hbm.shape
    slots_here = tokens // length

    def copies(u):
        unit = UNITS[u]
        shard, full = shards[unit[0]], fulls[unit[0]]
        wide = u in Z_FULL
        a, b = (x, y) if u % 2 == 0 else (y, x)
        first_peer = at(x, 1 - y, z, c) if u % 2 == 0 else at(1 - x, y, z, c)
        second_peer = at(1 - x, y, z, c) if u % 2 == 0 else at(x, 1 - y, z, c)
        quarter = pl.multiple_of(64 * a + 32 * b, 32)
        half = pl.multiple_of(64 * a, 64)
        rows = (0, ROWS) if wide else (quarter, 32)
        local = pltpu.make_async_copy(
            shard_view(shard, unit, *rows), full_view(full, unit, z, c, *rows), local_sem.at[u]
        )
        def along(origin, direction):
            block = full_view(full, unit, origin, c, *rows)
            return pltpu.make_async_remote_copy(
                src_ref=block,
                dst_ref=block,
                send_sem=z_send.at[u, (direction + 1) // 2, origin],
                recv_sem=z_recv.at[u, origin],
                device_id=at(x, y, z + direction, c),
                device_id_type=MESH,
            )

        def cross(start, size, sends, recvs, peer):
            part = full_view(full, unit, every, c, start, size)
            return pltpu.make_async_remote_copy(
                src_ref=part,
                dst_ref=part,
                send_sem=sends.at[u],
                recv_sem=recvs.at[u],
                device_id=peer,
                device_id_type=MESH,
            )

        first = None if wide else cross(quarter, 32, one_send, one_recv, first_peer)
        second = None if wide else cross(half, 64, two_send, two_recv, second_peer)
        sibling = cross(0, ROWS, d_send, d_recv, at(x, y, z, 1 - c))
        load = pltpu.make_async_copy(
            full_view(full, unit, every, every, 0, ROWS),
            wbuf.at[u % SLOTS_IN_FLIGHT],
            load_sem.at[u % SLOTS_IN_FLIGHT],
        )
        return local, along, first, second, sibling, load

    def norm_copy(src, dst, send, recv, peer):
        return pltpu.make_async_remote_copy(
            src_ref=src, dst_ref=dst, send_sem=send, recv_sem=recv, device_id=peer, device_id_type=MESH
        )

    norm_local = pltpu.make_async_copy(norm, norm_full.at[z, c], norm_sem)
    norm_along = [
        norm_copy(
            norm, norm_full.at[z, c], nz_send.at[d - 1], nz_recv.at[d - 1], at(x, y, lax.rem(z + d, 4), c)
        )
        for d in (1, 2, 3)
    ]
    norm_sibling = norm_copy(
        norm_full.at[:, c], norm_full.at[:, c], nd_send, nd_recv, at(x, y, z, 1 - c)
    )
    norm_local.start()
    for copy in norm_along:
        copy.start()

    lanes = pl.ds(pl.multiple_of(c * tokens, tokens), tokens)
    aux_local = pltpu.make_async_copy(aux, marks.at[y, x, z, :, lanes], ax_sem)
    aux_local.start()
    aux_steps = [
        norm_copy(part, part, ax_send.at[n], ax_recv.at[n], peer)
        for n, (part, peer) in enumerate(
            (
                (marks.at[y, x, z, :, lanes], at(x, y, z, 1 - c)),
                (marks.at[y, x, z], at(1 - x, y, z, c)),
                (marks.at[y, :, z], at(x, 1 - y, z, c)),
            )
        )
    ]
    aux_along = [
        norm_copy(
            marks.at[:, :, z], marks.at[:, :, z], axz_send.at[d - 1], axz_recv.at[d - 1],
            at(x, y, lax.rem(z + d, 4), c),
        )
        for d in (1, 2, 3)
    ]

    kept = (
        norm_full, packed, context, first_normed, first_inverse, first_low, cross_queries, pairs,
        cross_context, second_normed, second_inverse, second_low, inner, active, third_normed,
        third_inverse, third_low,
    )

    def keep(*numbers):
        for n in numbers:
            pltpu.make_async_copy(kept[n], kept_hbm[n], kept_sem.at[n]).start()

    states_copy = pltpu.make_async_copy(states_hbm, states, input_sem.at[0])
    encoded_copy = pltpu.make_async_copy(encoded_hbm, encoded, input_sem.at[1])
    states_copy.start()
    encoded_copy.start()

    def norm_row(n):
        return jnp.concatenate(
            [norm_full[p // 2, p % 2, n : n + 1, :] for p in range(8)], 1
        )

    def times(left_ref, u, write):
        slot = u % SLOTS_IN_FLIGHT

        @pl.loop(0, 4, unroll=True)
        def _(n):
            columns = pl.ds(pl.multiple_of(n * 256, 256), 256)
            right = wbuf[slot, :, :, :, columns].reshape(TILE, 256)
            write(columns, n, dot_nn(left_ref[...], right))

    def block_columns(k, n):
        return pl.ds(pl.multiple_of(k * TILE + n * 256, 256), 256)

    def attention(queries, keys, key_start, value_start, key_length, out, causal):
        @pl.loop(0, slots_here * (width // 128), unroll=2)
        def _(n):
            slot, group = n // (width // 128), lax.rem(n, width // 128)
            lanes = pl.ds(pl.multiple_of(group * 128, 128), 128)
            key_lanes = pl.ds(pl.multiple_of(key_start + group * 128, 128), 128)
            value_lanes = pl.ds(pl.multiple_of(value_start + group * 128, 128), 128)
            query_rows = pl.ds(pl.multiple_of(slot * length, length), length)
            key_rows = pl.ds(pl.multiple_of(slot * key_length, key_length), key_length)
            out[query_rows, lanes] = attend_pair(
                queries[query_rows, lanes], keys[key_rows, key_lanes], keys[key_rows, value_lanes], causal
            )

    def finish_norm(n, value, normed_ref, inverse_ref, low_ref):
        out, normed, inverse = normalise(value, norm_row(n), norm_row(n + 3))
        normed_ref[...] = normed
        inverse_ref[...] = jnp.broadcast_to(inverse, inverse_ref.shape)
        low_ref[...] = out.astype(BFLOAT)
        return out

    def use(u):
        weight, k = UNITS[u]
        if weight == 0:
            def write(columns, n, value):
                packed[:, block_columns(k, n)] = value.astype(BFLOAT)

            times(states, u, write)
            if k == 2:
                attention(packed, packed, width, 2 * width, length, context, True)
                keep(1, 2)
        elif weight == 1:
            def write(columns, n, value):
                residual[:, columns] = states[:, columns].astype(jnp.float32) + value

            times(context, u, write)
            residual[...] = finish_norm(0, residual[...], first_normed, first_inverse, first_low)
            keep(3, 4, 5)
        elif weight == 2:
            def write(columns, n, value):
                cross_queries[:, columns] = value.astype(BFLOAT)

            times(first_low, u, write)
        elif weight == 3:
            slot = u % SLOTS_IN_FLIGHT

            @pl.loop(0, 8)
            def _(n):
                m, n = n // 4, lax.rem(n, 4)
                columns = pl.ds(pl.multiple_of(n * 256, 256), 256)
                part = encoded.shape[0] // 2
                rows_here = pl.ds(pl.multiple_of(m * part, part), part)
                right = wbuf[slot, :, :, :, columns].reshape(TILE, 256)
                pairs[rows_here, block_columns(k, n)] = dot_nn(encoded[rows_here, :], right).astype(BFLOAT)

            if k == 1:
                attention(cross_queries, pairs, 0, width, mem_length, cross_context, False)
                keep(6, 7, 8)
        elif weight == 4:
            def write(columns, n, value):
                residual[:, columns] = residual[:, columns] + value

            times(cross_context, u, write)
            residual[...] = finish_norm(1, residual[...], second_normed, second_inverse, second_low)
            keep(9, 10, 11)
        elif weight == 5:
            def write(columns, n, value):
                inner[:, block_columns(k, n)] = value
                gate = 0.5 * (1.0 + lax.erf(value * math.sqrt(0.5)))
                active[:, block_columns(k, n)] = (value * gate).astype(BFLOAT)

            times(second_low, u, write)
            if k == 3:
                keep(12, 13)
        else:
            slot = u % SLOTS_IN_FLIGHT
            blocks = active.shape[1] // (8 * ROWS)
            left = jnp.concatenate(
                [active[:, (p * blocks + k) * ROWS : (p * blocks + k + 1) * ROWS] for p in range(8)], 1
            )

            @pl.loop(0, 4, unroll=True)
            def _(n):
                columns = pl.ds(pl.multiple_of(n * 256, 256), 256)
                right = wbuf[slot, :, :, :, columns].reshape(TILE, 256)
                residual[:, columns] = residual[:, columns] + dot_nn(left, right)

            if k == blocks - 1:
                finish_norm(2, residual[...], third_normed, third_inverse, third_low)
                keep(14, 15, 16)

    count = len(UNITS)
    every_copy = [copies(u) for u in range(count)]

    def hop(u, h):
        local, along = every_copy[u][:2]
        if h == 1:
            local.wait()
        for origin, there, edge, direction in (
            (z - (h - 1), z >= h - 1, z < 3, 1),
            (z + (h - 1), z + (h - 1) <= 3, z > 0, -1),
        ):
            @pl.when(there)
            def _():
                if h > 1:
                    along(origin, direction).wait_recv()
                if h < 4:
                    @pl.when(edge)
                    def _():
                        along(origin, direction).start()

    for copies_here in every_copy:
        copies_here[0].start()
    for h in range(1, 4):
        for u in range(HOP_LAG * (4 - h)):
            hop(u, h)
    for i in range(count + LAG_USE):
        for h in range(1, 5):
            u = i + HOP_LAG * (4 - h)
            if u < count:
                hop(u, h)
        if i < count:
            first = every_copy[i][2]
            if first is not None:
                first.start()
        if 0 <= i - LAG_TWO < count:
            first, second = every_copy[i - LAG_TWO][2:4]
            if first is not None:
                first.wait_recv()
                second.start()
        if 0 <= i - LAG_SIBLING < count:
            second, sibling = every_copy[i - LAG_SIBLING][3:5]
            if second is not None:
                second.wait_recv()
            sibling.start()
        if i == 2:
            norm_local.wait()
            for copy in norm_along:
                copy.wait()
            norm_sibling.start()
        if i == 4:
            norm_sibling.wait()
            keep(0)
            states_copy.wait()
            encoded_copy.wait()
        if 5 <= i < 9:
            if i == 5:
                aux_local.wait()
            else:
                aux_steps[i - 6].wait()
            for copy in aux_steps[i - 5 : i - 4] if i < 8 else aux_along:
                copy.start()
        if i == 9:
            for copy in aux_along:
                copy.wait()
        if 0 <= i - LAG_LOAD < count:
            sibling, load = every_copy[i - LAG_LOAD][4:]
            sibling.wait_recv()
            load.start()
        if 0 <= i - LAG_USE < count:
            every_copy[i - LAG_USE][5].wait()
            use(i - LAG_USE)
    for _, along, first, second, sibling, _ in every_copy:
        for origin in range(4):
            @pl.when((origin <= z) & (z < 3))
            def _():
                along(origin, 1).wait_send()

            @pl.when((origin >= z) & (z > 0))
            def _():
                along(origin, -1).wait_send()

        if first is not None:
            first.wait_send()
            second.wait_send()
        sibling.wait_send()
    for n in range(len(kept)):
        pltpu.make_async_copy(kept[n], kept_hbm[n], kept_sem.at[n]).wait()


def forward_layer(weights, norm, aux, states, encoded, length):
    count = len(UNITS)
    shapes = []
    for w, weight in enumerate(weights):
        if w == REDUCE_WEIGHT:
            shapes.append((4, 2, weight.shape[0] // ROWS, ROWS, weight.shape[1]))
        else:
            shapes.append((4, 2) + weight.shape)
    tokens, width = states.shape
    mem_tokens = encoded.shape[0]
    mem_length = mem_tokens // (tokens // length)
    units = weights[5].shape[1]
    f32 = jnp.float32
    kept = [
        ((4, 2) + norm.shape, f32),
        ((tokens, 3 * width), BFLOAT),
        ((tokens, width), BFLOAT),
        ((tokens, width), f32),
        ((tokens, 128), f32),
        ((tokens, width), BFLOAT),
        ((tokens, width), BFLOAT),
        ((mem_tokens, 2 * width), BFLOAT),
        ((tokens, width), BFLOAT),
        ((tokens, width), f32),
        ((tokens, 128), f32),
        ((tokens, width), BFLOAT),
        ((tokens, units), f32),
        ((tokens, units), BFLOAT),
        ((tokens, width), f32),
        ((tokens, 128), f32),
        ((tokens, width), BFLOAT),
    ]
    every = pl.BlockSpec(memory_space=pl.ANY)
    dma = pltpu.SemaphoreType.DMA
    results = pl.pallas_call(
        functools.partial(forward_kernel, length, mem_length),
        out_shape=tuple(jax.ShapeDtypeStruct(shape, BFLOAT) for shape in shapes)
        + (jax.ShapeDtypeStruct((2, 2, 4, aux.shape[0], 2 * tokens), f32),)
        + tuple(jax.ShapeDtypeStruct(shape, kind) for shape, kind in kept),
        in_specs=[every] * 11,
        out_specs=(every,) * (8 + len(kept)),
        scratch_shapes=[pltpu.VMEM(shape, kind) for shape, kind in kept]
        + [
            pltpu.VMEM((SLOTS_IN_FLIGHT, 4, 2, ROWS, TILE), BFLOAT),
            pltpu.VMEM((tokens, width), f32),
            pltpu.VMEM((tokens, width), BFLOAT),
            pltpu.VMEM((mem_tokens, width), BFLOAT),
            dma((count,)),
            dma((count, 2, 4)),
            dma((count, 4)),
        ]
        + [dma((count,))] * 6
        + [dma]
        + [dma((3,))] * 2
        + [dma] * 2
        + [dma((SLOTS_IN_FLIGHT,))]
        + [dma]
        + [dma((3,))] * 4
        + [dma((len(kept),)), dma((2,))],
        compiler_params=pltpu.CompilerParams(
            collective_id=0, has_side_effects=True, vmem_limit_bytes=62 * 2**20
        ),
        name="forward_layer",
    )(*weights, norm, aux, states, encoded)
    fulls = tuple(full.reshape(-1, full.shape[-1]) for full in results[:7])
    return fulls, results[7], results[8], results[9:]


SEQUENCE = tuple((6, k) for k in range(4)) + tuple((5, k) for k in range(4)) + (
    (4, 0), (2, 0), (3, 0), (3, 1), (1, 0), (0, 0), (0, 1), (0, 2),
)
LINE_FIRST = 9
HOP_LAGS = (4, 7, 10)
LINE_LAGS = (10, 12, 14, 16, 18)
CROSS_LAGS = (2, 4, 6, 8, 10)
TURNS = 27
GATHER_TURNS = (4, 8)
READS = tuple(read for k in range(4) for read in ((6, k), (5, k))) + (
    (4, 0), (2, 0), (1, 0), (0, 0), (0, 1), (0, 2), (3, 0), (3, 1),
)


def norm_back(upstream, normed, inverse, gain):
    scaled = upstream * gain
    mean_scaled = jnp.mean(scaled, -1, keepdims=True)
    along = jnp.mean(scaled * normed, -1, keepdims=True)
    return (
        inverse * (scaled - mean_scaled - normed * along),
        jnp.sum(upstream * normed, 0, keepdims=True),
        jnp.sum(upstream, 0, keepdims=True),
    )


def attend_pair_back(grad, queries, keys, values, causal):
    scale = 1.0 / math.sqrt(HEAD_DIM)
    queries, grad = stack_heads(queries), stack_heads(grad)
    probs = pair_scores(queries, keys, causal)
    grad_probs = dot_nt(grad, values)
    grad_values = dot_tn(probs.astype(BFLOAT), grad).astype(BFLOAT)
    grad_scores = (
        probs * (grad_probs - jnp.sum(probs * grad_probs, -1, keepdims=True))
    ).astype(BFLOAT)
    grad_queries = unstack_heads(dot_nn(grad_scores, keys) * scale).astype(BFLOAT)
    grad_keys = (dot_tn(grad_scores, queries) * scale).astype(BFLOAT)
    return grad_queries, grad_keys, grad_values


def backward_kernel(length, mem_length, *refs):
    weights = refs[:7]
    kept_hbm = refs[7:23]
    inner_hbm = refs[23]
    norm_full, grad_third, gemb = refs[24:27]
    outs = refs[27:34]
    norm_out, grad_states, grad_memory, pieces, landing = refs[34:39]
    kept = refs[39:55]
    (
        wbuf, inner, stage, got, zload, one_line, two_line, one, two, line, fin,
        resid, low, grad_low, grad_context, grad_queries, grad_packed, memory_part,
        norm_here, norm_there, norm_line,
    ) = refs[55:76]
    (
        kept_sem, w_sem, inner_sem, dd_send, dd_recv, z_send, z_recv, zload_sem,
        ra_send, ra_recv, rb_send, rb_recv, rz_send, rz_recv, ag_send, ag_recv, ah_send, ah_recv,
        fin_sem, memory_sem, n_send, n_recv, nz_send, nz_recv, gemb_sem, ga_send, ga_recv,
        gb_send, gb_recv,
    ) = refs[76:]
    (
        packed, context, first_normed, first_inverse, first_low, cross_queries, pairs, cross_context,
        second_normed, second_inverse, second_low, active, third_normed, third_inverse, states, encoded,
    ) = kept
    x, y, z, c = whereami()
    greet(neighbours(x, y, z, c))
    tokens, width = states.shape
    slots_here = tokens // length
    count = len(SEQUENCE)
    blocks = active.shape[1] // (8 * ROWS)

    def keep_copy(n):
        return pltpu.make_async_copy(kept_hbm[n], kept[n], kept_sem.at[n])

    first_needed = (12, 13, 11, 10)
    for n in first_needed:
        keep_copy(n).start()
    for n in range(16):
        if n not in first_needed:
            keep_copy(n).start()

    def need(*names):
        for n in names:
            keep_copy(n).wait()

    def read_copy(n):
        weight, k = READS[n]
        if weight == REDUCE_WEIGHT:
            source = weights[weight].at[pl.ds(k * TILE, TILE), :]
        else:
            source = weights[weight].at[:, pl.ds(k * TILE, TILE)]
        return pltpu.make_async_copy(source, wbuf.at[n % 2], w_sem.at[n % 2])

    def inner_copy(k):
        return pltpu.make_async_copy(
            inner_hbm.at[:, pl.ds(k * TILE, TILE)], inner.at[k % 2], inner_sem.at[k % 2]
        )

    read_copy(0).start()
    read_copy(1).start()
    inner_copy(0).start()
    inner_copy(1).start()

    def remote(src, dst, send, recv, peer):
        return pltpu.make_async_remote_copy(
            src_ref=src, dst_ref=dst, send_sem=send, recv_sem=recv, device_id=peer, device_id_type=MESH
        )

    def norm_row(n):
        return jnp.concatenate([norm_full[p // 2, p % 2, n : n + 1, :] for p in range(8)], 1)

    def place(q):
        even = lax.rem(q, 2) == 0
        a = jnp.where(even, x, y)
        b = jnp.where(even, y, x)
        x_peer = y * 2 + (1 - x)
        y_peer = (1 - y) * 2 + x
        a_peer = (jnp.where(even, x_peer, y_peer), z * 2 + c)
        b_peer = (jnp.where(even, y_peer, x_peer), z * 2 + c)
        return a, b, a_peer, b_peer

    def piece(index, size):
        return pl.ds(pl.multiple_of(index * size, size), size)

    def total(*parts):
        out = parts[0].astype(jnp.float32)
        for part in parts[1:]:
            out = out + part.astype(jnp.float32)
        return out.astype(BFLOAT)

    pb = y * 2 + x
    pb_x, pb_y = y * 2 + 1 - x, (1 - y) * 2 + x
    vocab_rows = gemb.shape[0]
    cut = 16 * (vocab_rows // 64)
    cuts = [(n * cut, cut if n < 3 else vocab_rows - 3 * cut) for n in range(4)]

    def gather_one(n):
        rows_here = pl.ds(*cuts[n])
        peer = at(1 - x, y, z, c) if n < 2 else at(x, 1 - y, z, c)
        return remote(gemb.at[rows_here, :], pieces.at[pb, rows_here, :], ga_send.at[n], ga_recv.at[n], peer)

    def gather_two(n, j):
        rows_here = pl.ds(*cuts[n])
        peer = at(x, 1 - y, z, c) if n < 2 else at(1 - x, y, z, c)
        origin = pb if j == 0 else (pb_x if n < 2 else pb_y)
        source = gemb.at[rows_here, :] if j == 0 else pieces.at[origin, rows_here, :]
        return remote(source, pieces.at[origin, rows_here, :], gb_send.at[n, j], gb_recv.at[n, j], peer)

    gemb_copy = pltpu.make_async_copy(gemb, pieces.at[pb], gemb_sem)
    for n in (0, 2, 1, 3):
        gather_one(n).start()
    for n in (2, 0, 3, 1):
        gather_two(n, 0).start()
    gemb_copy.start()

    def dd_copy(q):
        return remote(
            stage.at[lax.rem(q, 2), 1 - c], got.at[q], dd_send.at[q], dd_recv.at[q], at(x, y, z, 1 - c)
        )

    def line_copy(q, side, h, dest, step):
        return remote(
            got.at[q, dest], landing.at[q, side, h - 1], z_send.at[q, side, h - 1],
            z_recv.at[q, side, h - 1], at(x, y, z + step, c),
        )

    def line_sides(h):
        return (
            (0, z + 4 - h, z <= h - 1, z >= 1, 1),
            (1, z - 4 + h, z >= 4 - h, z <= 2, -1),
        )

    def line_load(q, side, h):
        return pltpu.make_async_copy(landing.at[q, side, h - 2], zload.at[side], zload_sem.at[side])

    def line_hop(q, h):
        if h > 1:
            for side, dest, there, fed, step in line_sides(h):
                @pl.when(there & fed)
                def _():
                    line_copy(q, side, h - 1, dest, step).wait_recv()
                    line_load(q, side, h).start()

        for side, dest, there, fed, step in line_sides(h):
            if h > 1:
                @pl.when(there & fed)
                def _():
                    line_load(q, side, h).wait()

                    @pl.loop(0, 8)
                    def _(j):
                        rows_here = piece(j, 16)
                        got[q, dest, rows_here, :] = total(
                            got[q, dest, rows_here, :], zload[side, rows_here, :]
                        )

            if h < 4:
                @pl.when(there)
                def _():
                    line_copy(q, side, h, dest, step).start()

    def ra_line(q):
        a, _, a_peer, _ = place(q)
        return remote(got.at[q, z, piece(1 - a, 64), :], one_line.at[q], ra_send.at[q], ra_recv.at[q], a_peer)

    def rb_line(q):
        _, b, _, b_peer = place(q)
        return remote(one_line.at[q, piece(1 - b, 32), :], two_line.at[q], rb_send.at[q], rb_recv.at[q], b_peer)

    def ra_cross(q):
        a, _, a_peer, _ = place(q)
        return remote(
            got.at[q, :, piece(1 - a, 64), :], one.at[q - LINE_FIRST], ra_send.at[q], ra_recv.at[q], a_peer
        )

    def rb_cross(q):
        _, b, _, b_peer = place(q)
        return remote(
            one.at[q - LINE_FIRST, :, piece(1 - b, 32), :], two.at[q - LINE_FIRST],
            rb_send.at[q], rb_recv.at[q], b_peer,
        )

    def rz_cross(q, d):
        other = lax.rem(z + d, 4)
        n = q - LINE_FIRST
        return remote(
            two.at[n, other], line.at[n, d - 1], rz_send.at[n, d - 1], rz_recv.at[n, d - 1],
            at(x, y, other, c),
        )

    def out_view(q, start, size):
        return shard_view(outs[SEQUENCE[q][0]], SEQUENCE[q], start, size)

    def quarter_start(q):
        a, b, _, _ = place(q)
        return pl.multiple_of(64 * a + 32 * b, 32)

    def fin_copy(q):
        return pltpu.make_async_copy(fin.at[q], out_view(q, quarter_start(q), 32), fin_sem.at[q])

    def ag_copy(q):
        return remote(
            fin.at[q], out_view(q, quarter_start(q), 32), ag_send.at[q], ag_recv.at[q], place(q)[3]
        )

    def ah_copy(q):
        a, _, a_peer, _ = place(q)
        part = out_view(q, pl.multiple_of(64 * a, 64), 64)
        return remote(part, part, ah_send.at[q], ah_recv.at[q], a_peer)

    norm_peers = (at(x, y, z, 1 - c), at(1 - x, y, z, c), at(x, 1 - y, z, c))

    def norm_copy(n):
        return remote(norm_here.at[n], norm_there.at[n], n_send.at[n], n_recv.at[n], norm_peers[n])

    def norm_line_copy(d):
        return remote(
            norm_here.at[3], norm_line.at[d - 1], nz_send.at[d - 1], nz_recv.at[d - 1],
            at(x, y, lax.rem(z + d, 4), c),
        )

    def outer(q, left, start, step, right):
        slot = q % 2

        @pl.loop(0, 8, unroll=4)
        def _(p):
            lanes = pl.ds(pl.multiple_of(start + p * step, 128), 128)
            stage[slot, lax.rem(p, 2), p // 2] = dot_tn(left[:, lanes], right()).astype(BFLOAT)

    def back_times(left, n, write):
        slot = n % 2
        read_copy(n).wait()

        @pl.loop(0, 4, unroll=True)
        def _(m):
            write(piece(m, 256), dot_nt(left[...], wbuf[slot, piece(m, 256), :]))

        if n + 2 < len(READS):
            read_copy(n + 2).start()

    def add_resid(columns, value):
        resid[:, columns] = resid[:, columns] + value

    def finish_norm(n, normed, inverse):
        value, gain, shift = norm_back(resid[...], normed[...], inverse[:, 0:1], norm_row(n))
        resid[...] = value
        low[...] = value.astype(BFLOAT)
        norm_here[0, n : n + 1, :] = gain
        norm_here[0, n + 3 : n + 4, :] = shift

    def attention_back(queries, keys, key_start, value_start, key_length, out, out_keys, causal):
        @pl.loop(0, slots_here * (width // 128), unroll=2)
        def _(n):
            slot, group = n // (width // 128), lax.rem(n, width // 128)
            lanes = piece(group, 128)
            key_lanes = pl.ds(pl.multiple_of(key_start + group * 128, 128), 128)
            value_lanes = pl.ds(pl.multiple_of(value_start + group * 128, 128), 128)
            query_rows = piece(slot, length)
            key_rows = piece(slot, key_length)
            grad_query, grad_key, grad_value = attend_pair_back(
                grad_context[query_rows, lanes],
                queries[query_rows, lanes],
                keys[key_rows, key_lanes],
                keys[key_rows, value_lanes],
                causal,
            )
            out[query_rows, lanes] = grad_query
            out_keys[key_rows, key_lanes] = grad_key
            out_keys[key_rows, value_lanes] = grad_value

    def produce(q):
        weight, k = SEQUENCE[q]
        if q == 0:
            norm_here[0] = jnp.zeros_like(norm_here[0])
            for p in range(8):
                resid[:, p * 128 : (p + 1) * 128] = grad_third[p * 128 : (p + 1) * 128, :].T
            need(12, 13, 11)
            finish_norm(2, third_normed, third_inverse)
        if weight == 6:
            outer(q, active, k * ROWS, blocks * ROWS, lambda: low[...])
        elif weight == 5:
            if k == 0:
                need(10)
            inner_copy(k).wait()

            def write(columns, value):
                pre = inner[k % 2, :, columns]
                slope = 0.5 * (1.0 + lax.erf(pre * math.sqrt(0.5))) + pre * jnp.exp(
                    -0.5 * pre * pre
                ) * (1.0 / math.sqrt(2.0 * math.pi))
                grad_low[:, columns] = (value * slope).astype(BFLOAT)

            back_times(low, 2 * k, write)
            if k + 2 < 4:
                inner_copy(k + 2).start()
            outer(q, second_low, 0, ROWS, lambda: grad_low[...])
            back_times(grad_low, 2 * k + 1, add_resid)
        elif weight == 4:
            need(8, 9, 7)
            finish_norm(1, second_normed, second_inverse)
            outer(q, cross_context, 0, ROWS, lambda: low[...])

            def write(columns, value):
                grad_context[:, columns] = value.astype(BFLOAT)

            back_times(low, 8, write)
        elif weight == 2:
            need(5, 6, 4, 2, 3)
            attention_back(cross_queries, pairs, 0, width, mem_length, grad_queries, pairs, False)
            outer(q, first_low, 0, ROWS, lambda: grad_queries[...])
            back_times(grad_queries, 9, add_resid)
            finish_norm(0, first_normed, first_inverse)
        elif weight == 3:
            if k == 0:
                need(15)
            outer(q, encoded, 0, ROWS, lambda: pairs[:, pl.ds(k * TILE, TILE)])
        elif weight == 1:
            need(1, 0, 14)
            outer(q, context, 0, ROWS, lambda: low[...])

            def write(columns, value):
                grad_context[:, columns] = value.astype(BFLOAT)

            back_times(low, 10, write)
            attention_back(packed, packed, width, 2 * width, length, grad_packed, grad_packed, True)
        else:
            def part():
                return grad_packed[:, pl.ds(k * TILE, TILE)]

            outer(q, states, 0, ROWS, part)
            back_times(grad_packed.at[:, pl.ds(k * TILE, TILE)], 11 + k, add_resid)
            if k == 2:
                grad_states[...] = resid[...]

    half = encoded.shape[0] // 2

    def memory_copy(m):
        return pltpu.make_async_copy(
            memory_part.at[m % 2],
            grad_memory.at[pl.ds(m // 4 * half, half), pl.ds(m % 4 * 256, 256)],
            memory_sem.at[m % 2],
        )

    def memory_chunk(m):
        if m == 0:
            read_copy(14).wait()
            read_copy(15).wait()
        if m >= 2:
            memory_copy(m - 2).wait()
        rows_here, columns = pl.ds(m // 4 * half, half), pl.ds(m % 4 * 256, 256)
        memory_part[m % 2] = dot_nt(pairs[rows_here, :width], wbuf[0, columns, :]) + dot_nt(
            pairs[rows_here, width:], wbuf[1, columns, :]
        )
        memory_copy(m).start()

    def each(q, action):
        for k in range(count):
            @pl.when(q == k)
            def _():
                action(k)

    def finish_block(q):
        def action(k):
            fin_copy(k).start()
            ag_copy(k).start()

        each(q, action)

    step = 16

    @pl.loop(0, TURNS)
    def _(i):
        for q in range(count):
            @pl.when(i == q)
            def _():
                if q >= 2:
                    dd_copy(q - 2).wait_send()
                produce(q)
                dd_copy(q).start()

        for n, turn in enumerate(GATHER_TURNS):
            @pl.when(i == turn)
            def _():
                for part in (n, n + 2):
                    gather_one(part).wait_recv()
                    gather_two(part, 1).start()

        for m in range(8):
            @pl.when(i == count + 1 + m)
            def _():
                memory_chunk(m)

        qs = i - 1

        @pl.when((qs >= 0) & (qs < count))
        def _():
            dd_copy(qs).wait_recv()
            slot = lax.rem(qs, 2)

            @pl.loop(0, 32)
            def _(j):
                zz, rows_here = j // 8, piece(lax.rem(j, 8), step)
                got[qs, zz, rows_here, :] = total(got[qs, zz, rows_here, :], stage[slot, c, zz, rows_here, :])

            @pl.when(qs < LINE_FIRST)
            def _():
                line_hop(qs, 1)

            @pl.when(qs >= LINE_FIRST)
            def _():
                ra_cross(qs).start()

        for h in (2, 3, 4):
            qh = i - HOP_LAGS[h - 2]

            @pl.when((qh >= 0) & (qh < LINE_FIRST))
            def _():
                line_hop(qh, h)
                if h == 4:
                    ra_line(qh).start()

        q1 = i - LINE_LAGS[1]

        @pl.when((q1 >= 0) & (q1 < LINE_FIRST))
        def _():
            ra_line(q1).wait_recv()
            a = place(q1)[0]

            @pl.loop(0, 4)
            def _(j):
                rows_here = piece(j, step)
                one_line[q1, rows_here, :] = total(
                    one_line[q1, rows_here, :],
                    got[q1, z, pl.ds(pl.multiple_of(64 * a + j * step, step), step), :],
                )

            rb_line(q1).start()

        q2 = i - LINE_LAGS[2]

        @pl.when((q2 >= 0) & (q2 < LINE_FIRST))
        def _():
            rb_line(q2).wait_recv()
            b = place(q2)[1]

            @pl.loop(0, 2)
            def _(j):
                rows_here = piece(j, step)
                fin[q2, rows_here, :] = total(
                    two_line[q2, rows_here, :],
                    one_line[q2, pl.ds(pl.multiple_of(32 * b + j * step, step), step), :],
                )

            finish_block(q2)

        p0 = i - CROSS_LAGS[0]

        @pl.when((p0 >= LINE_FIRST) & (p0 < count))
        def _():
            ra_cross(p0).wait_recv()
            a = place(p0)[0]

            @pl.loop(0, 16)
            def _(j):
                zz, r = j // 4, lax.rem(j, 4)
                rows_here = piece(r, step)
                one[p0 - LINE_FIRST, zz, rows_here, :] = total(
                    one[p0 - LINE_FIRST, zz, rows_here, :],
                    got[p0, zz, pl.ds(pl.multiple_of(64 * a + r * step, step), step), :],
                )

            rb_cross(p0).start()

        p1 = i - CROSS_LAGS[1]

        @pl.when((p1 >= LINE_FIRST) & (p1 < count))
        def _():
            rb_cross(p1).wait_recv()
            b = place(p1)[1]

            @pl.loop(0, 8)
            def _(j):
                zz, r = j // 2, lax.rem(j, 2)
                rows_here = piece(r, step)
                two[p1 - LINE_FIRST, zz, rows_here, :] = total(
                    two[p1 - LINE_FIRST, zz, rows_here, :],
                    one[p1 - LINE_FIRST, zz, pl.ds(pl.multiple_of(32 * b + r * step, step), step), :],
                )

            for d in (1, 2, 3):
                rz_cross(p1, d).start()

        p2 = i - CROSS_LAGS[2]

        @pl.when((p2 >= LINE_FIRST) & (p2 < count))
        def _():
            for d in (1, 2, 3):
                rz_cross(p2, d).wait_recv()
            n = p2 - LINE_FIRST

            @pl.loop(0, 2)
            def _(j):
                rows_here = piece(j, step)
                fin[p2, rows_here, :] = total(
                    two[n, z, rows_here, :], line[n, 0, rows_here, :], line[n, 1, rows_here, :],
                    line[n, 2, rows_here, :],
                )

            finish_block(p2)

        def pass_on(k):
            ag_copy(k).wait_recv()
            fin_copy(k).wait()
            ah_copy(k).start()

        for lags, low_q, high_q in ((LINE_LAGS, 0, LINE_FIRST), (CROSS_LAGS, LINE_FIRST, count)):
            q3 = i - lags[3]

            @pl.when((q3 >= low_q) & (q3 < high_q))
            def _():
                each(q3, pass_on)

            q4 = i - lags[4]

            @pl.when((q4 >= low_q) & (q4 < high_q))
            def _():
                each(q4, lambda k: ah_copy(k).wait_recv())

        @pl.when(i == count)
        def _():
            norm_copy(0).start()

        for n in range(3):
            @pl.when(i == count + 2 * (n + 1))
            def _():
                norm_copy(n).wait_recv()
                norm_here[n + 1] = norm_here[n] + norm_there[n]
                if n < 2:
                    norm_copy(n + 1).start()
                else:
                    for d in (1, 2, 3):
                        norm_line_copy(d).start()

        @pl.when(i == count + 8)
        def _():
            for d in (1, 2, 3):
                norm_line_copy(d).wait_recv()
            norm_out[...] = ((norm_here[3] + norm_line[0]) + norm_line[1]) + norm_line[2]

    gemb_copy.wait()
    for n in range(4):
        gather_one(n).wait_send()
        for j in range(2):
            gather_two(n, j).wait()
    memory_copy(6).wait()
    memory_copy(7).wait()
    dd_copy(count - 2).wait_send()
    dd_copy(count - 1).wait_send()

    @pl.loop(0, LINE_FIRST)
    def _(q):
        for h in (1, 2, 3):
            for side, dest, there, _, step in line_sides(h):
                @pl.when(there)
                def _():
                    line_copy(q, side, h, dest, step).wait_send()

        ra_line(q).wait_send()
        rb_line(q).wait_send()

    @pl.loop(LINE_FIRST, count)
    def _(q):
        ra_cross(q).wait_send()
        rb_cross(q).wait_send()
        for d in (1, 2, 3):
            rz_cross(q, d).wait_send()

    for q in range(count):
        ag_copy(q).wait_send()
        ah_copy(q).wait_send()
    for n in range(3):
        norm_copy(n).wait_send()
        norm_line_copy(n + 1).wait_send()


def backward_layer(weights, kept, inner, norm_full, grad_third, gemb, length):
    count = len(SEQUENCE)
    f32 = jnp.float32
    tokens, width = kept[14].shape
    mem_tokens = kept[15].shape[0]
    mem_length = mem_tokens // (tokens // length)
    shapes = [(weight.shape[0] // 8, weight.shape[1]) for weight in weights]
    every = pl.BlockSpec(memory_space=pl.ANY)
    vmem = pl.BlockSpec(memory_space=pltpu.VMEM)
    dma = pltpu.SemaphoreType.DMA
    sems = dma((count,))
    crossed = count - LINE_FIRST
    *shares, norm_sum, grad_states, grad_memory, pieces, _ = pl.pallas_call(
        functools.partial(backward_kernel, length, mem_length),
        out_shape=tuple(jax.ShapeDtypeStruct(shape, BFLOAT) for shape in shapes)
        + (
            jax.ShapeDtypeStruct((8, width), f32),
            jax.ShapeDtypeStruct((tokens, width), f32),
            jax.ShapeDtypeStruct((mem_tokens, width), f32),
            jax.ShapeDtypeStruct((4,) + gemb.shape, BFLOAT),
            jax.ShapeDtypeStruct((LINE_FIRST, 2, 3, ROWS, TILE), BFLOAT),
        ),
        in_specs=[every] * 24 + [vmem] * 2 + [every],
        out_specs=(every,) * 7 + (vmem, vmem, every, every, every),
        scratch_shapes=[pltpu.VMEM(part.shape, part.dtype) for part in kept]
        + [
            pltpu.VMEM((2, TILE, TILE), BFLOAT),
            pltpu.VMEM((2, tokens, TILE), f32),
            pltpu.VMEM((2, 2, 4, ROWS, TILE), BFLOAT),
            pltpu.VMEM((count, 4, ROWS, TILE), BFLOAT),
            pltpu.VMEM((2, ROWS, TILE), BFLOAT),
            pltpu.VMEM((LINE_FIRST, 64, TILE), BFLOAT),
            pltpu.VMEM((LINE_FIRST, 32, TILE), BFLOAT),
            pltpu.VMEM((crossed, 4, 64, TILE), BFLOAT),
            pltpu.VMEM((crossed, 4, 32, TILE), BFLOAT),
            pltpu.VMEM((crossed, 3, 32, TILE), BFLOAT),
            pltpu.VMEM((count, 32, TILE), BFLOAT),
            pltpu.VMEM((tokens, width), f32),
            pltpu.VMEM((tokens, width), BFLOAT),
            pltpu.VMEM((tokens, TILE), BFLOAT),
            pltpu.VMEM((tokens, width), BFLOAT),
            pltpu.VMEM((tokens, width), BFLOAT),
            pltpu.VMEM((tokens, 3 * width), BFLOAT),
            pltpu.VMEM((2, mem_tokens // 2, 256), f32),
            pltpu.VMEM((4, 8, width), f32),
            pltpu.VMEM((3, 8, width), f32),
            pltpu.VMEM((3, 8, width), f32),
            dma((16,)), dma((2,)), dma((2,)), sems, sems,
            dma((LINE_FIRST, 2, 3)), dma((LINE_FIRST, 2, 3)), dma((2,)),
            sems, sems, sems, sems,
            dma((crossed, 3)), dma((crossed, 3)),
            sems, sems, sems, sems, sems, dma((2,)),
            dma((3,)), dma((3,)), dma((3,)), dma((3,)),
            dma, dma((4,)), dma((4,)), dma((4, 2)), dma((4, 2)),
        ],
        compiler_params=pltpu.CompilerParams(
            collective_id=1, has_side_effects=True, vmem_limit_bytes=62 * 2**20
        ),
        name="backward_layer",
    )(*weights, *kept, inner, norm_full, grad_third, gemb)
    return shares, norm_sum, grad_states, grad_memory, pieces


WIDE_ROWS = 512
WIDE_SLOTS = 4


def widen_kernel(embed_rows, *refs):
    parts, pieces, norms = refs[:7], refs[7], refs[8]
    outs, embed_out, gains_out, shifts_out = refs[9:16], refs[16], refs[17], refs[18]
    low, wide = refs[19:26], refs[26:33]
    embed_low, embed_wide, norm_here = refs[33:36]
    in_sem, out_sem, embed_in, embed_out_sem, norm_sem = refs[36:]
    here = norm_here.shape[1]
    norm_copy = pltpu.make_async_copy(
        norms.at[:, pl.ds(pl.multiple_of(lax.axis_index("pa") * here, here), here)], norm_here, norm_sem
    )
    norm_copy.start()
    full = embed_rows // WIDE_ROWS
    rest = embed_rows - full * WIDE_ROWS

    def load(n, rows):
        return pltpu.make_async_copy(
            pieces.at[pl.ds(n * WIDE_ROWS, rows), :],
            embed_low.at[n % WIDE_SLOTS, pl.ds(0, rows), :],
            embed_in.at[n % WIDE_SLOTS],
        )

    def store(n, rows):
        return pltpu.make_async_copy(
            embed_wide.at[n % WIDE_SLOTS, pl.ds(0, rows), :],
            embed_out.at[pl.ds(n * WIDE_ROWS, rows), :],
            embed_out_sem.at[n % WIDE_SLOTS],
        )

    sizes = [WIDE_ROWS] * full + [rest] * (rest > 0)
    for n in range(WIDE_SLOTS):
        load(n, sizes[n]).start()
    for n in range(7):
        pltpu.make_async_copy(parts[n], low[n], in_sem.at[n]).start()
    for n, rows in enumerate(sizes):
        load(n, rows).wait()
        if n >= WIDE_SLOTS:
            store(n - WIDE_SLOTS, sizes[n - WIDE_SLOTS]).wait()

        @pl.loop(0, rows // 16, unroll=4)
        def _(j):
            part = pl.ds(pl.multiple_of(j * 16, 16), 16)
            embed_wide[n % WIDE_SLOTS, part, :] = embed_low[n % WIDE_SLOTS, part, :].astype(jnp.float32)

        store(n, rows).start()
        if n + WIDE_SLOTS < len(sizes):
            load(n + WIDE_SLOTS, sizes[n + WIDE_SLOTS]).start()
    for n in range(7):
        pltpu.make_async_copy(parts[n], low[n], in_sem.at[n]).wait()

        @pl.loop(0, low[n].shape[0] // 16)
        def _(j):
            part = pl.ds(pl.multiple_of(j * 16, 16), 16)
            wide[n][part, :] = low[n][part, :].astype(jnp.float32)

        pltpu.make_async_copy(wide[n], outs[n], out_sem.at[n]).start()
    norm_copy.wait()
    gains_out[...] = norm_here[0:3, :]
    shifts_out[...] = norm_here[3:6, :]
    for n in range(len(sizes) - WIDE_SLOTS, len(sizes)):
        store(n, sizes[n]).wait()
    for n in range(7):
        pltpu.make_async_copy(wide[n], outs[n], out_sem.at[n]).wait()


def widen(parts, pieces, norms, embed_rows, norm_here):
    every = pl.BlockSpec(memory_space=pl.ANY)
    vmem = pl.BlockSpec(memory_space=pltpu.VMEM)
    f32 = jnp.float32
    width = pieces.shape[1]
    dma = pltpu.SemaphoreType.DMA
    results = pl.pallas_call(
        functools.partial(widen_kernel, embed_rows),
        out_shape=tuple(jax.ShapeDtypeStruct(part.shape, f32) for part in parts)
        + (jax.ShapeDtypeStruct((embed_rows, width), f32),)
        + (jax.ShapeDtypeStruct((3, norm_here), f32),) * 2,
        in_specs=[every] * 9,
        out_specs=(every,) * 8 + (vmem,) * 2,
        scratch_shapes=[pltpu.VMEM(part.shape, BFLOAT) for part in parts]
        + [pltpu.VMEM(part.shape, f32) for part in parts]
        + [
            pltpu.VMEM((WIDE_SLOTS, WIDE_ROWS, width), BFLOAT),
            pltpu.VMEM((WIDE_SLOTS, WIDE_ROWS, width), f32),
            pltpu.VMEM((8, norm_here), f32),
            dma((7,)),
            dma((7,)),
            dma((WIDE_SLOTS,)),
            dma((WIDE_SLOTS,)),
            dma,
        ],
        compiler_params=pltpu.CompilerParams(vmem_limit_bytes=60 * 2**20),
        name="widen",
    )(*parts, pieces, norms)
    return results[:7], results[7], results[8], results[9]


VOCAB_CUTS = 3
ARRIVAL_PHASES = (0, 0, 1, 2, 0, 1, 2, 3, 0, 1, 2, 3, 1, 2, 3, 3)
ARRIVAL_TURNS = (0, 1, 0, 0, 2, 1, 1, 0, 3, 2, 2, 1, 3, 3, 2, 3)
NEAREST = ((0, 1, 2, 3), (1, 0, 1, 2), (2, 2, 3, 1), (3, 3, 0, 0))


def head_kernel(slots, length, vocab_here, *refs):
    hid, marks, emb_all = refs[:3]
    small_out, gemb_out, third_out = refs[3:6]
    (
        emb, emb_t, held, logit, expo, part, sib_part, part_one, part_two, part_z,
        mine, theirs, lined, prior, usable, weight, scaled, picked_grad,
    ) = refs[6:24]
    (
        local_sem, z_send, z_recv, one_send, one_recv, two_send, two_recv, sib_send, sib_recv,
        st_send, st_recv, stz_send, stz_recv,
        dd_send, dd_recv, r1_send, r1_recv, r2_send, r2_recv, rz_send, rz_recv,
    ) = refs[24:]
    x, y, z, c = whereami()
    pb, pa = y * 2 + x, z * 2 + c
    size = hid.shape[0]
    pair = 2 * size
    width = hid.shape[1]
    rows = emb.shape[0]
    cut = rows // VOCAB_CUTS
    start = pl.multiple_of(pb * rows, 16)
    last = vocab_here - 3 * rows
    valid = jnp.where(pb == 3, last, rows)
    base = pa * vocab_here + start
    own = pb * 4 + z

    def remote(src, dst, send, recv, peer):
        return pltpu.make_async_remote_copy(
            src_ref=src, dst_ref=dst, send_sem=send, recv_sem=recv, device_id=peer, device_id_type=MESH
        )

    sibling = at(x, y, z, 1 - c)
    x_peer, y_peer = at(1 - x, y, z, c), at(x, 1 - y, z, c)

    def spot(k, core, n=None):
        rows_here = size if n is None else size // 2
        first = (k * 2 + core) * size + (0 if n is None else n * rows_here)
        return held.at[pl.ds(pl.multiple_of(first, rows_here), rows_here), :]

    greet(neighbours(x, y, z, c))
    own_copy = pltpu.make_async_copy(hid, spot(own, c), local_sem.at[0])
    own_copy.start()
    emb_copy = pltpu.make_async_copy(
        emb_all.at[pl.ds(start, last), :], emb.at[pl.ds(0, last), :], local_sem.at[2]
    )
    rest_copy = pltpu.make_async_copy(
        emb_all.at[pl.ds(pl.multiple_of(jnp.minimum(start + last, vocab_here - (rows - last)), 16), rows - last), :],
        emb.at[pl.ds(last, rows - last), :],
        local_sem.at[3],
    )
    emb_copy.start()
    rest_copy.start()
    own_copy.wait()

    def up_copy(origin, n):
        block = spot(pb * 4 + origin, c, n)
        return remote(block, block, z_send.at[0, origin, n], z_recv.at[origin, n], at(x, y, z + 1, c))

    def down_copy(origin, n):
        block = spot(pb * 4 + origin, c, n)
        return remote(block, block, z_send.at[1, origin, n], z_recv.at[origin, n], at(x, y, z - 1, c))

    def pass_along(origin, n, action):
        @pl.when((origin <= z) & (z < 3))
        def _():
            action(up_copy(origin, n))

        @pl.when((origin >= z) & (z > 0))
        def _():
            action(down_copy(origin, n))

    def sib_copy(k, n):
        return remote(spot(k, c, n), spot(k, c, n), sib_send.at[k, n], sib_recv.at[k, n], sibling)

    def order(zz):
        x_first = zz < 2
        f = jnp.where(x_first, x, y)
        g = jnp.where(x_first, y, x)
        first_peer = (jnp.where(x_first, y * 2 + 1 - x, (1 - y) * 2 + x), pa)
        second_peer = (jnp.where(x_first, (1 - y) * 2 + x, y * 2 + 1 - x), pa)

        def block(first, second):
            return jnp.where(x_first, second * 2 + first, first * 2 + second) * 4 + zz

        return f, g, first_peer, second_peer, block

    def one_copy(zz, n):
        f, g, first_peer, _, block = order(zz)
        part = spot(block(f, g), c, n)
        return remote(part, part, one_send.at[zz, n], one_recv.at[zz, n], first_peer)

    def two_copy(zz, j, n):
        f, g, _, second_peer, block = order(zz)
        part = spot(block(f if j == 0 else 1 - f, g), c, n)
        return remote(part, part, two_send.at[zz, j, n], two_recv.at[zz, j, n], second_peer)

    for n in range(2):
        pass_along(z, n, lambda copy: copy.start())
        one_copy(z, n).start()
        two_copy(z, 0, n).start()
        sib_copy(own, n).start()

    emb_copy.wait()
    rest_copy.wait()
    full_cuts = rows // 128

    def target_rows(k):
        ypart, xpart, zpart = k // 8, lax.rem(k // 4, 2), lax.rem(k, 4)
        target = marks[ypart, xpart, zpart, 0:1, :].astype(jnp.int32) - base
        return jnp.where(target < valid, target, -1)

    def row_numbers(j):
        return lax.broadcasted_iota(jnp.int32, (cut, pair), 0) + j * cut

    def cut_rows(j):
        return pl.ds(pl.multiple_of(j * cut, cut), cut)

    def token_lanes(k):
        return pl.ds(pl.multiple_of(k * pair, pair), pair)

    def forward_block(k):
        target = target_rows(k)
        block = held[token_lanes(k), :]

        def scan_logits(j, carried):
            highest, picked = carried
            value = lax.dot_general(
                emb[cut_rows(j), :], block, (((1,), (1,)), ((), ())), preferred_element_type=jnp.float32
            )
            number = row_numbers(j)
            value = jnp.where(number < valid, value, NEGATIVE)
            logit[cut_rows(j), :] = value
            return (
                jnp.maximum(highest, jnp.max(value, 0, keepdims=True)),
                picked + jnp.sum(jnp.where(number == target, value, 0.0), 0, keepdims=True),
            )

        highest, picked = lax.fori_loop(
            0,
            VOCAB_CUTS,
            scan_logits,
            (jnp.full((1, pair), NEGATIVE, jnp.float32), jnp.zeros((1, pair), jnp.float32)),
            unroll=True,
        )

        def scan_exp(j, total):
            value = jnp.exp(logit[cut_rows(j), :] - highest)
            expo[cut_rows(j), token_lanes(k)] = value.astype(BFLOAT)
            return total + jnp.sum(value, 0, keepdims=True)

        total = lax.fori_loop(
            0, VOCAB_CUTS, scan_exp, jnp.zeros((1, pair), jnp.float32), unroll=True
        )
        mine[0, 0, pl.ds(k, 1), :] = highest
        mine[0, 1, pl.ds(k, 1), :] = total
        mine[0, 2, pl.ds(k, 1), :] = picked

    def listed(values, index):
        out = values[0]
        for n in range(1, len(values)):
            out = jnp.where(index == n, values[n], out)
        return out

    def step_block(s):
        phase = listed(ARRIVAL_PHASES, s)
        t = listed(ARRIVAL_TURNS, s)
        zz = listed([listed(row, z) for row in NEAREST], t)
        f, g, _, _, block = order(zz)
        k = listed((block(f, g), block(1 - f, g), block(f, 1 - g), block(1 - f, 1 - g)), phase)
        return phase, zz, k

    @pl.loop(0, 17)
    def _(s):
        phase, zz, k = step_block(s)

        @pl.when(s < full_cuts)
        def _():
            here = pl.ds(pl.multiple_of(s * 128, 128), 128)
            emb_t[:, here] = emb[here, :].T

        if rows % 128:
            @pl.when(s == full_cuts)
            def _():
                emb_t[:, full_cuts * 128 :] = emb[full_cuts * 128 :, :].T

        @pl.when((s > 0) & (s < 16) & (phase == 0))
        def _():
            for n in range(2):
                up_copy(zz, n).wait_recv()
                pass_along(zz, n, lambda copy: copy.start())
                one_copy(zz, n).start()
                two_copy(zz, 0, n).start()
                sib_copy(k, n).start()

        @pl.when((s < 16) & (phase == 1))
        def _():
            for n in range(2):
                one_copy(zz, n).wait_recv()
                two_copy(zz, 1, n).start()
                sib_copy(k, n).start()

        for j in range(2):
            @pl.when((s < 16) & (phase == 2 + j))
            def _():
                for n in range(2):
                    two_copy(zz, j, n).wait_recv()
                    sib_copy(k, n).start()

        @pl.when(s > 0)
        def _():
            former = step_block(s - 1)[2]
            for n in range(2):
                sib_copy(former, n).wait_recv()
            forward_block(former)

    def joined(parts):
        highest = functools.reduce(jnp.maximum, [p[0] for p in parts])
        total = functools.reduce(jnp.add, [p[1] * jnp.exp(p[0] - highest) for p in parts])
        picked = functools.reduce(jnp.add, [p[2] for p in parts])
        return highest, total, picked

    def rows_of(ref, n):
        return ref[n, 0], ref[n, 1], ref[n, 2]

    for n, (peer, side) in enumerate(((sibling, c), (x_peer, x), (y_peer, y))):
        copy = remote(mine.at[n], theirs.at[n], st_send.at[n], st_recv.at[n], peer)
        copy.start()
        copy.wait()
        here, there = rows_of(mine, n), rows_of(theirs, n)
        early = tuple(jnp.where(side == 0, a, b) for a, b in zip(here, there))
        late = tuple(jnp.where(side == 0, b, a) for a, b in zip(here, there))
        for r, value in enumerate(joined((early, late))):
            mine[n + 1, r] = value

    def stat_copy(d):
        other = lax.rem(z + d, 4)
        return remote(mine.at[3], lined.at[z], stz_send.at[d - 1], stz_recv.at[d - 1], at(x, y, other, c))

    for d in (1, 2, 3):
        stat_copy(d).start()
    for r in range(3):
        lined[z, r] = mine[3, r]
    for d in (1, 2, 3):
        stat_copy(d).wait()
    highest, total, picked = joined([rows_of(lined, n) for n in range(4)])
    logsum = highest + jnp.log(total)
    log_probs = picked - logsum
    for k in range(16):
        prior[k : k + 1, :] = marks[k // 8, (k // 4) % 2, k % 4, 1:2, :]
        usable[k : k + 1, :] = marks[k // 8, (k // 4) % 2, k % 4, 2:3, :]
    lane = lax.broadcasted_iota(jnp.int32, (16, pair), 1) // length
    mean = jnp.zeros((16, pair), jnp.float32)
    for n in range(pair // length):
        inside = lane == n
        slot_sum = jnp.sum(jnp.where(inside, log_probs, 0.0), 1, keepdims=True)
        mean = jnp.where(inside, slot_sum * (1.0 / length), mean)
    scores = prior[...] + mean
    counted = usable[...] > 0.5
    masked = jnp.where(counted, scores, NEGATIVE)
    question = lax.broadcasted_iota(jnp.int32, (16, pair), 0) // 4
    marginal = jnp.zeros((16, pair), jnp.float32)
    loss = jnp.zeros((1, 1), jnp.float32)
    for n in range(4):
        inside = question == n
        high = jnp.max(
            jnp.max(jnp.where(inside, masked, NEGATIVE), 1, keepdims=True), 0, keepdims=True
        )
        terms = jnp.where(inside & counted, jnp.exp(masked - high), 0.0)
        mass = jnp.sum(jnp.sum(terms, 1, keepdims=True), 0, keepdims=True) * (1.0 / length)
        value = high + jnp.log(mass)
        marginal = jnp.where(inside, value, marginal)
        loss = loss + value
    posterior = jnp.where(counted, jnp.exp(scores - marginal), 0.0)
    token_weight = -float(slots) * posterior
    weight[...] = posterior
    scaled[...] = token_weight * jnp.exp(mine[0, 0] - logsum)
    picked_grad[...] = token_weight * (1.0 - jnp.exp(log_probs))
    small_out[...] = jnp.broadcast_to(loss * (-1.0 / 4), small_out.shape)
    own_row = weight[pl.ds(own, 1), :]
    own_row = jnp.where(c == 0, own_row[:, :size], own_row[:, size:])
    small_out[1:2, :] = own_row * (-float(slots * length))

    def backward_block(k):
        target = target_rows(k)
        hit = picked_grad[pl.ds(k, 1), :]
        scale = scaled[pl.ds(k, 1), :]

        def make(j, carried):
            value = expo[cut_rows(j), token_lanes(k)].astype(jnp.float32)
            grad = jnp.where(row_numbers(j) == target, hit, -(value * scale))
            expo[cut_rows(j), token_lanes(k)] = grad.astype(BFLOAT)
            return carried

        lax.fori_loop(0, VOCAB_CUTS, make, 0, unroll=True)

        def to_rows(n, carried):
            cut_width = pl.ds(pl.multiple_of(n * 256, 256), 256)
            value = lax.dot_general(
                emb_t[cut_width, :],
                expo[:, token_lanes(k)],
                (((1,), (0,)), ((), ())),
                preferred_element_type=jnp.float32,
            ).astype(BFLOAT)
            part[k, 0, cut_width, :] = value[:, :size]
            part[k, 1, cut_width, :] = value[:, size:]
            return carried

        lax.fori_loop(0, width // 256, to_rows, 0, unroll=True)

    def dd_copy(k):
        return remote(part.at[k, 1 - c], sib_part.at[k], dd_send.at[k], dd_recv.at[k], sibling)

    def r1_copy(zz, j):
        f, _, first_peer, _, block = order(zz)
        return remote(
            sib_part.at[block(1 - f, j)], part_one.at[zz, j], r1_send.at[zz, j], r1_recv.at[zz, j],
            first_peer,
        )

    def r2_copy(zz):
        _, g, _, second_peer, _ = order(zz)
        return remote(part_one.at[zz, 1 - g], part_two.at[zz], r2_send.at[zz], r2_recv.at[zz], second_peer)

    def rz_copy(zz):
        return remote(part_two.at[zz], part_z.at[z], rz_send.at[zz], rz_recv.at[z], at(x, y, zz, c))

    def rz_arrival(zz):
        return remote(part_two.at[zz], part_z.at[zz], rz_send.at[zz], rz_recv.at[zz], at(x, y, zz, c))

    step = 128

    def add_into(target_ref, other_ref):
        @pl.loop(0, width // step)
        def _(n):
            rows_here = pl.ds(pl.multiple_of(n * step, step), step)
            target_ref[rows_here, :] = (
                target_ref[rows_here, :].astype(jnp.float32) + other_ref[rows_here, :].astype(jnp.float32)
            ).astype(BFLOAT)

    def group(n):
        return lax.rem(n, 2) * 2 + n // 2

    def chunk(q):
        j, n = q // 4, lax.rem(q, 4)
        columns = pl.ds(pl.multiple_of(n * 256, 256), 256)
        gemb_out[cut_rows(j), columns] = lax.dot_general(
            expo[cut_rows(j), :],
            held[:, columns],
            (((1,), (0,)), ((), ())),
            preferred_element_type=jnp.float32,
        ).astype(BFLOAT)

    def grad_block(s):
        leaves = s < 8
        zz = group(lax.rem(s, 8) // 2)
        j = lax.rem(s, 2)
        f, _, _, _, block = order(zz)
        return leaves, zz, j, block(jnp.where(leaves, 1 - f, f), j)

    @pl.loop(0, 28)
    def _(s):
        @pl.when((s >= 2) & (s < 18))
        def _():
            leaves, zz, turn, k = grad_block(s - 2)
            dd_copy(k).wait_recv()
            add_into(sib_part.at[k], part.at[k, c])
            for j in range(2):
                @pl.when(leaves & (turn == j))
                def _():
                    r1_copy(zz, j).start()

        @pl.when((lax.rem(s, 2) == 1) & (s >= 11) & (s < 18))
        def _():
            zz = group((s - 11) // 2)
            f, _, _, _, block = order(zz)
            for j in range(2):
                r1_copy(zz, j).wait_recv()
                add_into(part_one.at[zz, j], sib_part.at[block(f, j)])
            r2_copy(zz).start()

        @pl.when((lax.rem(s, 2) == 0) & (s >= 16) & (s < 24))
        def _():
            zz = group((s - 16) // 2)
            _, g, _, _, _ = order(zz)
            r2_copy(zz).wait_recv()
            add_into(part_two.at[zz], part_one.at[zz, g])

            @pl.when(zz != z)
            def _():
                rz_copy(zz).start()

        @pl.when(s < 16)
        def _():
            k = grad_block(s)[3]
            backward_block(k)
            dd_copy(k).start()

        @pl.when(s >= 16)
        def _():
            chunk(s - 16)

    for d in (1, 2, 3):
        rz_arrival(lax.rem(z + d, 4)).wait_recv()

    @pl.loop(0, width // step)
    def _(n):
        rows_here = pl.ds(pl.multiple_of(n * step, step), step)
        value = part_two[z, rows_here, :].astype(jnp.float32)
        for d in (1, 2, 3):
            value = value + part_z[lax.rem(z + d, 4), rows_here, :].astype(jnp.float32)
        third_out[rows_here, :] = value

    for d in (1, 2, 3):
        rz_copy(lax.rem(z + d, 4)).wait_send()

    @pl.loop(0, 4)
    def _(zz):
        for n in range(2):
            pass_along(zz, n, lambda copy: copy.wait_send())
            one_copy(zz, n).wait_send()
            for j in range(2):
                two_copy(zz, j, n).wait_send()
        for j in range(2):
            r1_copy(zz, j).wait_send()
        r2_copy(zz).wait_send()

    @pl.loop(0, 16)
    def _(k):
        for n in range(2):
            sib_copy(k, n).wait_send()
        dd_copy(k).wait_send()


def vocabulary_head(third_low, marks, embedding, slots, length):
    size, width = third_low.shape
    vocab_here = embedding.shape[0]
    rows = 16 * VOCAB_CUTS * -(-vocab_here // (4 * 16 * VOCAB_CUTS))
    dma = pltpu.SemaphoreType.DMA
    vmem = pl.BlockSpec(memory_space=pltpu.VMEM)
    stat = (3, 16, 2 * size)
    f32 = jnp.float32
    block = (width, size)
    small, gemb, third = pl.pallas_call(
        functools.partial(head_kernel, slots, length, vocab_here),
        out_shape=(
            jax.ShapeDtypeStruct((8, size), f32),
            jax.ShapeDtypeStruct((rows, width), BFLOAT),
            jax.ShapeDtypeStruct((width, size), f32),
        ),
        in_specs=[vmem, vmem, pl.BlockSpec(memory_space=pl.ANY)],
        out_specs=(vmem,) * 3,
        scratch_shapes=[
            pltpu.VMEM((rows, width), BFLOAT),
            pltpu.VMEM((width, rows), BFLOAT),
            pltpu.VMEM((32 * size, width), BFLOAT),
            pltpu.VMEM((rows, 2 * size), f32),
            pltpu.VMEM((rows, 32 * size), BFLOAT),
            pltpu.VMEM((16, 2) + block, BFLOAT),
            pltpu.VMEM((16,) + block, BFLOAT),
            pltpu.VMEM((4, 2) + block, BFLOAT),
            pltpu.VMEM((4,) + block, BFLOAT),
            pltpu.VMEM((4,) + block, BFLOAT),
            pltpu.VMEM((4,) + stat, f32),
            pltpu.VMEM((3,) + stat, f32),
            pltpu.VMEM((4,) + stat, f32),
        ]
        + [pltpu.VMEM((16, 2 * size), f32)] * 5
        + [dma((4,))]
        + [dma((2, 4, 2)), dma((4, 2))]
        + [dma((4, 2))] * 2
        + [dma((4, 2, 2))] * 2
        + [dma((16, 2))] * 2
        + [dma((3,))] * 4
        + [dma((16,))] * 2
        + [dma((4, 2))] * 2
        + [dma((4,))] * 4,
        compiler_params=pltpu.CompilerParams(
            collective_id=2, has_side_effects=True, vmem_limit_bytes=60 * 2**20
        ),
        name="vocabulary_head",
    )(third_low, marks, embedding)
    return small, gemb, third


def merged(part, axis, combine):
    gathered = jax.tree.map(lambda a: lax.all_gather(a, axis), part)

    def take(source):
        return jax.tree.map(lambda a: lax.dynamic_index_in_dim(a, source, 0, False), gathered)

    return lax.fori_loop(
        1, lax.axis_size(axis), lambda source, state: combine(state, take(source)), take(0)
    )


def matmul(matrix_left, matrix_right):
    return lax.dot_general(
        matrix_left,
        matrix_right,
        (((matrix_left.ndim - 1,), (0,)), ((), ())),
        preferred_element_type=jnp.float32,
    )


def matmul_back(matrix_left, matrix_right):
    return lax.dot_general(
        matrix_left,
        matrix_right,
        (((matrix_left.ndim - 1,), (1,)), ((), ())),
        preferred_element_type=jnp.float32,
    )


def outer_sum(matrix_left, matrix_right):
    flat_left = matrix_left.reshape(-1, matrix_left.shape[-1])
    flat_right = matrix_right.reshape(-1, matrix_right.shape[-1])
    return lax.dot_general(
        flat_left, flat_right, (((0,), (0,)), ((), ())), preferred_element_type=jnp.float32
    )


def split_heads(values):
    return values.reshape(values.shape[0], values.shape[1], HEADS, HEAD_DIM)


def join_heads(values):
    return values.reshape(values.shape[0], values.shape[1], HEADS * HEAD_DIM)


def exact_gelu(values):
    return jax.nn.gelu(values, approximate=False)


def norm_forward(values, gain_row, shift_row):
    centre = values - jnp.mean(values, -1, keepdims=True)
    inverse = lax.rsqrt(jnp.mean(centre * centre, -1, keepdims=True) + EPSILON)
    normed = centre * inverse
    return (normed * gain_row.astype(jnp.float32) + shift_row.astype(jnp.float32), normed, inverse)


def norm_backward(upstream, normed, inverse, gain_row):
    scaled = upstream * gain_row.astype(jnp.float32)
    mean_scaled = jnp.mean(scaled, -1, keepdims=True)
    along_normed = jnp.mean(scaled * normed, -1, keepdims=True)
    grad_values = inverse * (scaled - mean_scaled - normed * along_normed)
    model_width = upstream.shape[-1]
    grad_gain = jnp.sum((upstream * normed).reshape(-1, model_width), 0)
    grad_shift = jnp.sum(upstream.reshape(-1, model_width), 0)
    return (grad_values, grad_gain, grad_shift)


def score_block(queries, key_rows, causal):
    scores = jnp.einsum(
        "nqhd,nkhd->nhqk", queries, key_rows, preferred_element_type=jnp.float32
    ) * (1.0 / math.sqrt(HEAD_DIM))
    if causal:
        length = queries.shape[1]
        allowed = lax.broadcasted_iota(jnp.int32, (length, length), 0) >= lax.broadcasted_iota(
            jnp.int32, (length, length), 1
        )
        scores = jnp.where(allowed, scores, NEGATIVE)
    return scores


def attend(queries, key_rows, values, causal):
    scores = score_block(queries, key_rows, causal)
    highest = jnp.max(scores, -1, keepdims=True)
    totals = jnp.sum(jnp.exp(scores - highest), -1, keepdims=True)
    logsum = highest + jnp.log(totals)
    probs_low = jnp.exp(scores - logsum).astype(BFLOAT)
    context = jnp.einsum(
        "nhqk,nkhd->nqhd", probs_low, values, preferred_element_type=jnp.float32
    ).astype(BFLOAT)
    return (join_heads(context), logsum)


def attend_back(grad_context, queries, key_rows, values, logsum, causal):
    score_scale = 1.0 / math.sqrt(HEAD_DIM)
    probs_full = jnp.exp(score_block(queries, key_rows, causal) - logsum)
    grad_heads = split_heads(grad_context)
    grad_probs = jnp.einsum(
        "nqhd,nkhd->nhqk", grad_heads, values, preferred_element_type=jnp.float32
    )
    grad_values = jnp.einsum(
        "nhqk,nqhd->nkhd", probs_full.astype(BFLOAT), grad_heads, preferred_element_type=jnp.float32
    ).astype(BFLOAT)
    grad_scores = (
        probs_full * (grad_probs - jnp.sum(probs_full * grad_probs, -1, keepdims=True))
    ).astype(BFLOAT)
    grad_queries = (
        jnp.einsum("nhqk,nkhd->nqhd", grad_scores, key_rows, preferred_element_type=jnp.float32)
        * score_scale
    ).astype(BFLOAT)
    grad_keys = (
        jnp.einsum("nhqk,nqhd->nkhd", grad_scores, queries, preferred_element_type=jnp.float32)
        * score_scale
    ).astype(BFLOAT)
    return (join_heads(grad_queries), join_heads(grad_keys), join_heads(grad_values))


def layer_forward(inputs, encoded, weights):
    (
        packed_weight,
        output_weight,
        query_weight,
        memory_weight,
        cross_weight,
        expand_weight,
        reduce_weight,
        gains,
        shifts,
    ) = weights
    model_width = inputs.shape[-1]
    packed = matmul(inputs, packed_weight).astype(BFLOAT)
    context, self_logsum = attend(
        split_heads(packed[..., :model_width]),
        split_heads(packed[..., model_width : 2 * model_width]),
        split_heads(packed[..., 2 * model_width :]),
        True,
    )
    first_norm, first_normed, first_inverse = norm_forward(
        inputs.astype(jnp.float32) + matmul(context, output_weight), gains[0], shifts[0]
    )
    first_low = first_norm.astype(BFLOAT)
    cross_queries = matmul(first_low, query_weight).astype(BFLOAT)
    memory_pairs = matmul(encoded, memory_weight).astype(BFLOAT)
    cross_context, cross_logsum = attend(
        split_heads(cross_queries),
        split_heads(memory_pairs[..., :model_width]),
        split_heads(memory_pairs[..., model_width:]),
        False,
    )
    second, second_normed, second_inverse = norm_forward(
        first_norm + matmul(cross_context, cross_weight), gains[1], shifts[1]
    )
    second_low = second.astype(BFLOAT)
    inner_pre = matmul(second_low, expand_weight)
    active = exact_gelu(inner_pre).astype(BFLOAT)
    third_norm, third_normed, third_inverse = norm_forward(
        second + matmul(active, reduce_weight), gains[2], shifts[2]
    )
    stored = (
        packed,
        context,
        self_logsum,
        first_normed,
        first_inverse,
        first_low,
        cross_queries,
        memory_pairs,
        cross_context,
        cross_logsum,
        second_normed,
        second_inverse,
        second_low,
        inner_pre,
        active,
        third_normed,
        third_inverse,
    )
    return (third_norm.astype(BFLOAT), stored)


def layer_backward(grad_third, inputs, encoded, weights, stored):
    (
        packed_weight,
        output_weight,
        query_weight,
        memory_weight,
        cross_weight,
        expand_weight,
        reduce_weight,
        gains,
        shifts,
    ) = weights
    (
        packed,
        context,
        self_logsum,
        first_normed,
        first_inverse,
        first_low,
        cross_queries,
        memory_pairs,
        cross_context,
        cross_logsum,
        second_normed,
        second_inverse,
        second_low,
        inner_pre,
        active,
        third_normed,
        third_inverse,
    ) = stored
    model_width = inputs.shape[-1]
    grad_res3, gain_three, shift_three = norm_backward(
        grad_third, third_normed, third_inverse, gains[2]
    )
    grad_output = grad_res3.astype(BFLOAT)
    grad_reduce = outer_sum(active, grad_output)
    grad_active = matmul_back(grad_output, reduce_weight)
    _, gelu_pull = jax.vjp(exact_gelu, inner_pre)
    grad_inner = gelu_pull(grad_active)[0].astype(BFLOAT)
    grad_expand = outer_sum(second_low, grad_inner)
    grad_second = grad_res3 + matmul_back(grad_inner, expand_weight)
    grad_res2, gain_two, shift_two = norm_backward(
        grad_second, second_normed, second_inverse, gains[1]
    )
    grad_mixed = grad_res2.astype(BFLOAT)
    grad_cross_weight = outer_sum(cross_context, grad_mixed)
    grad_cross_context = matmul_back(grad_mixed, cross_weight).astype(BFLOAT)
    grad_cross_queries, grad_memory_keys, grad_memory_values = attend_back(
        grad_cross_context,
        split_heads(cross_queries),
        split_heads(memory_pairs[..., :model_width]),
        split_heads(memory_pairs[..., model_width:]),
        cross_logsum,
        False,
    )
    grad_query_weight = outer_sum(first_low, grad_cross_queries)
    grad_first = grad_res2 + matmul_back(grad_cross_queries, query_weight)
    grad_pairs = jnp.concatenate([grad_memory_keys, grad_memory_values], -1)
    grad_memory_weight = outer_sum(encoded, grad_pairs)
    grad_encoded = matmul_back(grad_pairs, memory_weight)
    grad_res1, gain_one, shift_one = norm_backward(
        grad_first, first_normed, first_inverse, gains[0]
    )
    grad_merged = grad_res1.astype(BFLOAT)
    grad_output_weight = outer_sum(context, grad_merged)
    grad_context = matmul_back(grad_merged, output_weight).astype(BFLOAT)
    grad_queries, grad_keys, grad_values = attend_back(
        grad_context,
        split_heads(packed[..., :model_width]),
        split_heads(packed[..., model_width : 2 * model_width]),
        split_heads(packed[..., 2 * model_width :]),
        self_logsum,
        True,
    )
    grad_packed = jnp.concatenate([grad_queries, grad_keys, grad_values], -1)
    grad_packed_weight = outer_sum(inputs, grad_packed)
    grad_inputs = grad_res1 + matmul_back(grad_packed, packed_weight)
    grad_gains = jnp.stack([gain_one, gain_two, gain_three])
    grad_shifts = jnp.stack([shift_one, shift_two, shift_three])
    return (
        grad_inputs,
        grad_encoded,
        (
            grad_packed_weight,
            grad_output_weight,
            grad_query_weight,
            grad_memory_weight,
            grad_cross_weight,
            grad_expand,
            grad_reduce,
            grad_gains,
            grad_shifts,
        ),
    )


def combine_scores(former, latter):
    highest = jnp.maximum(former[0], latter[0])
    totals = former[1] * jnp.exp(former[0] - highest) + latter[1] * jnp.exp(latter[0] - highest)
    return (highest, totals, former[2] + latter[2])


def combine_pairs(former, latter):
    highest = jnp.maximum(former[0], latter[0])
    totals = former[1] * jnp.exp(former[0] - highest) + latter[1] * jnp.exp(latter[0] - highest)
    return (highest, totals)


def per_device(
    decoder_states,
    encoder_memory,
    target_tokens,
    log_prior,
    slot_counts,
    slot_mask,
    self_packed,
    self_output,
    cross_query,
    cross_memory,
    cross_output,
    feed_expand,
    feed_reduce,
    embedding,
    norm_gains,
    norm_shifts,
):
    weights = (
        lax.all_gather(self_packed, "pa", axis=0, tiled=True),
        lax.all_gather(self_output, "pa", axis=0, tiled=True),
        lax.all_gather(cross_query, "pa", axis=0, tiled=True),
        lax.all_gather(cross_memory, "pa", axis=0, tiled=True),
        lax.all_gather(cross_output, "pa", axis=0, tiled=True),
        lax.all_gather(feed_expand, "pa", axis=0, tiled=True),
        lax.all_gather(feed_reduce, "pa", axis=0, tiled=True),
        lax.all_gather(norm_gains, "pa", axis=1, tiled=True),
        lax.all_gather(norm_shifts, "pa", axis=1, tiled=True),
    )
    questions, slots_here, length, model_width = decoder_states.shape
    mem_length = encoder_memory.shape[2]
    batch_size = questions * slots_here
    inputs = decoder_states.reshape(batch_size, length, model_width)
    encoded = encoder_memory.reshape(batch_size, mem_length, model_width)
    third_low, stored = layer_forward(inputs, encoded, weights)
    tokens_here = batch_size * length
    rows_all, tokens_all = (
        lax.all_gather(third_low.reshape(tokens_here, model_width), "pa", axis=0, tiled=True),
        lax.all_gather(target_tokens.reshape(tokens_here), "pa", axis=0, tiled=True),
    )
    total_rows = rows_all.shape[0]
    block_rows = min(total_rows, 2048)
    block_count = total_rows // block_rows
    vocab_start = lax.axis_index("pa") * embedding.shape[0]
    row_blocks = rows_all.reshape(block_count, block_rows, model_width)
    token_blocks = tokens_all.reshape(block_count, block_rows)

    def vocab_logits(hidden_rows, token_rows):
        logits = matmul_back(hidden_rows, embedding)
        column = lax.broadcasted_iota(jnp.int32, logits.shape, 1) + vocab_start
        return (logits, column == token_rows[:, None])

    def vocab_partial(pieces):
        logits, chosen = vocab_logits(pieces[0], pieces[1])
        highest = jnp.max(logits, -1)
        totals = jnp.sum(jnp.exp(logits - highest[:, None]), -1)
        picked = jnp.sum(jnp.where(chosen, logits, 0.0), -1)
        return (highest, totals, picked)

    highest, totals, picked = lax.map(vocab_partial, (row_blocks, token_blocks))
    highest, totals, picked = merged(
        (highest.reshape(total_rows), totals.reshape(total_rows), picked.reshape(total_rows)),
        "pa",
        combine_scores,
    )
    row_logsum = highest + jnp.log(totals)
    own_start = lax.axis_index("pa") * tokens_here
    own_logsum = lax.dynamic_slice_in_dim(row_logsum, own_start, tokens_here)
    own_picked = lax.dynamic_slice_in_dim(picked, own_start, tokens_here)
    log_probs = (own_picked - own_logsum).reshape(questions, slots_here, length)
    scores = log_prior + jnp.mean(log_probs, -1)
    slot_index = lax.axis_index("pa") * slots_here + lax.broadcasted_iota(
        jnp.int32, (questions, slots_here), 1
    )
    usable = (slot_mask == 1) & (slot_index < slot_counts[:, None])
    masked = jnp.where(usable, scores, NEGATIVE)
    local_high = jnp.max(masked, -1)
    local_total = jnp.sum(jnp.where(usable, jnp.exp(masked - local_high[:, None]), 0.0), -1)
    slot_high, slot_total = merged((local_high, local_total), "pa", combine_pairs)
    marginal = slot_high + jnp.log(slot_total)
    posterior = jnp.where(usable, jnp.exp(scores - marginal[:, None]), 0.0)
    loss_value = -lax.psum(jnp.sum(marginal), "pb") / (questions * lax.axis_size("pb"))
    slot_number = slots_here * lax.axis_size("pa")
    grad_prior = -(slot_number * length) * posterior
    token_grad = jnp.broadcast_to(
        (-slot_number * posterior)[:, :, None], (questions, slots_here, length)
    ).reshape(tokens_here)
    weights_all = lax.all_gather(token_grad, "pa", axis=0, tiled=True)

    def vocab_grads(accumulated, pieces):
        hidden_rows, token_rows, logsum_rows, weight_rows = pieces
        logits, chosen = vocab_logits(hidden_rows, token_rows)
        softmax_rows = jnp.exp(logits - logsum_rows[:, None])
        grad_logits = (weight_rows[:, None] * (jnp.where(chosen, 1.0, 0.0) - softmax_rows)).astype(
            BFLOAT
        )
        return (accumulated + outer_sum(grad_logits, hidden_rows), matmul(grad_logits, embedding))

    grad_embed, grad_rows = lax.scan(
        vocab_grads,
        jnp.zeros(embedding.shape, jnp.float32),
        (
            row_blocks,
            token_blocks,
            row_logsum.reshape(block_count, block_rows),
            weights_all.reshape(block_count, block_rows),
        ),
    )
    grad_third = lax.psum_scatter(
        grad_rows.reshape(total_rows, model_width).astype(BFLOAT),
        "pa",
        scatter_dimension=0,
        tiled=True,
    ).astype(jnp.float32).reshape(batch_size, length, model_width)
    grad_inputs, grad_encoded, grads = layer_backward(grad_third, inputs, encoded, weights, stored)
    shares = (
        lax.psum_scatter(grads[0].astype(BFLOAT), "pa", scatter_dimension=0, tiled=True),
        lax.psum_scatter(grads[1].astype(BFLOAT), "pa", scatter_dimension=0, tiled=True),
        lax.psum_scatter(grads[2].astype(BFLOAT), "pa", scatter_dimension=0, tiled=True),
        lax.psum_scatter(grads[3].astype(BFLOAT), "pa", scatter_dimension=0, tiled=True),
        lax.psum_scatter(grads[4].astype(BFLOAT), "pa", scatter_dimension=0, tiled=True),
        lax.psum_scatter(grads[5].astype(BFLOAT), "pa", scatter_dimension=0, tiled=True),
        lax.psum_scatter(grads[6].astype(BFLOAT), "pa", scatter_dimension=0, tiled=True),
        lax.psum_scatter(grads[7], "pa", scatter_dimension=1, tiled=True),
        lax.psum_scatter(grads[8], "pa", scatter_dimension=1, tiled=True),
    )
    outputs = lax.psum(
        (
            shares[0],
            shares[1],
            shares[2],
            shares[3],
            shares[4],
            shares[5],
            shares[6],
            shares[7],
            shares[8],
            grad_embed.astype(BFLOAT),
        ),
        "pb",
    )
    outputs = tuple(part.astype(jnp.float32) for part in outputs)
    return (
        loss_value,
        grad_inputs.reshape(decoder_states.shape),
        grad_encoded.reshape(encoder_memory.shape),
        grad_prior,
        outputs[0],
        outputs[1],
        outputs[2],
        outputs[3],
        outputs[4],
        outputs[5],
        outputs[6],
        outputs[9],
        outputs[7],
        outputs[8],
    )


def per_device_kernels(
    decoder_states,
    encoder_memory,
    target_tokens,
    log_prior,
    slot_counts,
    slot_mask,
    self_packed,
    self_output,
    cross_query,
    cross_memory,
    cross_output,
    feed_expand,
    feed_reduce,
    embedding,
    norm_gains,
    norm_shifts,
):
    shards = (
        self_packed,
        self_output,
        cross_query,
        cross_memory,
        cross_output,
        feed_expand,
        feed_reduce,
    )
    norm_rows = jnp.concatenate(
        [norm_gains, norm_shifts, jnp.zeros((2, norm_gains.shape[1]), BFLOAT)]
    ).astype(jnp.float32)
    _, slots_here, length, model_width = decoder_states.shape
    slots = slots_here * lax.axis_size("pa")
    states = decoder_states.reshape(slots_here * length, model_width)
    memory = encoder_memory.reshape(-1, model_width)
    slot_index = lax.axis_index("pa") * slots_here + jnp.arange(slots_here)
    usable = (slot_mask[0] == 1) & (slot_index < slot_counts[0])
    marks = jnp.concatenate(
        [
            target_tokens.reshape(1, slots_here * length).astype(jnp.float32),
            jnp.repeat(log_prior, length, axis=1),
            jnp.repeat(usable[None].astype(jnp.float32), length, axis=1),
            jnp.zeros((5, slots_here * length), jnp.float32),
        ]
    )
    matrices, marks, norms, kept = forward_layer(
        shards, norm_rows, marks, states, memory, length
    )
    small, grad_embed, grad_third = vocabulary_head(
        kept[-1], marks, embedding, slots, length
    )
    loss_value = small[0, 0]
    grad_prior = small[1].reshape(1, slots_here, length)[:, :, 0]
    shares, norm_sums, grad_inputs, grad_encoded, pieces = backward_layer(
        matrices,
        kept[:11] + kept[12:15] + (states, memory),
        kept[11],
        norms,
        grad_third,
        grad_embed,
        length,
    )
    pieces = pieces.reshape(4 * grad_embed.shape[0], model_width)
    shares, grad_embed, grad_gains, grad_shifts = widen(
        shares, pieces, norm_sums, embedding.shape[0], norm_gains.shape[1]
    )
    return (
        loss_value,
        grad_inputs.reshape(decoder_states.shape),
        grad_encoded.reshape(encoder_memory.shape),
        grad_prior,
    ) + tuple(shares) + (grad_embed, grad_gains, grad_shifts)


def solution(mesh):
    own_kernels = mesh.shape["pb"] == 4 and mesh.shape["pa"] == 8
    return jax.shard_map(
        per_device_kernels if own_kernels else per_device,
        mesh=mesh,
        in_specs=(
            P("pb", "pa", None, None),
            P("pb", "pa", None, None),
            P("pb", "pa", None),
            P("pb", "pa"),
            P("pb"),
            P("pb", "pa"),
            P("pa", None),
            P("pa", None),
            P("pa", None),
            P("pa", None),
            P("pa", None),
            P("pa", None),
            P("pa", None),
            P("pa", None),
            P(None, "pa"),
            P(None, "pa"),
        ),
        out_specs=(
            P(),
            P("pb", "pa", None, None),
            P("pb", "pa", None, None),
            P("pb", "pa"),
            P("pa", None),
            P("pa", None),
            P("pa", None),
            P("pa", None),
            P("pa", None),
            P("pa", None),
            P("pa", None),
            P("pa", None),
            P(None, "pa"),
            P(None, "pa"),
        ),
        check_vma=False,
    )
```

```python
import functools
import math

import jax
import jax.numpy as jnp
from jax import lax
from jax.experimental import pallas as pl
from jax.experimental.pallas import tpu as pltpu
from jax.sharding import PartitionSpec as P

HEADS = 16
HEAD_DIM = 64


EPSILON = 1e-05
NEGATIVE = -1e30
BFLOAT = jnp.bfloat16
MESH = pl.DeviceIdType.MESH
TILE = 1024
ROWS = 128
WEIGHT_UNITS = (3, 1, 1, 2, 1, 4, 4)
UNITS = tuple((w, k) for w, n in enumerate(WEIGHT_UNITS) for k in range(n))
REDUCE_WEIGHT = 6


def whereami():
    pb = lax.axis_index("pb")
    pa = lax.axis_index("pa")
    return lax.rem(pb, 2), pb // 2, pa // 2, lax.rem(pa, 2)


def greet(peers):
    barrier = pltpu.get_barrier_semaphore()
    for peer in peers:
        pl.semaphore_signal(barrier, inc=1, device_id=peer, device_id_type=MESH)
    pl.semaphore_wait(barrier, len(peers))


def at(x, y, z, c):
    return (y * 2 + x, z * 2 + c)


def neighbours(x, y, z, c):
    return [at(1 - x, y, z, c), at(x, 1 - y, z, c), at(x, y, z, 1 - c)] + [
        at(x, y, lax.rem(z + d, 4), c) for d in (1, 2, 3)
    ]


def shard_view(ref, unit, start, size):
    weight, block = unit
    if weight == REDUCE_WEIGHT:
        return ref.at[pl.ds(block * ROWS + start, size), :]
    return ref.at[pl.ds(start, size), pl.ds(block * TILE, TILE)]


def full_view(ref, unit, place, core, start, size):
    weight, block = unit
    if weight == REDUCE_WEIGHT:
        return ref.at[place, core, block, pl.ds(start, size), :]
    return ref.at[place, core, pl.ds(start, size), pl.ds(block * TILE, TILE)]


Z_FULL = (13, 14, 15)


HOP_LAG = 1
LAG_TWO, LAG_SIBLING, LAG_LOAD, LAG_USE = 3, 6, 8, 9
SLOTS_IN_FLIGHT = 3


def dot_nn(left, right):
    return lax.dot_general(left, right, (((1,), (0,)), ((), ())), preferred_element_type=jnp.float32)


def dot_nt(left, right):
    return lax.dot_general(left, right, (((1,), (1,)), ((), ())), preferred_element_type=jnp.float32)


def dot_tn(left, right):
    return lax.dot_general(left, right, (((0,), (0,)), ((), ())), preferred_element_type=jnp.float32)


def stack_heads(pair):
    lane = lax.broadcasted_iota(jnp.int32, pair.shape, 1)
    zero = jnp.zeros_like(pair)
    return jnp.concatenate(
        [jnp.where(lane < HEAD_DIM, pair, zero), jnp.where(lane < HEAD_DIM, zero, pair)], 0
    )


def unstack_heads(stacked):
    rows = stacked.shape[0] // 2
    lane = lax.broadcasted_iota(jnp.int32, (rows, stacked.shape[1]), 1)
    return jnp.where(lane < HEAD_DIM, stacked[:rows], stacked[rows:])


def pair_scores(queries, keys, causal):
    scores = dot_nt(queries, keys) * (1.0 / math.sqrt(HEAD_DIM))
    if causal:
        length = keys.shape[0]
        row = lax.rem(lax.broadcasted_iota(jnp.int32, scores.shape, 0), length)
        column = lax.broadcasted_iota(jnp.int32, scores.shape, 1)
        scores = jnp.where(row >= column, scores, NEGATIVE)
    highest = jnp.max(scores, -1, keepdims=True)
    total = jnp.sum(jnp.exp(scores - highest), -1, keepdims=True)
    return jnp.exp(scores - (highest + jnp.log(total)))


def attend_pair(queries, keys, values, causal):
    probs = pair_scores(stack_heads(queries), keys, causal).astype(BFLOAT)
    return unstack_heads(dot_nn(probs, values)).astype(BFLOAT)


def normalise(values, gain, shift):
    centre = values - jnp.mean(values, -1, keepdims=True)
    inverse = lax.rsqrt(jnp.mean(centre * centre, -1, keepdims=True) + EPSILON)
    normed = centre * inverse
    return normed * gain + shift, normed, inverse


def forward_kernel(length, mem_length, *refs):
    shards, norm, aux, states_hbm, encoded_hbm = refs[:7], refs[7], refs[8], refs[9], refs[10]
    fulls, marks, kept_hbm = refs[11:18], refs[18], refs[19:36]
    (
        norm_full, packed, context, first_normed, first_inverse, first_low, cross_queries, pairs,
        cross_context, second_normed, second_inverse, second_low, inner, active, third_normed,
        third_inverse, third_low,
    ) = refs[36:53]
    wbuf, residual, states, encoded, held = refs[53:58]
    (
        local_sem, z_send, z_recv, one_send, one_recv, two_send, two_recv, d_send, d_recv,
        norm_sem, nz_send, nz_recv, nd_send, nd_recv, load_sem, ax_sem, ax_send, ax_recv,
        axz_send, axz_recv, kept_sem, input_sem, take_sem,
    ) = refs[58:]
    x, y, z, c = whereami()
    greet(neighbours(x, y, z, c))
    every = slice(None)
    tokens, width = states_hbm.shape
    slots_here = tokens // length

    def copies(u):
        unit = UNITS[u]
        shard, full = shards[unit[0]], fulls[unit[0]]
        wide = u in Z_FULL
        a, b = (x, y) if u % 2 == 0 else (y, x)
        first_peer = at(x, 1 - y, z, c) if u % 2 == 0 else at(1 - x, y, z, c)
        second_peer = at(1 - x, y, z, c) if u % 2 == 0 else at(x, 1 - y, z, c)
        quarter = pl.multiple_of(64 * a + 32 * b, 32)
        half = pl.multiple_of(64 * a, 64)
        rows = (0, ROWS) if wide else (quarter, 32)
        place = held.at[pl.ds(sum(ROWS if n in Z_FULL else 32 for n in range(u)), rows[1]), :]
        take = pltpu.make_async_copy(shard_view(shard, unit, *rows), place, take_sem.at[u])
        local = pltpu.make_async_copy(place, full_view(full, unit, z, c, *rows), local_sem.at[u])
        def along(origin, direction, own=False):
            block = full_view(full, unit, origin, c, *rows)
            return pltpu.make_async_remote_copy(
                src_ref=place if own else block,
                dst_ref=block,
                send_sem=z_send.at[u, (direction + 1) // 2, origin],
                recv_sem=z_recv.at[u, origin],
                device_id=at(x, y, z + direction, c),
                device_id_type=MESH,
            )

        def cross(start, size, sends, recvs, peer):
            part = full_view(full, unit, every, c, start, size)
            return pltpu.make_async_remote_copy(
                src_ref=part,
                dst_ref=part,
                send_sem=sends.at[u],
                recv_sem=recvs.at[u],
                device_id=peer,
                device_id_type=MESH,
            )

        first = None if wide else cross(quarter, 32, one_send, one_recv, first_peer)
        second = None if wide else cross(half, 64, two_send, two_recv, second_peer)
        sibling = cross(0, ROWS, d_send, d_recv, at(x, y, z, 1 - c))
        load = pltpu.make_async_copy(
            full_view(full, unit, every, every, 0, ROWS),
            wbuf.at[u % SLOTS_IN_FLIGHT],
            load_sem.at[u % SLOTS_IN_FLIGHT],
        )
        return (take, local), along, first, second, sibling, load

    def norm_copy(src, dst, send, recv, peer):
        return pltpu.make_async_remote_copy(
            src_ref=src, dst_ref=dst, send_sem=send, recv_sem=recv, device_id=peer, device_id_type=MESH
        )

    norm_local = pltpu.make_async_copy(norm, norm_full.at[z, c], norm_sem)
    norm_along = [
        norm_copy(
            norm, norm_full.at[z, c], nz_send.at[d - 1], nz_recv.at[d - 1], at(x, y, lax.rem(z + d, 4), c)
        )
        for d in (1, 2, 3)
    ]
    norm_sibling = norm_copy(
        norm_full.at[:, c], norm_full.at[:, c], nd_send, nd_recv, at(x, y, z, 1 - c)
    )
    norm_local.start()
    for copy in norm_along:
        copy.start()

    lanes = pl.ds(pl.multiple_of(c * tokens, tokens), tokens)
    aux_local = pltpu.make_async_copy(aux, marks.at[y, x, z, :, lanes], ax_sem)
    aux_local.start()
    aux_steps = [
        norm_copy(part, part, ax_send.at[n], ax_recv.at[n], peer)
        for n, (part, peer) in enumerate(
            (
                (marks.at[y, x, z, :, lanes], at(x, y, z, 1 - c)),
                (marks.at[y, x, z], at(1 - x, y, z, c)),
                (marks.at[y, :, z], at(x, 1 - y, z, c)),
            )
        )
    ]
    aux_along = [
        norm_copy(
            marks.at[:, :, z], marks.at[:, :, z], axz_send.at[d - 1], axz_recv.at[d - 1],
            at(x, y, lax.rem(z + d, 4), c),
        )
        for d in (1, 2, 3)
    ]

    kept = (
        norm_full, packed, context, first_normed, first_inverse, first_low, cross_queries, pairs,
        cross_context, second_normed, second_inverse, second_low, inner, active, third_normed,
        third_inverse, third_low,
    )

    def keep(*numbers):
        for n in numbers:
            pltpu.make_async_copy(kept[n], kept_hbm[n], kept_sem.at[n]).start()

    states_copy = pltpu.make_async_copy(states_hbm, states, input_sem.at[0])
    encoded_copy = pltpu.make_async_copy(encoded_hbm, encoded, input_sem.at[1])
    states_copy.start()
    encoded_copy.start()

    def norm_row(n):
        return jnp.concatenate(
            [norm_full[p // 2, p % 2, n : n + 1, :] for p in range(8)], 1
        )

    def times(left_ref, u, write):
        slot = u % SLOTS_IN_FLIGHT

        @pl.loop(0, 4, unroll=True)
        def _(n):
            columns = pl.ds(pl.multiple_of(n * 256, 256), 256)
            right = wbuf[slot, :, :, :, columns].reshape(TILE, 256)
            write(columns, n, dot_nn(left_ref[...], right))

    def block_columns(k, n):
        return pl.ds(pl.multiple_of(k * TILE + n * 256, 256), 256)

    def attention(queries, keys, key_start, value_start, key_length, out, causal):
        @pl.loop(0, slots_here * (width // 128), unroll=2)
        def _(n):
            slot, group = n // (width // 128), lax.rem(n, width // 128)
            lanes = pl.ds(pl.multiple_of(group * 128, 128), 128)
            key_lanes = pl.ds(pl.multiple_of(key_start + group * 128, 128), 128)
            value_lanes = pl.ds(pl.multiple_of(value_start + group * 128, 128), 128)
            query_rows = pl.ds(pl.multiple_of(slot * length, length), length)
            key_rows = pl.ds(pl.multiple_of(slot * key_length, key_length), key_length)
            out[query_rows, lanes] = attend_pair(
                queries[query_rows, lanes], keys[key_rows, key_lanes], keys[key_rows, value_lanes], causal
            )

    def finish_norm(n, value, normed_ref, inverse_ref, low_ref):
        out, normed, inverse = normalise(value, norm_row(n), norm_row(n + 3))
        normed_ref[...] = normed
        inverse_ref[...] = jnp.broadcast_to(inverse, inverse_ref.shape)
        low_ref[...] = out.astype(BFLOAT)
        return out

    def use(u):
        weight, k = UNITS[u]
        if weight == 0:
            def write(columns, n, value):
                packed[:, block_columns(k, n)] = value.astype(BFLOAT)

            times(states, u, write)
            if k == 2:
                attention(packed, packed, width, 2 * width, length, context, True)
                keep(1, 2)
        elif weight == 1:
            def write(columns, n, value):
                residual[:, columns] = states[:, columns].astype(jnp.float32) + value

            times(context, u, write)
            residual[...] = finish_norm(0, residual[...], first_normed, first_inverse, first_low)
            keep(3, 4, 5)
        elif weight == 2:
            def write(columns, n, value):
                cross_queries[:, columns] = value.astype(BFLOAT)

            times(first_low, u, write)
        elif weight == 3:
            slot = u % SLOTS_IN_FLIGHT

            @pl.loop(0, 8)
            def _(n):
                m, n = n // 4, lax.rem(n, 4)
                columns = pl.ds(pl.multiple_of(n * 256, 256), 256)
                part = encoded.shape[0] // 2
                rows_here = pl.ds(pl.multiple_of(m * part, part), part)
                right = wbuf[slot, :, :, :, columns].reshape(TILE, 256)
                pairs[rows_here, block_columns(k, n)] = dot_nn(encoded[rows_here, :], right).astype(BFLOAT)

            if k == 1:
                attention(cross_queries, pairs, 0, width, mem_length, cross_context, False)
                keep(6, 7, 8)
        elif weight == 4:
            def write(columns, n, value):
                residual[:, columns] = residual[:, columns] + value

            times(cross_context, u, write)
            residual[...] = finish_norm(1, residual[...], second_normed, second_inverse, second_low)
            keep(9, 10, 11)
        elif weight == 5:
            def write(columns, n, value):
                inner[:, block_columns(k, n)] = value
                gate = 0.5 * (1.0 + lax.erf(value * math.sqrt(0.5)))
                active[:, block_columns(k, n)] = (value * gate).astype(BFLOAT)

            times(second_low, u, write)
            if k == 3:
                keep(12, 13)
        else:
            slot = u % SLOTS_IN_FLIGHT
            blocks = active.shape[1] // (8 * ROWS)
            left = jnp.concatenate(
                [active[:, (p * blocks + k) * ROWS : (p * blocks + k + 1) * ROWS] for p in range(8)], 1
            )

            @pl.loop(0, 4, unroll=True)
            def _(n):
                columns = pl.ds(pl.multiple_of(n * 256, 256), 256)
                right = wbuf[slot, :, :, :, columns].reshape(TILE, 256)
                residual[:, columns] = residual[:, columns] + dot_nn(left, right)

            if k == blocks - 1:
                finish_norm(2, residual[...], third_normed, third_inverse, third_low)
                keep(14, 15, 16)

    count = len(UNITS)
    every_copy = [copies(u) for u in range(count)]

    def hop(u, h):
        (take, local), along = every_copy[u][:2]
        if h == 1:
            take.wait()
            local.start()
        if h == 4:
            local.wait()
        for origin, there, edge, direction in (
            (z - (h - 1), z >= h - 1, z < 3, 1),
            (z + (h - 1), z + (h - 1) <= 3, z > 0, -1),
        ):
            @pl.when(there)
            def _():
                if h > 1:
                    along(origin, direction).wait_recv()
                if h < 4:
                    @pl.when(edge)
                    def _():
                        along(origin, direction, h == 1).start()

    for copies_here in every_copy:
        copies_here[0][0].start()
    for h in range(1, 4):
        for u in range(HOP_LAG * (4 - h)):
            hop(u, h)
    for i in range(count + LAG_USE):
        for h in range(1, 5):
            u = i + HOP_LAG * (4 - h)
            if u < count:
                hop(u, h)
        if i < count:
            first = every_copy[i][2]
            if first is not None:
                first.start()
        if 0 <= i - LAG_TWO < count:
            first, second = every_copy[i - LAG_TWO][2:4]
            if first is not None:
                first.wait_recv()
                second.start()
        if 0 <= i - LAG_SIBLING < count:
            second, sibling = every_copy[i - LAG_SIBLING][3:5]
            if second is not None:
                second.wait_recv()
            sibling.start()
        if i == 2:
            norm_local.wait()
            for copy in norm_along:
                copy.wait()
            norm_sibling.start()
        if i == 4:
            norm_sibling.wait()
            keep(0)
            states_copy.wait()
            encoded_copy.wait()
        if 5 <= i < 9:
            if i == 5:
                aux_local.wait()
            else:
                aux_steps[i - 6].wait()
            for copy in aux_steps[i - 5 : i - 4] if i < 8 else aux_along:
                copy.start()
        if i == 9:
            for copy in aux_along:
                copy.wait()
        if 0 <= i - LAG_LOAD < count:
            sibling, load = every_copy[i - LAG_LOAD][4:]
            sibling.wait_recv()
            load.start()
        if 0 <= i - LAG_USE < count:
            every_copy[i - LAG_USE][5].wait()
            use(i - LAG_USE)
    for _, along, first, second, sibling, _ in every_copy:
        for origin in range(4):
            @pl.when((origin <= z) & (z < 3))
            def _():
                along(origin, 1).wait_send()

            @pl.when((origin >= z) & (z > 0))
            def _():
                along(origin, -1).wait_send()

        if first is not None:
            first.wait_send()
            second.wait_send()
        sibling.wait_send()
    for n in range(len(kept)):
        pltpu.make_async_copy(kept[n], kept_hbm[n], kept_sem.at[n]).wait()


def forward_layer(weights, norm, aux, states, encoded, length):
    count = len(UNITS)
    shapes = []
    for w, weight in enumerate(weights):
        if w == REDUCE_WEIGHT:
            shapes.append((4, 2, weight.shape[0] // ROWS, ROWS, weight.shape[1]))
        else:
            shapes.append((4, 2) + weight.shape)
    tokens, width = states.shape
    mem_tokens = encoded.shape[0]
    mem_length = mem_tokens // (tokens // length)
    units = weights[5].shape[1]
    f32 = jnp.float32
    kept = [
        ((4, 2) + norm.shape, f32),
        ((tokens, 3 * width), BFLOAT),
        ((tokens, width), BFLOAT),
        ((tokens, width), f32),
        ((tokens, 128), f32),
        ((tokens, width), BFLOAT),
        ((tokens, width), BFLOAT),
        ((mem_tokens, 2 * width), BFLOAT),
        ((tokens, width), BFLOAT),
        ((tokens, width), f32),
        ((tokens, 128), f32),
        ((tokens, width), BFLOAT),
        ((tokens, units), f32),
        ((tokens, units), BFLOAT),
        ((tokens, width), f32),
        ((tokens, 128), f32),
        ((tokens, width), BFLOAT),
    ]
    every = pl.BlockSpec(memory_space=pl.ANY)
    dma = pltpu.SemaphoreType.DMA
    results = pl.pallas_call(
        functools.partial(forward_kernel, length, mem_length),
        out_shape=tuple(jax.ShapeDtypeStruct(shape, BFLOAT) for shape in shapes)
        + (jax.ShapeDtypeStruct((2, 2, 4, aux.shape[0], 2 * tokens), f32),)
        + tuple(jax.ShapeDtypeStruct(shape, kind) for shape, kind in kept),
        in_specs=[every] * 11,
        out_specs=(every,) * (8 + len(kept)),
        scratch_shapes=[pltpu.VMEM(shape, kind) for shape, kind in kept]
        + [
            pltpu.VMEM((SLOTS_IN_FLIGHT, 4, 2, ROWS, TILE), BFLOAT),
            pltpu.VMEM((tokens, width), f32),
            pltpu.VMEM((tokens, width), BFLOAT),
            pltpu.VMEM((mem_tokens, width), BFLOAT),
            pltpu.VMEM((sum(ROWS if n in Z_FULL else 32 for n in range(count)), TILE), BFLOAT),
            dma((count,)),
            dma((count, 2, 4)),
            dma((count, 4)),
        ]
        + [dma((count,))] * 6
        + [dma]
        + [dma((3,))] * 2
        + [dma] * 2
        + [dma((SLOTS_IN_FLIGHT,))]
        + [dma]
        + [dma((3,))] * 4
        + [dma((len(kept),)), dma((2,)), dma((count,))],
        compiler_params=pltpu.CompilerParams(
            collective_id=0, has_side_effects=True, vmem_limit_bytes=62 * 2**20
        ),
        name="forward_layer",
    )(*weights, norm, aux, states, encoded)
    fulls = tuple(full.reshape(-1, full.shape[-1]) for full in results[:7])
    return fulls, results[7], results[8], results[9:]


SEQUENCE = tuple((6, k) for k in range(4)) + tuple((5, k) for k in range(4)) + (
    (4, 0), (2, 0), (3, 0), (3, 1), (1, 0), (0, 0), (0, 1), (0, 2),
)
LINE_FIRST = 9
HOP_LAGS = (4, 7, 10)
LINE_LAGS = (10, 12, 14, 16, 18)
CROSS_LAGS = (2, 4, 6, 8, 10)
TURNS = 27
GATHER_TURNS = (4, 8)
READS = tuple(read for k in range(4) for read in ((6, k), (5, k))) + (
    (4, 0), (2, 0), (1, 0), (0, 0), (0, 1), (0, 2), (3, 0), (3, 1),
)


def norm_back(upstream, normed, inverse, gain):
    scaled = upstream * gain
    mean_scaled = jnp.mean(scaled, -1, keepdims=True)
    along = jnp.mean(scaled * normed, -1, keepdims=True)
    return (
        inverse * (scaled - mean_scaled - normed * along),
        jnp.sum(upstream * normed, 0, keepdims=True),
        jnp.sum(upstream, 0, keepdims=True),
    )


def attend_pair_back(grad, queries, keys, values, causal):
    scale = 1.0 / math.sqrt(HEAD_DIM)
    queries, grad = stack_heads(queries), stack_heads(grad)
    probs = pair_scores(queries, keys, causal)
    grad_probs = dot_nt(grad, values)
    grad_values = dot_tn(probs.astype(BFLOAT), grad).astype(BFLOAT)
    grad_scores = (
        probs * (grad_probs - jnp.sum(probs * grad_probs, -1, keepdims=True))
    ).astype(BFLOAT)
    grad_queries = unstack_heads(dot_nn(grad_scores, keys) * scale).astype(BFLOAT)
    grad_keys = (dot_tn(grad_scores, queries) * scale).astype(BFLOAT)
    return grad_queries, grad_keys, grad_values


def backward_kernel(length, mem_length, *refs):
    weights = refs[:7]
    kept_hbm = refs[7:23]
    inner_hbm = refs[23]
    norm_full, grad_third, gemb = refs[24:27]
    outs = refs[27:34]
    norm_out, grad_states, grad_memory, pieces, landing = refs[34:39]
    kept = refs[39:55]
    (
        wbuf, inner, stage, got, zload, one_line, two_line, one, two, line, fin,
        resid, low, grad_low, grad_context, grad_queries, grad_packed, memory_part,
        norm_here, norm_there, norm_line,
    ) = refs[55:76]
    (
        kept_sem, w_sem, inner_sem, dd_send, dd_recv, z_send, z_recv, zload_sem,
        ra_send, ra_recv, rb_send, rb_recv, rz_send, rz_recv, ag_send, ag_recv, ah_send, ah_recv,
        fin_sem, memory_sem, n_send, n_recv, nz_send, nz_recv, gemb_sem, ga_send, ga_recv,
        gb_send, gb_recv,
    ) = refs[76:]
    (
        packed, context, first_normed, first_inverse, first_low, cross_queries, pairs, cross_context,
        second_normed, second_inverse, second_low, active, third_normed, third_inverse, states, encoded,
    ) = kept
    x, y, z, c = whereami()
    greet(neighbours(x, y, z, c))
    tokens, width = states.shape
    slots_here = tokens // length
    count = len(SEQUENCE)
    blocks = active.shape[1] // (8 * ROWS)

    def keep_copy(n):
        return pltpu.make_async_copy(kept_hbm[n], kept[n], kept_sem.at[n])

    first_needed = (12, 13, 11, 10)
    for n in first_needed:
        keep_copy(n).start()
    for n in range(16):
        if n not in first_needed:
            keep_copy(n).start()

    def need(*names):
        for n in names:
            keep_copy(n).wait()

    def read_copy(n):
        weight, k = READS[n]
        if weight == REDUCE_WEIGHT:
            source = weights[weight].at[pl.ds(k * TILE, TILE), :]
        else:
            source = weights[weight].at[:, pl.ds(k * TILE, TILE)]
        return pltpu.make_async_copy(source, wbuf.at[n % 2], w_sem.at[n % 2])

    def inner_copy(k):
        return pltpu.make_async_copy(
            inner_hbm.at[:, pl.ds(k * TILE, TILE)], inner.at[k % 2], inner_sem.at[k % 2]
        )

    read_copy(0).start()
    read_copy(1).start()
    inner_copy(0).start()
    inner_copy(1).start()

    def remote(src, dst, send, recv, peer):
        return pltpu.make_async_remote_copy(
            src_ref=src, dst_ref=dst, send_sem=send, recv_sem=recv, device_id=peer, device_id_type=MESH
        )

    def norm_row(n):
        return jnp.concatenate([norm_full[p // 2, p % 2, n : n + 1, :] for p in range(8)], 1)

    def place(q):
        even = lax.rem(q, 2) == 0
        a = jnp.where(even, x, y)
        b = jnp.where(even, y, x)
        x_peer = y * 2 + (1 - x)
        y_peer = (1 - y) * 2 + x
        a_peer = (jnp.where(even, x_peer, y_peer), z * 2 + c)
        b_peer = (jnp.where(even, y_peer, x_peer), z * 2 + c)
        return a, b, a_peer, b_peer

    def piece(index, size):
        return pl.ds(pl.multiple_of(index * size, size), size)

    def total(*parts):
        out = parts[0].astype(jnp.float32)
        for part in parts[1:]:
            out = out + part.astype(jnp.float32)
        return out.astype(BFLOAT)

    pb = y * 2 + x
    pb_x, pb_y = y * 2 + 1 - x, (1 - y) * 2 + x
    vocab_rows = gemb.shape[0]
    cut = 16 * (vocab_rows // 64)
    cuts = [(n * cut, cut if n < 3 else vocab_rows - 3 * cut) for n in range(4)]

    def gather_one(n):
        rows_here = pl.ds(*cuts[n])
        peer = at(1 - x, y, z, c) if n < 2 else at(x, 1 - y, z, c)
        return remote(gemb.at[rows_here, :], pieces.at[pb, rows_here, :], ga_send.at[n], ga_recv.at[n], peer)

    def gather_two(n, j):
        rows_here = pl.ds(*cuts[n])
        peer = at(x, 1 - y, z, c) if n < 2 else at(1 - x, y, z, c)
        origin = pb if j == 0 else (pb_x if n < 2 else pb_y)
        source = gemb.at[rows_here, :] if j == 0 else pieces.at[origin, rows_here, :]
        return remote(source, pieces.at[origin, rows_here, :], gb_send.at[n, j], gb_recv.at[n, j], peer)

    gemb_copy = pltpu.make_async_copy(gemb, pieces.at[pb], gemb_sem)
    for n in (0, 2, 1, 3):
        gather_one(n).start()
    for n in (2, 0, 3, 1):
        gather_two(n, 0).start()
    gemb_copy.start()

    def dd_copy(q):
        return remote(
            stage.at[lax.rem(q, 2), 1 - c], got.at[q], dd_send.at[q], dd_recv.at[q], at(x, y, z, 1 - c)
        )

    def line_copy(q, side, h, dest, step):
        return remote(
            got.at[q, dest], landing.at[q, side, h - 1], z_send.at[q, side, h - 1],
            z_recv.at[q, side, h - 1], at(x, y, z + step, c),
        )

    def line_sides(h):
        return (
            (0, z + 4 - h, z <= h - 1, z >= 1, 1),
            (1, z - 4 + h, z >= 4 - h, z <= 2, -1),
        )

    def line_load(q, side, h):
        return pltpu.make_async_copy(landing.at[q, side, h - 2], zload.at[side], zload_sem.at[side])

    def line_hop(q, h):
        if h > 1:
            for side, dest, there, fed, step in line_sides(h):
                @pl.when(there & fed)
                def _():
                    line_copy(q, side, h - 1, dest, step).wait_recv()
                    line_load(q, side, h).start()

        for side, dest, there, fed, step in line_sides(h):
            if h > 1:
                @pl.when(there & fed)
                def _():
                    line_load(q, side, h).wait()

                    @pl.loop(0, 8)
                    def _(j):
                        rows_here = piece(j, 16)
                        got[q, dest, rows_here, :] = total(
                            got[q, dest, rows_here, :], zload[side, rows_here, :]
                        )

            if h < 4:
                @pl.when(there)
                def _():
                    line_copy(q, side, h, dest, step).start()

    def ra_line(q):
        a, _, a_peer, _ = place(q)
        return remote(got.at[q, z, piece(1 - a, 64), :], one_line.at[q], ra_send.at[q], ra_recv.at[q], a_peer)

    def rb_line(q):
        _, b, _, b_peer = place(q)
        return remote(one_line.at[q, piece(1 - b, 32), :], two_line.at[q], rb_send.at[q], rb_recv.at[q], b_peer)

    def ra_cross(q):
        a, _, a_peer, _ = place(q)
        return remote(
            got.at[q, :, piece(1 - a, 64), :], one.at[q - LINE_FIRST], ra_send.at[q], ra_recv.at[q], a_peer
        )

    def rb_cross(q):
        _, b, _, b_peer = place(q)
        return remote(
            one.at[q - LINE_FIRST, :, piece(1 - b, 32), :], two.at[q - LINE_FIRST],
            rb_send.at[q], rb_recv.at[q], b_peer,
        )

    def rz_cross(q, d):
        other = lax.rem(z + d, 4)
        n = q - LINE_FIRST
        return remote(
            two.at[n, other], line.at[n, d - 1], rz_send.at[n, d - 1], rz_recv.at[n, d - 1],
            at(x, y, other, c),
        )

    def out_view(q, start, size):
        return shard_view(outs[SEQUENCE[q][0]], SEQUENCE[q], start, size)

    def quarter_start(q):
        a, b, _, _ = place(q)
        return pl.multiple_of(64 * a + 32 * b, 32)

    def fin_copy(q):
        return pltpu.make_async_copy(fin.at[q], out_view(q, quarter_start(q), 32), fin_sem.at[q])

    def ag_copy(q):
        return remote(
            fin.at[q], out_view(q, quarter_start(q), 32), ag_send.at[q], ag_recv.at[q], place(q)[3]
        )

    def ah_copy(q):
        a, _, a_peer, _ = place(q)
        part = out_view(q, pl.multiple_of(64 * a, 64), 64)
        return remote(part, part, ah_send.at[q], ah_recv.at[q], a_peer)

    norm_peers = (at(x, y, z, 1 - c), at(1 - x, y, z, c), at(x, 1 - y, z, c))

    def norm_copy(n):
        return remote(norm_here.at[n], norm_there.at[n], n_send.at[n], n_recv.at[n], norm_peers[n])

    def norm_line_copy(d):
        return remote(
            norm_here.at[3], norm_line.at[d - 1], nz_send.at[d - 1], nz_recv.at[d - 1],
            at(x, y, lax.rem(z + d, 4), c),
        )

    def outer(q, left, start, step, right):
        slot = q % 2

        @pl.loop(0, 8, unroll=4)
        def _(p):
            lanes = pl.ds(pl.multiple_of(start + p * step, 128), 128)
            stage[slot, lax.rem(p, 2), p // 2] = dot_tn(left[:, lanes], right()).astype(BFLOAT)

    def back_times(left, n, write):
        slot = n % 2
        read_copy(n).wait()

        @pl.loop(0, 4, unroll=True)
        def _(m):
            write(piece(m, 256), dot_nt(left[...], wbuf[slot, piece(m, 256), :]))

        if n + 2 < len(READS):
            read_copy(n + 2).start()

    def add_resid(columns, value):
        resid[:, columns] = resid[:, columns] + value

    def finish_norm(n, normed, inverse):
        value, gain, shift = norm_back(resid[...], normed[...], inverse[:, 0:1], norm_row(n))
        resid[...] = value
        low[...] = value.astype(BFLOAT)
        norm_here[0, n : n + 1, :] = gain
        norm_here[0, n + 3 : n + 4, :] = shift

    def attention_back(queries, keys, key_start, value_start, key_length, out, out_keys, causal):
        @pl.loop(0, slots_here * (width // 128), unroll=2)
        def _(n):
            slot, group = n // (width // 128), lax.rem(n, width // 128)
            lanes = piece(group, 128)
            key_lanes = pl.ds(pl.multiple_of(key_start + group * 128, 128), 128)
            value_lanes = pl.ds(pl.multiple_of(value_start + group * 128, 128), 128)
            query_rows = piece(slot, length)
            key_rows = piece(slot, key_length)
            grad_query, grad_key, grad_value = attend_pair_back(
                grad_context[query_rows, lanes],
                queries[query_rows, lanes],
                keys[key_rows, key_lanes],
                keys[key_rows, value_lanes],
                causal,
            )
            out[query_rows, lanes] = grad_query
            out_keys[key_rows, key_lanes] = grad_key
            out_keys[key_rows, value_lanes] = grad_value

    def produce(q):
        weight, k = SEQUENCE[q]
        if q == 0:
            norm_here[0] = jnp.zeros_like(norm_here[0])
            for p in range(8):
                resid[:, p * 128 : (p + 1) * 128] = grad_third[p * 128 : (p + 1) * 128, :].T
            need(12, 13, 11)
            finish_norm(2, third_normed, third_inverse)
        if weight == 6:
            outer(q, active, k * ROWS, blocks * ROWS, lambda: low[...])
        elif weight == 5:
            if k == 0:
                need(10)
            inner_copy(k).wait()

            def write(columns, value):
                pre = inner[k % 2, :, columns]
                slope = 0.5 * (1.0 + lax.erf(pre * math.sqrt(0.5))) + pre * jnp.exp(
                    -0.5 * pre * pre
                ) * (1.0 / math.sqrt(2.0 * math.pi))
                grad_low[:, columns] = (value * slope).astype(BFLOAT)

            back_times(low, 2 * k, write)
            if k + 2 < 4:
                inner_copy(k + 2).start()
            outer(q, second_low, 0, ROWS, lambda: grad_low[...])
            back_times(grad_low, 2 * k + 1, add_resid)
        elif weight == 4:
            need(8, 9, 7)
            finish_norm(1, second_normed, second_inverse)
            outer(q, cross_context, 0, ROWS, lambda: low[...])

            def write(columns, value):
                grad_context[:, columns] = value.astype(BFLOAT)

            back_times(low, 8, write)
        elif weight == 2:
            need(5, 6, 4, 2, 3)
            attention_back(cross_queries, pairs, 0, width, mem_length, grad_queries, pairs, False)
            outer(q, first_low, 0, ROWS, lambda: grad_queries[...])
            back_times(grad_queries, 9, add_resid)
            finish_norm(0, first_normed, first_inverse)
        elif weight == 3:
            if k == 0:
                need(15)
            outer(q, encoded, 0, ROWS, lambda: pairs[:, pl.ds(k * TILE, TILE)])
        elif weight == 1:
            need(1, 0, 14)
            outer(q, context, 0, ROWS, lambda: low[...])

            def write(columns, value):
                grad_context[:, columns] = value.astype(BFLOAT)

            back_times(low, 10, write)
            attention_back(packed, packed, width, 2 * width, length, grad_packed, grad_packed, True)
        else:
            def part():
                return grad_packed[:, pl.ds(k * TILE, TILE)]

            outer(q, states, 0, ROWS, part)
            back_times(grad_packed.at[:, pl.ds(k * TILE, TILE)], 11 + k, add_resid)
            if k == 2:
                grad_states[...] = resid[...]

    half = encoded.shape[0] // 2

    def memory_copy(m):
        return pltpu.make_async_copy(
            memory_part.at[m % 2],
            grad_memory.at[pl.ds(m // 4 * half, half), pl.ds(m % 4 * 256, 256)],
            memory_sem.at[m % 2],
        )

    def memory_chunk(m):
        if m == 0:
            read_copy(14).wait()
            read_copy(15).wait()
        if m >= 2:
            memory_copy(m - 2).wait()
        rows_here, columns = pl.ds(m // 4 * half, half), pl.ds(m % 4 * 256, 256)
        memory_part[m % 2] = dot_nt(pairs[rows_here, :width], wbuf[0, columns, :]) + dot_nt(
            pairs[rows_here, width:], wbuf[1, columns, :]
        )
        memory_copy(m).start()

    def each(q, action):
        for k in range(count):
            @pl.when(q == k)
            def _():
                action(k)

    def finish_block(q):
        def action(k):
            fin_copy(k).start()
            ag_copy(k).start()

        each(q, action)

    step = 16

    @pl.loop(0, TURNS)
    def _(i):
        for q in range(count):
            @pl.when(i == q)
            def _():
                if q >= 2:
                    dd_copy(q - 2).wait_send()
                produce(q)
                dd_copy(q).start()

        for n, turn in enumerate(GATHER_TURNS):
            @pl.when(i == turn)
            def _():
                for part in (n, n + 2):
                    gather_one(part).wait_recv()
                    gather_two(part, 1).start()

        for m in range(8):
            @pl.when(i == count + 1 + m)
            def _():
                memory_chunk(m)

        qs = i - 1

        @pl.when((qs >= 0) & (qs < count))
        def _():
            dd_copy(qs).wait_recv()
            slot = lax.rem(qs, 2)

            @pl.loop(0, 32)
            def _(j):
                zz, rows_here = j // 8, piece(lax.rem(j, 8), step)
                got[qs, zz, rows_here, :] = total(got[qs, zz, rows_here, :], stage[slot, c, zz, rows_here, :])

            @pl.when(qs < LINE_FIRST)
            def _():
                line_hop(qs, 1)

            @pl.when(qs >= LINE_FIRST)
            def _():
                ra_cross(qs).start()

        for h in (2, 3, 4):
            qh = i - HOP_LAGS[h - 2]

            @pl.when((qh >= 0) & (qh < LINE_FIRST))
            def _():
                line_hop(qh, h)
                if h == 4:
                    ra_line(qh).start()

        q1 = i - LINE_LAGS[1]

        @pl.when((q1 >= 0) & (q1 < LINE_FIRST))
        def _():
            ra_line(q1).wait_recv()
            a = place(q1)[0]

            @pl.loop(0, 4)
            def _(j):
                rows_here = piece(j, step)
                one_line[q1, rows_here, :] = total(
                    one_line[q1, rows_here, :],
                    got[q1, z, pl.ds(pl.multiple_of(64 * a + j * step, step), step), :],
                )

            rb_line(q1).start()

        q2 = i - LINE_LAGS[2]

        @pl.when((q2 >= 0) & (q2 < LINE_FIRST))
        def _():
            rb_line(q2).wait_recv()
            b = place(q2)[1]

            @pl.loop(0, 2)
            def _(j):
                rows_here = piece(j, step)
                fin[q2, rows_here, :] = total(
                    two_line[q2, rows_here, :],
                    one_line[q2, pl.ds(pl.multiple_of(32 * b + j * step, step), step), :],
                )

            finish_block(q2)

        p0 = i - CROSS_LAGS[0]

        @pl.when((p0 >= LINE_FIRST) & (p0 < count))
        def _():
            ra_cross(p0).wait_recv()
            a = place(p0)[0]

            @pl.loop(0, 16)
            def _(j):
                zz, r = j // 4, lax.rem(j, 4)
                rows_here = piece(r, step)
                one[p0 - LINE_FIRST, zz, rows_here, :] = total(
                    one[p0 - LINE_FIRST, zz, rows_here, :],
                    got[p0, zz, pl.ds(pl.multiple_of(64 * a + r * step, step), step), :],
                )

            rb_cross(p0).start()

        p1 = i - CROSS_LAGS[1]

        @pl.when((p1 >= LINE_FIRST) & (p1 < count))
        def _():
            rb_cross(p1).wait_recv()
            b = place(p1)[1]

            @pl.loop(0, 8)
            def _(j):
                zz, r = j // 2, lax.rem(j, 2)
                rows_here = piece(r, step)
                two[p1 - LINE_FIRST, zz, rows_here, :] = total(
                    two[p1 - LINE_FIRST, zz, rows_here, :],
                    one[p1 - LINE_FIRST, zz, pl.ds(pl.multiple_of(32 * b + r * step, step), step), :],
                )

            for d in (1, 2, 3):
                rz_cross(p1, d).start()

        p2 = i - CROSS_LAGS[2]

        @pl.when((p2 >= LINE_FIRST) & (p2 < count))
        def _():
            for d in (1, 2, 3):
                rz_cross(p2, d).wait_recv()
            n = p2 - LINE_FIRST

            @pl.loop(0, 2)
            def _(j):
                rows_here = piece(j, step)
                fin[p2, rows_here, :] = total(
                    two[n, z, rows_here, :], line[n, 0, rows_here, :], line[n, 1, rows_here, :],
                    line[n, 2, rows_here, :],
                )

            finish_block(p2)

        def pass_on(k):
            ag_copy(k).wait_recv()
            fin_copy(k).wait()
            ah_copy(k).start()

        for lags, low_q, high_q in ((LINE_LAGS, 0, LINE_FIRST), (CROSS_LAGS, LINE_FIRST, count)):
            q3 = i - lags[3]

            @pl.when((q3 >= low_q) & (q3 < high_q))
            def _():
                each(q3, pass_on)

            q4 = i - lags[4]

            @pl.when((q4 >= low_q) & (q4 < high_q))
            def _():
                each(q4, lambda k: ah_copy(k).wait_recv())

        @pl.when(i == count)
        def _():
            norm_copy(0).start()

        for n in range(3):
            @pl.when(i == count + 2 * (n + 1))
            def _():
                norm_copy(n).wait_recv()
                norm_here[n + 1] = norm_here[n] + norm_there[n]
                if n < 2:
                    norm_copy(n + 1).start()
                else:
                    for d in (1, 2, 3):
                        norm_line_copy(d).start()

        @pl.when(i == count + 8)
        def _():
            for d in (1, 2, 3):
                norm_line_copy(d).wait_recv()
            norm_out[...] = ((norm_here[3] + norm_line[0]) + norm_line[1]) + norm_line[2]

    gemb_copy.wait()
    for n in range(4):
        gather_one(n).wait_send()
        for j in range(2):
            gather_two(n, j).wait()
    memory_copy(6).wait()
    memory_copy(7).wait()
    dd_copy(count - 2).wait_send()
    dd_copy(count - 1).wait_send()

    @pl.loop(0, LINE_FIRST)
    def _(q):
        for h in (1, 2, 3):
            for side, dest, there, _, step in line_sides(h):
                @pl.when(there)
                def _():
                    line_copy(q, side, h, dest, step).wait_send()

        ra_line(q).wait_send()
        rb_line(q).wait_send()

    @pl.loop(LINE_FIRST, count)
    def _(q):
        ra_cross(q).wait_send()
        rb_cross(q).wait_send()
        for d in (1, 2, 3):
            rz_cross(q, d).wait_send()

    for q in range(count):
        ag_copy(q).wait_send()
        ah_copy(q).wait_send()
    for n in range(3):
        norm_copy(n).wait_send()
        norm_line_copy(n + 1).wait_send()


def backward_layer(weights, kept, inner, norm_full, grad_third, gemb, length):
    count = len(SEQUENCE)
    f32 = jnp.float32
    tokens, width = kept[14].shape
    mem_tokens = kept[15].shape[0]
    mem_length = mem_tokens // (tokens // length)
    shapes = [(weight.shape[0] // 8, weight.shape[1]) for weight in weights]
    every = pl.BlockSpec(memory_space=pl.ANY)
    vmem = pl.BlockSpec(memory_space=pltpu.VMEM)
    dma = pltpu.SemaphoreType.DMA
    sems = dma((count,))
    crossed = count - LINE_FIRST
    *shares, norm_sum, grad_states, grad_memory, pieces, _ = pl.pallas_call(
        functools.partial(backward_kernel, length, mem_length),
        out_shape=tuple(jax.ShapeDtypeStruct(shape, BFLOAT) for shape in shapes)
        + (
            jax.ShapeDtypeStruct((8, width), f32),
            jax.ShapeDtypeStruct((tokens, width), f32),
            jax.ShapeDtypeStruct((mem_tokens, width), f32),
            jax.ShapeDtypeStruct((4,) + gemb.shape, BFLOAT),
            jax.ShapeDtypeStruct((LINE_FIRST, 2, 3, ROWS, TILE), BFLOAT),
        ),
        in_specs=[every] * 24 + [vmem] * 2 + [every],
        out_specs=(every,) * 7 + (vmem, vmem, every, every, every),
        scratch_shapes=[pltpu.VMEM(part.shape, part.dtype) for part in kept]
        + [
            pltpu.VMEM((2, TILE, TILE), BFLOAT),
            pltpu.VMEM((2, tokens, TILE), f32),
            pltpu.VMEM((2, 2, 4, ROWS, TILE), BFLOAT),
            pltpu.VMEM((count, 4, ROWS, TILE), BFLOAT),
            pltpu.VMEM((2, ROWS, TILE), BFLOAT),
            pltpu.VMEM((LINE_FIRST, 64, TILE), BFLOAT),
            pltpu.VMEM((LINE_FIRST, 32, TILE), BFLOAT),
            pltpu.VMEM((crossed, 4, 64, TILE), BFLOAT),
            pltpu.VMEM((crossed, 4, 32, TILE), BFLOAT),
            pltpu.VMEM((crossed, 3, 32, TILE), BFLOAT),
            pltpu.VMEM((count, 32, TILE), BFLOAT),
            pltpu.VMEM((tokens, width), f32),
            pltpu.VMEM((tokens, width), BFLOAT),
            pltpu.VMEM((tokens, TILE), BFLOAT),
            pltpu.VMEM((tokens, width), BFLOAT),
            pltpu.VMEM((tokens, width), BFLOAT),
            pltpu.VMEM((tokens, 3 * width), BFLOAT),
            pltpu.VMEM((2, mem_tokens // 2, 256), f32),
            pltpu.VMEM((4, 8, width), f32),
            pltpu.VMEM((3, 8, width), f32),
            pltpu.VMEM((3, 8, width), f32),
            dma((16,)), dma((2,)), dma((2,)), sems, sems,
            dma((LINE_FIRST, 2, 3)), dma((LINE_FIRST, 2, 3)), dma((2,)),
            sems, sems, sems, sems,
            dma((crossed, 3)), dma((crossed, 3)),
            sems, sems, sems, sems, sems, dma((2,)),
            dma((3,)), dma((3,)), dma((3,)), dma((3,)),
            dma, dma((4,)), dma((4,)), dma((4, 2)), dma((4, 2)),
        ],
        compiler_params=pltpu.CompilerParams(
            collective_id=1, has_side_effects=True, vmem_limit_bytes=62 * 2**20
        ),
        name="backward_layer",
    )(*weights, *kept, inner, norm_full, grad_third, gemb)
    return shares, norm_sum, grad_states, grad_memory, pieces


WIDE_ROWS = 512
WIDE_SLOTS = 4


def widen_kernel(embed_rows, *refs):
    parts, pieces, norms, done = refs[:7], refs[7], refs[8], refs[9:11]
    outs, embed_out, done_out = refs[11:18], refs[18], refs[19:21]
    gains_out, shifts_out = refs[21:23]
    low, wide = refs[23:30], refs[30:37]
    embed_low, embed_wide, norm_here, done_here = refs[37:40] + (refs[40:42],)
    in_sem, out_sem, embed_in, embed_out_sem, norm_sem, done_sem = refs[42:]
    done_in = [pltpu.make_async_copy(done[n], done_here[n], done_sem.at[n]) for n in range(2)]
    done_copies = [
        pltpu.make_async_copy(done_here[n], done_out[n], done_sem.at[n + 2]) for n in range(2)
    ]
    here = norm_here.shape[1]
    norm_copy = pltpu.make_async_copy(
        norms.at[:, pl.ds(pl.multiple_of(lax.axis_index("pa") * here, here), here)], norm_here, norm_sem
    )
    norm_copy.start()
    full = embed_rows // WIDE_ROWS
    rest = embed_rows - full * WIDE_ROWS

    def load(n, rows):
        return pltpu.make_async_copy(
            pieces.at[pl.ds(n * WIDE_ROWS, rows), :],
            embed_low.at[n % WIDE_SLOTS, pl.ds(0, rows), :],
            embed_in.at[n % WIDE_SLOTS],
        )

    def store(n, rows):
        return pltpu.make_async_copy(
            embed_wide.at[n % WIDE_SLOTS, pl.ds(0, rows), :],
            embed_out.at[pl.ds(n * WIDE_ROWS, rows), :],
            embed_out_sem.at[n % WIDE_SLOTS],
        )

    sizes = [WIDE_ROWS] * full + [rest] * (rest > 0)
    for n in range(WIDE_SLOTS):
        load(n, sizes[n]).start()
    for n in range(7):
        pltpu.make_async_copy(parts[n], low[n], in_sem.at[n]).start()
    for copy in done_in:
        copy.start()
    for n, rows in enumerate(sizes):
        load(n, rows).wait()
        if n >= WIDE_SLOTS:
            store(n - WIDE_SLOTS, sizes[n - WIDE_SLOTS]).wait()

        @pl.loop(0, rows // 16, unroll=4)
        def _(j):
            part = pl.ds(pl.multiple_of(j * 16, 16), 16)
            embed_wide[n % WIDE_SLOTS, part, :] = embed_low[n % WIDE_SLOTS, part, :].astype(jnp.float32)

        store(n, rows).start()
        if n + WIDE_SLOTS < len(sizes):
            load(n + WIDE_SLOTS, sizes[n + WIDE_SLOTS]).start()
    for n in range(7):
        pltpu.make_async_copy(parts[n], low[n], in_sem.at[n]).wait()

        @pl.loop(0, low[n].shape[0] // 16)
        def _(j):
            part = pl.ds(pl.multiple_of(j * 16, 16), 16)
            wide[n][part, :] = low[n][part, :].astype(jnp.float32)

        pltpu.make_async_copy(wide[n], outs[n], out_sem.at[n]).start()
    for n in range(2):
        done_in[n].wait()
        done_copies[n].start()
    norm_copy.wait()
    gains_out[...] = norm_here[0:3, :]
    shifts_out[...] = norm_here[3:6, :]
    for n in range(len(sizes) - WIDE_SLOTS, len(sizes)):
        store(n, sizes[n]).wait()
    for n in range(7):
        pltpu.make_async_copy(wide[n], outs[n], out_sem.at[n]).wait()
    for copy in done_copies:
        copy.wait()


def widen(parts, pieces, norms, done, embed_rows, norm_here):
    every = pl.BlockSpec(memory_space=pl.ANY)
    vmem = pl.BlockSpec(memory_space=pltpu.VMEM)
    f32 = jnp.float32
    width = pieces.shape[1]
    dma = pltpu.SemaphoreType.DMA
    results = pl.pallas_call(
        functools.partial(widen_kernel, embed_rows),
        out_shape=tuple(jax.ShapeDtypeStruct(part.shape, f32) for part in parts)
        + (jax.ShapeDtypeStruct((embed_rows, width), f32),)
        + tuple(jax.ShapeDtypeStruct(part.shape, part.dtype) for part in done)
        + (jax.ShapeDtypeStruct((3, norm_here), f32),) * 2,
        in_specs=[every] * 11,
        out_specs=(every,) * 10 + (vmem,) * 2,
        scratch_shapes=[pltpu.VMEM(part.shape, BFLOAT) for part in parts]
        + [pltpu.VMEM(part.shape, f32) for part in parts]
        + [
            pltpu.VMEM((WIDE_SLOTS, WIDE_ROWS, width), BFLOAT),
            pltpu.VMEM((WIDE_SLOTS, WIDE_ROWS, width), f32),
            pltpu.VMEM((8, norm_here), f32),
            pltpu.VMEM(done[0].shape, f32),
            pltpu.VMEM(done[1].shape, f32),
            dma((7,)),
            dma((7,)),
            dma((WIDE_SLOTS,)),
            dma((WIDE_SLOTS,)),
            dma,
            dma((4,)),
        ],
        compiler_params=pltpu.CompilerParams(vmem_limit_bytes=60 * 2**20),
        name="widen",
    )(*parts, pieces, norms, *done)
    return results[:7], results[7:]


VOCAB_CUTS = 3
ARRIVAL_PHASES = (0, 0, 1, 2, 0, 1, 2, 3, 0, 1, 2, 3, 1, 2, 3, 3)
ARRIVAL_TURNS = (0, 1, 0, 0, 2, 1, 1, 0, 3, 2, 2, 1, 3, 3, 2, 3)
NEAREST = ((0, 1, 2, 3), (1, 0, 1, 2), (2, 2, 3, 1), (3, 3, 0, 0))


def head_kernel(slots, length, vocab_here, *refs):
    hid, marks, emb_all = refs[:3]
    small_out, gemb_out, third_out = refs[3:6]
    (
        emb, emb_t, held, logit, expo, part, sib_part, part_one, part_two, part_z,
        mine, theirs, crossed, lined, prior, usable, weight, scaled, picked_grad,
    ) = refs[6:25]
    (
        local_sem, z_send, z_recv, one_send, one_recv, two_send, two_recv, sib_send, sib_recv,
        st_send, st_recv, stz_send, stz_recv,
        dd_send, dd_recv, r1_send, r1_recv, r2_send, r2_recv, rz_send, rz_recv,
    ) = refs[25:]
    x, y, z, c = whereami()
    pb, pa = y * 2 + x, z * 2 + c
    size = hid.shape[0]
    pair = 2 * size
    width = hid.shape[1]
    rows = emb.shape[0]
    cut = rows // VOCAB_CUTS
    start = pl.multiple_of(pb * rows, 16)
    last = vocab_here - 3 * rows
    valid = jnp.where(pb == 3, last, rows)
    base = pa * vocab_here + start
    own = pb * 4 + z

    def remote(src, dst, send, recv, peer):
        return pltpu.make_async_remote_copy(
            src_ref=src, dst_ref=dst, send_sem=send, recv_sem=recv, device_id=peer, device_id_type=MESH
        )

    sibling = at(x, y, z, 1 - c)
    x_peer, y_peer = at(1 - x, y, z, c), at(x, 1 - y, z, c)

    def spot(k, core, n=None):
        rows_here = size if n is None else size // 2
        first = (k * 2 + core) * size + (0 if n is None else n * rows_here)
        return held.at[pl.ds(pl.multiple_of(first, rows_here), rows_here), :]

    across = [at(1 - x, y, z, c), at(x, 1 - y, z, c), at(1 - x, 1 - y, z, c)]
    greet(neighbours(x, y, z, c) + across[2:])
    own_copy = pltpu.make_async_copy(hid, spot(own, c), local_sem.at[0])
    own_copy.start()
    emb_copy = pltpu.make_async_copy(
        emb_all.at[pl.ds(start, last), :], emb.at[pl.ds(0, last), :], local_sem.at[2]
    )
    rest_copy = pltpu.make_async_copy(
        emb_all.at[pl.ds(pl.multiple_of(jnp.minimum(start + last, vocab_here - (rows - last)), 16), rows - last), :],
        emb.at[pl.ds(last, rows - last), :],
        local_sem.at[3],
    )
    emb_copy.start()
    rest_copy.start()
    own_copy.wait()

    def up_copy(origin, n):
        block = spot(pb * 4 + origin, c, n)
        return remote(block, block, z_send.at[0, origin, n], z_recv.at[origin, n], at(x, y, z + 1, c))

    def down_copy(origin, n):
        block = spot(pb * 4 + origin, c, n)
        return remote(block, block, z_send.at[1, origin, n], z_recv.at[origin, n], at(x, y, z - 1, c))

    def pass_along(origin, n, action):
        @pl.when((origin <= z) & (z < 3))
        def _():
            action(up_copy(origin, n))

        @pl.when((origin >= z) & (z > 0))
        def _():
            action(down_copy(origin, n))

    def sib_copy(k, n):
        return remote(spot(k, c, n), spot(k, c, n), sib_send.at[k, n], sib_recv.at[k, n], sibling)

    def order(zz):
        x_first = zz < 2
        f = jnp.where(x_first, x, y)
        g = jnp.where(x_first, y, x)
        first_peer = (jnp.where(x_first, y * 2 + 1 - x, (1 - y) * 2 + x), pa)
        second_peer = (jnp.where(x_first, (1 - y) * 2 + x, y * 2 + 1 - x), pa)

        def block(first, second):
            return jnp.where(x_first, second * 2 + first, first * 2 + second) * 4 + zz

        return f, g, first_peer, second_peer, block

    def one_copy(zz, n):
        f, g, first_peer, _, block = order(zz)
        part = spot(block(f, g), c, n)
        return remote(part, part, one_send.at[zz, n], one_recv.at[zz, n], first_peer)

    def two_copy(zz, j, n):
        f, g, _, second_peer, block = order(zz)
        part = spot(block(f if j == 0 else 1 - f, g), c, n)
        return remote(part, part, two_send.at[zz, j, n], two_recv.at[zz, j, n], second_peer)

    for n in range(2):
        pass_along(z, n, lambda copy: copy.start())
        one_copy(z, n).start()
        two_copy(z, 0, n).start()
        sib_copy(own, n).start()

    emb_copy.wait()
    rest_copy.wait()
    full_cuts = rows // 128

    def target_rows(k):
        ypart, xpart, zpart = k // 8, lax.rem(k // 4, 2), lax.rem(k, 4)
        target = marks[ypart, xpart, zpart, 0:1, :].astype(jnp.int32) - base
        return jnp.where(target < valid, target, -1)

    def row_numbers(j):
        return lax.broadcasted_iota(jnp.int32, (cut, pair), 0) + j * cut

    def cut_rows(j):
        return pl.ds(pl.multiple_of(j * cut, cut), cut)

    def token_lanes(k):
        return pl.ds(pl.multiple_of(k * pair, pair), pair)

    def forward_block(k):
        target = target_rows(k)
        block = held[token_lanes(k), :]

        def scan_logits(j, carried):
            highest, picked = carried
            value = lax.dot_general(
                emb[cut_rows(j), :], block, (((1,), (1,)), ((), ())), preferred_element_type=jnp.float32
            )
            number = row_numbers(j)
            value = jnp.where(number < valid, value, NEGATIVE)
            logit[cut_rows(j), :] = value
            return (
                jnp.maximum(highest, jnp.max(value, 0, keepdims=True)),
                picked + jnp.sum(jnp.where(number == target, value, 0.0), 0, keepdims=True),
            )

        highest, picked = lax.fori_loop(
            0,
            VOCAB_CUTS,
            scan_logits,
            (jnp.full((1, pair), NEGATIVE, jnp.float32), jnp.zeros((1, pair), jnp.float32)),
            unroll=True,
        )

        def scan_exp(j, total):
            value = jnp.exp(logit[cut_rows(j), :] - highest)
            expo[cut_rows(j), token_lanes(k)] = value.astype(BFLOAT)
            return total + jnp.sum(value, 0, keepdims=True)

        total = lax.fori_loop(
            0, VOCAB_CUTS, scan_exp, jnp.zeros((1, pair), jnp.float32), unroll=True
        )
        mine[0, 0, pl.ds(k, 1), :] = highest
        mine[0, 1, pl.ds(k, 1), :] = total
        mine[0, 2, pl.ds(k, 1), :] = picked

    def listed(values, index):
        out = values[0]
        for n in range(1, len(values)):
            out = jnp.where(index == n, values[n], out)
        return out

    def step_block(s):
        phase = listed(ARRIVAL_PHASES, s)
        t = listed(ARRIVAL_TURNS, s)
        zz = listed([listed(row, z) for row in NEAREST], t)
        f, g, _, _, block = order(zz)
        k = listed((block(f, g), block(1 - f, g), block(f, 1 - g), block(1 - f, 1 - g)), phase)
        return phase, zz, k

    @pl.loop(0, 17)
    def _(s):
        phase, zz, k = step_block(s)

        @pl.when(s < full_cuts)
        def _():
            here = pl.ds(pl.multiple_of(s * 128, 128), 128)
            emb_t[:, here] = emb[here, :].T

        if rows % 128:
            @pl.when(s == full_cuts)
            def _():
                emb_t[:, full_cuts * 128 :] = emb[full_cuts * 128 :, :].T

        @pl.when((s > 0) & (s < 16) & (phase == 0))
        def _():
            for n in range(2):
                up_copy(zz, n).wait_recv()
                pass_along(zz, n, lambda copy: copy.start())
                one_copy(zz, n).start()
                two_copy(zz, 0, n).start()
                sib_copy(k, n).start()

        @pl.when((s < 16) & (phase == 1))
        def _():
            for n in range(2):
                one_copy(zz, n).wait_recv()
                two_copy(zz, 1, n).start()
                sib_copy(k, n).start()

        for j in range(2):
            @pl.when((s < 16) & (phase == 2 + j))
            def _():
                for n in range(2):
                    two_copy(zz, j, n).wait_recv()
                    sib_copy(k, n).start()

        @pl.when(s > 0)
        def _():
            former = step_block(s - 1)[2]
            for n in range(2):
                sib_copy(former, n).wait_recv()
            forward_block(former)

    def joined(parts):
        highest = functools.reduce(jnp.maximum, [p[0] for p in parts])
        total = functools.reduce(jnp.add, [p[1] * jnp.exp(p[0] - highest) for p in parts])
        picked = functools.reduce(jnp.add, [p[2] for p in parts])
        return highest, total, picked

    def rows_of(ref, n):
        return ref[n, 0], ref[n, 1], ref[n, 2]

    copy = remote(mine.at[0], theirs, st_send.at[0], st_recv.at[0], sibling)
    copy.start()
    copy.wait()
    here, there = rows_of(mine, 0), (theirs[0], theirs[1], theirs[2])
    early = tuple(jnp.where(c == 0, p, q) for p, q in zip(here, there))
    late = tuple(jnp.where(c == 0, q, p) for p, q in zip(here, there))
    for r, value in enumerate(joined((early, late))):
        mine[1, r] = value
        crossed[pb, r] = value
    pb_copies = [
        remote(mine.at[1], crossed.at[pb], st_send.at[n + 1], st_recv.at[n + 1], peer)
        for n, peer in enumerate(across)
    ]
    for copy in pb_copies:
        copy.start()
    for copy in pb_copies:
        copy.wait()
    for r, value in enumerate(joined([rows_of(crossed, n) for n in range(4)])):
        mine[2, r] = value
        lined[z, r] = value

    def stat_copy(d):
        other = lax.rem(z + d, 4)
        return remote(mine.at[2], lined.at[z], stz_send.at[d - 1], stz_recv.at[d - 1], at(x, y, other, c))

    for d in (1, 2, 3):
        stat_copy(d).start()
    for d in (1, 2, 3):
        stat_copy(d).wait()
    highest, total, picked = joined([rows_of(lined, n) for n in range(4)])
    logsum = highest + jnp.log(total)
    log_probs = picked - logsum
    for k in range(16):
        prior[k : k + 1, :] = marks[k // 8, (k // 4) % 2, k % 4, 1:2, :]
        usable[k : k + 1, :] = marks[k // 8, (k // 4) % 2, k % 4, 2:3, :]
    lane = lax.broadcasted_iota(jnp.int32, (16, pair), 1) // length
    mean = jnp.zeros((16, pair), jnp.float32)
    for n in range(pair // length):
        inside = lane == n
        slot_sum = jnp.sum(jnp.where(inside, log_probs, 0.0), 1, keepdims=True)
        mean = jnp.where(inside, slot_sum * (1.0 / length), mean)
    scores = prior[...] + mean
    counted = usable[...] > 0.5
    masked = jnp.where(counted, scores, NEGATIVE)
    question = lax.broadcasted_iota(jnp.int32, (16, pair), 0) // 4
    marginal = jnp.zeros((16, pair), jnp.float32)
    loss = jnp.zeros((1, 1), jnp.float32)
    for n in range(4):
        inside = question == n
        high = jnp.max(
            jnp.max(jnp.where(inside, masked, NEGATIVE), 1, keepdims=True), 0, keepdims=True
        )
        terms = jnp.where(inside & counted, jnp.exp(masked - high), 0.0)
        mass = jnp.sum(jnp.sum(terms, 1, keepdims=True), 0, keepdims=True) * (1.0 / length)
        value = high + jnp.log(mass)
        marginal = jnp.where(inside, value, marginal)
        loss = loss + value
    posterior = jnp.where(counted, jnp.exp(scores - marginal), 0.0)
    token_weight = -float(slots) * posterior
    weight[...] = posterior
    scaled[...] = token_weight * jnp.exp(mine[0, 0] - logsum)
    picked_grad[...] = token_weight * (1.0 - jnp.exp(log_probs))
    small_out[...] = jnp.broadcast_to(loss * (-1.0 / 4), small_out.shape)
    own_row = weight[pl.ds(own, 1), :]
    own_row = jnp.where(c == 0, own_row[:, :size], own_row[:, size:])
    small_out[1:2, :] = own_row * (-float(slots * length))

    def backward_block(k):
        target = target_rows(k)
        hit = picked_grad[pl.ds(k, 1), :]
        scale = scaled[pl.ds(k, 1), :]

        def make(j, carried):
            value = expo[cut_rows(j), token_lanes(k)].astype(jnp.float32)
            grad = jnp.where(row_numbers(j) == target, hit, -(value * scale))
            expo[cut_rows(j), token_lanes(k)] = grad.astype(BFLOAT)
            return carried

        lax.fori_loop(0, VOCAB_CUTS, make, 0, unroll=True)

        def to_rows(n, carried):
            cut_width = pl.ds(pl.multiple_of(n * 256, 256), 256)
            value = lax.dot_general(
                emb_t[cut_width, :],
                expo[:, token_lanes(k)],
                (((1,), (0,)), ((), ())),
                preferred_element_type=jnp.float32,
            ).astype(BFLOAT)
            part[k, 0, cut_width, :] = value[:, :size]
            part[k, 1, cut_width, :] = value[:, size:]
            return carried

        lax.fori_loop(0, width // 256, to_rows, 0, unroll=True)

    def dd_copy(k):
        return remote(part.at[k, 1 - c], sib_part.at[k], dd_send.at[k], dd_recv.at[k], sibling)

    def r1_copy(zz, j):
        f, _, first_peer, _, block = order(zz)
        return remote(
            sib_part.at[block(1 - f, j)], part_one.at[zz, j], r1_send.at[zz, j], r1_recv.at[zz, j],
            first_peer,
        )

    def half(n):
        return pl.ds(n * (width // 2), width // 2)

    def r2_copy(zz, n):
        _, g, _, second_peer, _ = order(zz)
        return remote(
            part_one.at[zz, 1 - g, half(n), :], part_two.at[zz, half(n), :], r2_send.at[zz, n],
            r2_recv.at[zz, n], second_peer,
        )

    def rz_copy(zz, n):
        return remote(
            part_two.at[zz, half(n), :], part_z.at[z, half(n), :], rz_send.at[zz, n], rz_recv.at[z, n],
            at(x, y, zz, c),
        )

    def rz_arrival(zz, n):
        return remote(
            part_two.at[zz, half(n), :], part_z.at[zz, half(n), :], rz_send.at[zz, n],
            rz_recv.at[zz, n], at(x, y, zz, c),
        )

    step = 128

    def add_into(target_ref, other_ref):
        @pl.loop(0, target_ref.shape[0] // step)
        def _(n):
            rows_here = pl.ds(pl.multiple_of(n * step, step), step)
            target_ref[rows_here, :] = (
                target_ref[rows_here, :].astype(jnp.float32) + other_ref[rows_here, :].astype(jnp.float32)
            ).astype(BFLOAT)

    def group(n):
        return lax.rem(n, 2) * 2 + n // 2

    def chunk(q):
        j, n = q // 4, lax.rem(q, 4)
        columns = pl.ds(pl.multiple_of(n * 256, 256), 256)
        gemb_out[cut_rows(j), columns] = lax.dot_general(
            expo[cut_rows(j), :],
            held[:, columns],
            (((1,), (0,)), ((), ())),
            preferred_element_type=jnp.float32,
        ).astype(BFLOAT)

    def grad_block(s):
        leaves = s < 8
        zz = group(lax.rem(s, 8) // 2)
        j = lax.rem(s, 2)
        f, _, _, _, block = order(zz)
        return leaves, zz, j, block(jnp.where(leaves, 1 - f, f), j)

    @pl.loop(0, 28)
    def _(s):
        @pl.when((s >= 2) & (s < 18))
        def _():
            leaves, zz, turn, k = grad_block(s - 2)
            dd_copy(k).wait_recv()
            add_into(sib_part.at[k], part.at[k, c])
            for j in range(2):
                @pl.when(leaves & (turn == j))
                def _():
                    r1_copy(zz, j).start()

        @pl.when((lax.rem(s, 2) == 1) & (s >= 11) & (s < 18))
        def _():
            zz = group((s - 11) // 2)
            f, _, _, _, block = order(zz)
            for j in range(2):
                r1_copy(zz, j).wait_recv()
                add_into(part_one.at[zz, j], sib_part.at[block(f, j)])
            for n in range(2):
                r2_copy(zz, n).start()

        @pl.when((lax.rem(s, 2) == 0) & (s >= 16) & (s < 24))
        def _():
            zz = group((s - 16) // 2)
            _, g, _, _, _ = order(zz)
            for n in range(2):
                r2_copy(zz, n).wait_recv()
                add_into(part_two.at[zz, half(n), :], part_one.at[zz, g, half(n), :])

                @pl.when(zz != z)
                def _():
                    rz_copy(zz, n).start()

        @pl.when(s < 16)
        def _():
            k = grad_block(s)[3]
            backward_block(k)
            dd_copy(k).start()

        @pl.when(s >= 16)
        def _():
            chunk(s - 16)

    for d in (1, 2, 3):
        for n in range(2):
            rz_arrival(lax.rem(z + d, 4), n).wait_recv()

    @pl.loop(0, width // step)
    def _(n):
        rows_here = pl.ds(pl.multiple_of(n * step, step), step)
        value = part_two[z, rows_here, :].astype(jnp.float32)
        for d in (1, 2, 3):
            value = value + part_z[lax.rem(z + d, 4), rows_here, :].astype(jnp.float32)
        third_out[rows_here, :] = value

    for d in (1, 2, 3):
        for n in range(2):
            rz_copy(lax.rem(z + d, 4), n).wait_send()

    @pl.loop(0, 4)
    def _(zz):
        for n in range(2):
            pass_along(zz, n, lambda copy: copy.wait_send())
            one_copy(zz, n).wait_send()
            for j in range(2):
                two_copy(zz, j, n).wait_send()
        for j in range(2):
            r1_copy(zz, j).wait_send()
        for n in range(2):
            r2_copy(zz, n).wait_send()

    @pl.loop(0, 16)
    def _(k):
        for n in range(2):
            sib_copy(k, n).wait_send()
        dd_copy(k).wait_send()


def vocabulary_head(third_low, marks, embedding, slots, length):
    size, width = third_low.shape
    vocab_here = embedding.shape[0]
    rows = 16 * VOCAB_CUTS * -(-vocab_here // (4 * 16 * VOCAB_CUTS))
    dma = pltpu.SemaphoreType.DMA
    vmem = pl.BlockSpec(memory_space=pltpu.VMEM)
    stat = (3, 16, 2 * size)
    f32 = jnp.float32
    block = (width, size)
    small, gemb, third = pl.pallas_call(
        functools.partial(head_kernel, slots, length, vocab_here),
        out_shape=(
            jax.ShapeDtypeStruct((8, size), f32),
            jax.ShapeDtypeStruct((rows, width), BFLOAT),
            jax.ShapeDtypeStruct((width, size), f32),
        ),
        in_specs=[vmem, vmem, pl.BlockSpec(memory_space=pl.ANY)],
        out_specs=(vmem,) * 3,
        scratch_shapes=[
            pltpu.VMEM((rows, width), BFLOAT),
            pltpu.VMEM((width, rows), BFLOAT),
            pltpu.VMEM((32 * size, width), BFLOAT),
            pltpu.VMEM((rows, 2 * size), f32),
            pltpu.VMEM((rows, 32 * size), BFLOAT),
            pltpu.VMEM((16, 2) + block, BFLOAT),
            pltpu.VMEM((16,) + block, BFLOAT),
            pltpu.VMEM((4, 2) + block, BFLOAT),
            pltpu.VMEM((4,) + block, BFLOAT),
            pltpu.VMEM((4,) + block, BFLOAT),
            pltpu.VMEM((3,) + stat, f32),
            pltpu.VMEM(stat, f32),
            pltpu.VMEM((4,) + stat, f32),
            pltpu.VMEM((4,) + stat, f32),
        ]
        + [pltpu.VMEM((16, 2 * size), f32)] * 5
        + [dma((4,))]
        + [dma((2, 4, 2)), dma((4, 2))]
        + [dma((4, 2))] * 2
        + [dma((4, 2, 2))] * 2
        + [dma((16, 2))] * 2
        + [dma((4,))] * 2
        + [dma((3,))] * 2
        + [dma((16,))] * 2
        + [dma((4, 2))] * 2
        + [dma((4, 2))] * 4,
        compiler_params=pltpu.CompilerParams(
            collective_id=2, has_side_effects=True, vmem_limit_bytes=60 * 2**20
        ),
        name="vocabulary_head",
    )(third_low, marks, embedding)
    return small, gemb, third


def merged(part, axis, combine):
    gathered = jax.tree.map(lambda a: lax.all_gather(a, axis), part)

    def take(source):
        return jax.tree.map(lambda a: lax.dynamic_index_in_dim(a, source, 0, False), gathered)

    return lax.fori_loop(
        1, lax.axis_size(axis), lambda source, state: combine(state, take(source)), take(0)
    )


def matmul(matrix_left, matrix_right):
    return lax.dot_general(
        matrix_left,
        matrix_right,
        (((matrix_left.ndim - 1,), (0,)), ((), ())),
        preferred_element_type=jnp.float32,
    )


def matmul_back(matrix_left, matrix_right):
    return lax.dot_general(
        matrix_left,
        matrix_right,
        (((matrix_left.ndim - 1,), (1,)), ((), ())),
        preferred_element_type=jnp.float32,
    )


def outer_sum(matrix_left, matrix_right):
    flat_left = matrix_left.reshape(-1, matrix_left.shape[-1])
    flat_right = matrix_right.reshape(-1, matrix_right.shape[-1])
    return lax.dot_general(
        flat_left, flat_right, (((0,), (0,)), ((), ())), preferred_element_type=jnp.float32
    )


def split_heads(values):
    return values.reshape(values.shape[0], values.shape[1], HEADS, HEAD_DIM)


def join_heads(values):
    return values.reshape(values.shape[0], values.shape[1], HEADS * HEAD_DIM)


def exact_gelu(values):
    return jax.nn.gelu(values, approximate=False)


def norm_forward(values, gain_row, shift_row):
    centre = values - jnp.mean(values, -1, keepdims=True)
    inverse = lax.rsqrt(jnp.mean(centre * centre, -1, keepdims=True) + EPSILON)
    normed = centre * inverse
    return (normed * gain_row.astype(jnp.float32) + shift_row.astype(jnp.float32), normed, inverse)


def norm_backward(upstream, normed, inverse, gain_row):
    scaled = upstream * gain_row.astype(jnp.float32)
    mean_scaled = jnp.mean(scaled, -1, keepdims=True)
    along_normed = jnp.mean(scaled * normed, -1, keepdims=True)
    grad_values = inverse * (scaled - mean_scaled - normed * along_normed)
    model_width = upstream.shape[-1]
    grad_gain = jnp.sum((upstream * normed).reshape(-1, model_width), 0)
    grad_shift = jnp.sum(upstream.reshape(-1, model_width), 0)
    return (grad_values, grad_gain, grad_shift)


def score_block(queries, key_rows, causal):
    scores = jnp.einsum(
        "nqhd,nkhd->nhqk", queries, key_rows, preferred_element_type=jnp.float32
    ) * (1.0 / math.sqrt(HEAD_DIM))
    if causal:
        length = queries.shape[1]
        allowed = lax.broadcasted_iota(jnp.int32, (length, length), 0) >= lax.broadcasted_iota(
            jnp.int32, (length, length), 1
        )
        scores = jnp.where(allowed, scores, NEGATIVE)
    return scores


def attend(queries, key_rows, values, causal):
    scores = score_block(queries, key_rows, causal)
    highest = jnp.max(scores, -1, keepdims=True)
    totals = jnp.sum(jnp.exp(scores - highest), -1, keepdims=True)
    logsum = highest + jnp.log(totals)
    probs_low = jnp.exp(scores - logsum).astype(BFLOAT)
    context = jnp.einsum(
        "nhqk,nkhd->nqhd", probs_low, values, preferred_element_type=jnp.float32
    ).astype(BFLOAT)
    return (join_heads(context), logsum)


def attend_back(grad_context, queries, key_rows, values, logsum, causal):
    score_scale = 1.0 / math.sqrt(HEAD_DIM)
    probs_full = jnp.exp(score_block(queries, key_rows, causal) - logsum)
    grad_heads = split_heads(grad_context)
    grad_probs = jnp.einsum(
        "nqhd,nkhd->nhqk", grad_heads, values, preferred_element_type=jnp.float32
    )
    grad_values = jnp.einsum(
        "nhqk,nqhd->nkhd", probs_full.astype(BFLOAT), grad_heads, preferred_element_type=jnp.float32
    ).astype(BFLOAT)
    grad_scores = (
        probs_full * (grad_probs - jnp.sum(probs_full * grad_probs, -1, keepdims=True))
    ).astype(BFLOAT)
    grad_queries = (
        jnp.einsum("nhqk,nkhd->nqhd", grad_scores, key_rows, preferred_element_type=jnp.float32)
        * score_scale
    ).astype(BFLOAT)
    grad_keys = (
        jnp.einsum("nhqk,nqhd->nkhd", grad_scores, queries, preferred_element_type=jnp.float32)
        * score_scale
    ).astype(BFLOAT)
    return (join_heads(grad_queries), join_heads(grad_keys), join_heads(grad_values))


def layer_forward(inputs, encoded, weights):
    (
        packed_weight,
        output_weight,
        query_weight,
        memory_weight,
        cross_weight,
        expand_weight,
        reduce_weight,
        gains,
        shifts,
    ) = weights
    model_width = inputs.shape[-1]
    packed = matmul(inputs, packed_weight).astype(BFLOAT)
    context, self_logsum = attend(
        split_heads(packed[..., :model_width]),
        split_heads(packed[..., model_width : 2 * model_width]),
        split_heads(packed[..., 2 * model_width :]),
        True,
    )
    first_norm, first_normed, first_inverse = norm_forward(
        inputs.astype(jnp.float32) + matmul(context, output_weight), gains[0], shifts[0]
    )
    first_low = first_norm.astype(BFLOAT)
    cross_queries = matmul(first_low, query_weight).astype(BFLOAT)
    memory_pairs = matmul(encoded, memory_weight).astype(BFLOAT)
    cross_context, cross_logsum = attend(
        split_heads(cross_queries),
        split_heads(memory_pairs[..., :model_width]),
        split_heads(memory_pairs[..., model_width:]),
        False,
    )
    second, second_normed, second_inverse = norm_forward(
        first_norm + matmul(cross_context, cross_weight), gains[1], shifts[1]
    )
    second_low = second.astype(BFLOAT)
    inner_pre = matmul(second_low, expand_weight)
    active = exact_gelu(inner_pre).astype(BFLOAT)
    third_norm, third_normed, third_inverse = norm_forward(
        second + matmul(active, reduce_weight), gains[2], shifts[2]
    )
    stored = (
        packed,
        context,
        self_logsum,
        first_normed,
        first_inverse,
        first_low,
        cross_queries,
        memory_pairs,
        cross_context,
        cross_logsum,
        second_normed,
        second_inverse,
        second_low,
        inner_pre,
        active,
        third_normed,
        third_inverse,
    )
    return (third_norm.astype(BFLOAT), stored)


def layer_backward(grad_third, inputs, encoded, weights, stored):
    (
        packed_weight,
        output_weight,
        query_weight,
        memory_weight,
        cross_weight,
        expand_weight,
        reduce_weight,
        gains,
        shifts,
    ) = weights
    (
        packed,
        context,
        self_logsum,
        first_normed,
        first_inverse,
        first_low,
        cross_queries,
        memory_pairs,
        cross_context,
        cross_logsum,
        second_normed,
        second_inverse,
        second_low,
        inner_pre,
        active,
        third_normed,
        third_inverse,
    ) = stored
    model_width = inputs.shape[-1]
    grad_res3, gain_three, shift_three = norm_backward(
        grad_third, third_normed, third_inverse, gains[2]
    )
    grad_output = grad_res3.astype(BFLOAT)
    grad_reduce = outer_sum(active, grad_output)
    grad_active = matmul_back(grad_output, reduce_weight)
    _, gelu_pull = jax.vjp(exact_gelu, inner_pre)
    grad_inner = gelu_pull(grad_active)[0].astype(BFLOAT)
    grad_expand = outer_sum(second_low, grad_inner)
    grad_second = grad_res3 + matmul_back(grad_inner, expand_weight)
    grad_res2, gain_two, shift_two = norm_backward(
        grad_second, second_normed, second_inverse, gains[1]
    )
    grad_mixed = grad_res2.astype(BFLOAT)
    grad_cross_weight = outer_sum(cross_context, grad_mixed)
    grad_cross_context = matmul_back(grad_mixed, cross_weight).astype(BFLOAT)
    grad_cross_queries, grad_memory_keys, grad_memory_values = attend_back(
        grad_cross_context,
        split_heads(cross_queries),
        split_heads(memory_pairs[..., :model_width]),
        split_heads(memory_pairs[..., model_width:]),
        cross_logsum,
        False,
    )
    grad_query_weight = outer_sum(first_low, grad_cross_queries)
    grad_first = grad_res2 + matmul_back(grad_cross_queries, query_weight)
    grad_pairs = jnp.concatenate([grad_memory_keys, grad_memory_values], -1)
    grad_memory_weight = outer_sum(encoded, grad_pairs)
    grad_encoded = matmul_back(grad_pairs, memory_weight)
    grad_res1, gain_one, shift_one = norm_backward(
        grad_first, first_normed, first_inverse, gains[0]
    )
    grad_merged = grad_res1.astype(BFLOAT)
    grad_output_weight = outer_sum(context, grad_merged)
    grad_context = matmul_back(grad_merged, output_weight).astype(BFLOAT)
    grad_queries, grad_keys, grad_values = attend_back(
        grad_context,
        split_heads(packed[..., :model_width]),
        split_heads(packed[..., model_width : 2 * model_width]),
        split_heads(packed[..., 2 * model_width :]),
        self_logsum,
        True,
    )
    grad_packed = jnp.concatenate([grad_queries, grad_keys, grad_values], -1)
    grad_packed_weight = outer_sum(inputs, grad_packed)
    grad_inputs = grad_res1 + matmul_back(grad_packed, packed_weight)
    grad_gains = jnp.stack([gain_one, gain_two, gain_three])
    grad_shifts = jnp.stack([shift_one, shift_two, shift_three])
    return (
        grad_inputs,
        grad_encoded,
        (
            grad_packed_weight,
            grad_output_weight,
            grad_query_weight,
            grad_memory_weight,
            grad_cross_weight,
            grad_expand,
            grad_reduce,
            grad_gains,
            grad_shifts,
        ),
    )


def combine_scores(former, latter):
    highest = jnp.maximum(former[0], latter[0])
    totals = former[1] * jnp.exp(former[0] - highest) + latter[1] * jnp.exp(latter[0] - highest)
    return (highest, totals, former[2] + latter[2])


def combine_pairs(former, latter):
    highest = jnp.maximum(former[0], latter[0])
    totals = former[1] * jnp.exp(former[0] - highest) + latter[1] * jnp.exp(latter[0] - highest)
    return (highest, totals)


def per_device(
    decoder_states,
    encoder_memory,
    target_tokens,
    log_prior,
    slot_counts,
    slot_mask,
    self_packed,
    self_output,
    cross_query,
    cross_memory,
    cross_output,
    feed_expand,
    feed_reduce,
    embedding,
    norm_gains,
    norm_shifts,
):
    weights = (
        lax.all_gather(self_packed, "pa", axis=0, tiled=True),
        lax.all_gather(self_output, "pa", axis=0, tiled=True),
        lax.all_gather(cross_query, "pa", axis=0, tiled=True),
        lax.all_gather(cross_memory, "pa", axis=0, tiled=True),
        lax.all_gather(cross_output, "pa", axis=0, tiled=True),
        lax.all_gather(feed_expand, "pa", axis=0, tiled=True),
        lax.all_gather(feed_reduce, "pa", axis=0, tiled=True),
        lax.all_gather(norm_gains, "pa", axis=1, tiled=True),
        lax.all_gather(norm_shifts, "pa", axis=1, tiled=True),
    )
    questions, slots_here, length, model_width = decoder_states.shape
    mem_length = encoder_memory.shape[2]
    batch_size = questions * slots_here
    inputs = decoder_states.reshape(batch_size, length, model_width)
    encoded = encoder_memory.reshape(batch_size, mem_length, model_width)
    third_low, stored = layer_forward(inputs, encoded, weights)
    tokens_here = batch_size * length
    rows_all, tokens_all = (
        lax.all_gather(third_low.reshape(tokens_here, model_width), "pa", axis=0, tiled=True),
        lax.all_gather(target_tokens.reshape(tokens_here), "pa", axis=0, tiled=True),
    )
    total_rows = rows_all.shape[0]
    block_rows = min(total_rows, 2048)
    block_count = total_rows // block_rows
    vocab_start = lax.axis_index("pa") * embedding.shape[0]
    row_blocks = rows_all.reshape(block_count, block_rows, model_width)
    token_blocks = tokens_all.reshape(block_count, block_rows)

    def vocab_logits(hidden_rows, token_rows):
        logits = matmul_back(hidden_rows, embedding)
        column = lax.broadcasted_iota(jnp.int32, logits.shape, 1) + vocab_start
        return (logits, column == token_rows[:, None])

    def vocab_partial(pieces):
        logits, chosen = vocab_logits(pieces[0], pieces[1])
        highest = jnp.max(logits, -1)
        totals = jnp.sum(jnp.exp(logits - highest[:, None]), -1)
        picked = jnp.sum(jnp.where(chosen, logits, 0.0), -1)
        return (highest, totals, picked)

    highest, totals, picked = lax.map(vocab_partial, (row_blocks, token_blocks))
    highest, totals, picked = merged(
        (highest.reshape(total_rows), totals.reshape(total_rows), picked.reshape(total_rows)),
        "pa",
        combine_scores,
    )
    row_logsum = highest + jnp.log(totals)
    own_start = lax.axis_index("pa") * tokens_here
    own_logsum = lax.dynamic_slice_in_dim(row_logsum, own_start, tokens_here)
    own_picked = lax.dynamic_slice_in_dim(picked, own_start, tokens_here)
    log_probs = (own_picked - own_logsum).reshape(questions, slots_here, length)
    scores = log_prior + jnp.mean(log_probs, -1)
    slot_index = lax.axis_index("pa") * slots_here + lax.broadcasted_iota(
        jnp.int32, (questions, slots_here), 1
    )
    usable = (slot_mask == 1) & (slot_index < slot_counts[:, None])
    masked = jnp.where(usable, scores, NEGATIVE)
    local_high = jnp.max(masked, -1)
    local_total = jnp.sum(jnp.where(usable, jnp.exp(masked - local_high[:, None]), 0.0), -1)
    slot_high, slot_total = merged((local_high, local_total), "pa", combine_pairs)
    marginal = slot_high + jnp.log(slot_total)
    posterior = jnp.where(usable, jnp.exp(scores - marginal[:, None]), 0.0)
    loss_value = -lax.psum(jnp.sum(marginal), "pb") / (questions * lax.axis_size("pb"))
    slot_number = slots_here * lax.axis_size("pa")
    grad_prior = -(slot_number * length) * posterior
    token_grad = jnp.broadcast_to(
        (-slot_number * posterior)[:, :, None], (questions, slots_here, length)
    ).reshape(tokens_here)
    weights_all = lax.all_gather(token_grad, "pa", axis=0, tiled=True)

    def vocab_grads(accumulated, pieces):
        hidden_rows, token_rows, logsum_rows, weight_rows = pieces
        logits, chosen = vocab_logits(hidden_rows, token_rows)
        softmax_rows = jnp.exp(logits - logsum_rows[:, None])
        grad_logits = (weight_rows[:, None] * (jnp.where(chosen, 1.0, 0.0) - softmax_rows)).astype(
            BFLOAT
        )
        return (accumulated + outer_sum(grad_logits, hidden_rows), matmul(grad_logits, embedding))

    grad_embed, grad_rows = lax.scan(
        vocab_grads,
        jnp.zeros(embedding.shape, jnp.float32),
        (
            row_blocks,
            token_blocks,
            row_logsum.reshape(block_count, block_rows),
            weights_all.reshape(block_count, block_rows),
        ),
    )
    grad_third = lax.psum_scatter(
        grad_rows.reshape(total_rows, model_width).astype(BFLOAT),
        "pa",
        scatter_dimension=0,
        tiled=True,
    ).astype(jnp.float32).reshape(batch_size, length, model_width)
    grad_inputs, grad_encoded, grads = layer_backward(grad_third, inputs, encoded, weights, stored)
    shares = (
        lax.psum_scatter(grads[0].astype(BFLOAT), "pa", scatter_dimension=0, tiled=True),
        lax.psum_scatter(grads[1].astype(BFLOAT), "pa", scatter_dimension=0, tiled=True),
        lax.psum_scatter(grads[2].astype(BFLOAT), "pa", scatter_dimension=0, tiled=True),
        lax.psum_scatter(grads[3].astype(BFLOAT), "pa", scatter_dimension=0, tiled=True),
        lax.psum_scatter(grads[4].astype(BFLOAT), "pa", scatter_dimension=0, tiled=True),
        lax.psum_scatter(grads[5].astype(BFLOAT), "pa", scatter_dimension=0, tiled=True),
        lax.psum_scatter(grads[6].astype(BFLOAT), "pa", scatter_dimension=0, tiled=True),
        lax.psum_scatter(grads[7], "pa", scatter_dimension=1, tiled=True),
        lax.psum_scatter(grads[8], "pa", scatter_dimension=1, tiled=True),
    )
    outputs = lax.psum(
        (
            shares[0],
            shares[1],
            shares[2],
            shares[3],
            shares[4],
            shares[5],
            shares[6],
            shares[7],
            shares[8],
            grad_embed.astype(BFLOAT),
        ),
        "pb",
    )
    outputs = tuple(part.astype(jnp.float32) for part in outputs)
    return (
        loss_value,
        grad_inputs.reshape(decoder_states.shape),
        grad_encoded.reshape(encoder_memory.shape),
        grad_prior,
        outputs[0],
        outputs[1],
        outputs[2],
        outputs[3],
        outputs[4],
        outputs[5],
        outputs[6],
        outputs[9],
        outputs[7],
        outputs[8],
    )


def per_device_kernels(
    decoder_states,
    encoder_memory,
    target_tokens,
    log_prior,
    slot_counts,
    slot_mask,
    self_packed,
    self_output,
    cross_query,
    cross_memory,
    cross_output,
    feed_expand,
    feed_reduce,
    embedding,
    norm_gains,
    norm_shifts,
):
    shards = (
        self_packed,
        self_output,
        cross_query,
        cross_memory,
        cross_output,
        feed_expand,
        feed_reduce,
    )
    norm_rows = jnp.concatenate(
        [norm_gains, norm_shifts, jnp.zeros((2, norm_gains.shape[1]), BFLOAT)]
    ).astype(jnp.float32)
    _, slots_here, length, model_width = decoder_states.shape
    slots = slots_here * lax.axis_size("pa")
    states = decoder_states.reshape(slots_here * length, model_width)
    memory = encoder_memory.reshape(-1, model_width)
    slot_index = lax.axis_index("pa") * slots_here + jnp.arange(slots_here)
    usable = (slot_mask[0] == 1) & (slot_index < slot_counts[0])
    marks = jnp.concatenate(
        [
            target_tokens.reshape(1, slots_here * length).astype(jnp.float32),
            jnp.repeat(log_prior, length, axis=1),
            jnp.repeat(usable[None].astype(jnp.float32), length, axis=1),
            jnp.zeros((5, slots_here * length), jnp.float32),
        ]
    )
    matrices, marks, norms, kept = forward_layer(
        shards, norm_rows, marks, states, memory, length
    )
    small, grad_embed, grad_third = vocabulary_head(
        kept[-1], marks, embedding, slots, length
    )
    loss_value = small[0, 0]
    grad_prior = small[1].reshape(1, slots_here, length)[:, :, 0]
    shares, norm_sums, grad_inputs, grad_encoded, pieces = backward_layer(
        matrices,
        kept[:11] + kept[12:15] + (states, memory),
        kept[11],
        norms,
        grad_third,
        grad_embed,
        length,
    )
    pieces = pieces.reshape(4 * grad_embed.shape[0], model_width)
    shares, (grad_embed, grad_inputs, grad_encoded, grad_gains, grad_shifts) = widen(
        shares,
        pieces,
        norm_sums,
        (grad_inputs, grad_encoded),
        embedding.shape[0],
        norm_gains.shape[1],
    )
    return (
        loss_value,
        grad_inputs.reshape(decoder_states.shape),
        grad_encoded.reshape(encoder_memory.shape),
        grad_prior,
    ) + tuple(shares) + (grad_embed, grad_gains, grad_shifts)


def solution(mesh):
    own_kernels = mesh.shape["pb"] == 4 and mesh.shape["pa"] == 8
    return jax.shard_map(
        per_device_kernels if own_kernels else per_device,
        mesh=mesh,
        in_specs=(
            P("pb", "pa", None, None),
            P("pb", "pa", None, None),
            P("pb", "pa", None),
            P("pb", "pa"),
            P("pb"),
            P("pb", "pa"),
            P("pa", None),
            P("pa", None),
            P("pa", None),
            P("pa", None),
            P("pa", None),
            P("pa", None),
            P("pa", None),
            P("pa", None),
            P(None, "pa"),
            P(None, "pa"),
        ),
        out_specs=(
            P(),
            P("pb", "pa", None, None),
            P("pb", "pa", None, None),
            P("pb", "pa"),
            P("pa", None),
            P("pa", None),
            P("pa", None),
            P("pa", None),
            P("pa", None),
            P("pa", None),
            P("pa", None),
            P("pa", None),
            P(None, "pa"),
            P(None, "pa"),
        ),
        check_vma=False,
    )
```

```python
import functools
import math

import jax
import jax.numpy as jnp
from jax import lax
from jax.experimental import pallas as pl
from jax.experimental.pallas import tpu as pltpu
from jax.sharding import PartitionSpec as P

HEADS = 16
HEAD_DIM = 64


EPSILON = 1e-05
NEGATIVE = -1e30
BFLOAT = jnp.bfloat16
MESH = pl.DeviceIdType.MESH
TILE = 1024
ROWS = 128
WEIGHT_UNITS = (3, 1, 1, 2, 1, 4, 4)
UNITS = tuple((w, k) for w, n in enumerate(WEIGHT_UNITS) for k in range(n))
REDUCE_WEIGHT = 6


def whereami():
    pb = lax.axis_index("pb")
    pa = lax.axis_index("pa")
    return lax.rem(pb, 2), pb // 2, pa // 2, lax.rem(pa, 2)


def greet(peers):
    barrier = pltpu.get_barrier_semaphore()
    for peer in peers:
        pl.semaphore_signal(barrier, inc=1, device_id=peer, device_id_type=MESH)
    pl.semaphore_wait(barrier, len(peers))


def at(x, y, z, c):
    return (y * 2 + x, z * 2 + c)


def neighbours(x, y, z, c):
    return [at(1 - x, y, z, c), at(x, 1 - y, z, c), at(x, y, z, 1 - c)] + [
        at(x, y, lax.rem(z + d, 4), c) for d in (1, 2, 3)
    ]


def shard_view(ref, unit, start, size):
    weight, block = unit
    if weight == REDUCE_WEIGHT:
        return ref.at[pl.ds(block * ROWS + start, size), :]
    return ref.at[pl.ds(start, size), pl.ds(block * TILE, TILE)]


def full_view(ref, unit, place, core, start, size):
    weight, block = unit
    if weight == REDUCE_WEIGHT:
        return ref.at[place, core, block, pl.ds(start, size), :]
    return ref.at[place, core, pl.ds(start, size), pl.ds(block * TILE, TILE)]


Z_FULL = (13, 14, 15)


HOP_LAG = 1
LAG_TWO, LAG_SIBLING, LAG_LOAD, LAG_USE = 3, 6, 8, 9
SLOTS_IN_FLIGHT = 3


def dot_nn(left, right):
    return lax.dot_general(left, right, (((1,), (0,)), ((), ())), preferred_element_type=jnp.float32)


def dot_nt(left, right):
    return lax.dot_general(left, right, (((1,), (1,)), ((), ())), preferred_element_type=jnp.float32)


def dot_tn(left, right):
    return lax.dot_general(left, right, (((0,), (0,)), ((), ())), preferred_element_type=jnp.float32)


def stack_heads(pair):
    lane = lax.broadcasted_iota(jnp.int32, pair.shape, 1)
    zero = jnp.zeros_like(pair)
    return jnp.concatenate(
        [jnp.where(lane < HEAD_DIM, pair, zero), jnp.where(lane < HEAD_DIM, zero, pair)], 0
    )


def unstack_heads(stacked):
    rows = stacked.shape[0] // 2
    lane = lax.broadcasted_iota(jnp.int32, (rows, stacked.shape[1]), 1)
    return jnp.where(lane < HEAD_DIM, stacked[:rows], stacked[rows:])


def pair_scores(queries, keys, causal):
    scores = dot_nt(queries, keys) * (1.0 / math.sqrt(HEAD_DIM))
    if causal:
        length = keys.shape[0]
        row = lax.rem(lax.broadcasted_iota(jnp.int32, scores.shape, 0), length)
        column = lax.broadcasted_iota(jnp.int32, scores.shape, 1)
        scores = jnp.where(row >= column, scores, NEGATIVE)
    highest = jnp.max(scores, -1, keepdims=True)
    total = jnp.sum(jnp.exp(scores - highest), -1, keepdims=True)
    return jnp.exp(scores - (highest + jnp.log(total)))


def attend_pair(queries, keys, values, causal):
    probs = pair_scores(stack_heads(queries), keys, causal).astype(BFLOAT)
    return unstack_heads(dot_nn(probs, values)).astype(BFLOAT)


def normalise(values, gain, shift):
    centre = values - jnp.mean(values, -1, keepdims=True)
    inverse = lax.rsqrt(jnp.mean(centre * centre, -1, keepdims=True) + EPSILON)
    normed = centre * inverse
    return normed * gain + shift, normed, inverse


def forward_kernel(length, mem_length, *refs):
    shards, norm, aux, states_hbm, encoded_hbm = refs[:7], refs[7], refs[8], refs[9], refs[10]
    fulls, marks, kept_hbm = refs[11:18], refs[18], refs[19:36]
    (
        norm_full, packed, context, first_normed, first_inverse, first_low, cross_queries, pairs,
        cross_context, second_normed, second_inverse, second_low, inner, active, third_normed,
        third_inverse, third_low,
    ) = refs[36:53]
    wbuf, residual, states, encoded, held = refs[53:58]
    (
        local_sem, z_send, z_recv, one_send, one_recv, two_send, two_recv, d_send, d_recv,
        norm_sem, nz_send, nz_recv, nd_send, nd_recv, load_sem, ax_sem, ax_send, ax_recv,
        axz_send, axz_recv, kept_sem, input_sem, take_sem,
    ) = refs[58:]
    x, y, z, c = whereami()
    greet(neighbours(x, y, z, c))
    every = slice(None)
    tokens, width = states_hbm.shape
    slots_here = tokens // length

    def copies(u):
        unit = UNITS[u]
        shard, full = shards[unit[0]], fulls[unit[0]]
        wide = u in Z_FULL
        a, b = (x, y) if u % 2 == 0 else (y, x)
        first_peer = at(x, 1 - y, z, c) if u % 2 == 0 else at(1 - x, y, z, c)
        second_peer = at(1 - x, y, z, c) if u % 2 == 0 else at(x, 1 - y, z, c)
        quarter = pl.multiple_of(64 * a + 32 * b, 32)
        half = pl.multiple_of(64 * a, 64)
        rows = (0, ROWS) if wide else (quarter, 32)
        place = held.at[pl.ds(sum(ROWS if n in Z_FULL else 32 for n in range(u)), rows[1]), :]
        take = pltpu.make_async_copy(shard_view(shard, unit, *rows), place, take_sem.at[u])
        local = pltpu.make_async_copy(place, full_view(full, unit, z, c, *rows), local_sem.at[u])
        def along(origin, direction, own=False):
            block = full_view(full, unit, origin, c, *rows)
            return pltpu.make_async_remote_copy(
                src_ref=place if own else block,
                dst_ref=block,
                send_sem=z_send.at[u, (direction + 1) // 2, origin],
                recv_sem=z_recv.at[u, origin],
                device_id=at(x, y, lax.rem(z + direction + 4, 4), c),
                device_id_type=MESH,
            )

        def cross(start, size, sends, recvs, peer):
            part = full_view(full, unit, every, c, start, size)
            return pltpu.make_async_remote_copy(
                src_ref=part,
                dst_ref=part,
                send_sem=sends.at[u],
                recv_sem=recvs.at[u],
                device_id=peer,
                device_id_type=MESH,
            )

        first = None if wide else cross(quarter, 32, one_send, one_recv, first_peer)
        second = None if wide else cross(half, 64, two_send, two_recv, second_peer)
        sibling = cross(0, ROWS, d_send, d_recv, at(x, y, z, 1 - c))
        load = pltpu.make_async_copy(
            full_view(full, unit, every, every, 0, ROWS),
            wbuf.at[u % SLOTS_IN_FLIGHT],
            load_sem.at[u % SLOTS_IN_FLIGHT],
        )
        return (take, local), along, first, second, sibling, load

    def norm_copy(src, dst, send, recv, peer):
        return pltpu.make_async_remote_copy(
            src_ref=src, dst_ref=dst, send_sem=send, recv_sem=recv, device_id=peer, device_id_type=MESH
        )

    norm_local = pltpu.make_async_copy(norm, norm_full.at[z, c], norm_sem)
    norm_along = [
        norm_copy(
            norm, norm_full.at[z, c], nz_send.at[d - 1], nz_recv.at[d - 1], at(x, y, lax.rem(z + d, 4), c)
        )
        for d in (1, 2, 3)
    ]
    norm_sibling = norm_copy(
        norm_full.at[:, c], norm_full.at[:, c], nd_send, nd_recv, at(x, y, z, 1 - c)
    )
    norm_local.start()
    for copy in norm_along:
        copy.start()

    lanes = pl.ds(pl.multiple_of(c * tokens, tokens), tokens)
    aux_local = pltpu.make_async_copy(aux, marks.at[y, x, z, :, lanes], ax_sem)
    aux_local.start()
    aux_steps = [
        norm_copy(part, part, ax_send.at[n], ax_recv.at[n], peer)
        for n, (part, peer) in enumerate(
            (
                (marks.at[y, x, z, :, lanes], at(x, y, z, 1 - c)),
                (marks.at[y, x, z], at(1 - x, y, z, c)),
                (marks.at[y, :, z], at(x, 1 - y, z, c)),
            )
        )
    ]
    aux_along = [
        norm_copy(
            marks.at[:, :, z], marks.at[:, :, z], axz_send.at[d - 1], axz_recv.at[d - 1],
            at(x, y, lax.rem(z + d, 4), c),
        )
        for d in (1, 2, 3)
    ]

    kept = (
        norm_full, packed, context, first_normed, first_inverse, first_low, cross_queries, pairs,
        cross_context, second_normed, second_inverse, second_low, inner, active, third_normed,
        third_inverse, third_low,
    )

    def keep(*numbers):
        for n in numbers:
            pltpu.make_async_copy(kept[n], kept_hbm[n], kept_sem.at[n]).start()

    states_copy = pltpu.make_async_copy(states_hbm, states, input_sem.at[0])
    encoded_copy = pltpu.make_async_copy(encoded_hbm, encoded, input_sem.at[1])
    states_copy.start()
    encoded_copy.start()

    def norm_row(n):
        return jnp.concatenate(
            [norm_full[p // 2, p % 2, n : n + 1, :] for p in range(8)], 1
        )

    def times(left_ref, u, write):
        slot = u % SLOTS_IN_FLIGHT

        @pl.loop(0, 4, unroll=True)
        def _(n):
            columns = pl.ds(pl.multiple_of(n * 256, 256), 256)
            right = wbuf[slot, :, :, :, columns].reshape(TILE, 256)
            write(columns, n, dot_nn(left_ref[...], right))

    def block_columns(k, n):
        return pl.ds(pl.multiple_of(k * TILE + n * 256, 256), 256)

    def attention(queries, keys, key_start, value_start, key_length, out, causal):
        @pl.loop(0, slots_here * (width // 128), unroll=2)
        def _(n):
            slot, group = n // (width // 128), lax.rem(n, width // 128)
            lanes = pl.ds(pl.multiple_of(group * 128, 128), 128)
            key_lanes = pl.ds(pl.multiple_of(key_start + group * 128, 128), 128)
            value_lanes = pl.ds(pl.multiple_of(value_start + group * 128, 128), 128)
            query_rows = pl.ds(pl.multiple_of(slot * length, length), length)
            key_rows = pl.ds(pl.multiple_of(slot * key_length, key_length), key_length)
            out[query_rows, lanes] = attend_pair(
                queries[query_rows, lanes], keys[key_rows, key_lanes], keys[key_rows, value_lanes], causal
            )

    def finish_norm(n, value, normed_ref, inverse_ref, low_ref):
        out, normed, inverse = normalise(value, norm_row(n), norm_row(n + 3))
        normed_ref[...] = normed
        inverse_ref[...] = jnp.broadcast_to(inverse, inverse_ref.shape)
        low_ref[...] = out.astype(BFLOAT)
        return out

    def use(u):
        weight, k = UNITS[u]
        if weight == 0:
            def write(columns, n, value):
                packed[:, block_columns(k, n)] = value.astype(BFLOAT)

            times(states, u, write)
            if k == 2:
                attention(packed, packed, width, 2 * width, length, context, True)
                keep(1, 2)
        elif weight == 1:
            def write(columns, n, value):
                residual[:, columns] = states[:, columns].astype(jnp.float32) + value

            times(context, u, write)
            residual[...] = finish_norm(0, residual[...], first_normed, first_inverse, first_low)
            keep(3, 4, 5)
        elif weight == 2:
            def write(columns, n, value):
                cross_queries[:, columns] = value.astype(BFLOAT)

            times(first_low, u, write)
        elif weight == 3:
            slot = u % SLOTS_IN_FLIGHT

            @pl.loop(0, 8)
            def _(n):
                m, n = n // 4, lax.rem(n, 4)
                columns = pl.ds(pl.multiple_of(n * 256, 256), 256)
                part = encoded.shape[0] // 2
                rows_here = pl.ds(pl.multiple_of(m * part, part), part)
                right = wbuf[slot, :, :, :, columns].reshape(TILE, 256)
                pairs[rows_here, block_columns(k, n)] = dot_nn(encoded[rows_here, :], right).astype(BFLOAT)

            if k == 1:
                attention(cross_queries, pairs, 0, width, mem_length, cross_context, False)
                keep(6, 7, 8)
        elif weight == 4:
            def write(columns, n, value):
                residual[:, columns] = residual[:, columns] + value

            times(cross_context, u, write)
            residual[...] = finish_norm(1, residual[...], second_normed, second_inverse, second_low)
            keep(9, 10, 11)
        elif weight == 5:
            def write(columns, n, value):
                inner[:, block_columns(k, n)] = value
                gate = 0.5 * (1.0 + lax.erf(value * math.sqrt(0.5)))
                active[:, block_columns(k, n)] = (value * gate).astype(BFLOAT)

            times(second_low, u, write)
            if k == 3:
                keep(12, 13)
        else:
            slot = u % SLOTS_IN_FLIGHT
            blocks = active.shape[1] // (8 * ROWS)
            left = jnp.concatenate(
                [active[:, (p * blocks + k) * ROWS : (p * blocks + k + 1) * ROWS] for p in range(8)], 1
            )

            @pl.loop(0, 4, unroll=True)
            def _(n):
                columns = pl.ds(pl.multiple_of(n * 256, 256), 256)
                right = wbuf[slot, :, :, :, columns].reshape(TILE, 256)
                residual[:, columns] = residual[:, columns] + dot_nn(left, right)

            if k == blocks - 1:
                finish_norm(2, residual[...], third_normed, third_inverse, third_low)
                keep(14, 15, 16)

    count = len(UNITS)
    every_copy = [copies(u) for u in range(count)]

    def hop(u, h):
        (take, local), along = every_copy[u][:2]
        if h == 1:
            take.wait()
            local.start()
        if h == 4:
            local.wait()
        for origin, there, edge, direction in (
            (z - (h - 1), z >= h - 1, z < 3, 1),
            (z + (h - 1), z + (h - 1) <= 3, z > 0, -1),
        ):
            @pl.when(there)
            def _():
                if h > 1:
                    along(origin, direction).wait_recv()
                if h < 4:
                    @pl.when(edge)
                    def _():
                        along(origin, direction, h == 1).start()

    for copies_here in every_copy:
        copies_here[0][0].start()
    for h in range(1, 4):
        for u in range(HOP_LAG * (4 - h)):
            hop(u, h)
    for i in range(count + LAG_USE):
        for h in range(1, 5):
            u = i + HOP_LAG * (4 - h)
            if u < count:
                hop(u, h)
        if i < count:
            first = every_copy[i][2]
            if first is not None:
                first.start()
        if 0 <= i - LAG_TWO < count:
            first, second = every_copy[i - LAG_TWO][2:4]
            if first is not None:
                first.wait_recv()
                second.start()
        if 0 <= i - LAG_SIBLING < count:
            second, sibling = every_copy[i - LAG_SIBLING][3:5]
            if second is not None:
                second.wait_recv()
            sibling.start()
        if i == 2:
            norm_local.wait()
            for copy in norm_along:
                copy.wait()
            norm_sibling.start()
        if i == 4:
            norm_sibling.wait()
            keep(0)
            states_copy.wait()
            encoded_copy.wait()
        if 5 <= i < 9:
            if i == 5:
                aux_local.wait()
            else:
                aux_steps[i - 6].wait()
            for copy in aux_steps[i - 5 : i - 4] if i < 8 else aux_along:
                copy.start()
        if i == 9:
            for copy in aux_along:
                copy.wait()
        if 0 <= i - LAG_LOAD < count:
            sibling, load = every_copy[i - LAG_LOAD][4:]
            sibling.wait_recv()
            load.start()
        if 0 <= i - LAG_USE < count:
            every_copy[i - LAG_USE][5].wait()
            use(i - LAG_USE)
    for _, along, first, second, sibling, _ in every_copy:
        for origin in range(4):
            @pl.when((origin <= z) & (z < 3))
            def _():
                along(origin, 1).wait_send()

            @pl.when((origin >= z) & (z > 0))
            def _():
                along(origin, -1).wait_send()

        if first is not None:
            first.wait_send()
            second.wait_send()
        sibling.wait_send()
    for n in range(len(kept)):
        pltpu.make_async_copy(kept[n], kept_hbm[n], kept_sem.at[n]).wait()


def forward_layer(weights, norm, aux, states, encoded, length):
    count = len(UNITS)
    shapes = []
    for w, weight in enumerate(weights):
        if w == REDUCE_WEIGHT:
            shapes.append((4, 2, weight.shape[0] // ROWS, ROWS, weight.shape[1]))
        else:
            shapes.append((4, 2) + weight.shape)
    tokens, width = states.shape
    mem_tokens = encoded.shape[0]
    mem_length = mem_tokens // (tokens // length)
    units = weights[5].shape[1]
    f32 = jnp.float32
    kept = [
        ((4, 2) + norm.shape, f32),
        ((tokens, 3 * width), BFLOAT),
        ((tokens, width), BFLOAT),
        ((tokens, width), f32),
        ((tokens, 128), f32),
        ((tokens, width), BFLOAT),
        ((tokens, width), BFLOAT),
        ((mem_tokens, 2 * width), BFLOAT),
        ((tokens, width), BFLOAT),
        ((tokens, width), f32),
        ((tokens, 128), f32),
        ((tokens, width), BFLOAT),
        ((tokens, units), f32),
        ((tokens, units), BFLOAT),
        ((tokens, width), f32),
        ((tokens, 128), f32),
        ((tokens, width), BFLOAT),
    ]
    every = pl.BlockSpec(memory_space=pl.ANY)
    dma = pltpu.SemaphoreType.DMA
    results = pl.pallas_call(
        functools.partial(forward_kernel, length, mem_length),
        out_shape=tuple(jax.ShapeDtypeStruct(shape, BFLOAT) for shape in shapes)
        + (jax.ShapeDtypeStruct((2, 2, 4, aux.shape[0], 2 * tokens), f32),)
        + tuple(jax.ShapeDtypeStruct(shape, kind) for shape, kind in kept),
        in_specs=[every] * 11,
        out_specs=(every,) * (8 + len(kept)),
        scratch_shapes=[pltpu.VMEM(shape, kind) for shape, kind in kept]
        + [
            pltpu.VMEM((SLOTS_IN_FLIGHT, 4, 2, ROWS, TILE), BFLOAT),
            pltpu.VMEM((tokens, width), f32),
            pltpu.VMEM((tokens, width), BFLOAT),
            pltpu.VMEM((mem_tokens, width), BFLOAT),
            pltpu.VMEM((sum(ROWS if n in Z_FULL else 32 for n in range(count)), TILE), BFLOAT),
            dma((count,)),
            dma((count, 2, 4)),
            dma((count, 4)),
        ]
        + [dma((count,))] * 6
        + [dma]
        + [dma((3,))] * 2
        + [dma] * 2
        + [dma((SLOTS_IN_FLIGHT,))]
        + [dma]
        + [dma((3,))] * 4
        + [dma((len(kept),)), dma((2,)), dma((count,))],
        compiler_params=pltpu.CompilerParams(
            collective_id=0, has_side_effects=True, vmem_limit_bytes=62 * 2**20
        ),
        name="forward_layer",
    )(*weights, norm, aux, states, encoded)
    fulls = tuple(full.reshape(-1, full.shape[-1]) for full in results[:7])
    return fulls, results[7], results[8], results[9:]


SEQUENCE = tuple((6, k) for k in range(4)) + tuple((5, k) for k in range(4)) + (
    (4, 0), (2, 0), (3, 0), (3, 1), (1, 0), (0, 0), (0, 1), (0, 2),
)
LINE_FIRST = 9
HOP_LAGS = (4, 7, 10)
LINE_LAGS = (10, 12, 14, 16, 18)
CROSS_LAGS = (2, 4, 6, 8, 10)
TURNS = 27
GATHER_TURNS = (4, 8)
READS = tuple(read for k in range(4) for read in ((6, k), (5, k))) + (
    (4, 0), (2, 0), (1, 0), (0, 0), (0, 1), (0, 2), (3, 0), (3, 1),
)


def norm_back(upstream, normed, inverse, gain):
    scaled = upstream * gain
    mean_scaled = jnp.mean(scaled, -1, keepdims=True)
    along = jnp.mean(scaled * normed, -1, keepdims=True)
    return (
        inverse * (scaled - mean_scaled - normed * along),
        jnp.sum(upstream * normed, 0, keepdims=True),
        jnp.sum(upstream, 0, keepdims=True),
    )


def attend_pair_back(grad, queries, keys, values, causal):
    scale = 1.0 / math.sqrt(HEAD_DIM)
    queries, grad = stack_heads(queries), stack_heads(grad)
    probs = pair_scores(queries, keys, causal)
    grad_probs = dot_nt(grad, values)
    grad_values = dot_tn(probs.astype(BFLOAT), grad).astype(BFLOAT)
    grad_scores = (
        probs * (grad_probs - jnp.sum(probs * grad_probs, -1, keepdims=True))
    ).astype(BFLOAT)
    grad_queries = unstack_heads(dot_nn(grad_scores, keys) * scale).astype(BFLOAT)
    grad_keys = (dot_tn(grad_scores, queries) * scale).astype(BFLOAT)
    return grad_queries, grad_keys, grad_values


def backward_kernel(length, mem_length, *refs):
    weights = refs[:7]
    kept_hbm = refs[7:23]
    inner_hbm = refs[23]
    norm_full, grad_third, gemb = refs[24:27]
    outs = refs[27:34]
    norm_out, grad_states, grad_memory, pieces, landing = refs[34:39]
    kept = refs[39:55]
    (
        wbuf, inner, stage, got, zload, one_line, two_line, one, two, line, fin,
        resid, low, grad_low, grad_context, grad_queries, grad_packed, memory_part,
        norm_here, norm_there, norm_line,
    ) = refs[55:76]
    (
        kept_sem, w_sem, inner_sem, dd_send, dd_recv, z_send, z_recv, zload_sem,
        ra_send, ra_recv, rb_send, rb_recv, rz_send, rz_recv, ag_send, ag_recv, ah_send, ah_recv,
        fin_sem, memory_sem, n_send, n_recv, nz_send, nz_recv, gemb_sem, ga_send, ga_recv,
        gb_send, gb_recv,
    ) = refs[76:]
    (
        packed, context, first_normed, first_inverse, first_low, cross_queries, pairs, cross_context,
        second_normed, second_inverse, second_low, active, third_normed, third_inverse, states, encoded,
    ) = kept
    x, y, z, c = whereami()
    greet(neighbours(x, y, z, c))
    tokens, width = states.shape
    slots_here = tokens // length
    count = len(SEQUENCE)
    blocks = active.shape[1] // (8 * ROWS)

    def keep_copy(n):
        return pltpu.make_async_copy(kept_hbm[n], kept[n], kept_sem.at[n])

    first_needed = (12, 13, 11, 10)
    for n in first_needed:
        keep_copy(n).start()
    for n in range(16):
        if n not in first_needed:
            keep_copy(n).start()

    def need(*names):
        for n in names:
            keep_copy(n).wait()

    def read_copy(n):
        weight, k = READS[n]
        if weight == REDUCE_WEIGHT:
            source = weights[weight].at[pl.ds(k * TILE, TILE), :]
        else:
            source = weights[weight].at[:, pl.ds(k * TILE, TILE)]
        return pltpu.make_async_copy(source, wbuf.at[n % 2], w_sem.at[n % 2])

    def inner_copy(k):
        return pltpu.make_async_copy(
            inner_hbm.at[:, pl.ds(k * TILE, TILE)], inner.at[k % 2], inner_sem.at[k % 2]
        )

    read_copy(0).start()
    read_copy(1).start()
    inner_copy(0).start()
    inner_copy(1).start()

    def remote(src, dst, send, recv, peer):
        return pltpu.make_async_remote_copy(
            src_ref=src, dst_ref=dst, send_sem=send, recv_sem=recv, device_id=peer, device_id_type=MESH
        )

    def norm_row(n):
        return jnp.concatenate([norm_full[p // 2, p % 2, n : n + 1, :] for p in range(8)], 1)

    def place(q):
        even = lax.rem(q, 2) == 0
        a = jnp.where(even, x, y)
        b = jnp.where(even, y, x)
        x_peer = y * 2 + (1 - x)
        y_peer = (1 - y) * 2 + x
        a_peer = (jnp.where(even, x_peer, y_peer), z * 2 + c)
        b_peer = (jnp.where(even, y_peer, x_peer), z * 2 + c)
        return a, b, a_peer, b_peer

    def piece(index, size):
        return pl.ds(pl.multiple_of(index * size, size), size)

    def total(*parts):
        out = parts[0].astype(jnp.float32)
        for part in parts[1:]:
            out = out + part.astype(jnp.float32)
        return out.astype(BFLOAT)

    pb = y * 2 + x
    pb_x, pb_y = y * 2 + 1 - x, (1 - y) * 2 + x
    vocab_rows = gemb.shape[0]
    cut = 16 * (vocab_rows // 64)
    cuts = [(n * cut, cut if n < 3 else vocab_rows - 3 * cut) for n in range(4)]

    def gather_one(n):
        rows_here = pl.ds(*cuts[n])
        peer = at(1 - x, y, z, c) if n < 2 else at(x, 1 - y, z, c)
        return remote(gemb.at[rows_here, :], pieces.at[pb, rows_here, :], ga_send.at[n], ga_recv.at[n], peer)

    def gather_two(n, j):
        rows_here = pl.ds(*cuts[n])
        peer = at(x, 1 - y, z, c) if n < 2 else at(1 - x, y, z, c)
        origin = pb if j == 0 else (pb_x if n < 2 else pb_y)
        source = gemb.at[rows_here, :] if j == 0 else pieces.at[origin, rows_here, :]
        return remote(source, pieces.at[origin, rows_here, :], gb_send.at[n, j], gb_recv.at[n, j], peer)

    gemb_copy = pltpu.make_async_copy(gemb, pieces.at[pb], gemb_sem)
    for n in (0, 2, 1, 3):
        gather_one(n).start()
    for n in (2, 0, 3, 1):
        gather_two(n, 0).start()
    gemb_copy.start()

    def dd_copy(q):
        return remote(
            stage.at[lax.rem(q, 2), 1 - c], got.at[q], dd_send.at[q], dd_recv.at[q], at(x, y, z, 1 - c)
        )

    def line_copy(q, side, h, dest, step):
        return remote(
            got.at[q, dest], landing.at[q, side, h - 1], z_send.at[q, side, h - 1],
            z_recv.at[q, side, h - 1], at(x, y, lax.rem(z + step + 4, 4), c),
        )

    def line_sides(h):
        return (
            (0, z + 4 - h, z <= h - 1, z >= 1, 1),
            (1, z - 4 + h, z >= 4 - h, z <= 2, -1),
        )

    def line_load(q, side, h):
        return pltpu.make_async_copy(landing.at[q, side, h - 2], zload.at[side], zload_sem.at[side])

    def line_hop(q, h):
        if h > 1:
            for side, dest, there, fed, step in line_sides(h):
                @pl.when(there & fed)
                def _():
                    line_copy(q, side, h - 1, dest, step).wait_recv()
                    line_load(q, side, h).start()

        for side, dest, there, fed, step in line_sides(h):
            if h > 1:
                @pl.when(there & fed)
                def _():
                    line_load(q, side, h).wait()

                    @pl.loop(0, 8)
                    def _(j):
                        rows_here = piece(j, 16)
                        got[q, dest, rows_here, :] = total(
                            got[q, dest, rows_here, :], zload[side, rows_here, :]
                        )

            if h < 4:
                @pl.when(there)
                def _():
                    line_copy(q, side, h, dest, step).start()

    def ra_line(q):
        a, _, a_peer, _ = place(q)
        return remote(got.at[q, z, piece(1 - a, 64), :], one_line.at[q], ra_send.at[q], ra_recv.at[q], a_peer)

    def rb_line(q):
        _, b, _, b_peer = place(q)
        return remote(one_line.at[q, piece(1 - b, 32), :], two_line.at[q], rb_send.at[q], rb_recv.at[q], b_peer)

    def ra_cross(q):
        a, _, a_peer, _ = place(q)
        return remote(
            got.at[q, :, piece(1 - a, 64), :], one.at[q - LINE_FIRST], ra_send.at[q], ra_recv.at[q], a_peer
        )

    def rb_cross(q):
        _, b, _, b_peer = place(q)
        return remote(
            one.at[q - LINE_FIRST, :, piece(1 - b, 32), :], two.at[q - LINE_FIRST],
            rb_send.at[q], rb_recv.at[q], b_peer,
        )

    def rz_cross(q, d):
        other = lax.rem(z + d, 4)
        n = q - LINE_FIRST
        return remote(
            two.at[n, other], line.at[n, d - 1], rz_send.at[n, d - 1], rz_recv.at[n, d - 1],
            at(x, y, other, c),
        )

    def out_view(q, start, size):
        return shard_view(outs[SEQUENCE[q][0]], SEQUENCE[q], start, size)

    def quarter_start(q):
        a, b, _, _ = place(q)
        return pl.multiple_of(64 * a + 32 * b, 32)

    def fin_copy(q):
        return pltpu.make_async_copy(fin.at[q], out_view(q, quarter_start(q), 32), fin_sem.at[q])

    def ag_copy(q):
        return remote(
            fin.at[q], out_view(q, quarter_start(q), 32), ag_send.at[q], ag_recv.at[q], place(q)[3]
        )

    def ah_copy(q):
        a, _, a_peer, _ = place(q)
        part = out_view(q, pl.multiple_of(64 * a, 64), 64)
        return remote(part, part, ah_send.at[q], ah_recv.at[q], a_peer)

    norm_peers = (at(x, y, z, 1 - c), at(1 - x, y, z, c), at(x, 1 - y, z, c))

    def norm_copy(n):
        return remote(norm_here.at[n], norm_there.at[n], n_send.at[n], n_recv.at[n], norm_peers[n])

    def norm_line_copy(d):
        return remote(
            norm_here.at[3], norm_line.at[d - 1], nz_send.at[d - 1], nz_recv.at[d - 1],
            at(x, y, lax.rem(z + d, 4), c),
        )

    def outer(q, left, start, step, right):
        slot = q % 2

        @pl.loop(0, 8, unroll=4)
        def _(p):
            lanes = pl.ds(pl.multiple_of(start + p * step, 128), 128)
            stage[slot, lax.rem(p, 2), p // 2] = dot_tn(left[:, lanes], right()).astype(BFLOAT)

    def back_times(left, n, write):
        slot = n % 2
        read_copy(n).wait()

        @pl.loop(0, 4, unroll=True)
        def _(m):
            write(piece(m, 256), dot_nt(left[...], wbuf[slot, piece(m, 256), :]))

        if n + 2 < len(READS):
            read_copy(n + 2).start()

    def add_resid(columns, value):
        resid[:, columns] = resid[:, columns] + value

    def finish_norm(n, normed, inverse):
        value, gain, shift = norm_back(resid[...], normed[...], inverse[:, 0:1], norm_row(n))
        resid[...] = value
        low[...] = value.astype(BFLOAT)
        norm_here[0, n : n + 1, :] = gain
        norm_here[0, n + 3 : n + 4, :] = shift

    def attention_back(queries, keys, key_start, value_start, key_length, out, out_keys, causal):
        @pl.loop(0, slots_here * (width // 128), unroll=2)
        def _(n):
            slot, group = n // (width // 128), lax.rem(n, width // 128)
            lanes = piece(group, 128)
            key_lanes = pl.ds(pl.multiple_of(key_start + group * 128, 128), 128)
            value_lanes = pl.ds(pl.multiple_of(value_start + group * 128, 128), 128)
            query_rows = piece(slot, length)
            key_rows = piece(slot, key_length)
            grad_query, grad_key, grad_value = attend_pair_back(
                grad_context[query_rows, lanes],
                queries[query_rows, lanes],
                keys[key_rows, key_lanes],
                keys[key_rows, value_lanes],
                causal,
            )
            out[query_rows, lanes] = grad_query
            out_keys[key_rows, key_lanes] = grad_key
            out_keys[key_rows, value_lanes] = grad_value

    def produce(q):
        weight, k = SEQUENCE[q]
        if q == 0:
            norm_here[0] = jnp.zeros_like(norm_here[0])
            for p in range(8):
                resid[:, p * 128 : (p + 1) * 128] = grad_third[p * 128 : (p + 1) * 128, :].T
            need(12, 13, 11)
            finish_norm(2, third_normed, third_inverse)
        if weight == 6:
            outer(q, active, k * ROWS, blocks * ROWS, lambda: low[...])
        elif weight == 5:
            if k == 0:
                need(10)
            inner_copy(k).wait()

            def write(columns, value):
                pre = inner[k % 2, :, columns]
                slope = 0.5 * (1.0 + lax.erf(pre * math.sqrt(0.5))) + pre * jnp.exp(
                    -0.5 * pre * pre
                ) * (1.0 / math.sqrt(2.0 * math.pi))
                grad_low[:, columns] = (value * slope).astype(BFLOAT)

            back_times(low, 2 * k, write)
            if k + 2 < 4:
                inner_copy(k + 2).start()
            outer(q, second_low, 0, ROWS, lambda: grad_low[...])
            back_times(grad_low, 2 * k + 1, add_resid)
        elif weight == 4:
            need(8, 9, 7)
            finish_norm(1, second_normed, second_inverse)
            outer(q, cross_context, 0, ROWS, lambda: low[...])

            def write(columns, value):
                grad_context[:, columns] = value.astype(BFLOAT)

            back_times(low, 8, write)
        elif weight == 2:
            need(5, 6, 4, 2, 3)
            attention_back(cross_queries, pairs, 0, width, mem_length, grad_queries, pairs, False)
            outer(q, first_low, 0, ROWS, lambda: grad_queries[...])
            back_times(grad_queries, 9, add_resid)
            finish_norm(0, first_normed, first_inverse)
        elif weight == 3:
            if k == 0:
                need(15)
            outer(q, encoded, 0, ROWS, lambda: pairs[:, pl.ds(k * TILE, TILE)])
        elif weight == 1:
            need(1, 0, 14)
            outer(q, context, 0, ROWS, lambda: low[...])

            def write(columns, value):
                grad_context[:, columns] = value.astype(BFLOAT)

            back_times(low, 10, write)
            attention_back(packed, packed, width, 2 * width, length, grad_packed, grad_packed, True)
        else:
            def part():
                return grad_packed[:, pl.ds(k * TILE, TILE)]

            outer(q, states, 0, ROWS, part)
            back_times(grad_packed.at[:, pl.ds(k * TILE, TILE)], 11 + k, add_resid)
            if k == 2:
                grad_states[...] = resid[...]

    half = encoded.shape[0] // 2

    def memory_copy(m):
        return pltpu.make_async_copy(
            memory_part.at[m % 2],
            grad_memory.at[pl.ds(m // 4 * half, half), pl.ds(m % 4 * 256, 256)],
            memory_sem.at[m % 2],
        )

    def memory_chunk(m):
        if m == 0:
            read_copy(14).wait()
            read_copy(15).wait()
        if m >= 2:
            memory_copy(m - 2).wait()
        rows_here, columns = pl.ds(m // 4 * half, half), pl.ds(m % 4 * 256, 256)
        memory_part[m % 2] = dot_nt(pairs[rows_here, :width], wbuf[0, columns, :]) + dot_nt(
            pairs[rows_here, width:], wbuf[1, columns, :]
        )
        memory_copy(m).start()

    def each(q, action):
        for k in range(count):
            @pl.when(q == k)
            def _():
                action(k)

    def finish_block(q):
        def action(k):
            fin_copy(k).start()
            ag_copy(k).start()

        each(q, action)

    step = 16

    @pl.loop(0, TURNS)
    def _(i):
        for q in range(count):
            @pl.when(i == q)
            def _():
                if q >= 2:
                    dd_copy(q - 2).wait_send()
                produce(q)
                dd_copy(q).start()

        for n, turn in enumerate(GATHER_TURNS):
            @pl.when(i == turn)
            def _():
                for part in (n, n + 2):
                    gather_one(part).wait_recv()
                    gather_two(part, 1).start()

        for m in range(8):
            @pl.when(i == count + 1 + m)
            def _():
                memory_chunk(m)

        qs = i - 1

        @pl.when((qs >= 0) & (qs < count))
        def _():
            dd_copy(qs).wait_recv()
            slot = lax.rem(qs, 2)

            @pl.loop(0, 32)
            def _(j):
                zz, rows_here = j // 8, piece(lax.rem(j, 8), step)
                got[qs, zz, rows_here, :] = total(got[qs, zz, rows_here, :], stage[slot, c, zz, rows_here, :])

            @pl.when(qs < LINE_FIRST)
            def _():
                line_hop(qs, 1)

            @pl.when(qs >= LINE_FIRST)
            def _():
                ra_cross(qs).start()

        for h in (2, 3, 4):
            qh = i - HOP_LAGS[h - 2]

            @pl.when((qh >= 0) & (qh < LINE_FIRST))
            def _():
                line_hop(qh, h)
                if h == 4:
                    ra_line(qh).start()

        q1 = i - LINE_LAGS[1]

        @pl.when((q1 >= 0) & (q1 < LINE_FIRST))
        def _():
            ra_line(q1).wait_recv()
            a = place(q1)[0]

            @pl.loop(0, 4)
            def _(j):
                rows_here = piece(j, step)
                one_line[q1, rows_here, :] = total(
                    one_line[q1, rows_here, :],
                    got[q1, z, pl.ds(pl.multiple_of(64 * a + j * step, step), step), :],
                )

            rb_line(q1).start()

        q2 = i - LINE_LAGS[2]

        @pl.when((q2 >= 0) & (q2 < LINE_FIRST))
        def _():
            rb_line(q2).wait_recv()
            b = place(q2)[1]

            @pl.loop(0, 2)
            def _(j):
                rows_here = piece(j, step)
                fin[q2, rows_here, :] = total(
                    two_line[q2, rows_here, :],
                    one_line[q2, pl.ds(pl.multiple_of(32 * b + j * step, step), step), :],
                )

            finish_block(q2)

        p0 = i - CROSS_LAGS[0]

        @pl.when((p0 >= LINE_FIRST) & (p0 < count))
        def _():
            ra_cross(p0).wait_recv()
            a = place(p0)[0]

            @pl.loop(0, 16)
            def _(j):
                zz, r = j // 4, lax.rem(j, 4)
                rows_here = piece(r, step)
                one[p0 - LINE_FIRST, zz, rows_here, :] = total(
                    one[p0 - LINE_FIRST, zz, rows_here, :],
                    got[p0, zz, pl.ds(pl.multiple_of(64 * a + r * step, step), step), :],
                )

            rb_cross(p0).start()

        p1 = i - CROSS_LAGS[1]

        @pl.when((p1 >= LINE_FIRST) & (p1 < count))
        def _():
            rb_cross(p1).wait_recv()
            b = place(p1)[1]

            @pl.loop(0, 8)
            def _(j):
                zz, r = j // 2, lax.rem(j, 2)
                rows_here = piece(r, step)
                two[p1 - LINE_FIRST, zz, rows_here, :] = total(
                    two[p1 - LINE_FIRST, zz, rows_here, :],
                    one[p1 - LINE_FIRST, zz, pl.ds(pl.multiple_of(32 * b + r * step, step), step), :],
                )

            for d in (1, 2, 3):
                rz_cross(p1, d).start()

        p2 = i - CROSS_LAGS[2]

        @pl.when((p2 >= LINE_FIRST) & (p2 < count))
        def _():
            for d in (1, 2, 3):
                rz_cross(p2, d).wait_recv()
            n = p2 - LINE_FIRST

            @pl.loop(0, 2)
            def _(j):
                rows_here = piece(j, step)
                fin[p2, rows_here, :] = total(
                    two[n, z, rows_here, :], line[n, 0, rows_here, :], line[n, 1, rows_here, :],
                    line[n, 2, rows_here, :],
                )

            finish_block(p2)

        def pass_on(k):
            ag_copy(k).wait_recv()
            fin_copy(k).wait()
            ah_copy(k).start()

        for lags, low_q, high_q in ((LINE_LAGS, 0, LINE_FIRST), (CROSS_LAGS, LINE_FIRST, count)):
            q3 = i - lags[3]

            @pl.when((q3 >= low_q) & (q3 < high_q))
            def _():
                each(q3, pass_on)

            q4 = i - lags[4]

            @pl.when((q4 >= low_q) & (q4 < high_q))
            def _():
                each(q4, lambda k: ah_copy(k).wait_recv())

        @pl.when(i == count)
        def _():
            norm_copy(0).start()

        for n in range(3):
            @pl.when(i == count + 2 * (n + 1))
            def _():
                norm_copy(n).wait_recv()
                norm_here[n + 1] = norm_here[n] + norm_there[n]
                if n < 2:
                    norm_copy(n + 1).start()
                else:
                    for d in (1, 2, 3):
                        norm_line_copy(d).start()

        @pl.when(i == count + 8)
        def _():
            for d in (1, 2, 3):
                norm_line_copy(d).wait_recv()
            norm_out[...] = ((norm_here[3] + norm_line[0]) + norm_line[1]) + norm_line[2]

    gemb_copy.wait()
    for n in range(4):
        gather_one(n).wait_send()
        for j in range(2):
            gather_two(n, j).wait()
    memory_copy(6).wait()
    memory_copy(7).wait()
    dd_copy(count - 2).wait_send()
    dd_copy(count - 1).wait_send()

    @pl.loop(0, LINE_FIRST)
    def _(q):
        for h in (1, 2, 3):
            for side, dest, there, _, step in line_sides(h):
                @pl.when(there)
                def _():
                    line_copy(q, side, h, dest, step).wait_send()

        ra_line(q).wait_send()
        rb_line(q).wait_send()

    @pl.loop(LINE_FIRST, count)
    def _(q):
        ra_cross(q).wait_send()
        rb_cross(q).wait_send()
        for d in (1, 2, 3):
            rz_cross(q, d).wait_send()

    for q in range(count):
        ag_copy(q).wait_send()
        ah_copy(q).wait_send()
    for n in range(3):
        norm_copy(n).wait_send()
        norm_line_copy(n + 1).wait_send()


def backward_layer(weights, kept, inner, norm_full, grad_third, gemb, length):
    count = len(SEQUENCE)
    f32 = jnp.float32
    tokens, width = kept[14].shape
    mem_tokens = kept[15].shape[0]
    mem_length = mem_tokens // (tokens // length)
    shapes = [(weight.shape[0] // 8, weight.shape[1]) for weight in weights]
    every = pl.BlockSpec(memory_space=pl.ANY)
    vmem = pl.BlockSpec(memory_space=pltpu.VMEM)
    dma = pltpu.SemaphoreType.DMA
    sems = dma((count,))
    crossed = count - LINE_FIRST
    *shares, norm_sum, grad_states, grad_memory, pieces, _ = pl.pallas_call(
        functools.partial(backward_kernel, length, mem_length),
        out_shape=tuple(jax.ShapeDtypeStruct(shape, BFLOAT) for shape in shapes)
        + (
            jax.ShapeDtypeStruct((8, width), f32),
            jax.ShapeDtypeStruct((tokens, width), f32),
            jax.ShapeDtypeStruct((mem_tokens, width), f32),
            jax.ShapeDtypeStruct((4,) + gemb.shape, BFLOAT),
            jax.ShapeDtypeStruct((LINE_FIRST, 2, 3, ROWS, TILE), BFLOAT),
        ),
        in_specs=[every] * 24 + [vmem] * 2 + [every],
        out_specs=(every,) * 7 + (vmem, vmem, every, every, every),
        scratch_shapes=[pltpu.VMEM(part.shape, part.dtype) for part in kept]
        + [
            pltpu.VMEM((2, TILE, TILE), BFLOAT),
            pltpu.VMEM((2, tokens, TILE), f32),
            pltpu.VMEM((2, 2, 4, ROWS, TILE), BFLOAT),
            pltpu.VMEM((count, 4, ROWS, TILE), BFLOAT),
            pltpu.VMEM((2, ROWS, TILE), BFLOAT),
            pltpu.VMEM((LINE_FIRST, 64, TILE), BFLOAT),
            pltpu.VMEM((LINE_FIRST, 32, TILE), BFLOAT),
            pltpu.VMEM((crossed, 4, 64, TILE), BFLOAT),
            pltpu.VMEM((crossed, 4, 32, TILE), BFLOAT),
            pltpu.VMEM((crossed, 3, 32, TILE), BFLOAT),
            pltpu.VMEM((count, 32, TILE), BFLOAT),
            pltpu.VMEM((tokens, width), f32),
            pltpu.VMEM((tokens, width), BFLOAT),
            pltpu.VMEM((tokens, TILE), BFLOAT),
            pltpu.VMEM((tokens, width), BFLOAT),
            pltpu.VMEM((tokens, width), BFLOAT),
            pltpu.VMEM((tokens, 3 * width), BFLOAT),
            pltpu.VMEM((2, mem_tokens // 2, 256), f32),
            pltpu.VMEM((4, 8, width), f32),
            pltpu.VMEM((3, 8, width), f32),
            pltpu.VMEM((3, 8, width), f32),
            dma((16,)), dma((2,)), dma((2,)), sems, sems,
            dma((LINE_FIRST, 2, 3)), dma((LINE_FIRST, 2, 3)), dma((2,)),
            sems, sems, sems, sems,
            dma((crossed, 3)), dma((crossed, 3)),
            sems, sems, sems, sems, sems, dma((2,)),
            dma((3,)), dma((3,)), dma((3,)), dma((3,)),
            dma, dma((4,)), dma((4,)), dma((4, 2)), dma((4, 2)),
        ],
        compiler_params=pltpu.CompilerParams(
            collective_id=1, has_side_effects=True, vmem_limit_bytes=62 * 2**20
        ),
        name="backward_layer",
    )(*weights, *kept, inner, norm_full, grad_third, gemb)
    return shares, norm_sum, grad_states, grad_memory, pieces


WIDE_ROWS = 512
WIDE_SLOTS = 4


def widen_kernel(embed_rows, *refs):
    parts, pieces, norms, done = refs[:7], refs[7], refs[8], refs[9:11]
    outs, embed_out, done_out = refs[11:18], refs[18], refs[19:21]
    gains_out, shifts_out = refs[21:23]
    low, wide = refs[23:30], refs[30:37]
    embed_low, embed_wide, norm_here, done_here = refs[37:40] + (refs[40:42],)
    in_sem, out_sem, embed_in, embed_out_sem, norm_sem, done_sem = refs[42:]
    done_in = [pltpu.make_async_copy(done[n], done_here[n], done_sem.at[n]) for n in range(2)]
    done_copies = [
        pltpu.make_async_copy(done_here[n], done_out[n], done_sem.at[n + 2]) for n in range(2)
    ]
    here = norm_here.shape[1]
    norm_copy = pltpu.make_async_copy(
        norms.at[:, pl.ds(pl.multiple_of(lax.axis_index("pa") * here, here), here)], norm_here, norm_sem
    )
    norm_copy.start()
    full = embed_rows // WIDE_ROWS
    rest = embed_rows - full * WIDE_ROWS

    def load(n, rows):
        return pltpu.make_async_copy(
            pieces.at[pl.ds(n * WIDE_ROWS, rows), :],
            embed_low.at[n % WIDE_SLOTS, pl.ds(0, rows), :],
            embed_in.at[n % WIDE_SLOTS],
        )

    def store(n, rows):
        return pltpu.make_async_copy(
            embed_wide.at[n % WIDE_SLOTS, pl.ds(0, rows), :],
            embed_out.at[pl.ds(n * WIDE_ROWS, rows), :],
            embed_out_sem.at[n % WIDE_SLOTS],
        )

    sizes = [WIDE_ROWS] * full + [rest] * (rest > 0)
    for n in range(WIDE_SLOTS):
        load(n, sizes[n]).start()
    for n in range(7):
        pltpu.make_async_copy(parts[n], low[n], in_sem.at[n]).start()
    for copy in done_in:
        copy.start()
    for n, rows in enumerate(sizes):
        load(n, rows).wait()
        if n >= WIDE_SLOTS:
            store(n - WIDE_SLOTS, sizes[n - WIDE_SLOTS]).wait()

        @pl.loop(0, rows // 16, unroll=4)
        def _(j):
            part = pl.ds(pl.multiple_of(j * 16, 16), 16)
            embed_wide[n % WIDE_SLOTS, part, :] = embed_low[n % WIDE_SLOTS, part, :].astype(jnp.float32)

        store(n, rows).start()
        if n + WIDE_SLOTS < len(sizes):
            load(n + WIDE_SLOTS, sizes[n + WIDE_SLOTS]).start()
    for n in range(7):
        pltpu.make_async_copy(parts[n], low[n], in_sem.at[n]).wait()

        @pl.loop(0, low[n].shape[0] // 16)
        def _(j):
            part = pl.ds(pl.multiple_of(j * 16, 16), 16)
            wide[n][part, :] = low[n][part, :].astype(jnp.float32)

        pltpu.make_async_copy(wide[n], outs[n], out_sem.at[n]).start()
    for n in range(2):
        done_in[n].wait()
        done_copies[n].start()
    norm_copy.wait()
    gains_out[...] = norm_here[0:3, :]
    shifts_out[...] = norm_here[3:6, :]
    for n in range(len(sizes) - WIDE_SLOTS, len(sizes)):
        store(n, sizes[n]).wait()
    for n in range(7):
        pltpu.make_async_copy(wide[n], outs[n], out_sem.at[n]).wait()
    for copy in done_copies:
        copy.wait()


def widen(parts, pieces, norms, done, embed_rows, norm_here):
    every = pl.BlockSpec(memory_space=pl.ANY)
    vmem = pl.BlockSpec(memory_space=pltpu.VMEM)
    f32 = jnp.float32
    width = pieces.shape[1]
    dma = pltpu.SemaphoreType.DMA
    results = pl.pallas_call(
        functools.partial(widen_kernel, embed_rows),
        out_shape=tuple(jax.ShapeDtypeStruct(part.shape, f32) for part in parts)
        + (jax.ShapeDtypeStruct((embed_rows, width), f32),)
        + tuple(jax.ShapeDtypeStruct(part.shape, part.dtype) for part in done)
        + (jax.ShapeDtypeStruct((3, norm_here), f32),) * 2,
        in_specs=[every] * 11,
        out_specs=(every,) * 10 + (vmem,) * 2,
        scratch_shapes=[pltpu.VMEM(part.shape, BFLOAT) for part in parts]
        + [pltpu.VMEM(part.shape, f32) for part in parts]
        + [
            pltpu.VMEM((WIDE_SLOTS, WIDE_ROWS, width), BFLOAT),
            pltpu.VMEM((WIDE_SLOTS, WIDE_ROWS, width), f32),
            pltpu.VMEM((8, norm_here), f32),
            pltpu.VMEM(done[0].shape, f32),
            pltpu.VMEM(done[1].shape, f32),
            dma((7,)),
            dma((7,)),
            dma((WIDE_SLOTS,)),
            dma((WIDE_SLOTS,)),
            dma,
            dma((4,)),
        ],
        compiler_params=pltpu.CompilerParams(vmem_limit_bytes=60 * 2**20),
        name="widen",
    )(*parts, pieces, norms, *done)
    return results[:7], results[7:]


VOCAB_CUTS = 3
ARRIVAL_PHASES = (0, 0, 1, 2, 0, 1, 2, 3, 0, 1, 2, 3, 1, 2, 3, 3)
ARRIVAL_TURNS = (0, 1, 0, 0, 2, 1, 1, 0, 3, 2, 2, 1, 3, 3, 2, 3)
NEAREST = ((0, 1, 2, 3), (1, 0, 1, 2), (2, 2, 3, 1), (3, 3, 0, 0))


def head_kernel(slots, length, vocab_here, *refs):
    hid, marks, emb_all = refs[:3]
    small_out, gemb_out, third_out = refs[3:6]
    (
        emb, emb_t, held, logit, expo, part, sib_part, part_one, part_two, part_z,
        mine, theirs, crossed, lined, prior, usable, weight, scaled, picked_grad,
    ) = refs[6:25]
    (
        local_sem, z_send, z_recv, one_send, one_recv, two_send, two_recv, sib_send, sib_recv,
        st_send, st_recv, stz_send, stz_recv,
        dd_send, dd_recv, r1_send, r1_recv, r2_send, r2_recv, rz_send, rz_recv,
    ) = refs[25:]
    x, y, z, c = whereami()
    pb, pa = y * 2 + x, z * 2 + c
    size = hid.shape[0]
    pair = 2 * size
    width = hid.shape[1]
    rows = emb.shape[0]
    cut = rows // VOCAB_CUTS
    start = pl.multiple_of(pb * rows, 16)
    last = vocab_here - 3 * rows
    valid = jnp.where(pb == 3, last, rows)
    base = pa * vocab_here + start
    own = pb * 4 + z

    def remote(src, dst, send, recv, peer):
        return pltpu.make_async_remote_copy(
            src_ref=src, dst_ref=dst, send_sem=send, recv_sem=recv, device_id=peer, device_id_type=MESH
        )

    sibling = at(x, y, z, 1 - c)
    x_peer, y_peer = at(1 - x, y, z, c), at(x, 1 - y, z, c)

    def spot(k, core, n=None):
        rows_here = size if n is None else size // 2
        first = (k * 2 + core) * size + (0 if n is None else n * rows_here)
        return held.at[pl.ds(pl.multiple_of(first, rows_here), rows_here), :]

    across = [at(1 - x, y, z, c), at(x, 1 - y, z, c), at(1 - x, 1 - y, z, c)]
    greet(neighbours(x, y, z, c) + across[2:])
    own_copy = pltpu.make_async_copy(hid, spot(own, c), local_sem.at[0])
    own_copy.start()
    emb_copy = pltpu.make_async_copy(
        emb_all.at[pl.ds(start, last), :], emb.at[pl.ds(0, last), :], local_sem.at[2]
    )
    rest_copy = pltpu.make_async_copy(
        emb_all.at[pl.ds(pl.multiple_of(jnp.minimum(start + last, vocab_here - (rows - last)), 16), rows - last), :],
        emb.at[pl.ds(last, rows - last), :],
        local_sem.at[3],
    )
    emb_copy.start()
    rest_copy.start()
    own_copy.wait()

    def up_copy(origin, n):
        block = spot(pb * 4 + origin, c, n)
        return remote(block, block, z_send.at[0, origin, n], z_recv.at[origin, n], at(x, y, lax.rem(z + 1, 4), c))

    def down_copy(origin, n):
        block = spot(pb * 4 + origin, c, n)
        return remote(block, block, z_send.at[1, origin, n], z_recv.at[origin, n], at(x, y, lax.rem(z + 3, 4), c))

    def pass_along(origin, n, action):
        @pl.when((origin <= z) & (z < 3))
        def _():
            action(up_copy(origin, n))

        @pl.when((origin >= z) & (z > 0))
        def _():
            action(down_copy(origin, n))

    def sib_copy(k, n):
        return remote(spot(k, c, n), spot(k, c, n), sib_send.at[k, n], sib_recv.at[k, n], sibling)

    def order(zz):
        x_first = zz < 2
        f = jnp.where(x_first, x, y)
        g = jnp.where(x_first, y, x)
        first_peer = (jnp.where(x_first, y * 2 + 1 - x, (1 - y) * 2 + x), pa)
        second_peer = (jnp.where(x_first, (1 - y) * 2 + x, y * 2 + 1 - x), pa)

        def block(first, second):
            return jnp.where(x_first, second * 2 + first, first * 2 + second) * 4 + zz

        return f, g, first_peer, second_peer, block

    def one_copy(zz, n):
        f, g, first_peer, _, block = order(zz)
        part = spot(block(f, g), c, n)
        return remote(part, part, one_send.at[zz, n], one_recv.at[zz, n], first_peer)

    def two_copy(zz, j, n):
        f, g, _, second_peer, block = order(zz)
        part = spot(block(f if j == 0 else 1 - f, g), c, n)
        return remote(part, part, two_send.at[zz, j, n], two_recv.at[zz, j, n], second_peer)

    for n in range(2):
        pass_along(z, n, lambda copy: copy.start())
        one_copy(z, n).start()
        two_copy(z, 0, n).start()
        sib_copy(own, n).start()

    emb_copy.wait()
    rest_copy.wait()
    full_cuts = rows // 128

    def target_rows(k):
        ypart, xpart, zpart = k // 8, lax.rem(k // 4, 2), lax.rem(k, 4)
        target = marks[ypart, xpart, zpart, 0:1, :].astype(jnp.int32) - base
        return jnp.where(target < valid, target, -1)

    def row_numbers(j):
        return lax.broadcasted_iota(jnp.int32, (cut, pair), 0) + j * cut

    def cut_rows(j):
        return pl.ds(pl.multiple_of(j * cut, cut), cut)

    def token_lanes(k):
        return pl.ds(pl.multiple_of(k * pair, pair), pair)

    def forward_block(k):
        target = target_rows(k)
        block = held[token_lanes(k), :]

        def scan_logits(j, carried):
            highest, picked = carried
            value = lax.dot_general(
                emb[cut_rows(j), :], block, (((1,), (1,)), ((), ())), preferred_element_type=jnp.float32
            )
            number = row_numbers(j)
            value = jnp.where(number < valid, value, NEGATIVE)
            logit[cut_rows(j), :] = value
            return (
                jnp.maximum(highest, jnp.max(value, 0, keepdims=True)),
                picked + jnp.sum(jnp.where(number == target, value, 0.0), 0, keepdims=True),
            )

        highest, picked = lax.fori_loop(
            0,
            VOCAB_CUTS,
            scan_logits,
            (jnp.full((1, pair), NEGATIVE, jnp.float32), jnp.zeros((1, pair), jnp.float32)),
            unroll=True,
        )

        def scan_exp(j, total):
            value = jnp.exp(logit[cut_rows(j), :] - highest)
            expo[cut_rows(j), token_lanes(k)] = value.astype(BFLOAT)
            return total + jnp.sum(value, 0, keepdims=True)

        total = lax.fori_loop(
            0, VOCAB_CUTS, scan_exp, jnp.zeros((1, pair), jnp.float32), unroll=True
        )
        mine[0, 0, pl.ds(k, 1), :] = highest
        mine[0, 1, pl.ds(k, 1), :] = total
        mine[0, 2, pl.ds(k, 1), :] = picked

    def listed(values, index):
        out = values[0]
        for n in range(1, len(values)):
            out = jnp.where(index == n, values[n], out)
        return out

    def step_block(s):
        phase = listed(ARRIVAL_PHASES, s)
        t = listed(ARRIVAL_TURNS, s)
        zz = listed([listed(row, z) for row in NEAREST], t)
        f, g, _, _, block = order(zz)
        k = listed((block(f, g), block(1 - f, g), block(f, 1 - g), block(1 - f, 1 - g)), phase)
        return phase, zz, k

    @pl.loop(0, 17)
    def _(s):
        phase, zz, k = step_block(s)

        @pl.when(s < full_cuts)
        def _():
            here = pl.ds(pl.multiple_of(s * 128, 128), 128)
            emb_t[:, here] = emb[here, :].T

        if rows % 128:
            @pl.when(s == full_cuts)
            def _():
                emb_t[:, full_cuts * 128 :] = emb[full_cuts * 128 :, :].T

        @pl.when((s > 0) & (s < 16) & (phase == 0))
        def _():
            for n in range(2):
                up_copy(zz, n).wait_recv()
                pass_along(zz, n, lambda copy: copy.start())
                one_copy(zz, n).start()
                two_copy(zz, 0, n).start()
                sib_copy(k, n).start()

        @pl.when((s < 16) & (phase == 1))
        def _():
            for n in range(2):
                one_copy(zz, n).wait_recv()
                two_copy(zz, 1, n).start()
                sib_copy(k, n).start()

        for j in range(2):
            @pl.when((s < 16) & (phase == 2 + j))
            def _():
                for n in range(2):
                    two_copy(zz, j, n).wait_recv()
                    sib_copy(k, n).start()

        @pl.when(s > 0)
        def _():
            former = step_block(s - 1)[2]
            for n in range(2):
                sib_copy(former, n).wait_recv()
            forward_block(former)

    def joined(parts):
        highest = functools.reduce(jnp.maximum, [p[0] for p in parts])
        total = functools.reduce(jnp.add, [p[1] * jnp.exp(p[0] - highest) for p in parts])
        picked = functools.reduce(jnp.add, [p[2] for p in parts])
        return highest, total, picked

    def rows_of(ref, n):
        return ref[n, 0], ref[n, 1], ref[n, 2]

    copy = remote(mine.at[0], theirs, st_send.at[0], st_recv.at[0], sibling)
    copy.start()
    copy.wait()
    here, there = rows_of(mine, 0), (theirs[0], theirs[1], theirs[2])
    early = tuple(jnp.where(c == 0, p, q) for p, q in zip(here, there))
    late = tuple(jnp.where(c == 0, q, p) for p, q in zip(here, there))
    for r, value in enumerate(joined((early, late))):
        mine[1, r] = value
        crossed[pb, r] = value
    pb_copies = [
        remote(mine.at[1], crossed.at[pb], st_send.at[n + 1], st_recv.at[n + 1], peer)
        for n, peer in enumerate(across)
    ]
    for copy in pb_copies:
        copy.start()
    for copy in pb_copies:
        copy.wait()
    for r, value in enumerate(joined([rows_of(crossed, n) for n in range(4)])):
        mine[2, r] = value
        lined[z, r] = value

    def stat_copy(d):
        other = lax.rem(z + d, 4)
        return remote(mine.at[2], lined.at[z], stz_send.at[d - 1], stz_recv.at[d - 1], at(x, y, other, c))

    for d in (1, 2, 3):
        stat_copy(d).start()
    for d in (1, 2, 3):
        stat_copy(d).wait()
    highest, total, picked = joined([rows_of(lined, n) for n in range(4)])
    logsum = highest + jnp.log(total)
    log_probs = picked - logsum
    for k in range(16):
        prior[k : k + 1, :] = marks[k // 8, (k // 4) % 2, k % 4, 1:2, :]
        usable[k : k + 1, :] = marks[k // 8, (k // 4) % 2, k % 4, 2:3, :]
    lane = lax.broadcasted_iota(jnp.int32, (16, pair), 1) // length
    mean = jnp.zeros((16, pair), jnp.float32)
    for n in range(pair // length):
        inside = lane == n
        slot_sum = jnp.sum(jnp.where(inside, log_probs, 0.0), 1, keepdims=True)
        mean = jnp.where(inside, slot_sum * (1.0 / length), mean)
    scores = prior[...] + mean
    counted = usable[...] > 0.5
    masked = jnp.where(counted, scores, NEGATIVE)
    question = lax.broadcasted_iota(jnp.int32, (16, pair), 0) // 4
    marginal = jnp.zeros((16, pair), jnp.float32)
    loss = jnp.zeros((1, 1), jnp.float32)
    for n in range(4):
        inside = question == n
        high = jnp.max(
            jnp.max(jnp.where(inside, masked, NEGATIVE), 1, keepdims=True), 0, keepdims=True
        )
        terms = jnp.where(inside & counted, jnp.exp(masked - high), 0.0)
        mass = jnp.sum(jnp.sum(terms, 1, keepdims=True), 0, keepdims=True) * (1.0 / length)
        value = high + jnp.log(mass)
        marginal = jnp.where(inside, value, marginal)
        loss = loss + value
    posterior = jnp.where(counted, jnp.exp(scores - marginal), 0.0)
    token_weight = -float(slots) * posterior
    weight[...] = posterior
    scaled[...] = token_weight * jnp.exp(mine[0, 0] - logsum)
    picked_grad[...] = token_weight * (1.0 - jnp.exp(log_probs))
    small_out[...] = jnp.broadcast_to(loss * (-1.0 / 4), small_out.shape)
    own_row = weight[pl.ds(own, 1), :]
    own_row = jnp.where(c == 0, own_row[:, :size], own_row[:, size:])
    small_out[1:2, :] = own_row * (-float(slots * length))

    def backward_block(k):
        target = target_rows(k)
        hit = picked_grad[pl.ds(k, 1), :]
        scale = scaled[pl.ds(k, 1), :]

        def make(j, carried):
            value = expo[cut_rows(j), token_lanes(k)].astype(jnp.float32)
            grad = jnp.where(row_numbers(j) == target, hit, -(value * scale))
            expo[cut_rows(j), token_lanes(k)] = grad.astype(BFLOAT)
            return carried

        lax.fori_loop(0, VOCAB_CUTS, make, 0, unroll=True)

        def to_rows(n, carried):
            cut_width = pl.ds(pl.multiple_of(n * 256, 256), 256)
            value = lax.dot_general(
                emb_t[cut_width, :],
                expo[:, token_lanes(k)],
                (((1,), (0,)), ((), ())),
                preferred_element_type=jnp.float32,
            ).astype(BFLOAT)
            part[k, 0, cut_width, :] = value[:, :size]
            part[k, 1, cut_width, :] = value[:, size:]
            return carried

        lax.fori_loop(0, width // 256, to_rows, 0, unroll=True)

    def dd_copy(k):
        return remote(part.at[k, 1 - c], sib_part.at[k], dd_send.at[k], dd_recv.at[k], sibling)

    def r1_copy(zz, j):
        f, _, first_peer, _, block = order(zz)
        return remote(
            sib_part.at[block(1 - f, j)], part_one.at[zz, j], r1_send.at[zz, j], r1_recv.at[zz, j],
            first_peer,
        )

    def half(n):
        return pl.ds(n * (width // 2), width // 2)

    def r2_copy(zz, n):
        _, g, _, second_peer, _ = order(zz)
        return remote(
            part_one.at[zz, 1 - g, half(n), :], part_two.at[zz, half(n), :], r2_send.at[zz, n],
            r2_recv.at[zz, n], second_peer,
        )

    def rz_copy(zz, n):
        return remote(
            part_two.at[zz, half(n), :], part_z.at[z, half(n), :], rz_send.at[zz, n], rz_recv.at[z, n],
            at(x, y, zz, c),
        )

    def rz_arrival(zz, n):
        return remote(
            part_two.at[zz, half(n), :], part_z.at[zz, half(n), :], rz_send.at[zz, n],
            rz_recv.at[zz, n], at(x, y, zz, c),
        )

    step = 128

    def add_into(target_ref, other_ref):
        @pl.loop(0, target_ref.shape[0] // step)
        def _(n):
            rows_here = pl.ds(pl.multiple_of(n * step, step), step)
            target_ref[rows_here, :] = (
                target_ref[rows_here, :].astype(jnp.float32) + other_ref[rows_here, :].astype(jnp.float32)
            ).astype(BFLOAT)

    def group(n):
        return lax.rem(n, 2) * 2 + n // 2

    def chunk(q):
        j, n = q // 4, lax.rem(q, 4)
        columns = pl.ds(pl.multiple_of(n * 256, 256), 256)
        gemb_out[cut_rows(j), columns] = lax.dot_general(
            expo[cut_rows(j), :],
            held[:, columns],
            (((1,), (0,)), ((), ())),
            preferred_element_type=jnp.float32,
        ).astype(BFLOAT)

    def grad_block(s):
        leaves = s < 8
        zz = group(lax.rem(s, 8) // 2)
        j = lax.rem(s, 2)
        f, _, _, _, block = order(zz)
        return leaves, zz, j, block(jnp.where(leaves, 1 - f, f), j)

    @pl.loop(0, 28)
    def _(s):
        @pl.when((s >= 2) & (s < 18))
        def _():
            leaves, zz, turn, k = grad_block(s - 2)
            dd_copy(k).wait_recv()
            add_into(sib_part.at[k], part.at[k, c])
            for j in range(2):
                @pl.when(leaves & (turn == j))
                def _():
                    r1_copy(zz, j).start()

        @pl.when((lax.rem(s, 2) == 1) & (s >= 11) & (s < 18))
        def _():
            zz = group((s - 11) // 2)
            f, _, _, _, block = order(zz)
            for j in range(2):
                r1_copy(zz, j).wait_recv()
                add_into(part_one.at[zz, j], sib_part.at[block(f, j)])
            for n in range(2):
                r2_copy(zz, n).start()

        @pl.when((lax.rem(s, 2) == 0) & (s >= 16) & (s < 24))
        def _():
            zz = group((s - 16) // 2)
            _, g, _, _, _ = order(zz)
            for n in range(2):
                r2_copy(zz, n).wait_recv()
                add_into(part_two.at[zz, half(n), :], part_one.at[zz, g, half(n), :])

                @pl.when(zz != z)
                def _():
                    rz_copy(zz, n).start()

        @pl.when(s < 16)
        def _():
            k = grad_block(s)[3]
            backward_block(k)
            dd_copy(k).start()

        @pl.when(s >= 16)
        def _():
            chunk(s - 16)

    for d in (1, 2, 3):
        for n in range(2):
            rz_arrival(lax.rem(z + d, 4), n).wait_recv()

    @pl.loop(0, width // step)
    def _(n):
        rows_here = pl.ds(pl.multiple_of(n * step, step), step)
        value = part_two[z, rows_here, :].astype(jnp.float32)
        for d in (1, 2, 3):
            value = value + part_z[lax.rem(z + d, 4), rows_here, :].astype(jnp.float32)
        third_out[rows_here, :] = value

    for d in (1, 2, 3):
        for n in range(2):
            rz_copy(lax.rem(z + d, 4), n).wait_send()

    @pl.loop(0, 4)
    def _(zz):
        for n in range(2):
            pass_along(zz, n, lambda copy: copy.wait_send())
            one_copy(zz, n).wait_send()
            for j in range(2):
                two_copy(zz, j, n).wait_send()
        for j in range(2):
            r1_copy(zz, j).wait_send()
        for n in range(2):
            r2_copy(zz, n).wait_send()

    @pl.loop(0, 16)
    def _(k):
        for n in range(2):
            sib_copy(k, n).wait_send()
        dd_copy(k).wait_send()


def vocabulary_head(third_low, marks, embedding, slots, length):
    size, width = third_low.shape
    vocab_here = embedding.shape[0]
    rows = 16 * VOCAB_CUTS * -(-vocab_here // (4 * 16 * VOCAB_CUTS))
    dma = pltpu.SemaphoreType.DMA
    vmem = pl.BlockSpec(memory_space=pltpu.VMEM)
    stat = (3, 16, 2 * size)
    f32 = jnp.float32
    block = (width, size)
    small, gemb, third = pl.pallas_call(
        functools.partial(head_kernel, slots, length, vocab_here),
        out_shape=(
            jax.ShapeDtypeStruct((8, size), f32),
            jax.ShapeDtypeStruct((rows, width), BFLOAT),
            jax.ShapeDtypeStruct((width, size), f32),
        ),
        in_specs=[vmem, vmem, pl.BlockSpec(memory_space=pl.ANY)],
        out_specs=(vmem,) * 3,
        scratch_shapes=[
            pltpu.VMEM((rows, width), BFLOAT),
            pltpu.VMEM((width, rows), BFLOAT),
            pltpu.VMEM((32 * size, width), BFLOAT),
            pltpu.VMEM((rows, 2 * size), f32),
            pltpu.VMEM((rows, 32 * size), BFLOAT),
            pltpu.VMEM((16, 2) + block, BFLOAT),
            pltpu.VMEM((16,) + block, BFLOAT),
            pltpu.VMEM((4, 2) + block, BFLOAT),
            pltpu.VMEM((4,) + block, BFLOAT),
            pltpu.VMEM((4,) + block, BFLOAT),
            pltpu.VMEM((3,) + stat, f32),
            pltpu.VMEM(stat, f32),
            pltpu.VMEM((4,) + stat, f32),
            pltpu.VMEM((4,) + stat, f32),
        ]
        + [pltpu.VMEM((16, 2 * size), f32)] * 5
        + [dma((4,))]
        + [dma((2, 4, 2)), dma((4, 2))]
        + [dma((4, 2))] * 2
        + [dma((4, 2, 2))] * 2
        + [dma((16, 2))] * 2
        + [dma((4,))] * 2
        + [dma((3,))] * 2
        + [dma((16,))] * 2
        + [dma((4, 2))] * 2
        + [dma((4, 2))] * 4,
        compiler_params=pltpu.CompilerParams(
            collective_id=2, has_side_effects=True, vmem_limit_bytes=60 * 2**20
        ),
        name="vocabulary_head",
    )(third_low, marks, embedding)
    return small, gemb, third


def merged(part, axis, combine):
    gathered = jax.tree.map(lambda a: lax.all_gather(a, axis), part)

    def take(source):
        return jax.tree.map(lambda a: lax.dynamic_index_in_dim(a, source, 0, False), gathered)

    return lax.fori_loop(
        1, lax.axis_size(axis), lambda source, state: combine(state, take(source)), take(0)
    )


def matmul(matrix_left, matrix_right):
    return lax.dot_general(
        matrix_left,
        matrix_right,
        (((matrix_left.ndim - 1,), (0,)), ((), ())),
        preferred_element_type=jnp.float32,
    )


def matmul_back(matrix_left, matrix_right):
    return lax.dot_general(
        matrix_left,
        matrix_right,
        (((matrix_left.ndim - 1,), (1,)), ((), ())),
        preferred_element_type=jnp.float32,
    )


def outer_sum(matrix_left, matrix_right):
    flat_left = matrix_left.reshape(-1, matrix_left.shape[-1])
    flat_right = matrix_right.reshape(-1, matrix_right.shape[-1])
    return lax.dot_general(
        flat_left, flat_right, (((0,), (0,)), ((), ())), preferred_element_type=jnp.float32
    )


def split_heads(values):
    return values.reshape(values.shape[0], values.shape[1], HEADS, HEAD_DIM)


def join_heads(values):
    return values.reshape(values.shape[0], values.shape[1], HEADS * HEAD_DIM)


def exact_gelu(values):
    return jax.nn.gelu(values, approximate=False)


def norm_forward(values, gain_row, shift_row):
    centre = values - jnp.mean(values, -1, keepdims=True)
    inverse = lax.rsqrt(jnp.mean(centre * centre, -1, keepdims=True) + EPSILON)
    normed = centre * inverse
    return (normed * gain_row.astype(jnp.float32) + shift_row.astype(jnp.float32), normed, inverse)


def norm_backward(upstream, normed, inverse, gain_row):
    scaled = upstream * gain_row.astype(jnp.float32)
    mean_scaled = jnp.mean(scaled, -1, keepdims=True)
    along_normed = jnp.mean(scaled * normed, -1, keepdims=True)
    grad_values = inverse * (scaled - mean_scaled - normed * along_normed)
    model_width = upstream.shape[-1]
    grad_gain = jnp.sum((upstream * normed).reshape(-1, model_width), 0)
    grad_shift = jnp.sum(upstream.reshape(-1, model_width), 0)
    return (grad_values, grad_gain, grad_shift)


def score_block(queries, key_rows, causal):
    scores = jnp.einsum(
        "nqhd,nkhd->nhqk", queries, key_rows, preferred_element_type=jnp.float32
    ) * (1.0 / math.sqrt(HEAD_DIM))
    if causal:
        length = queries.shape[1]
        allowed = lax.broadcasted_iota(jnp.int32, (length, length), 0) >= lax.broadcasted_iota(
            jnp.int32, (length, length), 1
        )
        scores = jnp.where(allowed, scores, NEGATIVE)
    return scores


def attend(queries, key_rows, values, causal):
    scores = score_block(queries, key_rows, causal)
    highest = jnp.max(scores, -1, keepdims=True)
    totals = jnp.sum(jnp.exp(scores - highest), -1, keepdims=True)
    logsum = highest + jnp.log(totals)
    probs_low = jnp.exp(scores - logsum).astype(BFLOAT)
    context = jnp.einsum(
        "nhqk,nkhd->nqhd", probs_low, values, preferred_element_type=jnp.float32
    ).astype(BFLOAT)
    return (join_heads(context), logsum)


def attend_back(grad_context, queries, key_rows, values, logsum, causal):
    score_scale = 1.0 / math.sqrt(HEAD_DIM)
    probs_full = jnp.exp(score_block(queries, key_rows, causal) - logsum)
    grad_heads = split_heads(grad_context)
    grad_probs = jnp.einsum(
        "nqhd,nkhd->nhqk", grad_heads, values, preferred_element_type=jnp.float32
    )
    grad_values = jnp.einsum(
        "nhqk,nqhd->nkhd", probs_full.astype(BFLOAT), grad_heads, preferred_element_type=jnp.float32
    ).astype(BFLOAT)
    grad_scores = (
        probs_full * (grad_probs - jnp.sum(probs_full * grad_probs, -1, keepdims=True))
    ).astype(BFLOAT)
    grad_queries = (
        jnp.einsum("nhqk,nkhd->nqhd", grad_scores, key_rows, preferred_element_type=jnp.float32)
        * score_scale
    ).astype(BFLOAT)
    grad_keys = (
        jnp.einsum("nhqk,nqhd->nkhd", grad_scores, queries, preferred_element_type=jnp.float32)
        * score_scale
    ).astype(BFLOAT)
    return (join_heads(grad_queries), join_heads(grad_keys), join_heads(grad_values))


def layer_forward(inputs, encoded, weights):
    (
        packed_weight,
        output_weight,
        query_weight,
        memory_weight,
        cross_weight,
        expand_weight,
        reduce_weight,
        gains,
        shifts,
    ) = weights
    model_width = inputs.shape[-1]
    packed = matmul(inputs, packed_weight).astype(BFLOAT)
    context, self_logsum = attend(
        split_heads(packed[..., :model_width]),
        split_heads(packed[..., model_width : 2 * model_width]),
        split_heads(packed[..., 2 * model_width :]),
        True,
    )
    first_norm, first_normed, first_inverse = norm_forward(
        inputs.astype(jnp.float32) + matmul(context, output_weight), gains[0], shifts[0]
    )
    first_low = first_norm.astype(BFLOAT)
    cross_queries = matmul(first_low, query_weight).astype(BFLOAT)
    memory_pairs = matmul(encoded, memory_weight).astype(BFLOAT)
    cross_context, cross_logsum = attend(
        split_heads(cross_queries),
        split_heads(memory_pairs[..., :model_width]),
        split_heads(memory_pairs[..., model_width:]),
        False,
    )
    second, second_normed, second_inverse = norm_forward(
        first_norm + matmul(cross_context, cross_weight), gains[1], shifts[1]
    )
    second_low = second.astype(BFLOAT)
    inner_pre = matmul(second_low, expand_weight)
    active = exact_gelu(inner_pre).astype(BFLOAT)
    third_norm, third_normed, third_inverse = norm_forward(
        second + matmul(active, reduce_weight), gains[2], shifts[2]
    )
    stored = (
        packed,
        context,
        self_logsum,
        first_normed,
        first_inverse,
        first_low,
        cross_queries,
        memory_pairs,
        cross_context,
        cross_logsum,
        second_normed,
        second_inverse,
        second_low,
        inner_pre,
        active,
        third_normed,
        third_inverse,
    )
    return (third_norm.astype(BFLOAT), stored)


def layer_backward(grad_third, inputs, encoded, weights, stored):
    (
        packed_weight,
        output_weight,
        query_weight,
        memory_weight,
        cross_weight,
        expand_weight,
        reduce_weight,
        gains,
        shifts,
    ) = weights
    (
        packed,
        context,
        self_logsum,
        first_normed,
        first_inverse,
        first_low,
        cross_queries,
        memory_pairs,
        cross_context,
        cross_logsum,
        second_normed,
        second_inverse,
        second_low,
        inner_pre,
        active,
        third_normed,
        third_inverse,
    ) = stored
    model_width = inputs.shape[-1]
    grad_res3, gain_three, shift_three = norm_backward(
        grad_third, third_normed, third_inverse, gains[2]
    )
    grad_output = grad_res3.astype(BFLOAT)
    grad_reduce = outer_sum(active, grad_output)
    grad_active = matmul_back(grad_output, reduce_weight)
    _, gelu_pull = jax.vjp(exact_gelu, inner_pre)
    grad_inner = gelu_pull(grad_active)[0].astype(BFLOAT)
    grad_expand = outer_sum(second_low, grad_inner)
    grad_second = grad_res3 + matmul_back(grad_inner, expand_weight)
    grad_res2, gain_two, shift_two = norm_backward(
        grad_second, second_normed, second_inverse, gains[1]
    )
    grad_mixed = grad_res2.astype(BFLOAT)
    grad_cross_weight = outer_sum(cross_context, grad_mixed)
    grad_cross_context = matmul_back(grad_mixed, cross_weight).astype(BFLOAT)
    grad_cross_queries, grad_memory_keys, grad_memory_values = attend_back(
        grad_cross_context,
        split_heads(cross_queries),
        split_heads(memory_pairs[..., :model_width]),
        split_heads(memory_pairs[..., model_width:]),
        cross_logsum,
        False,
    )
    grad_query_weight = outer_sum(first_low, grad_cross_queries)
    grad_first = grad_res2 + matmul_back(grad_cross_queries, query_weight)
    grad_pairs = jnp.concatenate([grad_memory_keys, grad_memory_values], -1)
    grad_memory_weight = outer_sum(encoded, grad_pairs)
    grad_encoded = matmul_back(grad_pairs, memory_weight)
    grad_res1, gain_one, shift_one = norm_backward(
        grad_first, first_normed, first_inverse, gains[0]
    )
    grad_merged = grad_res1.astype(BFLOAT)
    grad_output_weight = outer_sum(context, grad_merged)
    grad_context = matmul_back(grad_merged, output_weight).astype(BFLOAT)
    grad_queries, grad_keys, grad_values = attend_back(
        grad_context,
        split_heads(packed[..., :model_width]),
        split_heads(packed[..., model_width : 2 * model_width]),
        split_heads(packed[..., 2 * model_width :]),
        self_logsum,
        True,
    )
    grad_packed = jnp.concatenate([grad_queries, grad_keys, grad_values], -1)
    grad_packed_weight = outer_sum(inputs, grad_packed)
    grad_inputs = grad_res1 + matmul_back(grad_packed, packed_weight)
    grad_gains = jnp.stack([gain_one, gain_two, gain_three])
    grad_shifts = jnp.stack([shift_one, shift_two, shift_three])
    return (
        grad_inputs,
        grad_encoded,
        (
            grad_packed_weight,
            grad_output_weight,
            grad_query_weight,
            grad_memory_weight,
            grad_cross_weight,
            grad_expand,
            grad_reduce,
            grad_gains,
            grad_shifts,
        ),
    )


def combine_scores(former, latter):
    highest = jnp.maximum(former[0], latter[0])
    totals = former[1] * jnp.exp(former[0] - highest) + latter[1] * jnp.exp(latter[0] - highest)
    return (highest, totals, former[2] + latter[2])


def combine_pairs(former, latter):
    highest = jnp.maximum(former[0], latter[0])
    totals = former[1] * jnp.exp(former[0] - highest) + latter[1] * jnp.exp(latter[0] - highest)
    return (highest, totals)


def per_device(
    decoder_states,
    encoder_memory,
    target_tokens,
    log_prior,
    slot_counts,
    slot_mask,
    self_packed,
    self_output,
    cross_query,
    cross_memory,
    cross_output,
    feed_expand,
    feed_reduce,
    embedding,
    norm_gains,
    norm_shifts,
):
    weights = (
        lax.all_gather(self_packed, "pa", axis=0, tiled=True),
        lax.all_gather(self_output, "pa", axis=0, tiled=True),
        lax.all_gather(cross_query, "pa", axis=0, tiled=True),
        lax.all_gather(cross_memory, "pa", axis=0, tiled=True),
        lax.all_gather(cross_output, "pa", axis=0, tiled=True),
        lax.all_gather(feed_expand, "pa", axis=0, tiled=True),
        lax.all_gather(feed_reduce, "pa", axis=0, tiled=True),
        lax.all_gather(norm_gains, "pa", axis=1, tiled=True),
        lax.all_gather(norm_shifts, "pa", axis=1, tiled=True),
    )
    questions, slots_here, length, model_width = decoder_states.shape
    mem_length = encoder_memory.shape[2]
    batch_size = questions * slots_here
    inputs = decoder_states.reshape(batch_size, length, model_width)
    encoded = encoder_memory.reshape(batch_size, mem_length, model_width)
    third_low, stored = layer_forward(inputs, encoded, weights)
    tokens_here = batch_size * length
    rows_all, tokens_all = (
        lax.all_gather(third_low.reshape(tokens_here, model_width), "pa", axis=0, tiled=True),
        lax.all_gather(target_tokens.reshape(tokens_here), "pa", axis=0, tiled=True),
    )
    total_rows = rows_all.shape[0]
    block_rows = min(total_rows, 2048)
    block_count = total_rows // block_rows
    vocab_start = lax.axis_index("pa") * embedding.shape[0]
    row_blocks = rows_all.reshape(block_count, block_rows, model_width)
    token_blocks = tokens_all.reshape(block_count, block_rows)

    def vocab_logits(hidden_rows, token_rows):
        logits = matmul_back(hidden_rows, embedding)
        column = lax.broadcasted_iota(jnp.int32, logits.shape, 1) + vocab_start
        return (logits, column == token_rows[:, None])

    def vocab_partial(pieces):
        logits, chosen = vocab_logits(pieces[0], pieces[1])
        highest = jnp.max(logits, -1)
        totals = jnp.sum(jnp.exp(logits - highest[:, None]), -1)
        picked = jnp.sum(jnp.where(chosen, logits, 0.0), -1)
        return (highest, totals, picked)

    highest, totals, picked = lax.map(vocab_partial, (row_blocks, token_blocks))
    highest, totals, picked = merged(
        (highest.reshape(total_rows), totals.reshape(total_rows), picked.reshape(total_rows)),
        "pa",
        combine_scores,
    )
    row_logsum = highest + jnp.log(totals)
    own_start = lax.axis_index("pa") * tokens_here
    own_logsum = lax.dynamic_slice_in_dim(row_logsum, own_start, tokens_here)
    own_picked = lax.dynamic_slice_in_dim(picked, own_start, tokens_here)
    log_probs = (own_picked - own_logsum).reshape(questions, slots_here, length)
    scores = log_prior + jnp.mean(log_probs, -1)
    slot_index = lax.axis_index("pa") * slots_here + lax.broadcasted_iota(
        jnp.int32, (questions, slots_here), 1
    )
    usable = (slot_mask == 1) & (slot_index < slot_counts[:, None])
    masked = jnp.where(usable, scores, NEGATIVE)
    local_high = jnp.max(masked, -1)
    local_total = jnp.sum(jnp.where(usable, jnp.exp(masked - local_high[:, None]), 0.0), -1)
    slot_high, slot_total = merged((local_high, local_total), "pa", combine_pairs)
    marginal = slot_high + jnp.log(slot_total)
    posterior = jnp.where(usable, jnp.exp(scores - marginal[:, None]), 0.0)
    loss_value = -lax.psum(jnp.sum(marginal), "pb") / (questions * lax.axis_size("pb"))
    slot_number = slots_here * lax.axis_size("pa")
    grad_prior = -(slot_number * length) * posterior
    token_grad = jnp.broadcast_to(
        (-slot_number * posterior)[:, :, None], (questions, slots_here, length)
    ).reshape(tokens_here)
    weights_all = lax.all_gather(token_grad, "pa", axis=0, tiled=True)

    def vocab_grads(accumulated, pieces):
        hidden_rows, token_rows, logsum_rows, weight_rows = pieces
        logits, chosen = vocab_logits(hidden_rows, token_rows)
        softmax_rows = jnp.exp(logits - logsum_rows[:, None])
        grad_logits = (weight_rows[:, None] * (jnp.where(chosen, 1.0, 0.0) - softmax_rows)).astype(
            BFLOAT
        )
        return (accumulated + outer_sum(grad_logits, hidden_rows), matmul(grad_logits, embedding))

    grad_embed, grad_rows = lax.scan(
        vocab_grads,
        jnp.zeros(embedding.shape, jnp.float32),
        (
            row_blocks,
            token_blocks,
            row_logsum.reshape(block_count, block_rows),
            weights_all.reshape(block_count, block_rows),
        ),
    )
    grad_third = lax.psum_scatter(
        grad_rows.reshape(total_rows, model_width).astype(BFLOAT),
        "pa",
        scatter_dimension=0,
        tiled=True,
    ).astype(jnp.float32).reshape(batch_size, length, model_width)
    grad_inputs, grad_encoded, grads = layer_backward(grad_third, inputs, encoded, weights, stored)
    shares = (
        lax.psum_scatter(grads[0].astype(BFLOAT), "pa", scatter_dimension=0, tiled=True),
        lax.psum_scatter(grads[1].astype(BFLOAT), "pa", scatter_dimension=0, tiled=True),
        lax.psum_scatter(grads[2].astype(BFLOAT), "pa", scatter_dimension=0, tiled=True),
        lax.psum_scatter(grads[3].astype(BFLOAT), "pa", scatter_dimension=0, tiled=True),
        lax.psum_scatter(grads[4].astype(BFLOAT), "pa", scatter_dimension=0, tiled=True),
        lax.psum_scatter(grads[5].astype(BFLOAT), "pa", scatter_dimension=0, tiled=True),
        lax.psum_scatter(grads[6].astype(BFLOAT), "pa", scatter_dimension=0, tiled=True),
        lax.psum_scatter(grads[7], "pa", scatter_dimension=1, tiled=True),
        lax.psum_scatter(grads[8], "pa", scatter_dimension=1, tiled=True),
    )
    outputs = lax.psum(
        (
            shares[0],
            shares[1],
            shares[2],
            shares[3],
            shares[4],
            shares[5],
            shares[6],
            shares[7],
            shares[8],
            grad_embed.astype(BFLOAT),
        ),
        "pb",
    )
    outputs = tuple(part.astype(jnp.float32) for part in outputs)
    return (
        loss_value,
        grad_inputs.reshape(decoder_states.shape),
        grad_encoded.reshape(encoder_memory.shape),
        grad_prior,
        outputs[0],
        outputs[1],
        outputs[2],
        outputs[3],
        outputs[4],
        outputs[5],
        outputs[6],
        outputs[9],
        outputs[7],
        outputs[8],
    )


def per_device_kernels(
    decoder_states,
    encoder_memory,
    target_tokens,
    log_prior,
    slot_counts,
    slot_mask,
    self_packed,
    self_output,
    cross_query,
    cross_memory,
    cross_output,
    feed_expand,
    feed_reduce,
    embedding,
    norm_gains,
    norm_shifts,
):
    shards = (
        self_packed,
        self_output,
        cross_query,
        cross_memory,
        cross_output,
        feed_expand,
        feed_reduce,
    )
    norm_rows = jnp.concatenate(
        [norm_gains, norm_shifts, jnp.zeros((2, norm_gains.shape[1]), BFLOAT)]
    ).astype(jnp.float32)
    _, slots_here, length, model_width = decoder_states.shape
    slots = slots_here * lax.axis_size("pa")
    states = decoder_states.reshape(slots_here * length, model_width)
    memory = encoder_memory.reshape(-1, model_width)
    slot_index = lax.axis_index("pa") * slots_here + jnp.arange(slots_here)
    usable = (slot_mask[0] == 1) & (slot_index < slot_counts[0])
    marks = jnp.concatenate(
        [
            target_tokens.reshape(1, slots_here * length).astype(jnp.float32),
            jnp.repeat(log_prior, length, axis=1),
            jnp.repeat(usable[None].astype(jnp.float32), length, axis=1),
            jnp.zeros((5, slots_here * length), jnp.float32),
        ]
    )
    matrices, marks, norms, kept = forward_layer(
        shards, norm_rows, marks, states, memory, length
    )
    small, grad_embed, grad_third = vocabulary_head(
        kept[-1], marks, embedding, slots, length
    )
    loss_value = small[0, 0]
    grad_prior = small[1].reshape(1, slots_here, length)[:, :, 0]
    shares, norm_sums, grad_inputs, grad_encoded, pieces = backward_layer(
        matrices,
        kept[:11] + kept[12:15] + (states, memory),
        kept[11],
        norms,
        grad_third,
        grad_embed,
        length,
    )
    pieces = pieces.reshape(4 * grad_embed.shape[0], model_width)
    shares, (grad_embed, grad_inputs, grad_encoded, grad_gains, grad_shifts) = widen(
        shares,
        pieces,
        norm_sums,
        (grad_inputs, grad_encoded),
        embedding.shape[0],
        norm_gains.shape[1],
    )
    return (
        loss_value,
        grad_inputs.reshape(decoder_states.shape),
        grad_encoded.reshape(encoder_memory.shape),
        grad_prior,
    ) + tuple(shares) + (grad_embed, grad_gains, grad_shifts)


def solution(mesh):
    own_kernels = mesh.shape["pb"] == 4 and mesh.shape["pa"] == 8
    return jax.shard_map(
        per_device_kernels if own_kernels else per_device,
        mesh=mesh,
        in_specs=(
            P("pb", "pa", None, None),
            P("pb", "pa", None, None),
            P("pb", "pa", None),
            P("pb", "pa"),
            P("pb"),
            P("pb", "pa"),
            P("pa", None),
            P("pa", None),
            P("pa", None),
            P("pa", None),
            P("pa", None),
            P("pa", None),
            P("pa", None),
            P("pa", None),
            P(None, "pa"),
            P(None, "pa"),
        ),
        out_specs=(
            P(),
            P("pb", "pa", None, None),
            P("pb", "pa", None, None),
            P("pb", "pa"),
            P("pa", None),
            P("pa", None),
            P("pa", None),
            P("pa", None),
            P("pa", None),
            P("pa", None),
            P("pa", None),
            P("pa", None),
            P(None, "pa"),
            P(None, "pa"),
        ),
        check_vma=False,
    )
```
